32 devices in a mesh: gz: 16 (over z, y, core), gx: 2 (over x).
Axes of the slice: x: 2, y: 2, z: 4, core: 2. Of those that a mesh axis runs over, the one named last changes fastest.
Arguments:
- ending_rightward_adjoint: float32 [2, 1024, 2048], P(None, 'gz', 'gx'), may hold values from -6 to 6
- ending_leftward_adjoint: float32 [2, 1024, 2048], P(None, 'gz', 'gx'), may hold values from -6 to 6
- ending_population_adjoint: float32 [1024, 2048], P('gz', 'gx'), may hold values from -6 to 6
- ending_holeburn_adjoint: float32 [1024, 2048], P('gz', 'gx'), may hold values from -6 to 6
- history_rightward: bfloat16 [4, 2, 1024, 2048], P(None, None, 'gz', 'gx'), may hold values from -4 to 4
- history_leftward: bfloat16 [4, 2, 1024, 2048], P(None, None, 'gz', 'gx'), may hold values from -4 to 4
- history_population: bfloat16 [4, 1024, 2048], P(None, 'gz', 'gx'), may hold values from 0.5 to 2
- history_holeburn: bfloat16 [4, 1024, 2048], P(None, 'gz', 'gx'), may hold values from -4 to 4
- segment_passive_attenuation: bfloat16 [1024, 2048], P('gz', 'gx'), may hold values from 0.049804688 to 0.59765625
Outputs:
- forward_adjoint: float32 [2, 1024, 2048], P(None, 'gz', 'gx')
- backward_adjoint: float32 [2, 1024, 2048], P(None, 'gz', 'gx')
- carrier_adjoint: float32 [1024, 2048], P('gz', 'gx')
- grating_adjoint: float32 [1024, 2048], P('gz', 'gx')
- current_gradient: float32 [2048], P('gx')
The draws below stay inside these ranges and needn't reach their ends.
All inputs are finite; a program needn't handle non-finite values.
Results may differ from the reference program's by a relative error of at most 0.0004.
Values may be sent and summed in bfloat16 or wider, within the bound.
No kernel may reach another device: no remote copies, remote signals or barrier semaphores. Data moves between devices by JAX's collectives and lax.ppermute only.
A program may use at most 64 MiB of HBM per device.

```python
import math
import jax
import jax.numpy as jnp
from jax import lax

TRANSVERSE_NODES = 2048
ADJOINT_PASSES = 4
AXIAL_SEGMENTS = 1024
DIFF = 512


def level_of(key, shape, shards, least, high):
    level = 1.0
    for position, blocks in shards:
        draws = jax.random.uniform(jax.random.fold_in(jax.random.fold_in(key, 6), position), (blocks,), jnp.float32, least / len(shards), high / len(shards))
        level = level * jnp.repeat(jnp.exp(draws), shape[position] // blocks).reshape((-1,) + (1,) * (len(shape) - 1 - position))
    return level


def normal_values(own_key, extent, scale, reach, cuts=(), held_as=jnp.bfloat16):
    entries = scale * jax.random.normal(own_key, extent, jnp.float32)
    if cuts:
        entries = entries * level_of(own_key, extent, cuts, -0.22, 0.18)
    return jnp.clip(entries, -reach, reach).astype(held_as)


def setup_inputs(seed: int = 0) -> dict:
    streams_of = jax.random.split(jax.random.key(seed), 10)
    ending_rightward_adjoint = normal_values(streams_of[0], (2, AXIAL_SEGMENTS, TRANSVERSE_NODES), 1.0, 6.0, ((1, 16), (2, 2)), jnp.float32)
    ending_leftward_adjoint = normal_values(streams_of[1], (2, AXIAL_SEGMENTS, TRANSVERSE_NODES), 1.0, 6.0, ((1, 16), (2, 2)), jnp.float32)
    ending_population_adjoint = normal_values(streams_of[2], (AXIAL_SEGMENTS, TRANSVERSE_NODES), 1.0, 6.0, ((0, 16), (1, 2)), jnp.float32)
    ending_holeburn_adjoint = normal_values(streams_of[3], (AXIAL_SEGMENTS, TRANSVERSE_NODES), 1.0, 6.0, ((0, 16), (1, 2)), jnp.float32)
    history_rightward = normal_values(streams_of[4], (ADJOINT_PASSES, 2, AXIAL_SEGMENTS, TRANSVERSE_NODES), 0.7, 4.0, ((2, 16), (3, 2)))
    history_leftward = normal_values(streams_of[5], (ADJOINT_PASSES, 2, AXIAL_SEGMENTS, TRANSVERSE_NODES), 0.7, 4.0, ((2, 16), (3, 2)))
    history_population = jnp.clip(0.5 + 1.5 * jax.random.uniform(streams_of[6], (ADJOINT_PASSES, AXIAL_SEGMENTS, TRANSVERSE_NODES), jnp.float32) ** level_of(streams_of[6], (ADJOINT_PASSES, AXIAL_SEGMENTS, TRANSVERSE_NODES), ((1, 16), (2, 2)), -0.2, 0.2), 0.5, 2.0).astype(jnp.bfloat16)
    history_holeburn = normal_values(streams_of[7], (ADJOINT_PASSES, AXIAL_SEGMENTS, TRANSVERSE_NODES), 0.5, 4.0, ((1, 16), (2, 2)))
    segment_passive_attenuation = jnp.clip(jnp.exp(math.log(0.59765625) - 2.4849066 * jax.random.uniform(streams_of[8], (AXIAL_SEGMENTS, TRANSVERSE_NODES), jnp.float32) ** level_of(streams_of[8], (AXIAL_SEGMENTS, TRANSVERSE_NODES), ((0, 16), (1, 2)), -0.2, 0.2)), 0.049804688, 0.59765625).astype(jnp.bfloat16)
    return {"ending_rightward_adjoint": ending_rightward_adjoint, "ending_leftward_adjoint": ending_leftward_adjoint, "ending_population_adjoint": ending_population_adjoint, "ending_holeburn_adjoint": ending_holeburn_adjoint, "history_rightward": history_rightward, "history_leftward": history_leftward, "history_population": history_population, "history_holeburn": history_holeburn, "segment_passive_attenuation": segment_passive_attenuation}


FRONT_FACET = 0.3
REAR_FACET = 0.9
GAIN_SLOPE_RATE = 0.3
ALPHA_LINEWIDTH = 2.0
COUPLING = 0.5
CLOCK_DELTA = 0.3
DENSITY_LIFETIME = 2.0
GRATING_LIFE = 0.75
TRANSVERSE_DIFFUS = 0.2

def diffract(stacked):
    width = stacked.shape[-1]
    wavenum = jnp.arange(width, dtype=jnp.int32)
    signed = jnp.where(wavenum < width // 2, wavenum, wavenum - width)
    angle = (signed * signed).astype(jnp.float32) * (DIFF / (width / 2) ** 2)
    spectrum = jnp.fft.fft(stacked[0] + 1j * stacked[1], axis=-1)
    result = jnp.fft.ifft(spectrum * jnp.exp(1j * angle), axis=-1)
    return jnp.stack([jnp.real(result), jnp.imag(result)])

def multiplier_revision(rightward_multiplier, leftward_multiplier, population_multiplier, holeburn_multiplier, measured_rightward, measured_leftward, rightward_wave, leftward_wave, population_level, holeburn_magnitude, attenuation_factor, transverse_curvature):
    rightward_inphase, rightward_quadrature = (rightward_wave[0], rightward_wave[1])
    leftward_inphase, leftward_quadrature = (leftward_wave[0], leftward_wave[1])
    measured_rightward_inphase, measured_rightward_quadrature = (measured_rightward[0], measured_rightward[1])
    measured_leftward_inphase, measured_leftward_quadrature = (measured_leftward[0], measured_leftward[1])
    surplus_population = population_level - 1.0
    amplification_inphase = 1.0 + 0.5 * (GAIN_SLOPE_RATE * surplus_population - attenuation_factor)
    amplification_quadrature = 0.5 * GAIN_SLOPE_RATE * ALPHA_LINEWIDTH * surplus_population
    joined_waves = COUPLING * holeburn_magnitude
    population_derivative = 2.0 * CLOCK_DELTA * GAIN_SLOPE_RATE * surplus_population * population_multiplier
    holeburn_derivative = 2.0 * CLOCK_DELTA * holeburn_multiplier
    revised_rightward_inphase = amplification_inphase * measured_rightward_inphase - amplification_quadrature * measured_rightward_quadrature + joined_waves * measured_leftward_quadrature - population_derivative * rightward_inphase + holeburn_derivative * leftward_inphase
    revised_rightward_quadrature = amplification_inphase * measured_rightward_quadrature + amplification_quadrature * measured_rightward_inphase - joined_waves * measured_leftward_inphase - population_derivative * rightward_quadrature + holeburn_derivative * leftward_quadrature
    revised_leftward_inphase = amplification_inphase * measured_leftward_inphase - amplification_quadrature * measured_leftward_quadrature + joined_waves * measured_rightward_quadrature - population_derivative * leftward_inphase + holeburn_derivative * rightward_inphase
    revised_leftward_quadrature = amplification_inphase * measured_leftward_quadrature + amplification_quadrature * measured_leftward_inphase - joined_waves * measured_rightward_inphase - population_derivative * leftward_quadrature + holeburn_derivative * rightward_quadrature
    light_intensity = rightward_inphase * rightward_inphase + rightward_quadrature * rightward_quadrature + leftward_inphase * leftward_inphase + leftward_quadrature * leftward_quadrature
    amplification_share = measured_rightward_inphase * (rightward_inphase + ALPHA_LINEWIDTH * rightward_quadrature) + measured_rightward_quadrature * (rightward_quadrature - ALPHA_LINEWIDTH * rightward_inphase) + measured_leftward_inphase * (leftward_inphase + ALPHA_LINEWIDTH * leftward_quadrature) + measured_leftward_quadrature * (leftward_quadrature - ALPHA_LINEWIDTH * leftward_inphase)
    revised_population = population_multiplier * (1.0 - CLOCK_DELTA / DENSITY_LIFETIME - CLOCK_DELTA * GAIN_SLOPE_RATE * light_intensity) + TRANSVERSE_DIFFUS * transverse_curvature + 0.5 * GAIN_SLOPE_RATE * amplification_share
    fresh_holeburn = holeburn_multiplier * (1.0 - CLOCK_DELTA / GRATING_LIFE) + COUPLING * (measured_rightward_quadrature * leftward_inphase - measured_rightward_inphase * leftward_quadrature + measured_leftward_quadrature * rightward_inphase - measured_leftward_inphase * rightward_quadrature)
    return (jnp.stack([revised_rightward_inphase, revised_rightward_quadrature]), jnp.stack([revised_leftward_inphase, revised_leftward_quadrature]), revised_population, fresh_holeburn)

def reference(ending_rightward_adjoint, ending_leftward_adjoint, ending_population_adjoint, ending_holeburn_adjoint, history_rightward, history_leftward, history_population, history_holeburn, segment_passive_attenuation):
    rightward_multiplier, leftward_multiplier = (ending_rightward_adjoint, ending_leftward_adjoint)
    population_multiplier, holeburn_multiplier = (ending_population_adjoint, ending_holeburn_adjoint)
    attenuation_factor = segment_passive_attenuation.astype(jnp.float32)
    zpos = jnp.arange(AXIAL_SEGMENTS, dtype=jnp.int32).astype(jnp.float32)
    scaling_factor = 1.0 + 2.0 * zpos / (AXIAL_SEGMENTS - 1)
    shape_curve = jnp.zeros((TRANSVERSE_NODES,), jnp.float32)
    for moment_position in range(ADJOINT_PASSES - 1, -1, -1):
        shape_curve = shape_curve + lax.optimization_barrier(jnp.sum(scaling_factor[:, None] * population_multiplier, axis=0))
        lam_fwd = jnp.concatenate([rightward_multiplier[:, 1:, :], FRONT_FACET * leftward_multiplier[:, -1:, :]], axis=1)
        lam_bwd = jnp.concatenate([REAR_FACET * rightward_multiplier[:, :1, :], leftward_multiplier[:, :-1, :]], axis=1)
        measured_rightward = diffract(lam_fwd)
        measured_leftward = diffract(lam_bwd)
        bordered_array = jnp.pad(population_multiplier, ((0, 0), (1, 1)))
        transverse_curvature = bordered_array[:, 2:] + bordered_array[:, :-2] - 2.0 * population_multiplier
        rightward_multiplier, leftward_multiplier, population_multiplier, holeburn_multiplier = multiplier_revision(rightward_multiplier, leftward_multiplier, population_multiplier, holeburn_multiplier, measured_rightward, measured_leftward, history_rightward[moment_position].astype(jnp.float32), history_leftward[moment_position].astype(jnp.float32), history_population[moment_position].astype(jnp.float32), history_holeburn[moment_position].astype(jnp.float32), attenuation_factor, transverse_curvature)
    derivative_vector = CLOCK_DELTA * shape_curve / math.sqrt(AXIAL_SEGMENTS)
    return (rightward_multiplier, leftward_multiplier, population_multiplier, holeburn_multiplier, derivative_vector)
```

```python
import math

import jax
import jax.numpy as jnp
from jax import lax
from jax.sharding import PartitionSpec as P

DIFF = 512


FRONT_FACET = 0.3
REAR_FACET = 0.9
GAIN_SLOPE_RATE = 0.3
ALPHA_LINEWIDTH = 2.0
COUPLING = 0.5
CLOCK_DELTA = 0.3
DENSITY_LIFETIME = 2.0
GRATING_LIFE = 0.75
TRANSVERSE_DIFFUS = 0.2


def passed_along(value, axis, steps):
    count = lax.axis_size(axis)
    initial, last = (max(0, -steps), min(count, count - steps))
    return lax.ppermute(value, axis, [(source, source + steps) for source in range(initial, last)])


def with_halo(block, sides, width):
    for axis, dim in sides:
        count = lax.axis_size(axis)
        forward = [(i, i + 1) for i in range(count - 1)]
        backward = [(target, source) for source, target in forward]
        low = lax.ppermute(
            lax.slice_in_dim(block, block.shape[dim] - width, None, axis=dim), axis, forward
        )
        high = lax.ppermute(lax.slice_in_dim(block, 0, width, axis=dim), axis, backward)
        block = jnp.concatenate([low, block, high], axis=dim)
    return block


def rotate(source_re, source_im, cosine, sine, form, sign):
    exact = lax.Precision.HIGHEST
    out_re = jnp.einsum(form, source_re, cosine, precision=exact) + sign * jnp.einsum(
        form, source_im, sine, precision=exact
    )
    out_im = jnp.einsum(form, source_im, cosine, precision=exact) - sign * jnp.einsum(
        form, source_re, sine, precision=exact
    )
    return (out_re, out_im)


def transform(stacked):
    count = stacked.shape[1]
    width = stacked.shape[2]
    second = min(128, width // 2)
    first = width // second
    two_pi = 2.0 * math.pi
    index_a = jnp.arange(first, dtype=jnp.int32)
    index_b = jnp.arange(second, dtype=jnp.int32)
    angle_a = two_pi * (index_a[:, None] * index_a[None, :] % first).astype(jnp.float32) / first
    angle_b = two_pi * (index_b[:, None] * index_b[None, :] % second).astype(jnp.float32) / second
    angle_t = two_pi * (index_a[:, None] * index_b[None, :] % width).astype(jnp.float32) / width
    cos_a, sin_a = (jnp.cos(angle_a), jnp.sin(angle_a))
    cos_b, sin_b = (jnp.cos(angle_b), jnp.sin(angle_b))
    cos_t, sin_t = (jnp.cos(angle_t), jnp.sin(angle_t))
    wavenum = index_a[:, None] + first * index_b[None, :]
    signed = jnp.where(wavenum < width // 2, wavenum, wavenum - width)
    phase = (signed * signed).astype(jnp.float32) * (DIFF / (width / 2) ** 2)
    cos_p, sin_p = (jnp.cos(phase), jnp.sin(phase))
    real_in = stacked[0].reshape(count, first, second)
    imag_in = stacked[1].reshape(count, first, second)
    step_re, step_im = rotate(real_in, imag_in, cos_a, sin_a, "nab,ak->nkb", 1.0)
    twist_re = step_re * cos_t + step_im * sin_t
    twist_im = step_im * cos_t - step_re * sin_t
    spec_re, spec_im = rotate(twist_re, twist_im, cos_b, sin_b, "nkb,bj->nkj", 1.0)
    moved_re = spec_re * cos_p - spec_im * sin_p
    moved_im = spec_re * sin_p + spec_im * cos_p
    back_re, back_im = rotate(moved_re, moved_im, cos_b, sin_b, "nkj,jb->nkb", -1.0)
    untw_re = back_re * cos_t - back_im * sin_t
    untw_im = back_im * cos_t + back_re * sin_t
    final_re, final_im = rotate(untw_re, untw_im, cos_a, sin_a, "nkb,ka->nab", -1.0)
    return jnp.stack([final_re.reshape(count, width), final_im.reshape(count, width)]) / width


def encoded(value):
    top = jnp.maximum(jnp.max(jnp.abs(value)), 1e-30)
    unit = value / top
    square = unit * unit
    fourth = square * square
    return ((unit * jnp.abs(unit) * square * fourth) * 1e30).astype(jnp.bfloat16), top


def decoded(code, top):
    value = code.astype(jnp.float32)
    size = jnp.sqrt(jnp.sqrt(jnp.sqrt(jnp.abs(value) * 1e-30)))
    return jnp.where(value < 0.0, -size, size) * top


def other_half(value):
    swap = [(0, 1), (1, 0)]
    code, top = encoded(value)
    code = lax.ppermute(code, "gx", swap)
    top = lax.ppermute(jnp.full((8, 128), top, jnp.float32), "gx", swap)
    return decoded(code, top[0, 0])


def added_up(value, axis):
    count = lax.axis_size(axis)
    if count & (count - 1):
        return lax.psum(value, axis)
    reach = 1
    while reach < count:
        value = value + lax.ppermute(value, axis, [(i, i ^ reach) for i in range(count)])
        reach *= 2
    return value


def lateral_work(parts):
    return (transform(parts[0]), transform(parts[1]))


def multiplier_revision(
    population_multiplier,
    holeburn_multiplier,
    measured_rightward,
    measured_leftward,
    rightward_wave,
    leftward_wave,
    population_level,
    holeburn_magnitude,
    attenuation_factor,
    transverse_curvature,
):
    rightward_inphase, rightward_quadrature = (rightward_wave[0], rightward_wave[1])
    leftward_inphase, leftward_quadrature = (leftward_wave[0], leftward_wave[1])
    measured_rightward_inphase, measured_rightward_quadrature = (
        measured_rightward[0],
        measured_rightward[1],
    )
    measured_leftward_inphase, measured_leftward_quadrature = (
        measured_leftward[0],
        measured_leftward[1],
    )
    surplus_population = population_level - 1.0
    amplification_inphase = 1.0 + 0.5 * (GAIN_SLOPE_RATE * surplus_population - attenuation_factor)
    amplification_quadrature = 0.5 * GAIN_SLOPE_RATE * ALPHA_LINEWIDTH * surplus_population
    joined_waves = COUPLING * holeburn_magnitude
    population_derivative = (
        2.0 * CLOCK_DELTA * GAIN_SLOPE_RATE * surplus_population * population_multiplier
    )
    holeburn_derivative = 2.0 * CLOCK_DELTA * holeburn_multiplier
    revised_rightward_inphase = (
        amplification_inphase * measured_rightward_inphase
        - amplification_quadrature * measured_rightward_quadrature
        + joined_waves * measured_leftward_quadrature
        - population_derivative * rightward_inphase
        + holeburn_derivative * leftward_inphase
    )
    revised_rightward_quadrature = (
        amplification_inphase * measured_rightward_quadrature
        + amplification_quadrature * measured_rightward_inphase
        - joined_waves * measured_leftward_inphase
        - population_derivative * rightward_quadrature
        + holeburn_derivative * leftward_quadrature
    )
    revised_leftward_inphase = (
        amplification_inphase * measured_leftward_inphase
        - amplification_quadrature * measured_leftward_quadrature
        + joined_waves * measured_rightward_quadrature
        - population_derivative * leftward_inphase
        + holeburn_derivative * rightward_inphase
    )
    revised_leftward_quadrature = (
        amplification_inphase * measured_leftward_quadrature
        + amplification_quadrature * measured_leftward_inphase
        - joined_waves * measured_rightward_inphase
        - population_derivative * leftward_quadrature
        + holeburn_derivative * rightward_quadrature
    )
    light_intensity = (
        rightward_inphase * rightward_inphase
        + rightward_quadrature * rightward_quadrature
        + leftward_inphase * leftward_inphase
        + leftward_quadrature * leftward_quadrature
    )
    amplification_share = (
        measured_rightward_inphase * (rightward_inphase + ALPHA_LINEWIDTH * rightward_quadrature)
        + measured_rightward_quadrature
        * (rightward_quadrature - ALPHA_LINEWIDTH * rightward_inphase)
        + measured_leftward_inphase * (leftward_inphase + ALPHA_LINEWIDTH * leftward_quadrature)
        + measured_leftward_quadrature * (leftward_quadrature - ALPHA_LINEWIDTH * leftward_inphase)
    )
    revised_population = (
        population_multiplier
        * (1.0 - CLOCK_DELTA / DENSITY_LIFETIME - CLOCK_DELTA * GAIN_SLOPE_RATE * light_intensity)
        + TRANSVERSE_DIFFUS * transverse_curvature
        + 0.5 * GAIN_SLOPE_RATE * amplification_share
    )
    fresh_holeburn = holeburn_multiplier * (1.0 - CLOCK_DELTA / GRATING_LIFE) + COUPLING * (
        measured_rightward_quadrature * leftward_inphase
        - measured_rightward_inphase * leftward_quadrature
        + measured_leftward_quadrature * rightward_inphase
        - measured_leftward_inphase * rightward_quadrature
    )
    return (
        jnp.stack([revised_rightward_inphase, revised_rightward_quadrature]),
        jnp.stack([revised_leftward_inphase, revised_leftward_quadrature]),
        revised_population,
        fresh_holeburn,
    )


def per_device(
    ending_rightward_adjoint,
    ending_leftward_adjoint,
    ending_population_adjoint,
    ending_holeburn_adjoint,
    history_rightward,
    history_leftward,
    history_population,
    history_holeburn,
    segment_passive_attenuation,
):
    columns = ending_rightward_adjoint.shape[2]
    rows = ending_rightward_adjoint.shape[1]
    blocks = lax.axis_size("gz")
    position = lax.axis_index("gz")
    cells = rows * blocks
    zpos = (position * rows + jnp.arange(rows, dtype=jnp.int32)).astype(jnp.float32)
    scaling_factor = 1.0 + 2.0 * zpos / (cells - 1)
    rightward_multiplier, leftward_multiplier = (ending_rightward_adjoint, ending_leftward_adjoint)
    population_multiplier, holeburn_multiplier = (
        ending_population_adjoint,
        ending_holeburn_adjoint,
    )
    attenuation_factor = segment_passive_attenuation.astype(jnp.float32)
    shape_curve = jnp.zeros((columns,), jnp.float32)
    for moment_position in range(history_rightward.shape[0] - 1, -1, -1):
        shape_curve = shape_curve + jnp.sum(scaling_factor[:, None] * population_multiplier, axis=0)
        above = passed_along(rightward_multiplier[:, :1, :], "gz", -1)
        below = passed_along(leftward_multiplier[:, -1:, :], "gz", 1)
        top_row = jnp.where(
            position == blocks - 1, FRONT_FACET * leftward_multiplier[:, -1:, :], above
        )
        bottom_row = jnp.where(position == 0, REAR_FACET * rightward_multiplier[:, :1, :], below)
        lam_fwd = jnp.concatenate([rightward_multiplier[:, 1:, :], top_row], axis=1)
        lam_bwd = jnp.concatenate([bottom_row, leftward_multiplier[:, :-1, :]], axis=1)
        if lax.axis_size("gx") == 2:
            both = jnp.concatenate([lam_fwd, lam_bwd])
            other = other_half(both)
            first = lax.axis_index("gx") == 0
            whole = jnp.concatenate(
                [jnp.where(first, both, other), jnp.where(first, other, both)], axis=2
            )
            whole_fwd, whole_bwd = whole[:2], whole[2:]
        else:
            whole_fwd, whole_bwd = (
                lax.all_gather(lam_fwd, "gx", axis=2, tiled=True),
                lax.all_gather(lam_bwd, "gx", axis=2, tiled=True),
            )
        start = lax.axis_index("gx") * columns
        done_fwd, done_bwd = lateral_work((whole_fwd, whole_bwd))
        measured_rightward = lax.dynamic_slice_in_dim(done_fwd, start, columns, 2)
        measured_leftward = lax.dynamic_slice_in_dim(done_bwd, start, columns, 2)
        bordered_array = with_halo(population_multiplier, (("gx", 1),), 1)
        transverse_curvature = (
            bordered_array[:, 2:] + bordered_array[:, :-2] - 2.0 * population_multiplier
        )
        rightward_multiplier, leftward_multiplier, population_multiplier, holeburn_multiplier = (
            multiplier_revision(
                population_multiplier,
                holeburn_multiplier,
                measured_rightward,
                measured_leftward,
                history_rightward[moment_position].astype(jnp.float32),
                history_leftward[moment_position].astype(jnp.float32),
                history_population[moment_position].astype(jnp.float32),
                history_holeburn[moment_position].astype(jnp.float32),
                attenuation_factor,
                transverse_curvature,
            )
        )
    total = added_up(shape_curve, "gz")
    derivative_vector = CLOCK_DELTA * total / math.sqrt(cells)
    return (
        rightward_multiplier,
        leftward_multiplier,
        population_multiplier,
        holeburn_multiplier,
        derivative_vector,
    )


def solution(mesh):
    return jax.shard_map(
        per_device,
        mesh=mesh,
        in_specs=(
            P(None, "gz", "gx"),
            P(None, "gz", "gx"),
            P("gz", "gx"),
            P("gz", "gx"),
            P(None, None, "gz", "gx"),
            P(None, None, "gz", "gx"),
            P(None, "gz", "gx"),
            P(None, "gz", "gx"),
            P("gz", "gx"),
        ),
        out_specs=(P(None, "gz", "gx"), P(None, "gz", "gx"), P("gz", "gx"), P("gz", "gx"), P("gx")),
        check_vma=False,
    )
```

```python
import functools
import math

import jax
import jax.numpy as jnp
import ml_dtypes
import numpy as np
from jax import lax
from jax.experimental import pallas as pl
from jax.experimental.pallas import tpu as pltpu
from jax.sharding import PartitionSpec as P

DIFF = 512


FRONT_FACET = 0.3
REAR_FACET = 0.9
GAIN_SLOPE_RATE = 0.3
ALPHA_LINEWIDTH = 2.0
COUPLING = 0.5
CLOCK_DELTA = 0.3
DENSITY_LIFETIME = 2.0
GRATING_LIFE = 0.75
TRANSVERSE_DIFFUS = 0.2


def passed_along(value, axis, steps):
    count = lax.axis_size(axis)
    initial, last = (max(0, -steps), min(count, count - steps))
    return lax.ppermute(value, axis, [(source, source + steps) for source in range(initial, last)])


def with_halo(block, sides, width):
    for axis, dim in sides:
        count = lax.axis_size(axis)
        forward = [(i, i + 1) for i in range(count - 1)]
        backward = [(target, source) for source, target in forward]
        low = lax.ppermute(
            lax.slice_in_dim(block, block.shape[dim] - width, None, axis=dim), axis, forward
        )
        high = lax.ppermute(lax.slice_in_dim(block, 0, width, axis=dim), axis, backward)
        block = jnp.concatenate([low, block, high], axis=dim)
    return block


def rotate(source_re, source_im, cosine, sine, form, sign):
    exact = lax.Precision.HIGHEST
    out_re = jnp.einsum(form, source_re, cosine, precision=exact) + sign * jnp.einsum(
        form, source_im, sine, precision=exact
    )
    out_im = jnp.einsum(form, source_im, cosine, precision=exact) - sign * jnp.einsum(
        form, source_re, sine, precision=exact
    )
    return (out_re, out_im)


def transform(stacked):
    count = stacked.shape[1]
    width = stacked.shape[2]
    second = min(128, width // 2)
    first = width // second
    two_pi = 2.0 * math.pi
    index_a = jnp.arange(first, dtype=jnp.int32)
    index_b = jnp.arange(second, dtype=jnp.int32)
    angle_a = two_pi * (index_a[:, None] * index_a[None, :] % first).astype(jnp.float32) / first
    angle_b = two_pi * (index_b[:, None] * index_b[None, :] % second).astype(jnp.float32) / second
    angle_t = two_pi * (index_a[:, None] * index_b[None, :] % width).astype(jnp.float32) / width
    cos_a, sin_a = (jnp.cos(angle_a), jnp.sin(angle_a))
    cos_b, sin_b = (jnp.cos(angle_b), jnp.sin(angle_b))
    cos_t, sin_t = (jnp.cos(angle_t), jnp.sin(angle_t))
    wavenum = index_a[:, None] + first * index_b[None, :]
    signed = jnp.where(wavenum < width // 2, wavenum, wavenum - width)
    phase = (signed * signed).astype(jnp.float32) * (DIFF / (width / 2) ** 2)
    cos_p, sin_p = (jnp.cos(phase), jnp.sin(phase))
    real_in = stacked[0].reshape(count, first, second)
    imag_in = stacked[1].reshape(count, first, second)
    step_re, step_im = rotate(real_in, imag_in, cos_a, sin_a, "nab,ak->nkb", 1.0)
    twist_re = step_re * cos_t + step_im * sin_t
    twist_im = step_im * cos_t - step_re * sin_t
    spec_re, spec_im = rotate(twist_re, twist_im, cos_b, sin_b, "nkb,bj->nkj", 1.0)
    moved_re = spec_re * cos_p - spec_im * sin_p
    moved_im = spec_re * sin_p + spec_im * cos_p
    back_re, back_im = rotate(moved_re, moved_im, cos_b, sin_b, "nkj,jb->nkb", -1.0)
    untw_re = back_re * cos_t - back_im * sin_t
    untw_im = back_im * cos_t + back_re * sin_t
    final_re, final_im = rotate(untw_re, untw_im, cos_a, sin_a, "nkb,ka->nab", -1.0)
    return jnp.stack([final_re.reshape(count, width), final_im.reshape(count, width)]) / width


def added_up(value, axis):
    count = lax.axis_size(axis)
    if count & (count - 1):
        return lax.psum(value, axis)
    reach = 1
    while reach < count:
        value = value + lax.ppermute(value, axis, [(i, i ^ reach) for i in range(count)])
        reach *= 2
    return value


def lateral_work(parts):
    return (transform(parts[0]), transform(parts[1]))


def multiplier_revision(
    population_multiplier,
    holeburn_multiplier,
    measured_rightward,
    measured_leftward,
    rightward_wave,
    leftward_wave,
    population_level,
    holeburn_magnitude,
    attenuation_factor,
    transverse_curvature,
):
    rightward_inphase, rightward_quadrature = (rightward_wave[0], rightward_wave[1])
    leftward_inphase, leftward_quadrature = (leftward_wave[0], leftward_wave[1])
    measured_rightward_inphase, measured_rightward_quadrature = (
        measured_rightward[0],
        measured_rightward[1],
    )
    measured_leftward_inphase, measured_leftward_quadrature = (
        measured_leftward[0],
        measured_leftward[1],
    )
    surplus_population = population_level - 1.0
    amplification_inphase = 1.0 + 0.5 * (GAIN_SLOPE_RATE * surplus_population - attenuation_factor)
    amplification_quadrature = 0.5 * GAIN_SLOPE_RATE * ALPHA_LINEWIDTH * surplus_population
    joined_waves = COUPLING * holeburn_magnitude
    population_derivative = (
        2.0 * CLOCK_DELTA * GAIN_SLOPE_RATE * surplus_population * population_multiplier
    )
    holeburn_derivative = 2.0 * CLOCK_DELTA * holeburn_multiplier
    revised_rightward_inphase = (
        amplification_inphase * measured_rightward_inphase
        - amplification_quadrature * measured_rightward_quadrature
        + joined_waves * measured_leftward_quadrature
        - population_derivative * rightward_inphase
        + holeburn_derivative * leftward_inphase
    )
    revised_rightward_quadrature = (
        amplification_inphase * measured_rightward_quadrature
        + amplification_quadrature * measured_rightward_inphase
        - joined_waves * measured_leftward_inphase
        - population_derivative * rightward_quadrature
        + holeburn_derivative * leftward_quadrature
    )
    revised_leftward_inphase = (
        amplification_inphase * measured_leftward_inphase
        - amplification_quadrature * measured_leftward_quadrature
        + joined_waves * measured_rightward_quadrature
        - population_derivative * leftward_inphase
        + holeburn_derivative * rightward_inphase
    )
    revised_leftward_quadrature = (
        amplification_inphase * measured_leftward_quadrature
        + amplification_quadrature * measured_leftward_inphase
        - joined_waves * measured_rightward_inphase
        - population_derivative * leftward_quadrature
        + holeburn_derivative * rightward_quadrature
    )
    light_intensity = (
        rightward_inphase * rightward_inphase
        + rightward_quadrature * rightward_quadrature
        + leftward_inphase * leftward_inphase
        + leftward_quadrature * leftward_quadrature
    )
    amplification_share = (
        measured_rightward_inphase * (rightward_inphase + ALPHA_LINEWIDTH * rightward_quadrature)
        + measured_rightward_quadrature
        * (rightward_quadrature - ALPHA_LINEWIDTH * rightward_inphase)
        + measured_leftward_inphase * (leftward_inphase + ALPHA_LINEWIDTH * leftward_quadrature)
        + measured_leftward_quadrature * (leftward_quadrature - ALPHA_LINEWIDTH * leftward_inphase)
    )
    revised_population = (
        population_multiplier
        * (1.0 - CLOCK_DELTA / DENSITY_LIFETIME - CLOCK_DELTA * GAIN_SLOPE_RATE * light_intensity)
        + TRANSVERSE_DIFFUS * transverse_curvature
        + 0.5 * GAIN_SLOPE_RATE * amplification_share
    )
    fresh_holeburn = holeburn_multiplier * (1.0 - CLOCK_DELTA / GRATING_LIFE) + COUPLING * (
        measured_rightward_quadrature * leftward_inphase
        - measured_rightward_inphase * leftward_quadrature
        + measured_leftward_quadrature * rightward_inphase
        - measured_leftward_inphase * rightward_quadrature
    )
    return (
        jnp.stack([revised_rightward_inphase, revised_rightward_quadrature]),
        jnp.stack([revised_leftward_inphase, revised_leftward_quadrature]),
        revised_population,
        fresh_holeburn,
    )


def per_device(
    ending_rightward_adjoint,
    ending_leftward_adjoint,
    ending_population_adjoint,
    ending_holeburn_adjoint,
    history_rightward,
    history_leftward,
    history_population,
    history_holeburn,
    segment_passive_attenuation,
):
    columns = ending_rightward_adjoint.shape[2]
    rows = ending_rightward_adjoint.shape[1]
    blocks = lax.axis_size("gz")
    position = lax.axis_index("gz")
    cells = rows * blocks
    zpos = (position * rows + jnp.arange(rows, dtype=jnp.int32)).astype(jnp.float32)
    scaling_factor = 1.0 + 2.0 * zpos / (cells - 1)
    rightward_multiplier, leftward_multiplier = (ending_rightward_adjoint, ending_leftward_adjoint)
    population_multiplier, holeburn_multiplier = (
        ending_population_adjoint,
        ending_holeburn_adjoint,
    )
    attenuation_factor = segment_passive_attenuation.astype(jnp.float32)
    shape_curve = jnp.zeros((columns,), jnp.float32)
    for moment_position in range(history_rightward.shape[0] - 1, -1, -1):
        shape_curve = shape_curve + jnp.sum(scaling_factor[:, None] * population_multiplier, axis=0)
        above = passed_along(rightward_multiplier[:, :1, :], "gz", -1)
        below = passed_along(leftward_multiplier[:, -1:, :], "gz", 1)
        top_row = jnp.where(
            position == blocks - 1, FRONT_FACET * leftward_multiplier[:, -1:, :], above
        )
        bottom_row = jnp.where(position == 0, REAR_FACET * rightward_multiplier[:, :1, :], below)
        lam_fwd = jnp.concatenate([rightward_multiplier[:, 1:, :], top_row], axis=1)
        lam_bwd = jnp.concatenate([bottom_row, leftward_multiplier[:, :-1, :]], axis=1)
        whole_fwd, whole_bwd = (
            lax.all_gather(lam_fwd, "gx", axis=2, tiled=True),
            lax.all_gather(lam_bwd, "gx", axis=2, tiled=True),
        )
        start = lax.axis_index("gx") * columns
        done_fwd, done_bwd = lateral_work((whole_fwd, whole_bwd))
        measured_rightward = lax.dynamic_slice_in_dim(done_fwd, start, columns, 2)
        measured_leftward = lax.dynamic_slice_in_dim(done_bwd, start, columns, 2)
        bordered_array = with_halo(population_multiplier, (("gx", 1),), 1)
        transverse_curvature = (
            bordered_array[:, 2:] + bordered_array[:, :-2] - 2.0 * population_multiplier
        )
        rightward_multiplier, leftward_multiplier, population_multiplier, holeburn_multiplier = (
            multiplier_revision(
                population_multiplier,
                holeburn_multiplier,
                measured_rightward,
                measured_leftward,
                history_rightward[moment_position].astype(jnp.float32),
                history_leftward[moment_position].astype(jnp.float32),
                history_population[moment_position].astype(jnp.float32),
                history_holeburn[moment_position].astype(jnp.float32),
                attenuation_factor,
                transverse_curvature,
            )
        )
    total = added_up(shape_curve, "gz")
    derivative_vector = CLOCK_DELTA * total / math.sqrt(cells)
    return (
        rightward_multiplier,
        leftward_multiplier,
        population_multiplier,
        holeburn_multiplier,
        derivative_vector,
    )

LANES = 128
TILE = 16
POWER = 12
STRETCH = 1211.0
SCALE_LANE = 8


def lateral_matrices(width, blocks):
    lanes = width // blocks
    k = np.arange(width)
    signed = np.where(k < width // 2, k, k - width).astype(np.float64)
    response = np.fft.ifft(np.exp(1j * signed * signed * (DIFF / (width / 2) ** 2)))
    step = np.arange(lanes)
    shift = lanes * np.arange(blocks)[:, None, None] + step[None, None, :] - step[None, :, None]
    kernels = np.fft.fft(response[shift % width], axis=0) / blocks
    top = np.concatenate([kernels.real, kernels.imag], axis=2)
    low = np.concatenate([-kernels.imag, kernels.real], axis=2)
    whole = np.concatenate([top, low], axis=1)
    first = whole.astype(ml_dtypes.bfloat16)
    rest = (whole - first.astype(np.float64)).astype(ml_dtypes.bfloat16)
    return np.stack([first, rest], axis=1)


def block_dft(values, sign):
    count = len(values)
    if count == 1:
        return values
    even = block_dft(values[0::2], sign)
    odd = block_dft(values[1::2], sign)
    out = [None] * count
    for k in range(count // 2):
        (er, ei), (wr, wi) = even[k], odd[k]
        if 4 * k == count:
            plus, minus = (er - wi, ei + wr), (er + wi, ei - wr)
            out[k], out[k + count // 2] = (plus, minus) if sign > 0 else (minus, plus)
            continue
        if k:
            c, s = math.cos(2 * math.pi * k / count), sign * math.sin(2 * math.pi * k / count)
            if 8 * k == count:
                wr, wi = (c * (wr - wi), c * (wr + wi)) if sign > 0 else (c * (wr + wi), c * (wi - wr))
            elif 8 * k == 3 * count:
                wr, wi = (c * (wr + wi), c * (wi - wr)) if sign > 0 else (c * (wr - wi), c * (wr + wi))
            else:
                wr, wi = c * wr - s * wi, c * wi + s * wr
        out[k] = (er + wr, ei + wi)
        out[k + count // 2] = (er - wr, ei - wi)
    return out


def lane(j):
    return pl.ds(pl.multiple_of(j * LANES, LANES), LANES)


def slab(j, rows):
    return pl.ds(pl.multiple_of(j * rows, rows), rows)


def spread(field, work):
    rows = field.shape[1]
    blocks = work.shape[0]

    @pl.loop(0, rows // 8)
    def _(g):
        at = slab(g, 8)
        values = [
            (field[0, at, j * LANES : (j + 1) * LANES], field[1, at, j * LANES : (j + 1) * LANES])
            for j in range(blocks)
        ]
        for q, (re, im) in enumerate(block_dft(values, -1)):
            work[q, at, :LANES] = re
            work[q, at, LANES:] = im


def multiply(work, matrices):
    rows = work.shape[1]

    @pl.loop(0, work.shape[0], unroll=4)
    def _(q):
        value = work[q]
        first = value.astype(jnp.bfloat16)
        rest = (value - first.astype(jnp.float32)).astype(jnp.bfloat16)
        both = jnp.dot(
            jnp.concatenate([first, rest]), matrices[q, 0], preferred_element_type=jnp.float32
        )
        fine = jnp.dot(first, matrices[q, 1], preferred_element_type=jnp.float32)
        work[q] = both[:rows] + (both[rows:] + fine)


def gathered(work, at):
    values = [(work[q, at, :LANES], work[q, at, LANES:]) for q in range(work.shape[0])]
    return block_dft(values, 1)


def filtered(field, work, matrices, copy):
    spread(field, work)
    copy.wait()
    multiply(work, matrices)


def write_filtered(work, forward, backward, down, up):
    rows = work.shape[1] // 2
    for target, base, offset in ((forward, 0, 0), (backward, rows, 8)):

        @pl.loop(0, rows // 8)
        def _(g):
            here = pl.ds(pl.multiple_of(g * 8 + offset, 8), 8)
            for j, pair in enumerate(gathered(work, pl.ds(pl.multiple_of(g * 8 + base, 8), 8))):
                for part in range(2):
                    target[part, here, j * LANES : (j + 1) * LANES] = pair[part]

    for part in range(2):
        down[part : part + 1, :] = forward[part, 0:1, :]
        up[part : part + 1, :] = backward[part, rows + 7 : rows + 8, :]


def size_of(largest):
    top = jnp.max(jnp.max(largest, axis=1, keepdims=True), axis=0, keepdims=True)
    return jnp.maximum(top, 1e-30).astype(jnp.bfloat16).astype(jnp.float32)


def encoded(value, size):
    unit = value * (STRETCH / size)
    square = unit * unit
    fourth = square * square
    return (fourth * fourth * square * (unit * jnp.abs(unit))).astype(jnp.bfloat16)


def decoded(code, size):
    value = code.astype(jnp.float32)
    root = jnp.exp(jnp.log(jnp.abs(value)) * (1.0 / POWER)) * (size / STRETCH)
    return jnp.where(value < 0.0, -root, root)


def side_tile(columns, rows):
    index = lax.broadcasted_iota(jnp.int32, (rows, LANES), 1)
    tile = jnp.zeros((rows, LANES), jnp.float32)
    for at, column in columns:
        tile = jnp.where(index == at, column, tile)
    return tile.astype(jnp.bfloat16)


def sizes_in(tile, count):
    value = tile.astype(jnp.float32)
    return [value[0:1, SCALE_LANE + i : SCALE_LANE + i + 1] for i in range(count)]


def updated(fr, fi, br, bi, wave, population, hole, loss, carrier, grating, lap):
    rr, ri, lr, li = wave
    surplus = population - 1.0
    gain_re = 1.0 + 0.5 * (GAIN_SLOPE_RATE * surplus - loss)
    gain_im = (0.5 * GAIN_SLOPE_RATE * ALPHA_LINEWIDTH) * surplus
    joined = COUPLING * hole
    drive = (2.0 * CLOCK_DELTA * GAIN_SLOPE_RATE) * surplus * carrier
    mix = (2.0 * CLOCK_DELTA) * grating
    new_fr = gain_re * fr - gain_im * fi + joined * bi - drive * rr + mix * lr
    new_fi = gain_re * fi + gain_im * fr - joined * br - drive * ri + mix * li
    new_br = gain_re * br - gain_im * bi + joined * fi - drive * lr + mix * rr
    new_bi = gain_re * bi + gain_im * br - joined * fr - drive * li + mix * ri
    light = rr * rr + ri * ri + lr * lr + li * li
    share = (
        fr * (rr + ALPHA_LINEWIDTH * ri)
        + fi * (ri - ALPHA_LINEWIDTH * rr)
        + br * (lr + ALPHA_LINEWIDTH * li)
        + bi * (li - ALPHA_LINEWIDTH * lr)
    )
    new_carrier = (
        carrier * ((1.0 - CLOCK_DELTA / DENSITY_LIFETIME) - (CLOCK_DELTA * GAIN_SLOPE_RATE) * light)
        + TRANSVERSE_DIFFUS * lap
        + (0.5 * GAIN_SLOPE_RATE) * share
    )
    new_grating = grating * (1.0 - CLOCK_DELTA / GRATING_LIFE) + COUPLING * (
        fi * lr - fr * li + bi * rr - br * ri
    )
    return new_fr, new_fi, new_br, new_bi, new_carrier, new_grating


def curvature(left, mid, right, weight_left, weight_right):
    index = lax.broadcasted_iota(jnp.int32, mid.shape, 1)
    below = jnp.where(index == 0, pltpu.roll(left, 1, 1) * weight_left, pltpu.roll(mid, 1, 1))
    above = jnp.where(
        index == LANES - 1,
        pltpu.roll(right, LANES - 1, 1) * weight_right,
        pltpu.roll(mid, LANES - 1, 1),
    )
    return below + above - 2.0 * mid


def send_fields_kernel(info, forward, backward, out):
    rows, columns = forward.shape[1:]
    half = columns // LANES
    sizes = []
    for f, field in enumerate((forward, backward)):
        largest = jnp.maximum(jnp.abs(field[0]), jnp.abs(field[1]))
        size = size_of(largest)
        sizes.append((SCALE_LANE + f, size))
        for part in range(2):
            code = encoded(field[part], size)
            for j in range(half):
                at = ((2 * f + part) * half + j) * rows
                out[at : at + rows, :] = code[:, j * LANES : (j + 1) * LANES]
    out[4 * half * rows :, :] = side_tile(sizes, rows)


def put_tiles(out, first, value):
    rows, columns = value.shape
    for j in range(columns // LANES):
        at = (first + j) * rows
        out[at : at + rows, :] = value[:, j * LANES : (j + 1) * LANES]


def put_history(out, first, half, forward, backward, population, hole):
    parts = (forward[0], forward[1], backward[0], backward[1], population[...], hole[...])
    for i, value in enumerate(parts):
        put_tiles(out, first + i * half, value)


def send_history_kernel(info, forward, backward, population, hole, out):
    put_history(out, 0, population.shape[1] // LANES, forward, backward, population, hole)


def send_first_kernel(info, loss, carrier, grating, forward, backward, population, hole, out):
    rows, columns = loss.shape
    half = columns // LANES
    put_tiles(out, 0, loss[...])
    sizes = []
    for i, field in enumerate((carrier, grating)):
        value = field[...]
        size = size_of(jnp.abs(value))
        sizes.append((SCALE_LANE + i, size))
        put_tiles(out, (1 + i) * half, encoded(value, size))
    put_history(out, 3 * half, half, forward, backward, population, hole)
    out[9 * half * rows :, :] = side_tile(sizes, rows)


def enter_kernel(info, forward, backward, other, source, tp, tq, down, up, field, work, matrices, sem):
    copy = pltpu.make_async_copy(source, matrices, sem)
    copy.start()
    rows, columns = forward.shape[1:]
    half = columns // LANES
    sizes = sizes_in(other[4 * half * rows :, :], 2)
    for f, mine in enumerate((forward, backward)):
        for part in range(2):
            field[part, f * rows : (f + 1) * rows, :columns] = mine[part]

            @pl.loop(0, half)
            def _(j):
                code = other[slab((2 * f + part) * half + j, rows), :]
                field[part, f * rows : (f + 1) * rows, lane(half + j)] = decoded(code, sizes[f])

    filtered(field, work, matrices, copy)
    write_filtered(work, tp, tq, down, up)


def rows_update(
    info, tp, tq, from_next, from_before, carrier, grating, own, other, own_loss, other_loss,
    field, new_carrier, new_grating, sums_in, sums, cells, last
):
    rows, width = carrier.shape
    half = width // LANES // 2
    columns = half * LANES
    mid = jnp.where(info[0] == 0, 1.0, 0.0)
    wrap = 1.0 - mid
    is_first = info[1] == 1
    is_last = info[2] == 1
    row_index = lax.broadcasted_iota(jnp.int32, (TILE, LANES), 0)
    zero = jnp.zeros((8, LANES), jnp.float32)

    def step(jj, most):
        for side in range(2):
            j = jj + side * half
            here = lane(j)
            left_at = lane(jnp.where(j == 0, 2 * half - 1, j - 1))
            right_at = lane(jnp.where(j == 2 * half - 1, 0, j + 1))
            edge_at = lane(jj + (1 - side) * half)
            weight_left = jnp.where(jj == 0, wrap if side == 0 else mid, 1.0)
            weight_right = jnp.where(jj == half - 1, mid if side == 0 else wrap, 1.0)
            total = zero
            for r in range(0, rows, TILE):
                at = slice(r, r + TILE)

                def part_of(i):
                    if side == 0:
                        ref = own[i]
                        if len(ref) == 2:
                            return ref[0][ref[1], at, here].astype(jnp.float32)
                        return ref[0][at, here].astype(jnp.float32)
                    tile = pl.ds(pl.multiple_of((i * half + jj) * rows + r, TILE), TILE)
                    return other[0][pl.ds(other[1] + tile.start, TILE), :].astype(jnp.float32)

                if side == 0:
                    loss = own_loss[at, here].astype(jnp.float32)
                else:
                    loss = other_loss[
                        pl.ds(pl.multiple_of(jj * rows + r, TILE), TILE), :
                    ].astype(jnp.float32)
                f = [tp[part, r + 1 : r + 1 + TILE, here] for part in range(2)]
                b = [tq[part, r + 7 : r + 7 + TILE, here] for part in range(2)]
                if r + TILE == rows:
                    for part in range(2):
                        facet = FRONT_FACET * tq[part, rows + 7 : rows + 8, here]
                        edge = jnp.where(is_last, facet, from_next[part : part + 1, edge_at])
                        f[part] = jnp.where(row_index == TILE - 1, edge, f[part])
                if r == 0:
                    for part in range(2):
                        facet = REAR_FACET * tp[part, 0:1, here]
                        edge = jnp.where(is_first, facet, from_before[part : part + 1, edge_at])
                        b[part] = jnp.where(row_index == 0, edge, b[part])
                c = carrier[at, here]
                lap = curvature(
                    carrier[at, left_at], c, carrier[at, right_at], weight_left, weight_right
                )
                out = updated(
                    *f, *b, [part_of(i) for i in range(4)], part_of(4), part_of(5), loss,
                    c, grating[at, here], lap,
                )
                field[0, r : r + TILE, here] = out[0]
                field[1, r : r + TILE, here] = out[1]
                field[0, rows + r : rows + r + TILE, here] = out[2]
                field[1, rows + r : rows + r + TILE, here] = out[3]
                new_carrier[at, here] = out[4]
                new_grating[at, here] = out[5]
                z = (info[3] + r + row_index).astype(jnp.float32)
                weighted = (1.0 + 2.0 * z / (cells - 1)) * ((c + out[4]) if last else c)
                for k in range(0, TILE, 8):
                    total = total + weighted[k : k + 8]
                if last and side == 1:
                    for k in range(0, TILE, 8):
                        most = (
                            jnp.maximum(most[0], jnp.abs(out[4][k : k + 8])),
                            jnp.maximum(most[1], jnp.abs(out[5][k : k + 8])),
                        )
            summed = jnp.sum(total, axis=0, keepdims=True)
            sums[:, here] = summed if sums_in is None else summed + sums_in[:, here]
        return most

    return lax.fori_loop(0, half, step, (zero, zero))


def own_parts(forward, backward, population, hole):
    return (
        (forward, 0), (forward, 1), (backward, 0), (backward, 1), (population,), (hole,),
    )


def first_step_kernel(
    cells, info, tp, tq, from_next, from_before, my_carrier, my_grating, loss,
    forward, backward, population, hole, other, source,
    new_tp, new_tq, down, up, new_carrier, new_grating, sums,
    carrier, grating, field, work, matrices, sem,
):
    copy = pltpu.make_async_copy(source, matrices, sem)
    copy.start()
    rows, columns = loss.shape
    half = columns // LANES
    sizes = sizes_in(other[9 * half * rows :, :], 2)
    for i, (whole, mine) in enumerate(((carrier, my_carrier), (grating, my_grating))):
        whole[:, :columns] = mine[...]

        @pl.loop(0, half)
        def _(j):
            whole[:, lane(half + j)] = decoded(other[slab((1 + i) * half + j, rows), :], sizes[i])

    rows_update(
        info, tp, tq, from_next, from_before, carrier, grating,
        own_parts(forward, backward, population, hole), (other, 3 * half * rows), loss, other,
        field, new_carrier, new_grating, None, sums, cells, False,
    )
    filtered(field, work, matrices, copy)
    write_filtered(work, new_tp, new_tq, down, up)


def middle_step_kernel(
    cells, info, tp, tq, from_next, from_before, carrier, grating, loss,
    forward, backward, population, hole, other, other_loss, sums_in, source,
    new_tp, new_tq, down, up, new_carrier, new_grating, sums,
    field, work, matrices, sem,
):
    copy = pltpu.make_async_copy(source, matrices, sem)
    copy.start()
    rows_update(
        info, tp, tq, from_next, from_before, carrier, grating,
        own_parts(forward, backward, population, hole), (other, 0), loss, other_loss,
        field, new_carrier, new_grating, sums_in, sums, cells, False,
    )
    filtered(field, work, matrices, copy)
    write_filtered(work, new_tp, new_tq, down, up)


def leave_step_kernel(
    cells, info, tp, tq, from_next, from_before, carrier, grating, loss,
    forward, backward, population, hole, other, other_loss, sums_in,
    field, kept_carrier, kept_grating, sides, sent, sums,
    new_carrier, new_grating,
):
    rows, width = carrier.shape
    columns = width // 2
    half = columns // LANES
    most = rows_update(
        info, tp, tq, from_next, from_before, carrier, grating,
        own_parts(forward, backward, population, hole), (other, 0), loss, other_loss,
        field, new_carrier, new_grating, sums_in, sums, cells, True,
    )
    mid = jnp.where(info[0] == 0, 1.0, 0.0)
    wrap = 1.0 - mid
    kept_carrier[...] = new_carrier[:, :columns]
    kept_grating[...] = new_grating[:, :columns]
    first, before = new_carrier[:, 0:1] * wrap, new_carrier[:, columns - 1 : columns] * mid
    after, final = new_carrier[:, columns : columns + 1] * mid, new_carrier[:, width - 1 :] * wrap
    sides[0] = jnp.broadcast_to(final, (rows, LANES))
    sides[1] = jnp.broadcast_to(after, (rows, LANES))
    pairs = []
    for at, value in ((0, before), (2, first)):
        coarse = value.astype(jnp.bfloat16).astype(jnp.float32)
        pairs += [(at, coarse), (at + 1, value - coarse)]
    for i, field_of in enumerate((new_carrier, new_grating)):
        size = size_of(most[i])
        pairs.append((SCALE_LANE + i, size))

        @pl.loop(0, half)
        def _(j):
            sent[slab(i * half + j, rows), :] = encoded(field_of[:, lane(half + j)], size)

    sent[2 * half * rows :, :] = side_tile(pairs, rows)


def leave_filter_kernel(info, field, source, kept, sent, straight, across, work, matrices, sem):
    copy = pltpu.make_async_copy(source, matrices, sem)
    copy.start()
    rows, width = field.shape[1] // 2, field.shape[2]
    blocks = width // LANES
    half = blocks // 2
    columns = width // 2
    filtered(field, work, matrices, copy)
    zero = jnp.zeros((8, LANES), jnp.float32)
    sizes = []
    for f in range(2):

        def unmix(g, most):
            at = pl.ds(pl.multiple_of(g * 8 + f * rows, 8), 8)
            for j, pair in enumerate(gathered(work, at)):
                for part in range(2):
                    if j < half:
                        kept[part, at, j * LANES : (j + 1) * LANES] = pair[part]
                    else:
                        work[j, at, part * LANES : (part + 1) * LANES] = pair[part]
                        most = jnp.maximum(most, jnp.abs(pair[part]))
            return most

        size = size_of(lax.fori_loop(0, rows // 8, unmix, zero))
        sizes.append((SCALE_LANE + f, size))

        @pl.loop(0, half)
        def _(j):
            for part in range(2):
                value = work[half + j, f * rows : (f + 1) * rows, part * LANES : (part + 1) * LANES]
                sent[slab((2 * f + part) * half + j, rows), :] = encoded(value, size)

    sent[4 * half * rows :, :] = side_tile(sizes, rows)
    low = info[0] == 0
    for part in range(2):
        lanes = slice(part * LANES, (part + 1) * LANES)
        straight[part : part + 1, :] = jnp.where(
            low, kept[part, 0:1, :], kept[part, 2 * rows - 1 : 2 * rows, :]
        )
        for j in range(half):
            across[part : part + 1, j * LANES : (j + 1) * LANES] = jnp.where(
                low, work[half + j, 0:1, lanes], work[half + j, 2 * rows - 1 : 2 * rows, lanes]
            )


def final_kernel(
    info, kept, kept_carrier, kept_grating, sides, fields, pair, straight, across, loss,
    forward, backward, population, hole,
    out_forward, out_backward, out_carrier, out_grating,
    tp, tq, carrier, grating,
):
    rows, columns = kept_carrier.shape
    half = columns // LANES
    mine = info[0] * rows
    theirs = (1 - info[0]) * rows
    low = info[0] == 0
    extra = pair[2 * half * rows :, :]
    size_carrier, size_grating = sizes_in(extra, 2)
    size_forward, size_backward = sizes_in(fields[4 * half * rows :, :], 2)
    extra = extra.astype(jnp.float32)

    def at(start, offset, count):
        return pl.ds(pl.multiple_of(start + offset, 8), count)

    for part in range(2):
        tp[part, at(mine, 0, rows), :] = kept[part, :rows, :]
        tq[part, at(mine, 8, rows), :] = kept[part, rows:, :]
    carrier[at(mine, 0, rows), LANES : LANES + columns] = kept_carrier[...]
    carrier[at(mine, 0, rows), :LANES] = sides[0]
    carrier[at(mine, 0, rows), LANES + columns :] = sides[1]
    carrier[at(theirs, 0, rows), :LANES] = jnp.broadcast_to(
        extra[:, 0:1] + extra[:, 1:2], (rows, LANES)
    )
    carrier[at(theirs, 0, rows), LANES + columns :] = jnp.broadcast_to(
        extra[:, 2:3] + extra[:, 3:4], (rows, LANES)
    )
    grating[at(mine, 0, rows), :] = kept_grating[...]

    @pl.loop(0, half)
    def _(j):
        carrier[at(theirs, 0, rows), lane(1 + j)] = decoded(pair[slab(j, rows), :], size_carrier)
        grating[at(theirs, 0, rows), lane(j)] = decoded(pair[slab(half + j, rows), :], size_grating)
        for part in range(2):
            tp[part, at(theirs, 0, rows), lane(j)] = decoded(
                fields[slab(part * half + j, rows), :], size_forward
            )
            tq[part, at(theirs, 8, rows), lane(j)] = decoded(
                fields[slab((2 + part) * half + j, rows), :], size_backward
            )

    all_rows = 2 * rows
    for part in range(2):
        here = slice(part, part + 1)
        next_edge = jnp.where(low, straight[here, :], across[here, :])
        before_edge = jnp.where(low, across[here, :], straight[here, :])
        front = FRONT_FACET * tq[part, all_rows + 7 : all_rows + 8, :]
        rear = REAR_FACET * tp[part, 0:1, :]
        tp[part, all_rows : all_rows + 1, :] = jnp.where(info[2] == 1, front, next_edge)
        tq[part, 7:8, :] = jnp.where(info[1] == 1, rear, before_edge)

    @pl.loop(0, half)
    def _(j):
        here = lane(j)
        for r in range(0, all_rows, TILE):
            row = slice(r, r + TILE)
            c = carrier[row, lane(j + 1)]
            lap = curvature(carrier[row, lane(j)], c, carrier[row, lane(j + 2)], 1.0, 1.0)
            out = updated(
                tp[0, r + 1 : r + 1 + TILE, here], tp[1, r + 1 : r + 1 + TILE, here],
                tq[0, r + 7 : r + 7 + TILE, here], tq[1, r + 7 : r + 7 + TILE, here],
                [ref[part, row, here].astype(jnp.float32) for ref in (forward, backward) for part in range(2)],
                population[row, here].astype(jnp.float32), hole[row, here].astype(jnp.float32),
                loss[row, here].astype(jnp.float32), c, grating[row, here], lap,
            )
            out_forward[0, row, here] = out[0]
            out_forward[1, row, here] = out[1]
            out_backward[0, row, here] = out[2]
            out_backward[1, row, here] = out[3]
            out_carrier[row, here] = out[4]
            out_grating[row, here] = out[5]


def whole_spec(shape):
    return pl.BlockSpec(shape, lambda i, info, n=len(shape): (0,) * n)


def call(name, kernel, info, inputs, outputs, scratch, flops=0):
    arrays = [x[0] if isinstance(x, tuple) else x for x in inputs]
    specs = [x[1] if isinstance(x, tuple) else whole_spec(x.shape) for x in inputs]
    shapes = [jax.ShapeDtypeStruct(*out) for out in outputs]
    moved = sum(math.prod(s.shape) * s.dtype.itemsize for s in shapes)
    result = pl.pallas_call(
        kernel,
        grid_spec=pltpu.PrefetchScalarGridSpec(
            num_scalar_prefetch=1,
            grid=(1,),
            in_specs=specs,
            out_specs=[whole_spec(s.shape) for s in shapes],
            scratch_shapes=scratch,
        ),
        out_shape=shapes,
        compiler_params=pltpu.CompilerParams(vmem_limit_bytes=48 * 1024 * 1024),
        cost_estimate=pl.CostEstimate(
            flops=flops, bytes_accessed=moved + 4 * 1024 * 1024, transcendentals=0
        ),
        name=name,
    )(info, *arrays)
    return result


def per_pair(
    ending_rightward_adjoint,
    ending_leftward_adjoint,
    ending_population_adjoint,
    ending_holeburn_adjoint,
    history_rightward,
    history_leftward,
    history_population,
    history_holeburn,
    segment_passive_attenuation,
):
    cell_rows, columns = ending_population_adjoint.shape
    passes = history_population.shape[0]
    rows = cell_rows // 2
    half = columns // LANES
    blocks = 2 * half
    width = 2 * columns
    count = lax.axis_size("gz")
    cells = cell_rows * count
    x = lax.axis_index("gx")
    block = lax.axis_index("gz")
    place = 2 * block + x
    f32, bf16 = jnp.float32, jnp.bfloat16

    def info_of(first, last):
        return jnp.stack([x, first, last, place * rows]).astype(jnp.int32)

    info = info_of(place == 0, place == 2 * count - 1)
    info_block = info_of(block == 0, block == count - 1)
    swap = [(0, 1), (1, 0)]

    def field_rows(array, other):
        return array, pl.BlockSpec(
            (2, rows, columns), lambda i, info: (0, 1 - info[0] if other else info[0], 0)
        )

    def plain_rows(array, other):
        return array, pl.BlockSpec(
            (rows, columns), lambda i, info: (1 - info[0] if other else info[0], 0)
        )

    def history_rows(s, other):
        def at(info):
            return 1 - info[0] if other else info[0]

        wide = pl.BlockSpec((None, 2, rows, columns), lambda i, info: (s, 0, at(info), 0))
        plain = pl.BlockSpec((None, rows, columns), lambda i, info: (s, at(info), 0))
        return [
            (history_rightward, wide), (history_leftward, wide),
            (history_population, plain), (history_holeburn, plain),
        ]

    def tiles(n):
        return ((n * rows, LANES), bf16)

    ends = (ending_rightward_adjoint, ending_leftward_adjoint)
    matrices = jnp.asarray(lateral_matrices(width, blocks))
    matrix_input = (matrices, pl.BlockSpec(memory_space=pl.ANY))
    work = [
        pltpu.VMEM((blocks, 2 * rows, 2 * LANES), f32),
        pltpu.VMEM(matrices.shape, bf16),
        pltpu.SemaphoreType.DMA,
    ]
    field_scratch = pltpu.VMEM((2, 2 * rows, width), f32)
    state_out = [
        ((2, rows + 8, width), f32), ((2, rows + 8, width), f32), ((2, width), f32), ((2, width), f32),
    ]
    plane = ((rows, width), f32)
    plane_scratch = pltpu.VMEM((rows, width), f32)
    work_flops = 2 * 3 * 2 * rows * blocks * (2 * LANES) ** 2

    (coded,) = call(
        "send_fields", send_fields_kernel, info, [field_rows(a, True) for a in ends],
        [tiles(4 * half + 1)], [],
    )
    other_fields = lax.ppermute(coded, "gx", swap)
    (coded,) = call(
        "send_first", send_first_kernel, info,
        [plain_rows(segment_passive_attenuation, True), plain_rows(ending_population_adjoint, True),
         plain_rows(ending_holeburn_adjoint, True), *history_rows(passes - 1, True)],
        [tiles(9 * half + 1)], [],
    )
    other_first = lax.ppermute(coded, "gx", swap)
    later = [
        call("send_history", send_history_kernel, info, history_rows(s, True), [tiles(6 * half)], [])[0]
        for s in range(passes - 2, 0, -1)
    ]

    line = ("gz", "gx")
    ahead = [(i, i + 1) for i in range(2 * count - 1)]
    back = [(i + 1, i) for i in range(2 * count - 1)]

    def edges(down, up):
        return lax.ppermute(down, line, back), lax.ppermute(up, line, ahead)

    tp, tq, down, up = call(
        "enter", enter_kernel, info,
        [*(field_rows(a, False) for a in ends), other_fields, matrix_input],
        state_out, [field_scratch, *work], work_flops,
    )
    from_next, from_before = edges(down, up)

    loss = plain_rows(segment_passive_attenuation, False)
    other_loss = (other_first, pl.BlockSpec((half * rows, LANES), lambda i, info: (0, 0)))
    carrier = grating = sums = None
    for index, s in enumerate(range(passes - 1, 0, -1)):
        mine = history_rows(s, False)
        if index < len(later):
            held, from_next, from_before = lax.optimization_barrier(
                (later[index], from_next, from_before)
            )
            coming = lax.ppermute(held, "gx", swap)
        shared = [tp, tq, from_next, from_before]
        if index == 0:
            tp, tq, down, up, carrier, grating, sums = call(
                "first_step", functools.partial(first_step_kernel, cells), info,
                [*shared, plain_rows(ending_population_adjoint, False),
                 plain_rows(ending_holeburn_adjoint, False), loss, *mine, other_first, matrix_input],
                [*state_out, plane, plane, ((1, width), f32)],
                [plane_scratch, plane_scratch, field_scratch, *work], work_flops,
            )
        elif s > 1:
            tp, tq, down, up, carrier, grating, sums = call(
                "middle_step", functools.partial(middle_step_kernel, cells), info,
                [*shared, carrier, grating, loss, *mine, other, other_loss, sums, matrix_input],
                [*state_out, plane, plane, ((1, width), f32)],
                [field_scratch, *work], work_flops,
            )
        else:
            field, kept_carrier, kept_grating, sides, sent, sums = call(
                "leave_step", functools.partial(leave_step_kernel, cells), info,
                [*shared, carrier, grating, loss, *mine, other, other_loss, sums],
                [((2, 2 * rows, width), f32), ((rows, columns), f32), ((rows, columns), f32),
                 ((2, rows, LANES), f32), tiles(2 * half + 1), ((1, width), f32)],
                [plane_scratch, plane_scratch],
            )
        if s > 1:
            from_next, from_before = edges(down, up)
            other = coming

    pair = lax.ppermute(sent, "gx", swap)
    kept, sent, straight, across = call(
        "leave_filter", leave_filter_kernel, info, [field, matrix_input],
        [((2, 2 * rows, columns), f32), tiles(4 * half + 1), ((2, columns), f32), ((2, columns), f32)],
        work, work_flops,
    )
    fields = lax.ppermute(sent, "gx", swap)
    to_side, to_corner = [], []
    for b in range(count):
        if b > 0:
            to_side.append((2 * b, 2 * (b - 1)))
            to_corner.append((2 * b, 2 * (b - 1) + 1))
        if b < count - 1:
            to_side.append((2 * b + 1, 2 * (b + 1) + 1))
            to_corner.append((2 * b + 1, 2 * (b + 1)))
    straight = lax.ppermute(straight, line, to_side)
    across = lax.ppermute(across, line, to_corner)

    sums = sums.reshape(2, half, LANES)
    total = sums[0] + lax.ppermute(sums[1], "gx", swap)
    total = added_up(total, "gz").reshape(columns)

    def last_history(array):
        shape = array.shape[1:]
        return array, pl.BlockSpec((None, *shape), lambda i, info: (0,) * (len(shape) + 1))

    outs = call(
        "final", final_kernel, info_block,
        [kept, kept_carrier, kept_grating, sides, fields, pair, straight, across,
         segment_passive_attenuation, last_history(history_rightward), last_history(history_leftward),
         last_history(history_population), last_history(history_holeburn)],
        [((2, cell_rows, columns), f32), ((2, cell_rows, columns), f32),
         ((cell_rows, columns), f32), ((cell_rows, columns), f32)],
        [pltpu.VMEM((2, cell_rows + 8, columns), f32), pltpu.VMEM((2, cell_rows + 8, columns), f32),
         pltpu.VMEM((cell_rows, columns + 2 * LANES), f32), pltpu.VMEM((cell_rows, columns), f32)],
    )
    return (*outs, CLOCK_DELTA * total / math.sqrt(cells))


def shared_by_pairs(mesh, arguments):
    population = arguments[6]
    passes, cells, width = population.shape
    rows, columns = cells // mesh.shape["gz"], width // mesh.shape["gx"]
    return (
        mesh.shape["gx"] == 2
        and passes >= 3
        and rows % (2 * TILE) == 0
        and columns % LANES == 0
        and (columns // LANES) & (columns // LANES - 1) == 0
        and width <= 4096
    )


def solution(mesh):
    def run(*arguments):
        body = per_pair if shared_by_pairs(mesh, arguments) else per_device
        return jax.shard_map(
            body,
            mesh=mesh,
            in_specs=(
                P(None, "gz", "gx"),
                P(None, "gz", "gx"),
                P("gz", "gx"),
                P("gz", "gx"),
                P(None, None, "gz", "gx"),
                P(None, None, "gz", "gx"),
                P(None, "gz", "gx"),
                P(None, "gz", "gx"),
                P("gz", "gx"),
            ),
            out_specs=(
                P(None, "gz", "gx"), P(None, "gz", "gx"), P("gz", "gx"), P("gz", "gx"), P("gx"),
            ),
            check_vma=False,
        )(*arguments)

    return run
```

```python
import functools
import math

import jax
import jax.numpy as jnp
import ml_dtypes
import numpy as np
from jax import lax
from jax.experimental import pallas as pl
from jax.experimental.pallas import tpu as pltpu
from jax.sharding import PartitionSpec as P

DIFF = 512


FRONT_FACET = 0.3
REAR_FACET = 0.9
GAIN_SLOPE_RATE = 0.3
ALPHA_LINEWIDTH = 2.0
COUPLING = 0.5
CLOCK_DELTA = 0.3
DENSITY_LIFETIME = 2.0
GRATING_LIFE = 0.75
TRANSVERSE_DIFFUS = 0.2


def passed_along(value, axis, steps):
    count = lax.axis_size(axis)
    initial, last = (max(0, -steps), min(count, count - steps))
    return lax.ppermute(value, axis, [(source, source + steps) for source in range(initial, last)])


def with_halo(block, sides, width):
    for axis, dim in sides:
        count = lax.axis_size(axis)
        forward = [(i, i + 1) for i in range(count - 1)]
        backward = [(target, source) for source, target in forward]
        low = lax.ppermute(
            lax.slice_in_dim(block, block.shape[dim] - width, None, axis=dim), axis, forward
        )
        high = lax.ppermute(lax.slice_in_dim(block, 0, width, axis=dim), axis, backward)
        block = jnp.concatenate([low, block, high], axis=dim)
    return block


def rotate(source_re, source_im, cosine, sine, form, sign):
    exact = lax.Precision.HIGHEST
    out_re = jnp.einsum(form, source_re, cosine, precision=exact) + sign * jnp.einsum(
        form, source_im, sine, precision=exact
    )
    out_im = jnp.einsum(form, source_im, cosine, precision=exact) - sign * jnp.einsum(
        form, source_re, sine, precision=exact
    )
    return (out_re, out_im)


def transform(stacked):
    count = stacked.shape[1]
    width = stacked.shape[2]
    second = min(128, width // 2)
    first = width // second
    two_pi = 2.0 * math.pi
    index_a = jnp.arange(first, dtype=jnp.int32)
    index_b = jnp.arange(second, dtype=jnp.int32)
    angle_a = two_pi * (index_a[:, None] * index_a[None, :] % first).astype(jnp.float32) / first
    angle_b = two_pi * (index_b[:, None] * index_b[None, :] % second).astype(jnp.float32) / second
    angle_t = two_pi * (index_a[:, None] * index_b[None, :] % width).astype(jnp.float32) / width
    cos_a, sin_a = (jnp.cos(angle_a), jnp.sin(angle_a))
    cos_b, sin_b = (jnp.cos(angle_b), jnp.sin(angle_b))
    cos_t, sin_t = (jnp.cos(angle_t), jnp.sin(angle_t))
    wavenum = index_a[:, None] + first * index_b[None, :]
    signed = jnp.where(wavenum < width // 2, wavenum, wavenum - width)
    phase = (signed * signed).astype(jnp.float32) * (DIFF / (width / 2) ** 2)
    cos_p, sin_p = (jnp.cos(phase), jnp.sin(phase))
    real_in = stacked[0].reshape(count, first, second)
    imag_in = stacked[1].reshape(count, first, second)
    step_re, step_im = rotate(real_in, imag_in, cos_a, sin_a, "nab,ak->nkb", 1.0)
    twist_re = step_re * cos_t + step_im * sin_t
    twist_im = step_im * cos_t - step_re * sin_t
    spec_re, spec_im = rotate(twist_re, twist_im, cos_b, sin_b, "nkb,bj->nkj", 1.0)
    moved_re = spec_re * cos_p - spec_im * sin_p
    moved_im = spec_re * sin_p + spec_im * cos_p
    back_re, back_im = rotate(moved_re, moved_im, cos_b, sin_b, "nkj,jb->nkb", -1.0)
    untw_re = back_re * cos_t - back_im * sin_t
    untw_im = back_im * cos_t + back_re * sin_t
    final_re, final_im = rotate(untw_re, untw_im, cos_a, sin_a, "nkb,ka->nab", -1.0)
    return jnp.stack([final_re.reshape(count, width), final_im.reshape(count, width)]) / width


def added_up(value, axis):
    count = lax.axis_size(axis)
    if count & (count - 1):
        return lax.psum(value, axis)
    reach = 1
    while reach < count:
        value = value + lax.ppermute(value, axis, [(i, i ^ reach) for i in range(count)])
        reach *= 2
    return value


def lateral_work(parts):
    return (transform(parts[0]), transform(parts[1]))


def multiplier_revision(
    population_multiplier,
    holeburn_multiplier,
    measured_rightward,
    measured_leftward,
    rightward_wave,
    leftward_wave,
    population_level,
    holeburn_magnitude,
    attenuation_factor,
    transverse_curvature,
):
    rightward_inphase, rightward_quadrature = (rightward_wave[0], rightward_wave[1])
    leftward_inphase, leftward_quadrature = (leftward_wave[0], leftward_wave[1])
    measured_rightward_inphase, measured_rightward_quadrature = (
        measured_rightward[0],
        measured_rightward[1],
    )
    measured_leftward_inphase, measured_leftward_quadrature = (
        measured_leftward[0],
        measured_leftward[1],
    )
    surplus_population = population_level - 1.0
    amplification_inphase = 1.0 + 0.5 * (GAIN_SLOPE_RATE * surplus_population - attenuation_factor)
    amplification_quadrature = 0.5 * GAIN_SLOPE_RATE * ALPHA_LINEWIDTH * surplus_population
    joined_waves = COUPLING * holeburn_magnitude
    population_derivative = (
        2.0 * CLOCK_DELTA * GAIN_SLOPE_RATE * surplus_population * population_multiplier
    )
    holeburn_derivative = 2.0 * CLOCK_DELTA * holeburn_multiplier
    revised_rightward_inphase = (
        amplification_inphase * measured_rightward_inphase
        - amplification_quadrature * measured_rightward_quadrature
        + joined_waves * measured_leftward_quadrature
        - population_derivative * rightward_inphase
        + holeburn_derivative * leftward_inphase
    )
    revised_rightward_quadrature = (
        amplification_inphase * measured_rightward_quadrature
        + amplification_quadrature * measured_rightward_inphase
        - joined_waves * measured_leftward_inphase
        - population_derivative * rightward_quadrature
        + holeburn_derivative * leftward_quadrature
    )
    revised_leftward_inphase = (
        amplification_inphase * measured_leftward_inphase
        - amplification_quadrature * measured_leftward_quadrature
        + joined_waves * measured_rightward_quadrature
        - population_derivative * leftward_inphase
        + holeburn_derivative * rightward_inphase
    )
    revised_leftward_quadrature = (
        amplification_inphase * measured_leftward_quadrature
        + amplification_quadrature * measured_leftward_inphase
        - joined_waves * measured_rightward_inphase
        - population_derivative * leftward_quadrature
        + holeburn_derivative * rightward_quadrature
    )
    light_intensity = (
        rightward_inphase * rightward_inphase
        + rightward_quadrature * rightward_quadrature
        + leftward_inphase * leftward_inphase
        + leftward_quadrature * leftward_quadrature
    )
    amplification_share = (
        measured_rightward_inphase * (rightward_inphase + ALPHA_LINEWIDTH * rightward_quadrature)
        + measured_rightward_quadrature
        * (rightward_quadrature - ALPHA_LINEWIDTH * rightward_inphase)
        + measured_leftward_inphase * (leftward_inphase + ALPHA_LINEWIDTH * leftward_quadrature)
        + measured_leftward_quadrature * (leftward_quadrature - ALPHA_LINEWIDTH * leftward_inphase)
    )
    revised_population = (
        population_multiplier
        * (1.0 - CLOCK_DELTA / DENSITY_LIFETIME - CLOCK_DELTA * GAIN_SLOPE_RATE * light_intensity)
        + TRANSVERSE_DIFFUS * transverse_curvature
        + 0.5 * GAIN_SLOPE_RATE * amplification_share
    )
    fresh_holeburn = holeburn_multiplier * (1.0 - CLOCK_DELTA / GRATING_LIFE) + COUPLING * (
        measured_rightward_quadrature * leftward_inphase
        - measured_rightward_inphase * leftward_quadrature
        + measured_leftward_quadrature * rightward_inphase
        - measured_leftward_inphase * rightward_quadrature
    )
    return (
        jnp.stack([revised_rightward_inphase, revised_rightward_quadrature]),
        jnp.stack([revised_leftward_inphase, revised_leftward_quadrature]),
        revised_population,
        fresh_holeburn,
    )


def per_device(
    ending_rightward_adjoint,
    ending_leftward_adjoint,
    ending_population_adjoint,
    ending_holeburn_adjoint,
    history_rightward,
    history_leftward,
    history_population,
    history_holeburn,
    segment_passive_attenuation,
):
    columns = ending_rightward_adjoint.shape[2]
    rows = ending_rightward_adjoint.shape[1]
    blocks = lax.axis_size("gz")
    position = lax.axis_index("gz")
    cells = rows * blocks
    zpos = (position * rows + jnp.arange(rows, dtype=jnp.int32)).astype(jnp.float32)
    scaling_factor = 1.0 + 2.0 * zpos / (cells - 1)
    rightward_multiplier, leftward_multiplier = (ending_rightward_adjoint, ending_leftward_adjoint)
    population_multiplier, holeburn_multiplier = (
        ending_population_adjoint,
        ending_holeburn_adjoint,
    )
    attenuation_factor = segment_passive_attenuation.astype(jnp.float32)
    shape_curve = jnp.zeros((columns,), jnp.float32)
    for moment_position in range(history_rightward.shape[0] - 1, -1, -1):
        shape_curve = shape_curve + jnp.sum(scaling_factor[:, None] * population_multiplier, axis=0)
        above = passed_along(rightward_multiplier[:, :1, :], "gz", -1)
        below = passed_along(leftward_multiplier[:, -1:, :], "gz", 1)
        top_row = jnp.where(
            position == blocks - 1, FRONT_FACET * leftward_multiplier[:, -1:, :], above
        )
        bottom_row = jnp.where(position == 0, REAR_FACET * rightward_multiplier[:, :1, :], below)
        lam_fwd = jnp.concatenate([rightward_multiplier[:, 1:, :], top_row], axis=1)
        lam_bwd = jnp.concatenate([bottom_row, leftward_multiplier[:, :-1, :]], axis=1)
        whole_fwd, whole_bwd = (
            lax.all_gather(lam_fwd, "gx", axis=2, tiled=True),
            lax.all_gather(lam_bwd, "gx", axis=2, tiled=True),
        )
        start = lax.axis_index("gx") * columns
        done_fwd, done_bwd = lateral_work((whole_fwd, whole_bwd))
        measured_rightward = lax.dynamic_slice_in_dim(done_fwd, start, columns, 2)
        measured_leftward = lax.dynamic_slice_in_dim(done_bwd, start, columns, 2)
        bordered_array = with_halo(population_multiplier, (("gx", 1),), 1)
        transverse_curvature = (
            bordered_array[:, 2:] + bordered_array[:, :-2] - 2.0 * population_multiplier
        )
        rightward_multiplier, leftward_multiplier, population_multiplier, holeburn_multiplier = (
            multiplier_revision(
                population_multiplier,
                holeburn_multiplier,
                measured_rightward,
                measured_leftward,
                history_rightward[moment_position].astype(jnp.float32),
                history_leftward[moment_position].astype(jnp.float32),
                history_population[moment_position].astype(jnp.float32),
                history_holeburn[moment_position].astype(jnp.float32),
                attenuation_factor,
                transverse_curvature,
            )
        )
    total = added_up(shape_curve, "gz")
    derivative_vector = CLOCK_DELTA * total / math.sqrt(cells)
    return (
        rightward_multiplier,
        leftward_multiplier,
        population_multiplier,
        holeburn_multiplier,
        derivative_vector,
    )

LANES = 128
TILE = 16
POWER = 12
STRETCH = 1211.0
SCALE_LANE = 8


def lateral_matrices(width, blocks):
    lanes = width // blocks
    k = np.arange(width)
    signed = np.where(k < width // 2, k, k - width).astype(np.float64)
    response = np.fft.ifft(np.exp(1j * signed * signed * (DIFF / (width / 2) ** 2)))
    step = np.arange(lanes)
    shift = lanes * np.arange(blocks)[:, None, None] + step[None, None, :] - step[None, :, None]
    kernels = np.fft.fft(response[shift % width], axis=0) / blocks
    top = np.concatenate([kernels.real, kernels.imag], axis=2)
    low = np.concatenate([-kernels.imag, kernels.real], axis=2)
    whole = np.concatenate([top, low], axis=1)
    first = whole.astype(ml_dtypes.bfloat16)
    rest = (whole - first.astype(np.float64)).astype(ml_dtypes.bfloat16)
    return np.stack([first, rest], axis=1)


def block_dft(values, sign):
    count = len(values)
    if count == 1:
        return values
    even = block_dft(values[0::2], sign)
    odd = block_dft(values[1::2], sign)
    out = [None] * count
    for k in range(count // 2):
        (er, ei), (wr, wi) = even[k], odd[k]
        if 4 * k == count:
            plus, minus = (er - wi, ei + wr), (er + wi, ei - wr)
            out[k], out[k + count // 2] = (plus, minus) if sign > 0 else (minus, plus)
            continue
        if k:
            c, s = math.cos(2 * math.pi * k / count), sign * math.sin(2 * math.pi * k / count)
            if 8 * k == count:
                wr, wi = (c * (wr - wi), c * (wr + wi)) if sign > 0 else (c * (wr + wi), c * (wi - wr))
            elif 8 * k == 3 * count:
                wr, wi = (c * (wr + wi), c * (wi - wr)) if sign > 0 else (c * (wr - wi), c * (wr + wi))
            else:
                wr, wi = c * wr - s * wi, c * wi + s * wr
        out[k] = (er + wr, ei + wi)
        out[k + count // 2] = (er - wr, ei - wi)
    return out


def lane(j):
    return pl.ds(pl.multiple_of(j * LANES, LANES), LANES)


def slab(j, rows):
    return pl.ds(pl.multiple_of(j * rows, rows), rows)


def fetch(pairs, sems):
    copies = [pltpu.make_async_copy(a, b, sems.at[i]) for i, (a, b) in enumerate(pairs)]
    for copy in copies:
        copy.start()
    return copies


def rows_of(info, rows, other):
    part = 1 - info[4] if other else info[4]
    return pl.ds(pl.multiple_of(part * rows, rows), rows)


def spread(field, work):
    rows = field.shape[1]
    blocks = work.shape[0]

    @pl.loop(0, rows // 8)
    def _(g):
        at = slab(g, 8)
        values = [
            (field[0, at, j * LANES : (j + 1) * LANES], field[1, at, j * LANES : (j + 1) * LANES])
            for j in range(blocks)
        ]
        for q, (re, im) in enumerate(block_dft(values, -1)):
            work[q, at, :LANES] = re
            work[q, at, LANES:] = im


def multiply(work, matrices):
    rows = work.shape[1]

    @pl.loop(0, work.shape[0], unroll=True)
    def _(q):
        value = work[q]
        first = value.astype(jnp.bfloat16)
        rest = (value - first.astype(jnp.float32)).astype(jnp.bfloat16)
        both = jnp.dot(
            jnp.concatenate([first, rest]), matrices[q, 0], preferred_element_type=jnp.float32
        )
        fine = jnp.dot(first, matrices[q, 1], preferred_element_type=jnp.float32)
        work[q] = both[:rows] + (both[rows:] + fine)


def gathered(work, at):
    values = [(work[q, at, :LANES], work[q, at, LANES:]) for q in range(work.shape[0])]
    return block_dft(values, 1)


def filtered(field, work, matrices, copy):
    spread(field, work)
    copy.wait()
    multiply(work, matrices)


def write_filtered(info, work, forward, backward, inner, outer):
    rows = work.shape[1] // 2
    for target, base, offset in ((forward, 0, 0), (backward, rows, 8)):

        @pl.loop(0, rows // 8)
        def _(g):
            here = pl.ds(pl.multiple_of(g * 8 + offset, 8), 8)
            for j, pair in enumerate(gathered(work, pl.ds(pl.multiple_of(g * 8 + base, 8), 8))):
                for part in range(2):
                    target[part, here, j * LANES : (j + 1) * LANES] = pair[part]

    low = info[4] == 0
    for part in range(2):
        first, last = forward[part, 0:1, :], backward[part, rows + 7 : rows + 8, :]
        inner[part : part + 1, :] = jnp.where(low, last, first)
        outer[part : part + 1, :] = jnp.where(low, first, last)


def size_of(largest):
    top = jnp.max(jnp.max(largest, axis=1, keepdims=True), axis=0, keepdims=True)
    return jnp.maximum(top, 1e-30).astype(jnp.bfloat16).astype(jnp.float32)


def encoded(value, size):
    unit = value * (STRETCH / size)
    square = unit * unit
    fourth = square * square
    return (fourth * fourth * square * (unit * jnp.abs(unit))).astype(jnp.bfloat16)


def decoded(code, size):
    value = code.astype(jnp.float32)
    root = jnp.exp2(jnp.log(jnp.abs(value)) * (1.0 / (POWER * math.log(2.0)))) * (size / STRETCH)
    return jnp.where(value < 0.0, -root, root)


def side_tile(columns, rows):
    index = lax.broadcasted_iota(jnp.int32, (rows, LANES), 1)
    tile = jnp.zeros((rows, LANES), jnp.float32)
    for at, column in columns:
        tile = jnp.where(index == at, column, tile)
    return tile.astype(jnp.bfloat16)


def sizes_in(tile, count):
    value = tile.astype(jnp.float32)
    return [value[0:1, SCALE_LANE + i : SCALE_LANE + i + 1] for i in range(count)]


def updated(fr, fi, br, bi, wave, population, hole, loss, carrier, grating, lap):
    rr, ri, lr, li = wave
    surplus = population - 1.0
    gain_re = 1.0 + 0.5 * (GAIN_SLOPE_RATE * surplus - loss)
    gain_im = (0.5 * GAIN_SLOPE_RATE * ALPHA_LINEWIDTH) * surplus
    joined = COUPLING * hole
    drive = (2.0 * CLOCK_DELTA * GAIN_SLOPE_RATE) * surplus * carrier
    mix = (2.0 * CLOCK_DELTA) * grating
    new_fr = gain_re * fr - gain_im * fi + joined * bi - drive * rr + mix * lr
    new_fi = gain_re * fi + gain_im * fr - joined * br - drive * ri + mix * li
    new_br = gain_re * br - gain_im * bi + joined * fi - drive * lr + mix * rr
    new_bi = gain_re * bi + gain_im * br - joined * fr - drive * li + mix * ri
    light = rr * rr + ri * ri + lr * lr + li * li
    share = (
        fr * (rr + ALPHA_LINEWIDTH * ri)
        + fi * (ri - ALPHA_LINEWIDTH * rr)
        + br * (lr + ALPHA_LINEWIDTH * li)
        + bi * (li - ALPHA_LINEWIDTH * lr)
    )
    new_carrier = (
        carrier * ((1.0 - CLOCK_DELTA / DENSITY_LIFETIME) - (CLOCK_DELTA * GAIN_SLOPE_RATE) * light)
        + TRANSVERSE_DIFFUS * lap
        + (0.5 * GAIN_SLOPE_RATE) * share
    )
    new_grating = grating * (1.0 - CLOCK_DELTA / GRATING_LIFE) + COUPLING * (
        fi * lr - fr * li + bi * rr - br * ri
    )
    return new_fr, new_fi, new_br, new_bi, new_carrier, new_grating


def curvature(left, mid, right, weight_left, weight_right):
    index = lax.broadcasted_iota(jnp.int32, mid.shape, 1)
    below = jnp.where(index == 0, pltpu.roll(left, 1, 1) * weight_left, pltpu.roll(mid, 1, 1))
    above = jnp.where(
        index == LANES - 1,
        pltpu.roll(right, LANES - 1, 1) * weight_right,
        pltpu.roll(mid, LANES - 1, 1),
    )
    return below + above - 2.0 * mid


def send_fields_kernel(info, forward, backward, out, fields, sems):
    rows, columns = fields.shape[2:]
    half = columns // LANES
    at = rows_of(info, rows, True)
    copies = fetch(
        [(ref.at[:, at, :], fields.at[f]) for f, ref in enumerate((forward, backward))], sems
    )
    sizes = []
    for f in range(2):
        copies[f].wait()
        largest = jnp.maximum(jnp.abs(fields[f, 0]), jnp.abs(fields[f, 1]))
        size = size_of(largest)
        sizes.append((SCALE_LANE + f, size))
        for part in range(2):
            put_tiles(out, (2 * f + part) * half, encoded(fields[f, part], size))
    out[4 * half * rows :, :] = side_tile(sizes, rows)


def put_tiles(out, first, value):
    rows, columns = value.shape
    for j in range(columns // LANES):
        at = (first + j) * rows
        out[at : at + rows, :] = value[:, j * LANES : (j + 1) * LANES]


def history_copies(forward, backward, population, hole, s, at, wide, plain):
    return [
        (forward.at[s, :, at, :], wide.at[0]),
        (backward.at[s, :, at, :], wide.at[1]),
        (population.at[s, at, :], plain.at[0]),
        (hole.at[s, at, :], plain.at[1]),
    ]


def put_history(out, first, half, wide, plain, at):
    parts = [wide[f, part, at] for f in range(2) for part in range(2)] + [plain[0, at], plain[1, at]]
    for i, value in enumerate(parts):
        put_tiles(out, first + i * half, value)


def both_halves(info, rows):
    own = pl.ds(pl.multiple_of(info[4] * rows, rows), rows)
    other = pl.ds(pl.multiple_of((1 - info[4]) * rows, rows), rows)
    return own, other


def send_history_kernel(s, info, forward, backward, population, hole, own, out, wide, plain, sems):
    cell_rows, columns = plain.shape[1:]
    half = columns // LANES
    copies = fetch(
        history_copies(forward, backward, population, hole, s, pl.ds(0, cell_rows), wide, plain),
        sems,
    )
    for copy in copies:
        copy.wait()
    mine, theirs = both_halves(info, cell_rows // 2)
    put_history(out, 0, half, wide, plain, theirs)
    put_history(own, 0, half, wide, plain, mine)


def send_first_kernel(
    s, info, loss, carrier, grating, forward, backward, population, hole,
    own_loss, own, own_carrier, own_grating, out, wide, plain, losses, states, sems,
):
    cell_rows, columns = losses.shape
    rows = cell_rows // 2
    half = columns // LANES
    whole = pl.ds(0, cell_rows)
    copies = fetch(
        [(carrier, states.at[0]), (grating, states.at[1]), (loss, losses)]
        + history_copies(forward, backward, population, hole, s, whole, wide, plain),
        sems,
    )
    for copy in copies:
        copy.wait()
    mine, theirs = both_halves(info, rows)
    put_tiles(out, 0, losses[theirs])
    put_tiles(own_loss, 0, losses[mine])
    sizes = []
    for i, kept in enumerate((own_carrier, own_grating)):
        value = states[i, theirs]
        size = size_of(jnp.abs(value))
        sizes.append((SCALE_LANE + i, size))
        put_tiles(out, (1 + i) * half, encoded(value, size))
        kept[...] = states[i, mine]
    put_history(out, 3 * half, half, wide, plain, theirs)
    put_history(own, 0, half, wide, plain, mine)
    out[9 * half * rows :, :] = side_tile(sizes, rows)


def enter_kernel(
    info, forward, backward, other, source, tp, tq, inner, outer, field, work, matrices, sem, sems
):
    copy = pltpu.make_async_copy(source, matrices, sem)
    rows, width = field.shape[1] // 2, field.shape[2]
    columns = width // 2
    half = columns // LANES
    at = rows_of(info, rows, False)
    copies = fetch(
        [
            (ref.at[:, at, :], field.at[:, f * rows : (f + 1) * rows, :columns])
            for f, ref in enumerate((forward, backward))
        ],
        sems,
    )
    copy.start()
    sizes = sizes_in(other[4 * half * rows :, :], 2)
    for f in range(2):
        for part in range(2):

            @pl.loop(0, half, unroll=2)
            def _(j):
                code = other[slab((2 * f + part) * half + j, rows), :]
                field[part, f * rows : (f + 1) * rows, lane(half + j)] = decoded(code, sizes[f])

    for held in copies:
        held.wait()
    filtered(field, work, matrices, copy)
    write_filtered(info, work, tp, tq, inner, outer)


def rows_update(
    info, tp, tq, inner, outer, carrier, grating, own, other, own_loss, other_loss,
    field, new_carrier, new_grating, sums_in, sums, cells, last
):
    rows, width = carrier.shape
    half = width // LANES // 2
    columns = half * LANES
    mid = jnp.where(info[0] == 0, 1.0, 0.0)
    wrap = 1.0 - mid
    low = info[4] == 0
    is_first = info[1] == 1
    is_last = info[2] == 1
    row_index = lax.broadcasted_iota(jnp.int32, (TILE, LANES), 0)
    zero = jnp.zeros((8, LANES), jnp.float32)

    def step(jj, most):
        for side in range(2):
            j = jj + side * half
            here = lane(j)
            left_at = lane(jnp.where(j == 0, 2 * half - 1, j - 1))
            right_at = lane(jnp.where(j == 2 * half - 1, 0, j + 1))
            swapped = lane(jj + (1 - side) * half)
            weight_left = jnp.where(jj == 0, wrap if side == 0 else mid, 1.0)
            weight_right = jnp.where(jj == half - 1, mid if side == 0 else wrap, 1.0)
            total = zero
            for r in range(0, rows, TILE):
                at = slice(r, r + TILE)

                held, begin = (own, other)[side]

                def part_of(i):
                    tile = begin + (i * half + jj) * rows + r
                    return held[pl.ds(pl.multiple_of(tile, TILE), TILE), :].astype(jnp.float32)

                loss = (own_loss, other_loss)[side][
                    pl.ds(pl.multiple_of(jj * rows + r, TILE), TILE), :
                ].astype(jnp.float32)
                f = [tp[part, r + 1 : r + 1 + TILE, here] for part in range(2)]
                b = [tq[part, r + 7 : r + 7 + TILE, here] for part in range(2)]
                if r + TILE == rows:
                    for part in range(2):
                        facet = FRONT_FACET * tq[part, rows + 7 : rows + 8, here]
                        edge = jnp.where(
                            low, inner[part : part + 1, swapped], outer[part : part + 1, here]
                        )
                        edge = jnp.where(is_last, facet, edge)
                        f[part] = jnp.where(row_index == TILE - 1, edge, f[part])
                if r == 0:
                    for part in range(2):
                        facet = REAR_FACET * tp[part, 0:1, here]
                        edge = jnp.where(
                            low, outer[part : part + 1, here], inner[part : part + 1, swapped]
                        )
                        edge = jnp.where(is_first, facet, edge)
                        b[part] = jnp.where(row_index == 0, edge, b[part])
                c = carrier[at, here]
                lap = curvature(
                    carrier[at, left_at], c, carrier[at, right_at], weight_left, weight_right
                )
                out = updated(
                    *f, *b, [part_of(i) for i in range(4)], part_of(4), part_of(5), loss,
                    c, grating[at, here], lap,
                )
                field[0, r : r + TILE, here] = out[0]
                field[1, r : r + TILE, here] = out[1]
                field[0, rows + r : rows + r + TILE, here] = out[2]
                field[1, rows + r : rows + r + TILE, here] = out[3]
                new_carrier[at, here] = out[4]
                new_grating[at, here] = out[5]
                z = (info[3] + r + row_index).astype(jnp.float32)
                weighted = (1.0 + 2.0 * z / (cells - 1)) * ((c + out[4]) if last else c)
                for k in range(0, TILE, 8):
                    total = total + weighted[k : k + 8]
                if last and side == 1:
                    for k in range(0, TILE, 8):
                        most = (
                            jnp.maximum(most[0], jnp.abs(out[4][k : k + 8])),
                            jnp.maximum(most[1], jnp.abs(out[5][k : k + 8])),
                        )
            summed = jnp.sum(total, axis=0, keepdims=True)
            sums[:, here] = summed if sums_in is None else summed + sums_in[:, here]
        return most

    return lax.fori_loop(0, half, step, (zero, zero))


def first_step_kernel(
    cells, info, tp, tq, inner, outer, my_carrier, my_grating, loss, own, other, source,
    new_tp, new_tq, new_inner, new_outer, new_carrier, new_grating, sums,
    carrier, grating, field, work, matrices, sem,
):
    copy = pltpu.make_async_copy(source, matrices, sem)
    copy.start()
    rows, columns = my_carrier.shape
    half = columns // LANES
    sizes = sizes_in(other[9 * half * rows :, :], 2)
    for i, (whole, mine) in enumerate(((carrier, my_carrier), (grating, my_grating))):
        whole[:, :columns] = mine[...]

        @pl.loop(0, half, unroll=2)
        def _(j):
            whole[:, lane(half + j)] = decoded(other[slab((1 + i) * half + j, rows), :], sizes[i])

    rows_update(
        info, tp, tq, inner, outer, carrier, grating,
        (own, 0), (other, 3 * half * rows), loss, other,
        field, new_carrier, new_grating, None, sums, cells, False,
    )
    filtered(field, work, matrices, copy)
    write_filtered(info, work, new_tp, new_tq, new_inner, new_outer)


def middle_step_kernel(
    cells, info, tp, tq, inner, outer, carrier, grating, loss, own, other, other_loss, sums_in,
    source, new_tp, new_tq, new_inner, new_outer, new_carrier, new_grating, sums,
    field, work, matrices, sem,
):
    copy = pltpu.make_async_copy(source, matrices, sem)
    copy.start()
    rows_update(
        info, tp, tq, inner, outer, carrier, grating, (own, 0), (other, 0), loss, other_loss,
        field, new_carrier, new_grating, sums_in, sums, cells, False,
    )
    filtered(field, work, matrices, copy)
    write_filtered(info, work, new_tp, new_tq, new_inner, new_outer)


def leave_step_kernel(
    cells, info, tp, tq, inner, outer, carrier, grating, loss, own, other, other_loss, sums_in,
    field, kept_carrier, kept_grating, sides, sent, sums,
    new_carrier, new_grating,
):
    rows, width = carrier.shape
    columns = width // 2
    half = columns // LANES
    most = rows_update(
        info, tp, tq, inner, outer, carrier, grating, (own, 0), (other, 0), loss, other_loss,
        field, new_carrier, new_grating, sums_in, sums, cells, True,
    )
    mid = jnp.where(info[0] == 0, 1.0, 0.0)
    wrap = 1.0 - mid
    kept_carrier[...] = new_carrier[:, :columns]
    kept_grating[...] = new_grating[:, :columns]
    first, before = new_carrier[:, 0:1] * wrap, new_carrier[:, columns - 1 : columns] * mid
    after, final = new_carrier[:, columns : columns + 1] * mid, new_carrier[:, width - 1 :] * wrap
    sides[0] = jnp.broadcast_to(final, (rows, LANES))
    sides[1] = jnp.broadcast_to(after, (rows, LANES))
    pairs = []
    for at, value in ((0, before), (2, first)):
        coarse = value.astype(jnp.bfloat16).astype(jnp.float32)
        pairs += [(at, coarse), (at + 1, value - coarse)]
    for i, field_of in enumerate((new_carrier, new_grating)):
        size = size_of(most[i])
        pairs.append((SCALE_LANE + i, size))

        @pl.loop(0, half)
        def _(j):
            sent[slab(i * half + j, rows), :] = encoded(field_of[:, lane(half + j)], size)

    sent[2 * half * rows :, :] = side_tile(pairs, rows)


def leave_filter_kernel(info, field, source, kept, sent, straight, across, work, matrices, sem):
    copy = pltpu.make_async_copy(source, matrices, sem)
    copy.start()
    rows, width = field.shape[1] // 2, field.shape[2]
    blocks = width // LANES
    half = blocks // 2
    columns = width // 2
    filtered(field, work, matrices, copy)
    zero = jnp.zeros((8, LANES), jnp.float32)
    sizes = []
    for f in range(2):

        def unmix(g, most):
            at = pl.ds(pl.multiple_of(g * 8 + f * rows, 8), 8)
            for j, pair in enumerate(gathered(work, at)):
                for part in range(2):
                    if j < half:
                        kept[part, at, j * LANES : (j + 1) * LANES] = pair[part]
                    else:
                        work[j, at, part * LANES : (part + 1) * LANES] = pair[part]
                        most = jnp.maximum(most, jnp.abs(pair[part]))
            return most

        size = size_of(lax.fori_loop(0, rows // 8, unmix, zero))
        sizes.append((SCALE_LANE + f, size))

        @pl.loop(0, half)
        def _(j):
            for part in range(2):
                value = work[half + j, f * rows : (f + 1) * rows, part * LANES : (part + 1) * LANES]
                sent[slab((2 * f + part) * half + j, rows), :] = encoded(value, size)

    sent[4 * half * rows :, :] = side_tile(sizes, rows)
    low = info[4] == 0
    for part in range(2):
        lanes = slice(part * LANES, (part + 1) * LANES)
        straight[part : part + 1, :] = jnp.where(
            low, kept[part, 0:1, :], kept[part, 2 * rows - 1 : 2 * rows, :]
        )
        for j in range(half):
            across[part : part + 1, j * LANES : (j + 1) * LANES] = jnp.where(
                low, work[half + j, 0:1, lanes], work[half + j, 2 * rows - 1 : 2 * rows, lanes]
            )


def final_kernel(
    info, kept, kept_carrier, kept_grating, sides, fields, pair, straight, across, loss_in,
    forward, backward, population, hole,
    out_forward, out_backward, out_carrier, out_grating,
    tp, tq, carrier, grating, wide, plain, loss, sems,
):
    rows, columns = kept_carrier.shape
    half = columns // LANES
    copies = fetch(
        [(loss_in, loss)]
        + history_copies(forward, backward, population, hole, 0, pl.ds(0, 2 * rows), wide, plain),
        sems,
    )
    mine = info[4] * rows
    theirs = (1 - info[4]) * rows
    low = info[4] == 0
    extra = pair[2 * half * rows :, :]
    size_carrier, size_grating = sizes_in(extra, 2)
    size_forward, size_backward = sizes_in(fields[4 * half * rows :, :], 2)
    extra = extra.astype(jnp.float32)

    def at(start, offset, count):
        return pl.ds(pl.multiple_of(start + offset, 8), count)

    for part in range(2):
        tp[part, at(mine, 0, rows), :] = kept[part, :rows, :]
        tq[part, at(mine, 8, rows), :] = kept[part, rows:, :]
    carrier[at(mine, 0, rows), LANES : LANES + columns] = kept_carrier[...]
    carrier[at(mine, 0, rows), :LANES] = sides[0]
    carrier[at(mine, 0, rows), LANES + columns :] = sides[1]
    carrier[at(theirs, 0, rows), :LANES] = jnp.broadcast_to(
        extra[:, 0:1] + extra[:, 1:2], (rows, LANES)
    )
    carrier[at(theirs, 0, rows), LANES + columns :] = jnp.broadcast_to(
        extra[:, 2:3] + extra[:, 3:4], (rows, LANES)
    )
    grating[at(mine, 0, rows), :] = kept_grating[...]

    @pl.loop(0, half)
    def _(j):
        carrier[at(theirs, 0, rows), lane(1 + j)] = decoded(pair[slab(j, rows), :], size_carrier)
        grating[at(theirs, 0, rows), lane(j)] = decoded(pair[slab(half + j, rows), :], size_grating)
        for part in range(2):
            tp[part, at(theirs, 0, rows), lane(j)] = decoded(
                fields[slab(part * half + j, rows), :], size_forward
            )
            tq[part, at(theirs, 8, rows), lane(j)] = decoded(
                fields[slab((2 + part) * half + j, rows), :], size_backward
            )

    all_rows = 2 * rows
    for part in range(2):
        here = slice(part, part + 1)
        next_edge = jnp.where(low, across[here, :], straight[here, :])
        before_edge = jnp.where(low, straight[here, :], across[here, :])
        front = FRONT_FACET * tq[part, all_rows + 7 : all_rows + 8, :]
        rear = REAR_FACET * tp[part, 0:1, :]
        tp[part, all_rows : all_rows + 1, :] = jnp.where(info[2] == 1, front, next_edge)
        tq[part, 7:8, :] = jnp.where(info[1] == 1, rear, before_edge)

    for copy in copies:
        copy.wait()

    @pl.loop(0, half)
    def _(j):
        here = lane(j)
        for r in range(0, all_rows, TILE):
            row = slice(r, r + TILE)
            c = carrier[row, lane(j + 1)]
            lap = curvature(carrier[row, lane(j)], c, carrier[row, lane(j + 2)], 1.0, 1.0)
            out = updated(
                tp[0, r + 1 : r + 1 + TILE, here], tp[1, r + 1 : r + 1 + TILE, here],
                tq[0, r + 7 : r + 7 + TILE, here], tq[1, r + 7 : r + 7 + TILE, here],
                [wide[f, part, row, here].astype(jnp.float32) for f in range(2) for part in range(2)],
                plain[0, row, here].astype(jnp.float32), plain[1, row, here].astype(jnp.float32),
                loss[row, here].astype(jnp.float32), c, grating[row, here], lap,
            )
            out_forward[0, row, here] = out[0]
            out_forward[1, row, here] = out[1]
            out_backward[0, row, here] = out[2]
            out_backward[1, row, here] = out[3]
            out_carrier[row, here] = out[4]
            out_grating[row, here] = out[5]


def whole_spec(shape):
    return pl.BlockSpec(shape, lambda i, info, n=len(shape): (0,) * n)


def call(name, kernel, info, inputs, outputs, scratch, flops=0, grant=48):
    arrays = [x[0] if isinstance(x, tuple) else x for x in inputs]
    specs = [x[1] if isinstance(x, tuple) else whole_spec(x.shape) for x in inputs]
    shapes = [jax.ShapeDtypeStruct(*out) for out in outputs]
    moved = sum(math.prod(s.shape) * s.dtype.itemsize for s in shapes)
    result = pl.pallas_call(
        kernel,
        grid_spec=pltpu.PrefetchScalarGridSpec(
            num_scalar_prefetch=1,
            grid=(1,),
            in_specs=specs,
            out_specs=[whole_spec(s.shape) for s in shapes],
            scratch_shapes=scratch,
        ),
        out_shape=shapes,
        compiler_params=pltpu.CompilerParams(vmem_limit_bytes=grant * 1024 * 1024),
        cost_estimate=pl.CostEstimate(
            flops=flops, bytes_accessed=moved + 4 * 1024 * 1024, transcendentals=0
        ),
        name=name,
    )(info, *arrays)
    return result


def per_pair(
    ending_rightward_adjoint,
    ending_leftward_adjoint,
    ending_population_adjoint,
    ending_holeburn_adjoint,
    history_rightward,
    history_leftward,
    history_population,
    history_holeburn,
    segment_passive_attenuation,
):
    cell_rows, columns = ending_population_adjoint.shape
    passes = history_population.shape[0]
    rows = cell_rows // 2
    half = columns // LANES
    blocks = 2 * half
    width = 2 * columns
    count = lax.axis_size("gz")
    cells = cell_rows * count
    x = lax.axis_index("gx")
    block = lax.axis_index("gz")
    f32, bf16 = jnp.float32, jnp.bfloat16

    high = lax.rem(x + block, 2)
    place = 2 * block + high

    def info_of(first, last):
        return jnp.stack([x, first, last, place * rows, high]).astype(jnp.int32)

    info = info_of(place == 0, place == 2 * count - 1)
    info_block = info_of(block == 0, block == count - 1)
    swap = [(0, 1), (1, 0)]
    in_place = pl.BlockSpec(memory_space=pltpu.HBM)

    def held(*arrays):
        return [(a, in_place) for a in arrays]

    def tiles(n):
        return ((n * rows, LANES), bf16)

    ends = held(ending_rightward_adjoint, ending_leftward_adjoint)
    planes = held(ending_population_adjoint, ending_holeburn_adjoint)
    history = held(history_rightward, history_leftward, history_population, history_holeburn)
    losses = held(segment_passive_attenuation)
    matrices = jnp.asarray(lateral_matrices(width, blocks))
    matrix_input = held(matrices)
    work = [
        pltpu.VMEM((blocks, 2 * rows, 2 * LANES), f32),
        pltpu.VMEM(matrices.shape, bf16),
        pltpu.SemaphoreType.DMA,
    ]
    history_scratch = [
        pltpu.VMEM((2, 2, cell_rows, columns), bf16), pltpu.VMEM((2, cell_rows, columns), bf16),
    ]
    field_scratch = pltpu.VMEM((2, 2 * rows, width), f32)
    state_out = [
        ((2, rows + 8, width), f32), ((2, rows + 8, width), f32), ((2, width), f32), ((2, width), f32),
    ]
    plane = ((rows, width), f32)
    plane_scratch = pltpu.VMEM((rows, width), f32)
    half_plane = ((rows, columns), f32)
    work_flops = 2 * 3 * 2 * rows * blocks * (2 * LANES) ** 2

    (coded,) = call(
        "send_fields", send_fields_kernel, info, ends, [tiles(4 * half + 1)],
        [pltpu.VMEM((2, 2, rows, columns), f32), pltpu.SemaphoreType.DMA((2,))], grant=62,
    )
    coded, info = lax.optimization_barrier((coded, info))
    other_fields = lax.ppermute(coded, "gx", swap)
    loss, own_first, my_carrier, my_grating, coded = call(
        "send_first", functools.partial(send_first_kernel, passes - 1), info,
        [*losses, *planes, *history],
        [tiles(half), tiles(6 * half), half_plane, half_plane, tiles(9 * half + 1)],
        [*history_scratch, pltpu.VMEM((cell_rows, columns), bf16),
         pltpu.VMEM((2, cell_rows, columns), f32), pltpu.SemaphoreType.DMA((7,))], grant=62,
    )
    later = [
        call(
            "send_history", functools.partial(send_history_kernel, s), info, history,
            [tiles(6 * half), tiles(6 * half)],
            [*history_scratch, pltpu.SemaphoreType.DMA((4,))], grant=62,
        )
        for s in range(passes - 2, 0, -1)
    ]
    coded, later, other_fields = lax.optimization_barrier((coded, later, other_fields))
    other_first = lax.ppermute(coded, "gx", swap)

    line = ("gz", "gx")
    neighbours = []
    for b in range(count - 1):
        top = (1 + b) % 2
        neighbours += [(2 * b + top, 2 * b + 2 + top), (2 * b + 2 + top, 2 * b + top)]

    def edges(inner, outer):
        return lax.ppermute(inner, "gx", swap), lax.ppermute(outer, line, neighbours)

    tp, tq, inner, outer = call(
        "enter", enter_kernel, info, [*ends, other_fields, *matrix_input],
        state_out, [field_scratch, *work, pltpu.SemaphoreType.DMA((2,))], work_flops,
    )
    inner, outer = edges(inner, outer)

    other_loss = (other_first, pl.BlockSpec((half * rows, LANES), lambda i, info: (0, 0)))
    carrier = grating = sums = other = own = None
    for index, s in enumerate(range(passes - 1, 0, -1)):
        if index < len(later):
            own_next, sent = later[index]
            sent, inner, outer = lax.optimization_barrier((sent, inner, outer))
            coming = lax.ppermute(sent, "gx", swap)
        shared = [tp, tq, inner, outer]
        if index == 0:
            tp, tq, inner, outer, carrier, grating, sums = call(
                "first_step", functools.partial(first_step_kernel, cells), info,
                [*shared, my_carrier, my_grating, loss, own_first, other_first, *matrix_input],
                [*state_out, plane, plane, ((1, width), f32)],
                [plane_scratch, plane_scratch, field_scratch, *work], work_flops,
            )
        elif s > 1:
            tp, tq, inner, outer, carrier, grating, sums = call(
                "middle_step", functools.partial(middle_step_kernel, cells), info,
                [*shared, carrier, grating, loss, own, other, other_loss, sums, *matrix_input],
                [*state_out, plane, plane, ((1, width), f32)],
                [field_scratch, *work], work_flops,
            )
        else:
            field, kept_carrier, kept_grating, sides, sent, sums = call(
                "leave_step", functools.partial(leave_step_kernel, cells), info,
                [*shared, carrier, grating, loss, own, other, other_loss, sums],
                [((2, 2 * rows, width), f32), half_plane, half_plane,
                 ((2, rows, LANES), f32), tiles(2 * half + 1), ((1, width), f32)],
                [plane_scratch, plane_scratch],
            )
        if s > 1:
            inner, outer = edges(inner, outer)
            own, other = own_next, coming

    pair = lax.ppermute(sent, "gx", swap)
    kept, sent, straight, across = call(
        "leave_filter", leave_filter_kernel, info, [field, *matrix_input],
        [((2, 2 * rows, columns), f32), tiles(4 * half + 1), ((2, columns), f32), ((2, columns), f32)],
        work, work_flops,
    )
    sent, pair, sums = lax.optimization_barrier((sent, pair, sums))
    fields = lax.ppermute(sent, "gx", swap)

    sums = sums.reshape(2, half, LANES)
    sums = jnp.where(x == 0, sums, sums[::-1])
    sums = jnp.broadcast_to(sums, (count, 2, half, LANES)).reshape(2 * count, half, LANES)
    sums = lax.all_to_all(sums, line, 0, 0, tiled=True)
    sums, straight, across = lax.optimization_barrier((sums, straight, across))
    total = jnp.sum(sums, axis=0).reshape(columns)

    straight = lax.ppermute(straight, line, neighbours)
    along = []
    for b in range(count - 1):
        top, foot = (1 + b) % 2, b % 2
        along += [(2 * b + top, 2 * b + 2 + foot), (2 * b + 2 + top, 2 * b + foot)]
    across = lax.ppermute(across, line, along)

    outs = call(
        "final", final_kernel, info_block,
        [kept, kept_carrier, kept_grating, sides, fields, pair, straight, across, *losses, *history],
        [((2, cell_rows, columns), f32), ((2, cell_rows, columns), f32),
         ((cell_rows, columns), f32), ((cell_rows, columns), f32)],
        [pltpu.VMEM((2, cell_rows + 8, columns), f32), pltpu.VMEM((2, cell_rows + 8, columns), f32),
         pltpu.VMEM((cell_rows, columns + 2 * LANES), f32), pltpu.VMEM((cell_rows, columns), f32),
         *history_scratch, pltpu.VMEM((cell_rows, columns), bf16), pltpu.SemaphoreType.DMA((5,))],
        grant=48,
    )
    return (*outs, CLOCK_DELTA * total / math.sqrt(cells))


def shared_by_pairs(mesh, arguments):
    population = arguments[6]
    passes, cells, width = population.shape
    rows, columns = cells // mesh.shape["gz"], width // mesh.shape["gx"]
    return (
        mesh.shape["gx"] == 2
        and passes >= 3
        and rows % (2 * TILE) == 0
        and columns % LANES == 0
        and (columns // LANES) & (columns // LANES - 1) == 0
        and width <= 4096
    )


def solution(mesh):
    def run(*arguments):
        body = per_pair if shared_by_pairs(mesh, arguments) else per_device
        return jax.shard_map(
            body,
            mesh=mesh,
            in_specs=(
                P(None, "gz", "gx"),
                P(None, "gz", "gx"),
                P("gz", "gx"),
                P("gz", "gx"),
                P(None, None, "gz", "gx"),
                P(None, None, "gz", "gx"),
                P(None, "gz", "gx"),
                P(None, "gz", "gx"),
                P("gz", "gx"),
            ),
            out_specs=(
                P(None, "gz", "gx"), P(None, "gz", "gx"), P("gz", "gx"), P("gz", "gx"), P("gx"),
            ),
            check_vma=False,
        )(*arguments)

    return run
```

```python
import functools
import math

import jax
import jax.numpy as jnp
import ml_dtypes
import numpy as np
from jax import lax
from jax.experimental import pallas as pl
from jax.experimental.pallas import tpu as pltpu
from jax.sharding import PartitionSpec as P

DIFF = 512


FRONT_FACET = 0.3
REAR_FACET = 0.9
GAIN_SLOPE_RATE = 0.3
ALPHA_LINEWIDTH = 2.0
COUPLING = 0.5
CLOCK_DELTA = 0.3
DENSITY_LIFETIME = 2.0
GRATING_LIFE = 0.75
TRANSVERSE_DIFFUS = 0.2


def passed_along(value, axis, steps):
    count = lax.axis_size(axis)
    initial, last = (max(0, -steps), min(count, count - steps))
    return lax.ppermute(value, axis, [(source, source + steps) for source in range(initial, last)])


def with_halo(block, sides, width):
    for axis, dim in sides:
        count = lax.axis_size(axis)
        forward = [(i, i + 1) for i in range(count - 1)]
        backward = [(target, source) for source, target in forward]
        low = lax.ppermute(
            lax.slice_in_dim(block, block.shape[dim] - width, None, axis=dim), axis, forward
        )
        high = lax.ppermute(lax.slice_in_dim(block, 0, width, axis=dim), axis, backward)
        block = jnp.concatenate([low, block, high], axis=dim)
    return block


def rotate(source_re, source_im, cosine, sine, form, sign):
    exact = lax.Precision.HIGHEST
    out_re = jnp.einsum(form, source_re, cosine, precision=exact) + sign * jnp.einsum(
        form, source_im, sine, precision=exact
    )
    out_im = jnp.einsum(form, source_im, cosine, precision=exact) - sign * jnp.einsum(
        form, source_re, sine, precision=exact
    )
    return (out_re, out_im)


def transform(stacked):
    count = stacked.shape[1]
    width = stacked.shape[2]
    second = min(128, width // 2)
    first = width // second
    two_pi = 2.0 * math.pi
    index_a = jnp.arange(first, dtype=jnp.int32)
    index_b = jnp.arange(second, dtype=jnp.int32)
    angle_a = two_pi * (index_a[:, None] * index_a[None, :] % first).astype(jnp.float32) / first
    angle_b = two_pi * (index_b[:, None] * index_b[None, :] % second).astype(jnp.float32) / second
    angle_t = two_pi * (index_a[:, None] * index_b[None, :] % width).astype(jnp.float32) / width
    cos_a, sin_a = (jnp.cos(angle_a), jnp.sin(angle_a))
    cos_b, sin_b = (jnp.cos(angle_b), jnp.sin(angle_b))
    cos_t, sin_t = (jnp.cos(angle_t), jnp.sin(angle_t))
    wavenum = index_a[:, None] + first * index_b[None, :]
    signed = jnp.where(wavenum < width // 2, wavenum, wavenum - width)
    phase = (signed * signed).astype(jnp.float32) * (DIFF / (width / 2) ** 2)
    cos_p, sin_p = (jnp.cos(phase), jnp.sin(phase))
    real_in = stacked[0].reshape(count, first, second)
    imag_in = stacked[1].reshape(count, first, second)
    step_re, step_im = rotate(real_in, imag_in, cos_a, sin_a, "nab,ak->nkb", 1.0)
    twist_re = step_re * cos_t + step_im * sin_t
    twist_im = step_im * cos_t - step_re * sin_t
    spec_re, spec_im = rotate(twist_re, twist_im, cos_b, sin_b, "nkb,bj->nkj", 1.0)
    moved_re = spec_re * cos_p - spec_im * sin_p
    moved_im = spec_re * sin_p + spec_im * cos_p
    back_re, back_im = rotate(moved_re, moved_im, cos_b, sin_b, "nkj,jb->nkb", -1.0)
    untw_re = back_re * cos_t - back_im * sin_t
    untw_im = back_im * cos_t + back_re * sin_t
    final_re, final_im = rotate(untw_re, untw_im, cos_a, sin_a, "nkb,ka->nab", -1.0)
    return jnp.stack([final_re.reshape(count, width), final_im.reshape(count, width)]) / width


def added_up(value, axis):
    count = lax.axis_size(axis)
    if count & (count - 1):
        return lax.psum(value, axis)
    reach = 1
    while reach < count:
        value = value + lax.ppermute(value, axis, [(i, i ^ reach) for i in range(count)])
        reach *= 2
    return value


def lateral_work(parts):
    return (transform(parts[0]), transform(parts[1]))


def multiplier_revision(
    population_multiplier,
    holeburn_multiplier,
    measured_rightward,
    measured_leftward,
    rightward_wave,
    leftward_wave,
    population_level,
    holeburn_magnitude,
    attenuation_factor,
    transverse_curvature,
):
    rightward_inphase, rightward_quadrature = (rightward_wave[0], rightward_wave[1])
    leftward_inphase, leftward_quadrature = (leftward_wave[0], leftward_wave[1])
    measured_rightward_inphase, measured_rightward_quadrature = (
        measured_rightward[0],
        measured_rightward[1],
    )
    measured_leftward_inphase, measured_leftward_quadrature = (
        measured_leftward[0],
        measured_leftward[1],
    )
    surplus_population = population_level - 1.0
    amplification_inphase = 1.0 + 0.5 * (GAIN_SLOPE_RATE * surplus_population - attenuation_factor)
    amplification_quadrature = 0.5 * GAIN_SLOPE_RATE * ALPHA_LINEWIDTH * surplus_population
    joined_waves = COUPLING * holeburn_magnitude
    population_derivative = (
        2.0 * CLOCK_DELTA * GAIN_SLOPE_RATE * surplus_population * population_multiplier
    )
    holeburn_derivative = 2.0 * CLOCK_DELTA * holeburn_multiplier
    revised_rightward_inphase = (
        amplification_inphase * measured_rightward_inphase
        - amplification_quadrature * measured_rightward_quadrature
        + joined_waves * measured_leftward_quadrature
        - population_derivative * rightward_inphase
        + holeburn_derivative * leftward_inphase
    )
    revised_rightward_quadrature = (
        amplification_inphase * measured_rightward_quadrature
        + amplification_quadrature * measured_rightward_inphase
        - joined_waves * measured_leftward_inphase
        - population_derivative * rightward_quadrature
        + holeburn_derivative * leftward_quadrature
    )
    revised_leftward_inphase = (
        amplification_inphase * measured_leftward_inphase
        - amplification_quadrature * measured_leftward_quadrature
        + joined_waves * measured_rightward_quadrature
        - population_derivative * leftward_inphase
        + holeburn_derivative * rightward_inphase
    )
    revised_leftward_quadrature = (
        amplification_inphase * measured_leftward_quadrature
        + amplification_quadrature * measured_leftward_inphase
        - joined_waves * measured_rightward_inphase
        - population_derivative * leftward_quadrature
        + holeburn_derivative * rightward_quadrature
    )
    light_intensity = (
        rightward_inphase * rightward_inphase
        + rightward_quadrature * rightward_quadrature
        + leftward_inphase * leftward_inphase
        + leftward_quadrature * leftward_quadrature
    )
    amplification_share = (
        measured_rightward_inphase * (rightward_inphase + ALPHA_LINEWIDTH * rightward_quadrature)
        + measured_rightward_quadrature
        * (rightward_quadrature - ALPHA_LINEWIDTH * rightward_inphase)
        + measured_leftward_inphase * (leftward_inphase + ALPHA_LINEWIDTH * leftward_quadrature)
        + measured_leftward_quadrature * (leftward_quadrature - ALPHA_LINEWIDTH * leftward_inphase)
    )
    revised_population = (
        population_multiplier
        * (1.0 - CLOCK_DELTA / DENSITY_LIFETIME - CLOCK_DELTA * GAIN_SLOPE_RATE * light_intensity)
        + TRANSVERSE_DIFFUS * transverse_curvature
        + 0.5 * GAIN_SLOPE_RATE * amplification_share
    )
    fresh_holeburn = holeburn_multiplier * (1.0 - CLOCK_DELTA / GRATING_LIFE) + COUPLING * (
        measured_rightward_quadrature * leftward_inphase
        - measured_rightward_inphase * leftward_quadrature
        + measured_leftward_quadrature * rightward_inphase
        - measured_leftward_inphase * rightward_quadrature
    )
    return (
        jnp.stack([revised_rightward_inphase, revised_rightward_quadrature]),
        jnp.stack([revised_leftward_inphase, revised_leftward_quadrature]),
        revised_population,
        fresh_holeburn,
    )


def per_device(
    ending_rightward_adjoint,
    ending_leftward_adjoint,
    ending_population_adjoint,
    ending_holeburn_adjoint,
    history_rightward,
    history_leftward,
    history_population,
    history_holeburn,
    segment_passive_attenuation,
):
    columns = ending_rightward_adjoint.shape[2]
    rows = ending_rightward_adjoint.shape[1]
    blocks = lax.axis_size("gz")
    position = lax.axis_index("gz")
    cells = rows * blocks
    zpos = (position * rows + jnp.arange(rows, dtype=jnp.int32)).astype(jnp.float32)
    scaling_factor = 1.0 + 2.0 * zpos / (cells - 1)
    rightward_multiplier, leftward_multiplier = (ending_rightward_adjoint, ending_leftward_adjoint)
    population_multiplier, holeburn_multiplier = (
        ending_population_adjoint,
        ending_holeburn_adjoint,
    )
    attenuation_factor = segment_passive_attenuation.astype(jnp.float32)
    shape_curve = jnp.zeros((columns,), jnp.float32)
    for moment_position in range(history_rightward.shape[0] - 1, -1, -1):
        shape_curve = shape_curve + jnp.sum(scaling_factor[:, None] * population_multiplier, axis=0)
        above = passed_along(rightward_multiplier[:, :1, :], "gz", -1)
        below = passed_along(leftward_multiplier[:, -1:, :], "gz", 1)
        top_row = jnp.where(
            position == blocks - 1, FRONT_FACET * leftward_multiplier[:, -1:, :], above
        )
        bottom_row = jnp.where(position == 0, REAR_FACET * rightward_multiplier[:, :1, :], below)
        lam_fwd = jnp.concatenate([rightward_multiplier[:, 1:, :], top_row], axis=1)
        lam_bwd = jnp.concatenate([bottom_row, leftward_multiplier[:, :-1, :]], axis=1)
        whole_fwd, whole_bwd = (
            lax.all_gather(lam_fwd, "gx", axis=2, tiled=True),
            lax.all_gather(lam_bwd, "gx", axis=2, tiled=True),
        )
        start = lax.axis_index("gx") * columns
        done_fwd, done_bwd = lateral_work((whole_fwd, whole_bwd))
        measured_rightward = lax.dynamic_slice_in_dim(done_fwd, start, columns, 2)
        measured_leftward = lax.dynamic_slice_in_dim(done_bwd, start, columns, 2)
        bordered_array = with_halo(population_multiplier, (("gx", 1),), 1)
        transverse_curvature = (
            bordered_array[:, 2:] + bordered_array[:, :-2] - 2.0 * population_multiplier
        )
        rightward_multiplier, leftward_multiplier, population_multiplier, holeburn_multiplier = (
            multiplier_revision(
                population_multiplier,
                holeburn_multiplier,
                measured_rightward,
                measured_leftward,
                history_rightward[moment_position].astype(jnp.float32),
                history_leftward[moment_position].astype(jnp.float32),
                history_population[moment_position].astype(jnp.float32),
                history_holeburn[moment_position].astype(jnp.float32),
                attenuation_factor,
                transverse_curvature,
            )
        )
    total = added_up(shape_curve, "gz")
    derivative_vector = CLOCK_DELTA * total / math.sqrt(cells)
    return (
        rightward_multiplier,
        leftward_multiplier,
        population_multiplier,
        holeburn_multiplier,
        derivative_vector,
    )

LANES = 128
TILE = 16
POWER = 12
STRETCH = 1211.0
SCALE_LANE = 8


def lateral_matrices(width, blocks):
    lanes = width // blocks
    k = np.arange(width)
    signed = np.where(k < width // 2, k, k - width).astype(np.float64)
    response = np.fft.ifft(np.exp(1j * signed * signed * (DIFF / (width / 2) ** 2)))
    step = np.arange(lanes)
    shift = lanes * np.arange(blocks)[:, None, None] + step[None, None, :] - step[None, :, None]
    kernels = np.fft.fft(response[shift % width], axis=0) / blocks
    top = np.concatenate([kernels.real, kernels.imag], axis=2)
    low = np.concatenate([-kernels.imag, kernels.real], axis=2)
    whole = np.concatenate([top, low], axis=1)
    first = whole.astype(ml_dtypes.bfloat16)
    rest = (whole - first.astype(np.float64)).astype(ml_dtypes.bfloat16)
    return np.stack([first, rest], axis=1)


def block_dft(values, sign):
    count = len(values)
    if count == 1:
        return values
    even = block_dft(values[0::2], sign)
    odd = block_dft(values[1::2], sign)
    out = [None] * count
    for k in range(count // 2):
        (er, ei), (wr, wi) = even[k], odd[k]
        if 4 * k == count:
            plus, minus = (er - wi, ei + wr), (er + wi, ei - wr)
            out[k], out[k + count // 2] = (plus, minus) if sign > 0 else (minus, plus)
            continue
        if k:
            c, s = math.cos(2 * math.pi * k / count), sign * math.sin(2 * math.pi * k / count)
            if 8 * k == count:
                wr, wi = (c * (wr - wi), c * (wr + wi)) if sign > 0 else (c * (wr + wi), c * (wi - wr))
            elif 8 * k == 3 * count:
                wr, wi = (c * (wr + wi), c * (wi - wr)) if sign > 0 else (c * (wr - wi), c * (wr + wi))
            else:
                wr, wi = c * wr - s * wi, c * wi + s * wr
        out[k] = (er + wr, ei + wi)
        out[k + count // 2] = (er - wr, ei - wi)
    return out


def lane(j):
    return pl.ds(pl.multiple_of(j * LANES, LANES), LANES)


def slab(j, rows):
    return pl.ds(pl.multiple_of(j * rows, rows), rows)


def fetch(pairs, sems, first=0):
    copies = [pltpu.make_async_copy(a, b, sems.at[first + i]) for i, (a, b) in enumerate(pairs)]
    for copy in copies:
        copy.start()
    return copies


def rows_of(info, rows, other):
    part = 1 - info[4] if other else info[4]
    return pl.ds(pl.multiple_of(part * rows, rows), rows)


def spread(field, work):
    rows = field.shape[1]
    blocks = work.shape[0]

    @pl.loop(0, rows // 8)
    def _(g):
        at = slab(g, 8)
        values = [
            (field[0, at, j * LANES : (j + 1) * LANES], field[1, at, j * LANES : (j + 1) * LANES])
            for j in range(blocks)
        ]
        for q, (re, im) in enumerate(block_dft(values, -1)):
            work[q, at, :LANES] = re
            work[q, at, LANES:] = im


def multiply(work, matrices):
    rows = work.shape[1]

    @pl.loop(0, work.shape[0], unroll=True)
    def _(q):
        value = work[q]
        first = value.astype(jnp.bfloat16)
        rest = (value - first.astype(jnp.float32)).astype(jnp.bfloat16)
        both = jnp.dot(
            jnp.concatenate([first, rest]), matrices[q, 0], preferred_element_type=jnp.float32
        )
        fine = jnp.dot(first, matrices[q, 1], preferred_element_type=jnp.float32)
        work[q] = both[:rows] + (both[rows:] + fine)


def gathered(work, at):
    values = [(work[q, at, :LANES], work[q, at, LANES:]) for q in range(work.shape[0])]
    return block_dft(values, 1)


def filtered(field, work, matrices, copy):
    spread(field, work)
    copy.wait()
    multiply(work, matrices)


def write_filtered(info, work, forward, backward, inner, outer):
    rows = work.shape[1] // 2
    for target, base, offset in ((forward, 0, 0), (backward, rows, 8)):

        @pl.loop(0, rows // 8)
        def _(g):
            here = pl.ds(pl.multiple_of(g * 8 + offset, 8), 8)
            for j, pair in enumerate(gathered(work, pl.ds(pl.multiple_of(g * 8 + base, 8), 8))):
                for part in range(2):
                    target[part, here, j * LANES : (j + 1) * LANES] = pair[part]

    low = info[4] == 0
    for part in range(2):
        first, last = forward[part, 0:1, :], backward[part, rows + 7 : rows + 8, :]
        inner[part : part + 1, :] = jnp.where(low, last, first)
        outer[part : part + 1, :] = jnp.where(low, first, last)


def size_of(largest):
    top = jnp.max(jnp.max(largest, axis=1, keepdims=True), axis=0, keepdims=True)
    return jnp.maximum(top, 1e-30).astype(jnp.bfloat16).astype(jnp.float32)


def encoded(value, size):
    unit = value * (STRETCH / size)
    square = unit * unit
    fourth = square * square
    return (fourth * fourth * square * (unit * jnp.abs(unit))).astype(jnp.bfloat16)


def decoded(code, size):
    value = code.astype(jnp.float32)
    root = jnp.exp2(jnp.log(jnp.abs(value)) * (1.0 / (POWER * math.log(2.0)))) * (size / STRETCH)
    return jnp.where(value < 0.0, -root, root)


def side_tile(columns, rows):
    index = lax.broadcasted_iota(jnp.int32, (rows, LANES), 1)
    tile = jnp.zeros((rows, LANES), jnp.float32)
    for at, column in columns:
        tile = jnp.where(index == at, column, tile)
    return tile.astype(jnp.bfloat16)


def sizes_in(tile, count):
    value = tile.astype(jnp.float32)
    return [value[0:1, SCALE_LANE + i : SCALE_LANE + i + 1] for i in range(count)]


def updated(fr, fi, br, bi, wave, population, hole, loss, carrier, grating, lap):
    rr, ri, lr, li = wave
    surplus = population - 1.0
    gain_re = 1.0 + 0.5 * (GAIN_SLOPE_RATE * surplus - loss)
    gain_im = (0.5 * GAIN_SLOPE_RATE * ALPHA_LINEWIDTH) * surplus
    joined = COUPLING * hole
    drive = (2.0 * CLOCK_DELTA * GAIN_SLOPE_RATE) * surplus * carrier
    mix = (2.0 * CLOCK_DELTA) * grating
    new_fr = gain_re * fr - gain_im * fi + joined * bi - drive * rr + mix * lr
    new_fi = gain_re * fi + gain_im * fr - joined * br - drive * ri + mix * li
    new_br = gain_re * br - gain_im * bi + joined * fi - drive * lr + mix * rr
    new_bi = gain_re * bi + gain_im * br - joined * fr - drive * li + mix * ri
    light = rr * rr + ri * ri + lr * lr + li * li
    share = (
        fr * (rr + ALPHA_LINEWIDTH * ri)
        + fi * (ri - ALPHA_LINEWIDTH * rr)
        + br * (lr + ALPHA_LINEWIDTH * li)
        + bi * (li - ALPHA_LINEWIDTH * lr)
    )
    new_carrier = (
        carrier * ((1.0 - CLOCK_DELTA / DENSITY_LIFETIME) - (CLOCK_DELTA * GAIN_SLOPE_RATE) * light)
        + TRANSVERSE_DIFFUS * lap
        + (0.5 * GAIN_SLOPE_RATE) * share
    )
    new_grating = grating * (1.0 - CLOCK_DELTA / GRATING_LIFE) + COUPLING * (
        fi * lr - fr * li + bi * rr - br * ri
    )
    return new_fr, new_fi, new_br, new_bi, new_carrier, new_grating


def curvature(left, mid, right, weight_left, weight_right):
    index = lax.broadcasted_iota(jnp.int32, mid.shape, 1)
    below = jnp.where(index == 0, pltpu.roll(left, 1, 1) * weight_left, pltpu.roll(mid, 1, 1))
    above = jnp.where(
        index == LANES - 1,
        pltpu.roll(right, LANES - 1, 1) * weight_right,
        pltpu.roll(mid, LANES - 1, 1),
    )
    return below + above - 2.0 * mid


def send_fields_kernel(info, forward, backward, out, fields, sems):
    rows, columns = fields.shape[2:]
    half = columns // LANES
    at = rows_of(info, rows, True)
    copies = fetch(
        [(ref.at[:, at, :], fields.at[f]) for f, ref in enumerate((forward, backward))], sems
    )
    sizes = []
    for f in range(2):
        copies[f].wait()
        largest = jnp.maximum(jnp.abs(fields[f, 0]), jnp.abs(fields[f, 1]))
        size = size_of(largest)
        sizes.append((SCALE_LANE + f, size))
        for part in range(2):
            put_tiles(out, (2 * f + part) * half, encoded(fields[f, part], size))
    out[4 * half * rows :, :] = side_tile(sizes, rows)


def put_tiles(out, first, value):
    rows, columns = value.shape
    for j in range(columns // LANES):
        at = (first + j) * rows
        out[at : at + rows, :] = value[:, j * LANES : (j + 1) * LANES]


def history_rows(forward, backward, population, hole, s, at):
    return [
        forward.at[s, 0, at, :], forward.at[s, 1, at, :], backward.at[s, 0, at, :],
        backward.at[s, 1, at, :], population.at[s, at, :], hole.at[s, at, :],
    ]


def into_rows(parts, target, first, rows):
    return [(part, target.at[pl.ds(first + i * rows, rows), :]) for i, part in enumerate(parts)]


def send_later_kernel(steps, info, forward, backward, population, hole, *refs):
    targets, sems = refs[:-1], refs[-1]
    rows = targets[0].shape[0] // 6
    pairs = []
    for i, s in enumerate(steps):
        for k, other in enumerate((True, False)):
            at = rows_of(info, rows, other)
            parts = history_rows(forward, backward, population, hole, s, at)
            pairs += into_rows(parts, targets[2 * i + k], 0, rows)
    for copy in fetch(pairs, sems):
        copy.wait()


def send_first_kernel(
    s, info, loss, carrier, grating, forward, backward, population, hole,
    own_loss, own, own_carrier, own_grating, out, states, codes, sems,
):
    rows, columns = own_carrier.shape
    theirs, mine = rows_of(info, rows, True), rows_of(info, rows, False)
    history = (forward, backward, population, hole)
    copies = fetch(
        [(carrier.at[theirs, :], states.at[0]), (grating.at[theirs, :], states.at[1])]
        + into_rows([loss.at[theirs, :]], out, 0, rows)
        + into_rows(history_rows(*history, s, theirs), out, 3 * rows, rows)
        + [(loss.at[mine, :], own_loss), (carrier.at[mine, :], own_carrier)]
        + [(grating.at[mine, :], own_grating)]
        + into_rows(history_rows(*history, s, mine), own, 0, rows),
        sems,
    )
    for copy in copies[:2]:
        copy.wait()
    sizes = []
    for i in range(2):
        size = size_of(jnp.abs(states[i]))
        sizes.append(jnp.broadcast_to(size, (8, columns)))
        codes[i * rows : (i + 1) * rows, :] = encoded(states[i], size)
    codes[2 * rows :, :] = jnp.concatenate(sizes).astype(jnp.bfloat16)
    sent = fetch(
        [
            (codes.at[pl.ds(0, 2 * rows), :], out.at[pl.ds(rows, 2 * rows), :]),
            (codes.at[pl.ds(2 * rows, TILE), :], out.at[pl.ds(9 * rows, TILE), :]),
        ],
        sems,
        len(copies),
    )
    for copy in copies[2:] + sent:
        copy.wait()


def enter_kernel(
    info, forward, backward, other, source, tp, tq, inner, outer, field, work, matrices, sem, sems
):
    copy = pltpu.make_async_copy(source, matrices, sem)
    rows, width = field.shape[1] // 2, field.shape[2]
    columns = width // 2
    half = columns // LANES
    at = rows_of(info, rows, False)
    copies = fetch(
        [
            (ref.at[:, at, :], field.at[:, f * rows : (f + 1) * rows, :columns])
            for f, ref in enumerate((forward, backward))
        ],
        sems,
    )
    copy.start()
    sizes = sizes_in(other[4 * half * rows :, :], 2)
    for f in range(2):
        for part in range(2):

            @pl.loop(0, half, unroll=2)
            def _(j):
                code = other[slab((2 * f + part) * half + j, rows), :]
                field[part, f * rows : (f + 1) * rows, lane(half + j)] = decoded(code, sizes[f])

    for held in copies:
        held.wait()
    filtered(field, work, matrices, copy)
    write_filtered(info, work, tp, tq, inner, outer)


def rows_update(
    info, tp, tq, inner, outer, carrier, grating, own, other, own_loss, other_loss,
    field, new_carrier, new_grating, sums_in, sums, cells, last
):
    rows, width = carrier.shape
    half = width // LANES // 2
    columns = half * LANES
    mid = jnp.where(info[0] == 0, 1.0, 0.0)
    wrap = 1.0 - mid
    low = info[4] == 0
    is_first, is_last = info[1], info[2]
    row_index = lax.broadcasted_iota(jnp.int32, (TILE, LANES), 0)
    zero = jnp.zeros((8, LANES), jnp.float32)

    def step(jj, most):
        for side in range(2):
            j = jj + side * half
            here = lane(j)
            left_at = lane(jnp.where(j == 0, 2 * half - 1, j - 1))
            right_at = lane(jnp.where(j == 2 * half - 1, 0, j + 1))
            swapped = lane(jj + (1 - side) * half)
            weight_left = jnp.where(jj == 0, wrap if side == 0 else mid, 1.0)
            weight_right = jnp.where(jj == half - 1, mid if side == 0 else wrap, 1.0)
            total = zero
            for r in range(0, rows, TILE):
                at = slice(r, r + TILE)

                held, begin = (own, other)[side]

                def part_of(i):
                    tile = begin + i * rows + r
                    return held[tile : tile + TILE, lane(jj)].astype(jnp.float32)

                loss = (own_loss, other_loss)[side][at, lane(jj)].astype(jnp.float32)
                f = [tp[part, r + 1 : r + 1 + TILE, here] for part in range(2)]
                b = [tq[part, r + 7 : r + 7 + TILE, here] for part in range(2)]
                if r + TILE == rows:
                    for part in range(2):
                        facet = FRONT_FACET * tq[part, rows + 7 : rows + 8, here]
                        edge = jnp.where(
                            low, inner[part : part + 1, swapped], outer[part : part + 1, here]
                        )
                        edge = jnp.where(is_last, facet, edge)
                        f[part] = jnp.where(row_index == TILE - 1, edge, f[part])
                if r == 0:
                    for part in range(2):
                        facet = REAR_FACET * tp[part, 0:1, here]
                        edge = jnp.where(
                            low, outer[part : part + 1, here], inner[part : part + 1, swapped]
                        )
                        edge = jnp.where(is_first, facet, edge)
                        b[part] = jnp.where(row_index == 0, edge, b[part])
                c = carrier[at, here]
                lap = curvature(
                    carrier[at, left_at], c, carrier[at, right_at], weight_left, weight_right
                )
                out = updated(
                    *f, *b, [part_of(i) for i in range(4)], part_of(4), part_of(5), loss,
                    c, grating[at, here], lap,
                )
                field[0, r : r + TILE, here] = out[0]
                field[1, r : r + TILE, here] = out[1]
                field[0, rows + r : rows + r + TILE, here] = out[2]
                field[1, rows + r : rows + r + TILE, here] = out[3]
                new_carrier[at, here] = out[4]
                new_grating[at, here] = out[5]
                z = (info[3] + r + row_index).astype(jnp.float32)
                weighted = (1.0 + 2.0 * z / (cells - 1)) * ((c + out[4]) if last else c)
                for k in range(0, TILE, 8):
                    total = total + weighted[k : k + 8]
                if last and side == 1:
                    for k in range(0, TILE, 8):
                        most = (
                            jnp.maximum(most[0], jnp.abs(out[4][k : k + 8])),
                            jnp.maximum(most[1], jnp.abs(out[5][k : k + 8])),
                        )
            summed = jnp.sum(total, axis=0, keepdims=True)
            sums[:, here] = summed if sums_in is None else summed + sums_in[:, here]
        return most

    return lax.fori_loop(0, half, step, (zero, zero))


def first_step_kernel(
    cells, info, tp, tq, inner, outer, my_carrier, my_grating, loss, own, other, source,
    new_tp, new_tq, new_inner, new_outer, new_carrier, new_grating, sums,
    carrier, grating, field, work, matrices, sem,
):
    copy = pltpu.make_async_copy(source, matrices, sem)
    copy.start()
    rows, columns = my_carrier.shape
    half = columns // LANES
    sizes = other[9 * rows :, :LANES].astype(jnp.float32)
    sizes = [sizes[0:1, 0:1], sizes[8:9, 0:1]]
    for i, (whole, mine) in enumerate(((carrier, my_carrier), (grating, my_grating))):
        whole[:, :columns] = mine[...]

        @pl.loop(0, half, unroll=2)
        def _(j):
            whole[:, lane(half + j)] = decoded(
                other[(1 + i) * rows : (2 + i) * rows, lane(j)], sizes[i]
            )

    rows_update(
        info, tp, tq, inner, outer, carrier, grating, (own, 0), (other, 3 * rows), loss, other,
        field, new_carrier, new_grating, None, sums, cells, False,
    )
    filtered(field, work, matrices, copy)
    write_filtered(info, work, new_tp, new_tq, new_inner, new_outer)


def middle_step_kernel(
    cells, info, tp, tq, inner, outer, carrier, grating, loss, own, other, other_loss, sums_in,
    source, new_tp, new_tq, new_inner, new_outer, new_carrier, new_grating, sums,
    field, work, matrices, sem,
):
    copy = pltpu.make_async_copy(source, matrices, sem)
    copy.start()
    rows_update(
        info, tp, tq, inner, outer, carrier, grating, (own, 0), (other, 0), loss, other_loss,
        field, new_carrier, new_grating, sums_in, sums, cells, False,
    )
    filtered(field, work, matrices, copy)
    write_filtered(info, work, new_tp, new_tq, new_inner, new_outer)


def leave_step_kernel(
    cells, info, tp, tq, inner, outer, carrier, grating, loss, own, other, other_loss, sums_in,
    field, kept_carrier, kept_grating, sides, sent, sums,
    new_carrier, new_grating,
):
    rows, width = carrier.shape
    columns = width // 2
    half = columns // LANES
    most = rows_update(
        info, tp, tq, inner, outer, carrier, grating, (own, 0), (other, 0), loss, other_loss,
        field, new_carrier, new_grating, sums_in, sums, cells, True,
    )
    mid = jnp.where(info[0] == 0, 1.0, 0.0)
    wrap = 1.0 - mid
    kept_carrier[...] = new_carrier[:, :columns]
    kept_grating[...] = new_grating[:, :columns]
    first, before = new_carrier[:, 0:1] * wrap, new_carrier[:, columns - 1 : columns] * mid
    after, final = new_carrier[:, columns : columns + 1] * mid, new_carrier[:, width - 1 :] * wrap
    sides[0] = jnp.broadcast_to(final, (rows, LANES))
    sides[1] = jnp.broadcast_to(after, (rows, LANES))
    pairs = []
    for at, value in ((0, before), (2, first)):
        coarse = value.astype(jnp.bfloat16).astype(jnp.float32)
        pairs += [(at, coarse), (at + 1, value - coarse)]
    for i, field_of in enumerate((new_carrier, new_grating)):
        size = size_of(most[i])
        pairs.append((SCALE_LANE + i, size))

        @pl.loop(0, half)
        def _(j):
            sent[slab(i * half + j, rows), :] = encoded(field_of[:, lane(half + j)], size)

    sent[2 * half * rows :, :] = side_tile(pairs, rows)


def leave_filter_kernel(info, field, source, kept, sent, straight, across, work, matrices, sem):
    copy = pltpu.make_async_copy(source, matrices, sem)
    copy.start()
    rows, width = field.shape[1] // 2, field.shape[2]
    blocks = width // LANES
    half = blocks // 2
    columns = width // 2
    filtered(field, work, matrices, copy)
    zero = jnp.zeros((8, LANES), jnp.float32)
    sizes = []
    for f in range(2):

        def unmix(g, most):
            at = pl.ds(pl.multiple_of(g * 8 + f * rows, 8), 8)
            for j, pair in enumerate(gathered(work, at)):
                for part in range(2):
                    if j < half:
                        kept[part, at, j * LANES : (j + 1) * LANES] = pair[part]
                    else:
                        work[j, at, part * LANES : (part + 1) * LANES] = pair[part]
                        most = jnp.maximum(most, jnp.abs(pair[part]))
            return most

        size = size_of(lax.fori_loop(0, rows // 8, unmix, zero))
        sizes.append((SCALE_LANE + f, size))

        @pl.loop(0, half)
        def _(j):
            for part in range(2):
                value = work[half + j, f * rows : (f + 1) * rows, part * LANES : (part + 1) * LANES]
                sent[slab((2 * f + part) * half + j, rows), :] = encoded(value, size)

    sent[4 * half * rows :, :] = side_tile(sizes, rows)
    low = info[4] == 0
    for part in range(2):
        lanes = slice(part * LANES, (part + 1) * LANES)
        straight[part : part + 1, :] = jnp.where(
            low, kept[part, 0:1, :], kept[part, 2 * rows - 1 : 2 * rows, :]
        )
        for j in range(half):
            across[part : part + 1, j * LANES : (j + 1) * LANES] = jnp.where(
                low, work[half + j, 0:1, lanes], work[half + j, 2 * rows - 1 : 2 * rows, lanes]
            )


def final_kernel(
    info, kept, kept_carrier, kept_grating, sides, fields, pair, straight, across, loss_in,
    forward, backward, population, hole,
    out_forward, out_backward, out_carrier, out_grating,
    tp, tq, carrier, grating, wide, plain, loss, sems,
):
    rows, columns = kept_carrier.shape
    half = columns // LANES
    copies = fetch(
        [
            (loss_in, loss), (forward.at[0], wide.at[0]), (backward.at[0], wide.at[1]),
            (population.at[0], plain.at[0]), (hole.at[0], plain.at[1]),
        ],
        sems,
    )
    mine = info[4] * rows
    theirs = (1 - info[4]) * rows
    low = info[4] == 0
    extra = pair[2 * half * rows :, :]
    size_carrier, size_grating = sizes_in(extra, 2)
    size_forward, size_backward = sizes_in(fields[4 * half * rows :, :], 2)
    extra = extra.astype(jnp.float32)

    def at(start, offset, count):
        return pl.ds(pl.multiple_of(start + offset, 8), count)

    for part in range(2):
        tp[part, at(mine, 0, rows), :] = kept[part, :rows, :]
        tq[part, at(mine, 8, rows), :] = kept[part, rows:, :]
    carrier[at(mine, 0, rows), LANES : LANES + columns] = kept_carrier[...]
    carrier[at(mine, 0, rows), :LANES] = sides[0]
    carrier[at(mine, 0, rows), LANES + columns :] = sides[1]
    carrier[at(theirs, 0, rows), :LANES] = jnp.broadcast_to(
        extra[:, 0:1] + extra[:, 1:2], (rows, LANES)
    )
    carrier[at(theirs, 0, rows), LANES + columns :] = jnp.broadcast_to(
        extra[:, 2:3] + extra[:, 3:4], (rows, LANES)
    )
    grating[at(mine, 0, rows), :] = kept_grating[...]

    @pl.loop(0, half)
    def _(j):
        carrier[at(theirs, 0, rows), lane(1 + j)] = decoded(pair[slab(j, rows), :], size_carrier)
        grating[at(theirs, 0, rows), lane(j)] = decoded(pair[slab(half + j, rows), :], size_grating)
        for part in range(2):
            tp[part, at(theirs, 0, rows), lane(j)] = decoded(
                fields[slab(part * half + j, rows), :], size_forward
            )
            tq[part, at(theirs, 8, rows), lane(j)] = decoded(
                fields[slab((2 + part) * half + j, rows), :], size_backward
            )

    all_rows = 2 * rows
    for part in range(2):
        here = slice(part, part + 1)
        next_edge = jnp.where(low, across[here, :], straight[here, :])
        before_edge = jnp.where(low, straight[here, :], across[here, :])
        front = FRONT_FACET * tq[part, all_rows + 7 : all_rows + 8, :]
        rear = REAR_FACET * tp[part, 0:1, :]
        tp[part, all_rows : all_rows + 1, :] = jnp.where(info[2], front, next_edge)
        tq[part, 7:8, :] = jnp.where(info[1], rear, before_edge)

    for copy in copies:
        copy.wait()

    @pl.loop(0, half)
    def _(j):
        here = lane(j)
        for r in range(0, all_rows, TILE):
            row = slice(r, r + TILE)
            c = carrier[row, lane(j + 1)]
            lap = curvature(carrier[row, lane(j)], c, carrier[row, lane(j + 2)], 1.0, 1.0)
            out = updated(
                tp[0, r + 1 : r + 1 + TILE, here], tp[1, r + 1 : r + 1 + TILE, here],
                tq[0, r + 7 : r + 7 + TILE, here], tq[1, r + 7 : r + 7 + TILE, here],
                [wide[f, part, row, here].astype(jnp.float32) for f in range(2) for part in range(2)],
                plain[0, row, here].astype(jnp.float32), plain[1, row, here].astype(jnp.float32),
                loss[row, here].astype(jnp.float32), c, grating[row, here], lap,
            )
            out_forward[0, row, here] = out[0]
            out_forward[1, row, here] = out[1]
            out_backward[0, row, here] = out[2]
            out_backward[1, row, here] = out[3]
            out_carrier[row, here] = out[4]
            out_grating[row, here] = out[5]


def position(rows, whole):
    x, block, count = lax.axis_index("gx"), lax.axis_index("gz"), lax.axis_size("gz")
    high = lax.rem(x + block, 2)
    if whole:
        return x, block == 0, block == count - 1, block * rows, high
    place = 2 * block + high
    return x, place == 0, place == 2 * count - 1, place * rows, high


def whole_spec(shape):
    return pl.BlockSpec(shape, lambda i, n=len(shape): (0,) * n)


def call(name, kernel, rows, inputs, outputs, scratch, flops=0, grant=24, whole=False, spread_out=()):
    arrays = [x[0] if isinstance(x, tuple) else x for x in inputs]
    specs = [x[1] if isinstance(x, tuple) else whole_spec(x.shape) for x in inputs]
    shapes = [jax.ShapeDtypeStruct(*out) for out in outputs]
    moved = sum(math.prod(s.shape) * s.dtype.itemsize for s in shapes)

    def body(*refs):
        kernel(position(rows, whole), *refs)

    return pl.pallas_call(
        body,
        grid=(1,),
        in_specs=specs,
        out_specs=[
            pl.BlockSpec(memory_space=pl.ANY) if i in spread_out else whole_spec(s.shape)
            for i, s in enumerate(shapes)
        ],
        scratch_shapes=scratch,
        out_shape=shapes,
        compiler_params=pltpu.CompilerParams(vmem_limit_bytes=grant * 1024 * 1024),
        cost_estimate=pl.CostEstimate(
            flops=flops, bytes_accessed=moved + 4 * 1024 * 1024, transcendentals=0
        ),
        name=name,
    )(*arrays)


def per_pair(
    ending_rightward_adjoint,
    ending_leftward_adjoint,
    ending_population_adjoint,
    ending_holeburn_adjoint,
    history_rightward,
    history_leftward,
    history_population,
    history_holeburn,
    segment_passive_attenuation,
):
    cell_rows, columns = ending_population_adjoint.shape
    passes = history_population.shape[0]
    rows = cell_rows // 2
    half = columns // LANES
    blocks = 2 * half
    width = 2 * columns
    count = lax.axis_size("gz")
    cells = cell_rows * count
    x = lax.axis_index("gx")
    f32, bf16 = jnp.float32, jnp.bfloat16
    swap = [(0, 1), (1, 0)]
    in_place = pl.BlockSpec(memory_space=pltpu.HBM)

    def held(*arrays):
        return [(a, in_place) for a in arrays]

    def tiles(n):
        return ((n * rows, LANES), bf16)

    ends = held(ending_rightward_adjoint, ending_leftward_adjoint)
    planes = held(ending_population_adjoint, ending_holeburn_adjoint)
    history = held(history_rightward, history_leftward, history_population, history_holeburn)
    losses = held(segment_passive_attenuation)
    matrices = jnp.asarray(lateral_matrices(width, blocks))
    matrix_input = held(matrices)
    work = [
        pltpu.VMEM((blocks, 2 * rows, 2 * LANES), f32),
        pltpu.VMEM(matrices.shape, bf16),
        pltpu.SemaphoreType.DMA,
    ]
    field_scratch = pltpu.VMEM((2, 2 * rows, width), f32)
    state_out = [
        ((2, rows + 8, width), f32), ((2, rows + 8, width), f32), ((2, width), f32), ((2, width), f32),
    ]
    plane = ((rows, width), f32)
    plane_scratch = pltpu.VMEM((rows, width), f32)
    half_plane = ((rows, columns), f32)
    work_flops = 2 * 3 * 2 * rows * blocks * (2 * LANES) ** 2

    (coded,) = call(
        "send_fields", send_fields_kernel, rows, ends, [tiles(4 * half + 1)],
        [pltpu.VMEM((2, 2, rows, columns), f32), pltpu.SemaphoreType.DMA((2,))], grant=62,
    )
    other_fields = lax.ppermute(coded, "gx", swap)
    loss, own_first, my_carrier, my_grating, sent_first = call(
        "send_first", functools.partial(send_first_kernel, passes - 1), rows,
        [*losses, *planes, *history],
        [((rows, columns), bf16), ((6 * rows, columns), bf16), half_plane, half_plane,
         ((9 * rows + TILE, columns), bf16)],
        [pltpu.VMEM((2, rows, columns), f32), pltpu.VMEM((2 * rows + TILE, columns), bf16),
         pltpu.SemaphoreType.DMA((20,))], grant=62, spread_out=range(5),
    )
    steps = range(passes - 2, 0, -1)
    later = call(
        "send_later", functools.partial(send_later_kernel, steps), rows, history,
        [((6 * rows, columns), bf16)] * (2 * len(steps)),
        [pltpu.SemaphoreType.DMA((12 * len(steps),))], grant=62, spread_out=range(2 * len(steps)),
    )
    sent_first, later, other_fields = lax.optimization_barrier((sent_first, later, other_fields))
    other_first = lax.ppermute(sent_first, "gx", swap)

    line = ("gz", "gx")
    neighbours = []
    for b in range(count - 1):
        top = (1 + b) % 2
        neighbours += [(2 * b + top, 2 * b + 2 + top), (2 * b + 2 + top, 2 * b + top)]

    def edges(inner, outer):
        return lax.ppermute(inner, "gx", swap), lax.ppermute(outer, line, neighbours)

    tp, tq, inner, outer = call(
        "enter", enter_kernel, rows, [*ends, other_fields, *matrix_input],
        state_out, [field_scratch, *work, pltpu.SemaphoreType.DMA((2,))], work_flops,
    )
    inner, outer = edges(inner, outer)

    other_loss = (other_first, pl.BlockSpec((rows, columns), lambda i: (0, 0)))
    carrier = grating = sums = other = own = None
    for index, s in enumerate(range(passes - 1, 0, -1)):
        if index < len(steps):
            sent, own_next = later[2 * index : 2 * index + 2]
            sent, inner, outer = lax.optimization_barrier((sent, inner, outer))
            coming = lax.ppermute(sent, "gx", swap)
        shared = [tp, tq, inner, outer]
        if index == 0:
            tp, tq, inner, outer, carrier, grating, sums = call(
                "first_step", functools.partial(first_step_kernel, cells), rows,
                [*shared, my_carrier, my_grating, loss, own_first, other_first, *matrix_input],
                [*state_out, plane, plane, ((1, width), f32)],
                [plane_scratch, plane_scratch, field_scratch, *work], work_flops,
            )
        elif s > 1:
            tp, tq, inner, outer, carrier, grating, sums = call(
                "middle_step", functools.partial(middle_step_kernel, cells), rows,
                [*shared, carrier, grating, loss, own, other, other_loss, sums, *matrix_input],
                [*state_out, plane, plane, ((1, width), f32)],
                [field_scratch, *work], work_flops,
            )
        else:
            field, kept_carrier, kept_grating, sides, sent, sums = call(
                "leave_step", functools.partial(leave_step_kernel, cells), rows,
                [*shared, carrier, grating, loss, own, other, other_loss, sums],
                [((2, 2 * rows, width), f32), half_plane, half_plane,
                 ((2, rows, LANES), f32), tiles(2 * half + 1), ((1, width), f32)],
                [plane_scratch, plane_scratch],
            )
        if s > 1:
            inner, outer = edges(inner, outer)
            own, other = own_next, coming

    pair = lax.ppermute(sent, "gx", swap)
    sums = lax.all_gather(sums.reshape(2, half, LANES), line, axis=0, tiled=False)
    kept, sent, straight, across = call(
        "leave_filter", leave_filter_kernel, rows, [field, *matrix_input],
        [((2, 2 * rows, columns), f32), tiles(4 * half + 1), ((2, columns), f32), ((2, columns), f32)],
        work, work_flops,
    )
    fields = lax.ppermute(sent, "gx", swap)
    pair, straight, across = lax.optimization_barrier((pair, straight, across))

    straight = lax.ppermute(straight, line, neighbours)
    along = []
    for b in range(count - 1):
        top, foot = (1 + b) % 2, b % 2
        along += [(2 * b + top, 2 * b + 2 + foot), (2 * b + 2 + top, 2 * b + foot)]
    across = lax.ppermute(across, line, along)

    sums = sums.reshape(count, 2, 2, half, LANES)
    total = jnp.where(x == 0, sums[:, 0, 0] + sums[:, 1, 1], sums[:, 0, 1] + sums[:, 1, 0])
    total = jnp.sum(total, axis=0).reshape(columns)

    outs = call(
        "final", final_kernel, cell_rows,
        [kept, kept_carrier, kept_grating, sides, fields, pair, straight, across, *losses, *history],
        [((2, cell_rows, columns), f32), ((2, cell_rows, columns), f32),
         ((cell_rows, columns), f32), ((cell_rows, columns), f32)],
        [pltpu.VMEM((2, cell_rows + 8, columns), f32), pltpu.VMEM((2, cell_rows + 8, columns), f32),
         pltpu.VMEM((cell_rows, columns + 2 * LANES), f32), pltpu.VMEM((cell_rows, columns), f32),
         pltpu.VMEM((2, 2, cell_rows, columns), bf16), pltpu.VMEM((2, cell_rows, columns), bf16),
         pltpu.VMEM((cell_rows, columns), bf16), pltpu.SemaphoreType.DMA((5,))],
        whole=True,
    )
    return (*outs, CLOCK_DELTA * total / math.sqrt(cells))


def shared_by_pairs(mesh, arguments):
    population = arguments[6]
    passes, cells, width = population.shape
    rows, columns = cells // mesh.shape["gz"], width // mesh.shape["gx"]
    return (
        mesh.shape["gx"] == 2
        and passes >= 3
        and rows % (2 * TILE) == 0
        and columns % LANES == 0
        and (columns // LANES) & (columns // LANES - 1) == 0
        and width <= 4096
    )


def solution(mesh):
    def run(*arguments):
        body = per_pair if shared_by_pairs(mesh, arguments) else per_device
        return jax.shard_map(
            body,
            mesh=mesh,
            in_specs=(
                P(None, "gz", "gx"),
                P(None, "gz", "gx"),
                P("gz", "gx"),
                P("gz", "gx"),
                P(None, None, "gz", "gx"),
                P(None, None, "gz", "gx"),
                P(None, "gz", "gx"),
                P(None, "gz", "gx"),
                P("gz", "gx"),
            ),
            out_specs=(
                P(None, "gz", "gx"), P(None, "gz", "gx"), P("gz", "gx"), P("gz", "gx"), P("gx"),
            ),
            check_vma=False,
        )(*arguments)

    return run
```

```python
import functools
import math

import jax
import jax.numpy as jnp
import ml_dtypes
import numpy as np
from jax import lax
from jax.experimental import pallas as pl
from jax.experimental.pallas import tpu as pltpu
from jax.sharding import PartitionSpec as P

DIFF = 512


FRONT_FACET = 0.3
REAR_FACET = 0.9
GAIN_SLOPE_RATE = 0.3
ALPHA_LINEWIDTH = 2.0
COUPLING = 0.5
CLOCK_DELTA = 0.3
DENSITY_LIFETIME = 2.0
GRATING_LIFE = 0.75
TRANSVERSE_DIFFUS = 0.2


def passed_along(value, axis, steps):
    count = lax.axis_size(axis)
    initial, last = (max(0, -steps), min(count, count - steps))
    return lax.ppermute(value, axis, [(source, source + steps) for source in range(initial, last)])


def with_halo(block, sides, width):
    for axis, dim in sides:
        count = lax.axis_size(axis)
        forward = [(i, i + 1) for i in range(count - 1)]
        backward = [(target, source) for source, target in forward]
        low = lax.ppermute(
            lax.slice_in_dim(block, block.shape[dim] - width, None, axis=dim), axis, forward
        )
        high = lax.ppermute(lax.slice_in_dim(block, 0, width, axis=dim), axis, backward)
        block = jnp.concatenate([low, block, high], axis=dim)
    return block


def rotate(source_re, source_im, cosine, sine, form, sign):
    exact = lax.Precision.HIGHEST
    out_re = jnp.einsum(form, source_re, cosine, precision=exact) + sign * jnp.einsum(
        form, source_im, sine, precision=exact
    )
    out_im = jnp.einsum(form, source_im, cosine, precision=exact) - sign * jnp.einsum(
        form, source_re, sine, precision=exact
    )
    return (out_re, out_im)


def transform(stacked):
    count = stacked.shape[1]
    width = stacked.shape[2]
    second = min(128, width // 2)
    first = width // second
    two_pi = 2.0 * math.pi
    index_a = jnp.arange(first, dtype=jnp.int32)
    index_b = jnp.arange(second, dtype=jnp.int32)
    angle_a = two_pi * (index_a[:, None] * index_a[None, :] % first).astype(jnp.float32) / first
    angle_b = two_pi * (index_b[:, None] * index_b[None, :] % second).astype(jnp.float32) / second
    angle_t = two_pi * (index_a[:, None] * index_b[None, :] % width).astype(jnp.float32) / width
    cos_a, sin_a = (jnp.cos(angle_a), jnp.sin(angle_a))
    cos_b, sin_b = (jnp.cos(angle_b), jnp.sin(angle_b))
    cos_t, sin_t = (jnp.cos(angle_t), jnp.sin(angle_t))
    wavenum = index_a[:, None] + first * index_b[None, :]
    signed = jnp.where(wavenum < width // 2, wavenum, wavenum - width)
    phase = (signed * signed).astype(jnp.float32) * (DIFF / (width / 2) ** 2)
    cos_p, sin_p = (jnp.cos(phase), jnp.sin(phase))
    real_in = stacked[0].reshape(count, first, second)
    imag_in = stacked[1].reshape(count, first, second)
    step_re, step_im = rotate(real_in, imag_in, cos_a, sin_a, "nab,ak->nkb", 1.0)
    twist_re = step_re * cos_t + step_im * sin_t
    twist_im = step_im * cos_t - step_re * sin_t
    spec_re, spec_im = rotate(twist_re, twist_im, cos_b, sin_b, "nkb,bj->nkj", 1.0)
    moved_re = spec_re * cos_p - spec_im * sin_p
    moved_im = spec_re * sin_p + spec_im * cos_p
    back_re, back_im = rotate(moved_re, moved_im, cos_b, sin_b, "nkj,jb->nkb", -1.0)
    untw_re = back_re * cos_t - back_im * sin_t
    untw_im = back_im * cos_t + back_re * sin_t
    final_re, final_im = rotate(untw_re, untw_im, cos_a, sin_a, "nkb,ka->nab", -1.0)
    return jnp.stack([final_re.reshape(count, width), final_im.reshape(count, width)]) / width


def added_up(value, axis):
    count = lax.axis_size(axis)
    if count & (count - 1):
        return lax.psum(value, axis)
    reach = 1
    while reach < count:
        value = value + lax.ppermute(value, axis, [(i, i ^ reach) for i in range(count)])
        reach *= 2
    return value


def lateral_work(parts):
    return (transform(parts[0]), transform(parts[1]))


def multiplier_revision(
    population_multiplier,
    holeburn_multiplier,
    measured_rightward,
    measured_leftward,
    rightward_wave,
    leftward_wave,
    population_level,
    holeburn_magnitude,
    attenuation_factor,
    transverse_curvature,
):
    rightward_inphase, rightward_quadrature = (rightward_wave[0], rightward_wave[1])
    leftward_inphase, leftward_quadrature = (leftward_wave[0], leftward_wave[1])
    measured_rightward_inphase, measured_rightward_quadrature = (
        measured_rightward[0],
        measured_rightward[1],
    )
    measured_leftward_inphase, measured_leftward_quadrature = (
        measured_leftward[0],
        measured_leftward[1],
    )
    surplus_population = population_level - 1.0
    amplification_inphase = 1.0 + 0.5 * (GAIN_SLOPE_RATE * surplus_population - attenuation_factor)
    amplification_quadrature = 0.5 * GAIN_SLOPE_RATE * ALPHA_LINEWIDTH * surplus_population
    joined_waves = COUPLING * holeburn_magnitude
    population_derivative = (
        2.0 * CLOCK_DELTA * GAIN_SLOPE_RATE * surplus_population * population_multiplier
    )
    holeburn_derivative = 2.0 * CLOCK_DELTA * holeburn_multiplier
    revised_rightward_inphase = (
        amplification_inphase * measured_rightward_inphase
        - amplification_quadrature * measured_rightward_quadrature
        + joined_waves * measured_leftward_quadrature
        - population_derivative * rightward_inphase
        + holeburn_derivative * leftward_inphase
    )
    revised_rightward_quadrature = (
        amplification_inphase * measured_rightward_quadrature
        + amplification_quadrature * measured_rightward_inphase
        - joined_waves * measured_leftward_inphase
        - population_derivative * rightward_quadrature
        + holeburn_derivative * leftward_quadrature
    )
    revised_leftward_inphase = (
        amplification_inphase * measured_leftward_inphase
        - amplification_quadrature * measured_leftward_quadrature
        + joined_waves * measured_rightward_quadrature
        - population_derivative * leftward_inphase
        + holeburn_derivative * rightward_inphase
    )
    revised_leftward_quadrature = (
        amplification_inphase * measured_leftward_quadrature
        + amplification_quadrature * measured_leftward_inphase
        - joined_waves * measured_rightward_inphase
        - population_derivative * leftward_quadrature
        + holeburn_derivative * rightward_quadrature
    )
    light_intensity = (
        rightward_inphase * rightward_inphase
        + rightward_quadrature * rightward_quadrature
        + leftward_inphase * leftward_inphase
        + leftward_quadrature * leftward_quadrature
    )
    amplification_share = (
        measured_rightward_inphase * (rightward_inphase + ALPHA_LINEWIDTH * rightward_quadrature)
        + measured_rightward_quadrature
        * (rightward_quadrature - ALPHA_LINEWIDTH * rightward_inphase)
        + measured_leftward_inphase * (leftward_inphase + ALPHA_LINEWIDTH * leftward_quadrature)
        + measured_leftward_quadrature * (leftward_quadrature - ALPHA_LINEWIDTH * leftward_inphase)
    )
    revised_population = (
        population_multiplier
        * (1.0 - CLOCK_DELTA / DENSITY_LIFETIME - CLOCK_DELTA * GAIN_SLOPE_RATE * light_intensity)
        + TRANSVERSE_DIFFUS * transverse_curvature
        + 0.5 * GAIN_SLOPE_RATE * amplification_share
    )
    fresh_holeburn = holeburn_multiplier * (1.0 - CLOCK_DELTA / GRATING_LIFE) + COUPLING * (
        measured_rightward_quadrature * leftward_inphase
        - measured_rightward_inphase * leftward_quadrature
        + measured_leftward_quadrature * rightward_inphase
        - measured_leftward_inphase * rightward_quadrature
    )
    return (
        jnp.stack([revised_rightward_inphase, revised_rightward_quadrature]),
        jnp.stack([revised_leftward_inphase, revised_leftward_quadrature]),
        revised_population,
        fresh_holeburn,
    )


def per_device(
    ending_rightward_adjoint,
    ending_leftward_adjoint,
    ending_population_adjoint,
    ending_holeburn_adjoint,
    history_rightward,
    history_leftward,
    history_population,
    history_holeburn,
    segment_passive_attenuation,
):
    columns = ending_rightward_adjoint.shape[2]
    rows = ending_rightward_adjoint.shape[1]
    blocks = lax.axis_size("gz")
    position = lax.axis_index("gz")
    cells = rows * blocks
    zpos = (position * rows + jnp.arange(rows, dtype=jnp.int32)).astype(jnp.float32)
    scaling_factor = 1.0 + 2.0 * zpos / (cells - 1)
    rightward_multiplier, leftward_multiplier = (ending_rightward_adjoint, ending_leftward_adjoint)
    population_multiplier, holeburn_multiplier = (
        ending_population_adjoint,
        ending_holeburn_adjoint,
    )
    attenuation_factor = segment_passive_attenuation.astype(jnp.float32)
    shape_curve = jnp.zeros((columns,), jnp.float32)
    for moment_position in range(history_rightward.shape[0] - 1, -1, -1):
        shape_curve = shape_curve + jnp.sum(scaling_factor[:, None] * population_multiplier, axis=0)
        above = passed_along(rightward_multiplier[:, :1, :], "gz", -1)
        below = passed_along(leftward_multiplier[:, -1:, :], "gz", 1)
        top_row = jnp.where(
            position == blocks - 1, FRONT_FACET * leftward_multiplier[:, -1:, :], above
        )
        bottom_row = jnp.where(position == 0, REAR_FACET * rightward_multiplier[:, :1, :], below)
        lam_fwd = jnp.concatenate([rightward_multiplier[:, 1:, :], top_row], axis=1)
        lam_bwd = jnp.concatenate([bottom_row, leftward_multiplier[:, :-1, :]], axis=1)
        whole_fwd, whole_bwd = (
            lax.all_gather(lam_fwd, "gx", axis=2, tiled=True),
            lax.all_gather(lam_bwd, "gx", axis=2, tiled=True),
        )
        start = lax.axis_index("gx") * columns
        done_fwd, done_bwd = lateral_work((whole_fwd, whole_bwd))
        measured_rightward = lax.dynamic_slice_in_dim(done_fwd, start, columns, 2)
        measured_leftward = lax.dynamic_slice_in_dim(done_bwd, start, columns, 2)
        bordered_array = with_halo(population_multiplier, (("gx", 1),), 1)
        transverse_curvature = (
            bordered_array[:, 2:] + bordered_array[:, :-2] - 2.0 * population_multiplier
        )
        rightward_multiplier, leftward_multiplier, population_multiplier, holeburn_multiplier = (
            multiplier_revision(
                population_multiplier,
                holeburn_multiplier,
                measured_rightward,
                measured_leftward,
                history_rightward[moment_position].astype(jnp.float32),
                history_leftward[moment_position].astype(jnp.float32),
                history_population[moment_position].astype(jnp.float32),
                history_holeburn[moment_position].astype(jnp.float32),
                attenuation_factor,
                transverse_curvature,
            )
        )
    total = added_up(shape_curve, "gz")
    derivative_vector = CLOCK_DELTA * total / math.sqrt(cells)
    return (
        rightward_multiplier,
        leftward_multiplier,
        population_multiplier,
        holeburn_multiplier,
        derivative_vector,
    )

LANES = 128
TILE = 16
POWER = 12
STRETCH = 1211.0
SCALE_LANE = 8


def lateral_matrices(width, blocks):
    lanes = width // blocks
    k = np.arange(width)
    signed = np.where(k < width // 2, k, k - width).astype(np.float64)
    response = np.fft.ifft(np.exp(1j * signed * signed * (DIFF / (width / 2) ** 2)))
    step = np.arange(lanes)
    shift = lanes * np.arange(blocks)[:, None, None] + step[None, None, :] - step[None, :, None]
    kernels = np.fft.fft(response[shift % width], axis=0) / blocks
    top = np.concatenate([kernels.real, kernels.imag], axis=2)
    low = np.concatenate([-kernels.imag, kernels.real], axis=2)
    whole = np.concatenate([top, low], axis=1)
    first = whole.astype(ml_dtypes.bfloat16)
    rest = (whole - first.astype(np.float64)).astype(ml_dtypes.bfloat16)
    return np.stack([first, rest], axis=1)


def block_dft(values, sign):
    count = len(values)
    if count == 1:
        return values
    even = block_dft(values[0::2], sign)
    odd = block_dft(values[1::2], sign)
    out = [None] * count
    for k in range(count // 2):
        (er, ei), (wr, wi) = even[k], odd[k]
        if 4 * k == count:
            plus, minus = (er - wi, ei + wr), (er + wi, ei - wr)
            out[k], out[k + count // 2] = (plus, minus) if sign > 0 else (minus, plus)
            continue
        if k:
            c, s = math.cos(2 * math.pi * k / count), sign * math.sin(2 * math.pi * k / count)
            if 8 * k == count:
                wr, wi = (c * (wr - wi), c * (wr + wi)) if sign > 0 else (c * (wr + wi), c * (wi - wr))
            elif 8 * k == 3 * count:
                wr, wi = (c * (wr + wi), c * (wi - wr)) if sign > 0 else (c * (wr - wi), c * (wr + wi))
            else:
                wr, wi = c * wr - s * wi, c * wi + s * wr
        out[k] = (er + wr, ei + wi)
        out[k + count // 2] = (er - wr, ei - wi)
    return out


def lane(j):
    return pl.ds(pl.multiple_of(j * LANES, LANES), LANES)


def slab(j, rows):
    return pl.ds(pl.multiple_of(j * rows, rows), rows)


def fetch(pairs, sems, first=0):
    copies = [pltpu.make_async_copy(a, b, sems.at[first + i]) for i, (a, b) in enumerate(pairs)]
    for copy in copies:
        copy.start()
    return copies


def rows_of(info, rows, other):
    part = 1 - info[4] if other else info[4]
    return pl.ds(pl.multiple_of(part * rows, rows), rows)


def spread(field, work):
    rows = field.shape[1]
    blocks = work.shape[0]

    @pl.loop(0, rows // 8)
    def _(g):
        at = slab(g, 8)
        values = [
            (field[0, at, j * LANES : (j + 1) * LANES], field[1, at, j * LANES : (j + 1) * LANES])
            for j in range(blocks)
        ]
        for q, (re, im) in enumerate(block_dft(values, -1)):
            work[q, at, :LANES] = re
            work[q, at, LANES:] = im


def multiply(work, matrices):
    rows = work.shape[1]

    @pl.loop(0, work.shape[0], unroll=True)
    def _(q):
        value = work[q]
        first = value.astype(jnp.bfloat16)
        rest = (value - first.astype(jnp.float32)).astype(jnp.bfloat16)
        both = jnp.dot(
            jnp.concatenate([first, rest]), matrices[q, 0], preferred_element_type=jnp.float32
        )
        fine = jnp.dot(first, matrices[q, 1], preferred_element_type=jnp.float32)
        work[q] = both[:rows] + (both[rows:] + fine)


def gathered(work, at):
    values = [(work[q, at, :LANES], work[q, at, LANES:]) for q in range(work.shape[0])]
    return block_dft(values, 1)


def filtered(field, work, matrices, copy):
    spread(field, work)
    copy.wait()
    multiply(work, matrices)


def write_filtered(info, work, forward, backward, inner, outer):
    rows = work.shape[1] // 2
    for target, base, offset in ((forward, 0, 0), (backward, rows, 8)):

        @pl.loop(0, rows // 8)
        def _(g):
            here = pl.ds(pl.multiple_of(g * 8 + offset, 8), 8)
            for j, pair in enumerate(gathered(work, pl.ds(pl.multiple_of(g * 8 + base, 8), 8))):
                for part in range(2):
                    target[part, here, j * LANES : (j + 1) * LANES] = pair[part]

    low = info[4] == 0
    for part in range(2):
        first, last = forward[part, 0:1, :], backward[part, rows + 7 : rows + 8, :]
        inner[part : part + 1, :] = jnp.where(low, last, first)
        outer[part : part + 1, :] = jnp.where(low, first, last)


def size_of(largest):
    top = jnp.max(jnp.max(largest, axis=1, keepdims=True), axis=0, keepdims=True)
    return jnp.maximum(top, 1e-30).astype(jnp.bfloat16).astype(jnp.float32)


def encoded(value, size):
    unit = value * (STRETCH / size)
    square = unit * unit
    fourth = square * square
    return (fourth * fourth * square * (unit * jnp.abs(unit))).astype(jnp.bfloat16)


def decoded(code, size):
    value = code.astype(jnp.float32)
    root = jnp.exp2(jnp.log(jnp.abs(value)) * (1.0 / (POWER * math.log(2.0)))) * (size / STRETCH)
    return jnp.where(value < 0.0, -root, root)


def side_tile(columns, rows):
    index = lax.broadcasted_iota(jnp.int32, (rows, LANES), 1)
    tile = jnp.zeros((rows, LANES), jnp.float32)
    for at, column in columns:
        tile = jnp.where(index == at, column, tile)
    return tile.astype(jnp.bfloat16)


def sizes_in(tile, count):
    value = tile.astype(jnp.float32)
    return [value[0:1, SCALE_LANE + i : SCALE_LANE + i + 1] for i in range(count)]


def updated(fr, fi, br, bi, wave, population, hole, loss, carrier, grating, lap):
    rr, ri, lr, li = wave
    surplus = population - 1.0
    gain_re = 1.0 + 0.5 * (GAIN_SLOPE_RATE * surplus - loss)
    gain_im = (0.5 * GAIN_SLOPE_RATE * ALPHA_LINEWIDTH) * surplus
    joined = COUPLING * hole
    drive = (2.0 * CLOCK_DELTA * GAIN_SLOPE_RATE) * surplus * carrier
    mix = (2.0 * CLOCK_DELTA) * grating
    new_fr = gain_re * fr - gain_im * fi + joined * bi - drive * rr + mix * lr
    new_fi = gain_re * fi + gain_im * fr - joined * br - drive * ri + mix * li
    new_br = gain_re * br - gain_im * bi + joined * fi - drive * lr + mix * rr
    new_bi = gain_re * bi + gain_im * br - joined * fr - drive * li + mix * ri
    light = rr * rr + ri * ri + lr * lr + li * li
    share = (
        fr * (rr + ALPHA_LINEWIDTH * ri)
        + fi * (ri - ALPHA_LINEWIDTH * rr)
        + br * (lr + ALPHA_LINEWIDTH * li)
        + bi * (li - ALPHA_LINEWIDTH * lr)
    )
    new_carrier = (
        carrier * ((1.0 - CLOCK_DELTA / DENSITY_LIFETIME) - (CLOCK_DELTA * GAIN_SLOPE_RATE) * light)
        + TRANSVERSE_DIFFUS * lap
        + (0.5 * GAIN_SLOPE_RATE) * share
    )
    new_grating = grating * (1.0 - CLOCK_DELTA / GRATING_LIFE) + COUPLING * (
        fi * lr - fr * li + bi * rr - br * ri
    )
    return new_fr, new_fi, new_br, new_bi, new_carrier, new_grating


def curvature(left, mid, right, weight_left, weight_right):
    index = lax.broadcasted_iota(jnp.int32, mid.shape, 1)
    below = jnp.where(index == 0, pltpu.roll(left, 1, 1) * weight_left, pltpu.roll(mid, 1, 1))
    above = jnp.where(
        index == LANES - 1,
        pltpu.roll(right, LANES - 1, 1) * weight_right,
        pltpu.roll(mid, LANES - 1, 1),
    )
    return below + above - 2.0 * mid


def send_fields_kernel(info, forward, backward, out, fields, sems):
    rows, columns = fields.shape[2:]
    half = columns // LANES
    at = rows_of(info, rows, True)
    copies = fetch(
        [(ref.at[:, at, :], fields.at[f]) for f, ref in enumerate((forward, backward))], sems
    )
    sizes = []
    for f in range(2):
        copies[f].wait()
        largest = jnp.maximum(jnp.abs(fields[f, 0]), jnp.abs(fields[f, 1]))
        size = size_of(largest)
        sizes.append((SCALE_LANE + f, size))
        for part in range(2):
            put_tiles(out, (2 * f + part) * half, encoded(fields[f, part], size))
    out[4 * half * rows :, :] = side_tile(sizes, rows)


def put_tiles(out, first, value):
    rows, columns = value.shape
    for j in range(columns // LANES):
        at = (first + j) * rows
        out[at : at + rows, :] = value[:, j * LANES : (j + 1) * LANES]


def history_rows(forward, backward, population, hole, s, at):
    return [
        forward.at[s, 0, at, :], forward.at[s, 1, at, :], backward.at[s, 0, at, :],
        backward.at[s, 1, at, :], population.at[s, at, :], hole.at[s, at, :],
    ]


def into_rows(parts, target, first, rows):
    return [(part, target.at[pl.ds(first + i * rows, rows), :]) for i, part in enumerate(parts)]


def send_later_kernel(steps, info, forward, backward, population, hole, final, *refs):
    targets, sems = refs[:-1], refs[-1]
    rows = targets[0].shape[0] // 6
    history = (forward, backward, population, hole)
    pairs = []
    for i, s in enumerate(steps):
        for k, other in enumerate((True, False)):
            at = rows_of(info, rows, other)
            pairs += into_rows(history_rows(*history, s, at), targets[2 * i + k], 0, rows)
    pairs += into_rows(history_rows(*history, 0, pl.ds(0, 2 * rows)), final, 0, 2 * rows)
    for copy in fetch(pairs, sems):
        copy.wait()


def send_first_kernel(
    s, info, loss, carrier, grating, forward, backward, population, hole,
    own_loss, own, own_carrier, own_grating, out, states, sems,
):
    rows, columns = own_carrier.shape
    theirs, mine = rows_of(info, rows, True), rows_of(info, rows, False)
    history = (forward, backward, population, hole)
    copies = fetch(
        [(carrier.at[theirs, :], states.at[0]), (grating.at[theirs, :], states.at[1])]
        + into_rows([loss.at[theirs, :]], out, 0, rows)
        + into_rows(history_rows(*history, s, theirs), out, 3 * rows, rows)
        + [(loss.at[mine, :], own_loss), (carrier.at[mine, :], own_carrier)]
        + [(grating.at[mine, :], own_grating)]
        + into_rows(history_rows(*history, s, mine), own, 0, rows),
        sems,
    )
    for copy in copies[:2]:
        copy.wait()
    sizes = []
    for i in range(2):
        size = size_of(jnp.abs(states[i]))
        sizes.append(jnp.broadcast_to(size, (8, columns)))
        out[(1 + i) * rows : (2 + i) * rows, :] = encoded(states[i], size)
    out[9 * rows :, :] = jnp.concatenate(sizes).astype(jnp.bfloat16)
    for copy in copies[2:]:
        copy.wait()


def enter_kernel(
    info, forward, backward, other, source, tp, tq, inner, outer, field, work, matrices, sem, sems
):
    copy = pltpu.make_async_copy(source, matrices, sem)
    rows, width = field.shape[1] // 2, field.shape[2]
    columns = width // 2
    half = columns // LANES
    at = rows_of(info, rows, False)
    copies = fetch(
        [
            (ref.at[:, at, :], field.at[:, f * rows : (f + 1) * rows, :columns])
            for f, ref in enumerate((forward, backward))
        ],
        sems,
    )
    copy.start()
    sizes = sizes_in(other[4 * half * rows :, :], 2)
    for f in range(2):
        for part in range(2):

            @pl.loop(0, half, unroll=2)
            def _(j):
                code = other[slab((2 * f + part) * half + j, rows), :]
                field[part, f * rows : (f + 1) * rows, lane(half + j)] = decoded(code, sizes[f])

    for held in copies:
        held.wait()
    filtered(field, work, matrices, copy)
    write_filtered(info, work, tp, tq, inner, outer)


def rows_update(
    info, tp, tq, inner, outer, carrier, grating, own, other, own_loss, other_loss,
    field, new_carrier, new_grating, sums_in, sums, cells, last
):
    rows, width = carrier.shape
    half = width // LANES // 2
    columns = half * LANES
    mid = jnp.where(info[0] == 0, 1.0, 0.0)
    wrap = 1.0 - mid
    low = info[4] == 0
    is_first, is_last = info[1], info[2]
    row_index = lax.broadcasted_iota(jnp.int32, (TILE, LANES), 0)
    zero = jnp.zeros((8, LANES), jnp.float32)

    def step(jj, most):
        for side in range(2):
            j = jj + side * half
            here = lane(j)
            left_at = lane(jnp.where(j == 0, 2 * half - 1, j - 1))
            right_at = lane(jnp.where(j == 2 * half - 1, 0, j + 1))
            swapped = lane(jj + (1 - side) * half)
            weight_left = jnp.where(jj == 0, wrap if side == 0 else mid, 1.0)
            weight_right = jnp.where(jj == half - 1, mid if side == 0 else wrap, 1.0)
            total = zero
            for r in range(0, rows, TILE):
                at = slice(r, r + TILE)

                held, begin = (own, other)[side]

                def part_of(i):
                    tile = begin + i * rows + r
                    return held[tile : tile + TILE, lane(jj)].astype(jnp.float32)

                loss = (own_loss, other_loss)[side][at, lane(jj)].astype(jnp.float32)
                f = [tp[part, r + 1 : r + 1 + TILE, here] for part in range(2)]
                b = [tq[part, r + 7 : r + 7 + TILE, here] for part in range(2)]
                if r + TILE == rows:
                    for part in range(2):
                        facet = FRONT_FACET * tq[part, rows + 7 : rows + 8, here]
                        edge = jnp.where(
                            low, inner[part : part + 1, swapped], outer[part : part + 1, here]
                        )
                        edge = jnp.where(is_last, facet, edge)
                        f[part] = jnp.where(row_index == TILE - 1, edge, f[part])
                if r == 0:
                    for part in range(2):
                        facet = REAR_FACET * tp[part, 0:1, here]
                        edge = jnp.where(
                            low, outer[part : part + 1, here], inner[part : part + 1, swapped]
                        )
                        edge = jnp.where(is_first, facet, edge)
                        b[part] = jnp.where(row_index == 0, edge, b[part])
                c = carrier[at, here]
                lap = curvature(
                    carrier[at, left_at], c, carrier[at, right_at], weight_left, weight_right
                )
                out = updated(
                    *f, *b, [part_of(i) for i in range(4)], part_of(4), part_of(5), loss,
                    c, grating[at, here], lap,
                )
                field[0, r : r + TILE, here] = out[0]
                field[1, r : r + TILE, here] = out[1]
                field[0, rows + r : rows + r + TILE, here] = out[2]
                field[1, rows + r : rows + r + TILE, here] = out[3]
                new_carrier[at, here] = out[4]
                new_grating[at, here] = out[5]
                z = (info[3] + r + row_index).astype(jnp.float32)
                weighted = (1.0 + 2.0 * z / (cells - 1)) * ((c + out[4]) if last else c)
                for k in range(0, TILE, 8):
                    total = total + weighted[k : k + 8]
                if last and side == 1:
                    for k in range(0, TILE, 8):
                        most = (
                            jnp.maximum(most[0], jnp.abs(out[4][k : k + 8])),
                            jnp.maximum(most[1], jnp.abs(out[5][k : k + 8])),
                        )
            summed = jnp.sum(total, axis=0, keepdims=True)
            sums[:, here] = summed if sums_in is None else summed + sums_in[:, here]
        return most

    return lax.fori_loop(0, half, step, (zero, zero))


def first_step_kernel(
    cells, info, tp, tq, inner, outer, my_carrier, my_grating, loss, own, other, source,
    new_tp, new_tq, new_inner, new_outer, new_carrier, new_grating, sums,
    carrier, grating, field, work, matrices, sem,
):
    copy = pltpu.make_async_copy(source, matrices, sem)
    copy.start()
    rows, columns = my_carrier.shape
    half = columns // LANES
    sizes = other[9 * rows :, :LANES].astype(jnp.float32)
    sizes = [sizes[0:1, 0:1], sizes[8:9, 0:1]]
    for i, (whole, mine) in enumerate(((carrier, my_carrier), (grating, my_grating))):
        whole[:, :columns] = mine[...]

        @pl.loop(0, half, unroll=2)
        def _(j):
            whole[:, lane(half + j)] = decoded(
                other[(1 + i) * rows : (2 + i) * rows, lane(j)], sizes[i]
            )

    rows_update(
        info, tp, tq, inner, outer, carrier, grating, (own, 0), (other, 3 * rows), loss, other,
        field, new_carrier, new_grating, None, sums, cells, False,
    )
    filtered(field, work, matrices, copy)
    write_filtered(info, work, new_tp, new_tq, new_inner, new_outer)


def middle_step_kernel(
    cells, info, tp, tq, inner, outer, carrier, grating, loss, own, other, other_loss, sums_in,
    source, new_tp, new_tq, new_inner, new_outer, new_carrier, new_grating, sums,
    field, work, matrices, sem,
):
    copy = pltpu.make_async_copy(source, matrices, sem)
    copy.start()
    rows_update(
        info, tp, tq, inner, outer, carrier, grating, (own, 0), (other, 0), loss, other_loss,
        field, new_carrier, new_grating, sums_in, sums, cells, False,
    )
    filtered(field, work, matrices, copy)
    write_filtered(info, work, new_tp, new_tq, new_inner, new_outer)


def leave_kernel(
    cells, info, tp, tq, inner, outer, carrier, grating, loss, own, other, other_loss, sums_in,
    source, kept, kept_carrier, kept_grating, sides, sent, straight, across, sums,
    new_carrier, new_grating, field, work, matrices, sem,
):
    copy = pltpu.make_async_copy(source, matrices, sem)
    copy.start()
    rows, width = carrier.shape
    columns = width // 2
    half = columns // LANES
    most = rows_update(
        info, tp, tq, inner, outer, carrier, grating, (own, 0), (other, 0), loss, other_loss,
        field, new_carrier, new_grating, sums_in, sums, cells, True,
    )
    mid = jnp.where(info[0] == 0, 1.0, 0.0)
    wrap = 1.0 - mid
    kept_carrier[...] = new_carrier[:, :columns]
    kept_grating[...] = new_grating[:, :columns]
    first, before = new_carrier[:, 0:1] * wrap, new_carrier[:, columns - 1 : columns] * mid
    after, final = new_carrier[:, columns : columns + 1] * mid, new_carrier[:, width - 1 :] * wrap
    sides[0] = jnp.broadcast_to(final, (rows, LANES))
    sides[1] = jnp.broadcast_to(after, (rows, LANES))
    pairs = []
    for at, value in ((0, before), (2, first)):
        coarse = value.astype(jnp.bfloat16).astype(jnp.float32)
        pairs += [(at, coarse), (at + 1, value - coarse)]
    for i, field_of in enumerate((new_carrier, new_grating)):
        size = size_of(most[i])
        pairs.append((SCALE_LANE + 2 + i, size))

        @pl.loop(0, half, unroll=2)
        def _(j):
            sent[slab((4 + i) * half + j, rows), :] = encoded(field_of[:, lane(half + j)], size)

    filtered(field, work, matrices, copy)
    zero = jnp.zeros((8, LANES), jnp.float32)
    for f in range(2):

        def unmix(g, most):
            at = pl.ds(pl.multiple_of(g * 8 + f * rows, 8), 8)
            for j, pair in enumerate(gathered(work, at)):
                for part in range(2):
                    if j < half:
                        kept[part, at, j * LANES : (j + 1) * LANES] = pair[part]
                    else:
                        work[j, at, part * LANES : (part + 1) * LANES] = pair[part]
                        most = jnp.maximum(most, jnp.abs(pair[part]))
            return most

        size = size_of(lax.fori_loop(0, rows // 8, unmix, zero))
        pairs.append((SCALE_LANE + f, size))

        @pl.loop(0, half, unroll=2)
        def _(j):
            for part in range(2):
                value = work[half + j, f * rows : (f + 1) * rows, part * LANES : (part + 1) * LANES]
                sent[slab((2 * f + part) * half + j, rows), :] = encoded(value, size)

    sent[6 * half * rows :, :] = side_tile(pairs, rows)
    low = info[4] == 0
    for part in range(2):
        lanes = slice(part * LANES, (part + 1) * LANES)
        straight[part : part + 1, :] = jnp.where(
            low, kept[part, 0:1, :], kept[part, 2 * rows - 1 : 2 * rows, :]
        )
        for j in range(half):
            across[part : part + 1, j * LANES : (j + 1) * LANES] = jnp.where(
                low, work[half + j, 0:1, lanes], work[half + j, 2 * rows - 1 : 2 * rows, lanes]
            )


def final_kernel(
    cells, info, kept, kept_carrier, kept_grating, sides, came, straight, across, loss, history,
    partial, out_forward, out_backward, out_carrier, out_grating, out_sums,
    tp, tq, carrier, grating,
):
    rows, columns = kept_carrier.shape
    half = columns // LANES
    total = partial[0]
    for i in range(1, partial.shape[0]):
        total = total + partial[i]
    out_sums[...] = total * (CLOCK_DELTA / math.sqrt(cells))
    mine = info[4] * rows
    theirs = (1 - info[4]) * rows
    low = info[4] == 0
    extra = came[6 * half * rows :, :]
    size_forward, size_backward, size_carrier, size_grating = sizes_in(extra, 4)
    extra = extra.astype(jnp.float32)

    def at(start, offset, count):
        return pl.ds(pl.multiple_of(start + offset, 8), count)

    for part in range(2):
        tp[part, at(mine, 0, rows), :] = kept[part, :rows, :]
        tq[part, at(mine, 8, rows), :] = kept[part, rows:, :]
    carrier[at(mine, 0, rows), LANES : LANES + columns] = kept_carrier[...]
    carrier[at(mine, 0, rows), :LANES] = sides[0]
    carrier[at(mine, 0, rows), LANES + columns :] = sides[1]
    carrier[at(theirs, 0, rows), :LANES] = jnp.broadcast_to(
        extra[:, 0:1] + extra[:, 1:2], (rows, LANES)
    )
    carrier[at(theirs, 0, rows), LANES + columns :] = jnp.broadcast_to(
        extra[:, 2:3] + extra[:, 3:4], (rows, LANES)
    )
    grating[at(mine, 0, rows), :] = kept_grating[...]

    @pl.loop(0, half, unroll=2)
    def _(j):
        carrier[at(theirs, 0, rows), lane(1 + j)] = decoded(
            came[slab(4 * half + j, rows), :], size_carrier
        )
        grating[at(theirs, 0, rows), lane(j)] = decoded(
            came[slab(5 * half + j, rows), :], size_grating
        )
        for part in range(2):
            tp[part, at(theirs, 0, rows), lane(j)] = decoded(
                came[slab(part * half + j, rows), :], size_forward
            )
            tq[part, at(theirs, 8, rows), lane(j)] = decoded(
                came[slab((2 + part) * half + j, rows), :], size_backward
            )

    all_rows = 2 * rows
    for part in range(2):
        here = slice(part, part + 1)
        next_edge = jnp.where(low, across[here, :], straight[here, :])
        before_edge = jnp.where(low, straight[here, :], across[here, :])
        front = FRONT_FACET * tq[part, all_rows + 7 : all_rows + 8, :]
        rear = REAR_FACET * tp[part, 0:1, :]
        tp[part, all_rows : all_rows + 1, :] = jnp.where(info[2], front, next_edge)
        tq[part, 7:8, :] = jnp.where(info[1], rear, before_edge)

    @pl.loop(0, half)
    def _(j):
        here = lane(j)
        for r in range(0, all_rows, TILE):
            row = slice(r, r + TILE)
            c = carrier[row, lane(j + 1)]
            lap = curvature(carrier[row, lane(j)], c, carrier[row, lane(j + 2)], 1.0, 1.0)
            parts = [
                history[i * all_rows + r : i * all_rows + r + TILE, here].astype(jnp.float32)
                for i in range(6)
            ]
            out = updated(
                tp[0, r + 1 : r + 1 + TILE, here], tp[1, r + 1 : r + 1 + TILE, here],
                tq[0, r + 7 : r + 7 + TILE, here], tq[1, r + 7 : r + 7 + TILE, here],
                parts[:4], parts[4], parts[5],
                loss[row, here].astype(jnp.float32), c, grating[row, here], lap,
            )
            out_forward[0, row, here] = out[0]
            out_forward[1, row, here] = out[1]
            out_backward[0, row, here] = out[2]
            out_backward[1, row, here] = out[3]
            out_carrier[row, here] = out[4]
            out_grating[row, here] = out[5]


def position(rows, whole):
    x, block, count = lax.axis_index("gx"), lax.axis_index("gz"), lax.axis_size("gz")
    high = lax.rem(x + block, 2)
    if whole:
        return x, block == 0, block == count - 1, block * rows, high
    place = 2 * block + high
    return x, place == 0, place == 2 * count - 1, place * rows, high


def whole_spec(shape):
    return pl.BlockSpec(shape, lambda i, n=len(shape): (0,) * n)


def call(name, kernel, rows, inputs, outputs, scratch, flops=0, grant=24, whole=False):
    arrays = [x[0] if isinstance(x, tuple) else x for x in inputs]
    specs = [x[1] if isinstance(x, tuple) else whole_spec(x.shape) for x in inputs]
    shapes = [jax.ShapeDtypeStruct(*out) for out in outputs]
    moved = sum(math.prod(s.shape) * s.dtype.itemsize for s in shapes)

    def body(*refs):
        kernel(position(rows, whole), *refs)

    return pl.pallas_call(
        body,
        grid=(1,),
        in_specs=specs,
        out_specs=[whole_spec(s.shape) for s in shapes],
        scratch_shapes=scratch,
        out_shape=shapes,
        compiler_params=pltpu.CompilerParams(vmem_limit_bytes=grant * 1024 * 1024),
        cost_estimate=pl.CostEstimate(
            flops=flops, bytes_accessed=moved + 4 * 1024 * 1024, transcendentals=0
        ),
        name=name,
    )(*arrays)


def per_pair(
    ending_rightward_adjoint,
    ending_leftward_adjoint,
    ending_population_adjoint,
    ending_holeburn_adjoint,
    history_rightward,
    history_leftward,
    history_population,
    history_holeburn,
    segment_passive_attenuation,
):
    cell_rows, columns = ending_population_adjoint.shape
    passes = history_population.shape[0]
    rows = cell_rows // 2
    half = columns // LANES
    blocks = 2 * half
    width = 2 * columns
    count = lax.axis_size("gz")
    cells = cell_rows * count
    x = lax.axis_index("gx")
    f32, bf16 = jnp.float32, jnp.bfloat16
    swap = [(0, 1), (1, 0)]
    in_place = pl.BlockSpec(memory_space=pltpu.HBM)

    def held(*arrays):
        return [(a, in_place) for a in arrays]

    def tiles(n):
        return ((n * rows, LANES), bf16)

    ends = held(ending_rightward_adjoint, ending_leftward_adjoint)
    planes = held(ending_population_adjoint, ending_holeburn_adjoint)
    history = held(history_rightward, history_leftward, history_population, history_holeburn)
    losses = held(segment_passive_attenuation)
    matrices = jnp.asarray(lateral_matrices(width, blocks))
    matrix_input = held(matrices)
    work = [
        pltpu.VMEM((blocks, 2 * rows, 2 * LANES), f32),
        pltpu.VMEM(matrices.shape, bf16),
        pltpu.SemaphoreType.DMA,
    ]
    field_scratch = pltpu.VMEM((2, 2 * rows, width), f32)
    state_out = [
        ((2, rows + 8, width), f32), ((2, rows + 8, width), f32), ((2, width), f32), ((2, width), f32),
    ]
    plane = ((rows, width), f32)
    plane_scratch = pltpu.VMEM((rows, width), f32)
    half_plane = ((rows, columns), f32)
    work_flops = 2 * 3 * 2 * rows * blocks * (2 * LANES) ** 2

    (coded,) = call(
        "send_fields", send_fields_kernel, rows, ends, [tiles(4 * half + 1)],
        [pltpu.VMEM((2, 2, rows, columns), f32), pltpu.SemaphoreType.DMA((2,))], grant=62,
    )
    other_fields = lax.ppermute(coded, "gx", swap)
    loss, own_first, my_carrier, my_grating, sent_first = call(
        "send_first", functools.partial(send_first_kernel, passes - 1), rows,
        [*losses, *planes, *history],
        [((rows, columns), bf16), ((6 * rows, columns), bf16), half_plane, half_plane,
         ((9 * rows + TILE, columns), bf16)],
        [pltpu.VMEM((2, rows, columns), f32), pltpu.SemaphoreType.DMA((18,))], grant=62,
    )
    steps = range(passes - 2, 0, -1)
    history_last, *later = call(
        "send_later", functools.partial(send_later_kernel, steps), rows, history,
        [((6 * cell_rows, columns), bf16)] + [((6 * rows, columns), bf16)] * (2 * len(steps)),
        [pltpu.SemaphoreType.DMA((12 * len(steps) + 6,))], grant=62,
    )
    sent_first, history_last, later, other_fields = lax.optimization_barrier(
        (sent_first, history_last, later, other_fields)
    )
    other_first = lax.ppermute(sent_first, "gx", swap)

    line = ("gz", "gx")
    neighbours = []
    for b in range(count - 1):
        top = (1 + b) % 2
        neighbours += [(2 * b + top, 2 * b + 2 + top), (2 * b + 2 + top, 2 * b + top)]

    def edges(inner, outer):
        outer = lax.ppermute(outer, line, neighbours)
        return lax.ppermute(inner, "gx", swap), outer

    tp, tq, inner, outer = call(
        "enter", enter_kernel, rows, [*ends, other_fields, *matrix_input],
        state_out, [field_scratch, *work, pltpu.SemaphoreType.DMA((2,))], work_flops,
    )
    inner, outer = edges(inner, outer)

    other_loss = (other_first, pl.BlockSpec((rows, columns), lambda i: (0, 0)))
    carrier = grating = sums = other = own = None
    for index, s in enumerate(range(passes - 1, 0, -1)):
        if index < len(steps):
            sent, own_next = later[2 * index : 2 * index + 2]
            sent, inner, outer = lax.optimization_barrier((sent, inner, outer))
            coming = lax.ppermute(sent, "gx", swap)
        shared = [tp, tq, inner, outer]
        if index == 0:
            tp, tq, inner, outer, carrier, grating, sums = call(
                "first_step", functools.partial(first_step_kernel, cells), rows,
                [*shared, my_carrier, my_grating, loss, own_first, other_first, *matrix_input],
                [*state_out, plane, plane, ((1, width), f32)],
                [plane_scratch, plane_scratch, field_scratch, *work], work_flops,
            )
        elif s > 1:
            tp, tq, inner, outer, carrier, grating, sums = call(
                "middle_step", functools.partial(middle_step_kernel, cells), rows,
                [*shared, carrier, grating, loss, own, other, other_loss, sums, *matrix_input],
                [*state_out, plane, plane, ((1, width), f32)],
                [field_scratch, *work], work_flops,
            )
        else:
            kept, kept_carrier, kept_grating, sides, sent, straight, across, sums = call(
                "leave", functools.partial(leave_kernel, cells), rows,
                [*shared, carrier, grating, loss, own, other, other_loss, sums, *matrix_input],
                [((2, 2 * rows, columns), f32), half_plane, half_plane, ((2, rows, LANES), f32),
                 tiles(6 * half + 1), ((2, columns), f32), ((2, columns), f32), ((1, width), f32)],
                [plane_scratch, plane_scratch, field_scratch, *work], work_flops,
            )
        if s > 1:
            inner, outer = edges(inner, outer)
            own, other = own_next, coming

    came = lax.ppermute(sent, "gx", swap)
    sums = sums.reshape(2, half, LANES)
    sums = jnp.where(x == 0, sums, sums[::-1])
    sums = jnp.broadcast_to(sums, (count, 2, half, LANES)).reshape(2 * count, half, LANES)
    sums = lax.all_to_all(sums, line, 0, 0, tiled=True)

    straight = lax.ppermute(straight, line, neighbours)
    along = []
    for b in range(count - 1):
        top, foot = (1 + b) % 2, b % 2
        along += [(2 * b + top, 2 * b + 2 + foot), (2 * b + 2 + top, 2 * b + foot)]
    across = lax.ppermute(across, line, along)

    *outs, total = call(
        "final", functools.partial(final_kernel, cells), cell_rows,
        [kept, kept_carrier, kept_grating, sides, came, straight, across,
         segment_passive_attenuation, history_last, sums],
        [((2, cell_rows, columns), f32), ((2, cell_rows, columns), f32),
         ((cell_rows, columns), f32), ((cell_rows, columns), f32), ((half, LANES), f32)],
        [pltpu.VMEM((2, cell_rows + 8, columns), f32), pltpu.VMEM((2, cell_rows + 8, columns), f32),
         pltpu.VMEM((cell_rows, columns + 2 * LANES), f32), pltpu.VMEM((cell_rows, columns), f32)],
        whole=True,
    )
    return (*outs, total.reshape(columns))


def shared_by_pairs(mesh, arguments):
    population = arguments[6]
    passes, cells, width = population.shape
    rows, columns = cells // mesh.shape["gz"], width // mesh.shape["gx"]
    return (
        mesh.shape["gx"] == 2
        and passes >= 3
        and rows % (2 * TILE) == 0
        and columns % LANES == 0
        and (columns // LANES) & (columns // LANES - 1) == 0
        and width <= 4096
    )


def solution(mesh):
    def run(*arguments):
        body = per_pair if shared_by_pairs(mesh, arguments) else per_device
        return jax.shard_map(
            body,
            mesh=mesh,
            in_specs=(
                P(None, "gz", "gx"),
                P(None, "gz", "gx"),
                P("gz", "gx"),
                P("gz", "gx"),
                P(None, None, "gz", "gx"),
                P(None, None, "gz", "gx"),
                P(None, "gz", "gx"),
                P(None, "gz", "gx"),
                P("gz", "gx"),
            ),
            out_specs=(
                P(None, "gz", "gx"), P(None, "gz", "gx"), P("gz", "gx"), P("gz", "gx"), P("gx"),
            ),
            check_vma=False,
        )(*arguments)

    return run
```

```python
import functools
import math

import jax
import jax.numpy as jnp
import ml_dtypes
import numpy as np
from jax import lax
from jax.experimental import pallas as pl
from jax.experimental.pallas import tpu as pltpu
from jax.sharding import PartitionSpec as P

DIFF = 512


FRONT_FACET = 0.3
REAR_FACET = 0.9
GAIN_SLOPE_RATE = 0.3
ALPHA_LINEWIDTH = 2.0
COUPLING = 0.5
CLOCK_DELTA = 0.3
DENSITY_LIFETIME = 2.0
GRATING_LIFE = 0.75
TRANSVERSE_DIFFUS = 0.2


def passed_along(value, axis, steps):
    count = lax.axis_size(axis)
    initial, last = (max(0, -steps), min(count, count - steps))
    return lax.ppermute(value, axis, [(source, source + steps) for source in range(initial, last)])


def with_halo(block, sides, width):
    for axis, dim in sides:
        count = lax.axis_size(axis)
        forward = [(i, i + 1) for i in range(count - 1)]
        backward = [(target, source) for source, target in forward]
        low = lax.ppermute(
            lax.slice_in_dim(block, block.shape[dim] - width, None, axis=dim), axis, forward
        )
        high = lax.ppermute(lax.slice_in_dim(block, 0, width, axis=dim), axis, backward)
        block = jnp.concatenate([low, block, high], axis=dim)
    return block


def rotate(source_re, source_im, cosine, sine, form, sign):
    exact = lax.Precision.HIGHEST
    out_re = jnp.einsum(form, source_re, cosine, precision=exact) + sign * jnp.einsum(
        form, source_im, sine, precision=exact
    )
    out_im = jnp.einsum(form, source_im, cosine, precision=exact) - sign * jnp.einsum(
        form, source_re, sine, precision=exact
    )
    return (out_re, out_im)


def transform(stacked):
    count = stacked.shape[1]
    width = stacked.shape[2]
    second = min(128, width // 2)
    first = width // second
    two_pi = 2.0 * math.pi
    index_a = jnp.arange(first, dtype=jnp.int32)
    index_b = jnp.arange(second, dtype=jnp.int32)
    angle_a = two_pi * (index_a[:, None] * index_a[None, :] % first).astype(jnp.float32) / first
    angle_b = two_pi * (index_b[:, None] * index_b[None, :] % second).astype(jnp.float32) / second
    angle_t = two_pi * (index_a[:, None] * index_b[None, :] % width).astype(jnp.float32) / width
    cos_a, sin_a = (jnp.cos(angle_a), jnp.sin(angle_a))
    cos_b, sin_b = (jnp.cos(angle_b), jnp.sin(angle_b))
    cos_t, sin_t = (jnp.cos(angle_t), jnp.sin(angle_t))
    wavenum = index_a[:, None] + first * index_b[None, :]
    signed = jnp.where(wavenum < width // 2, wavenum, wavenum - width)
    phase = (signed * signed).astype(jnp.float32) * (DIFF / (width / 2) ** 2)
    cos_p, sin_p = (jnp.cos(phase), jnp.sin(phase))
    real_in = stacked[0].reshape(count, first, second)
    imag_in = stacked[1].reshape(count, first, second)
    step_re, step_im = rotate(real_in, imag_in, cos_a, sin_a, "nab,ak->nkb", 1.0)
    twist_re = step_re * cos_t + step_im * sin_t
    twist_im = step_im * cos_t - step_re * sin_t
    spec_re, spec_im = rotate(twist_re, twist_im, cos_b, sin_b, "nkb,bj->nkj", 1.0)
    moved_re = spec_re * cos_p - spec_im * sin_p
    moved_im = spec_re * sin_p + spec_im * cos_p
    back_re, back_im = rotate(moved_re, moved_im, cos_b, sin_b, "nkj,jb->nkb", -1.0)
    untw_re = back_re * cos_t - back_im * sin_t
    untw_im = back_im * cos_t + back_re * sin_t
    final_re, final_im = rotate(untw_re, untw_im, cos_a, sin_a, "nkb,ka->nab", -1.0)
    return jnp.stack([final_re.reshape(count, width), final_im.reshape(count, width)]) / width


def added_up(value, axis):
    count = lax.axis_size(axis)
    if count & (count - 1):
        return lax.psum(value, axis)
    reach = 1
    while reach < count:
        value = value + lax.ppermute(value, axis, [(i, i ^ reach) for i in range(count)])
        reach *= 2
    return value


def lateral_work(parts):
    return (transform(parts[0]), transform(parts[1]))


def multiplier_revision(
    population_multiplier,
    holeburn_multiplier,
    measured_rightward,
    measured_leftward,
    rightward_wave,
    leftward_wave,
    population_level,
    holeburn_magnitude,
    attenuation_factor,
    transverse_curvature,
):
    rightward_inphase, rightward_quadrature = (rightward_wave[0], rightward_wave[1])
    leftward_inphase, leftward_quadrature = (leftward_wave[0], leftward_wave[1])
    measured_rightward_inphase, measured_rightward_quadrature = (
        measured_rightward[0],
        measured_rightward[1],
    )
    measured_leftward_inphase, measured_leftward_quadrature = (
        measured_leftward[0],
        measured_leftward[1],
    )
    surplus_population = population_level - 1.0
    amplification_inphase = 1.0 + 0.5 * (GAIN_SLOPE_RATE * surplus_population - attenuation_factor)
    amplification_quadrature = 0.5 * GAIN_SLOPE_RATE * ALPHA_LINEWIDTH * surplus_population
    joined_waves = COUPLING * holeburn_magnitude
    population_derivative = (
        2.0 * CLOCK_DELTA * GAIN_SLOPE_RATE * surplus_population * population_multiplier
    )
    holeburn_derivative = 2.0 * CLOCK_DELTA * holeburn_multiplier
    revised_rightward_inphase = (
        amplification_inphase * measured_rightward_inphase
        - amplification_quadrature * measured_rightward_quadrature
        + joined_waves * measured_leftward_quadrature
        - population_derivative * rightward_inphase
        + holeburn_derivative * leftward_inphase
    )
    revised_rightward_quadrature = (
        amplification_inphase * measured_rightward_quadrature
        + amplification_quadrature * measured_rightward_inphase
        - joined_waves * measured_leftward_inphase
        - population_derivative * rightward_quadrature
        + holeburn_derivative * leftward_quadrature
    )
    revised_leftward_inphase = (
        amplification_inphase * measured_leftward_inphase
        - amplification_quadrature * measured_leftward_quadrature
        + joined_waves * measured_rightward_quadrature
        - population_derivative * leftward_inphase
        + holeburn_derivative * rightward_inphase
    )
    revised_leftward_quadrature = (
        amplification_inphase * measured_leftward_quadrature
        + amplification_quadrature * measured_leftward_inphase
        - joined_waves * measured_rightward_inphase
        - population_derivative * leftward_quadrature
        + holeburn_derivative * rightward_quadrature
    )
    light_intensity = (
        rightward_inphase * rightward_inphase
        + rightward_quadrature * rightward_quadrature
        + leftward_inphase * leftward_inphase
        + leftward_quadrature * leftward_quadrature
    )
    amplification_share = (
        measured_rightward_inphase * (rightward_inphase + ALPHA_LINEWIDTH * rightward_quadrature)
        + measured_rightward_quadrature
        * (rightward_quadrature - ALPHA_LINEWIDTH * rightward_inphase)
        + measured_leftward_inphase * (leftward_inphase + ALPHA_LINEWIDTH * leftward_quadrature)
        + measured_leftward_quadrature * (leftward_quadrature - ALPHA_LINEWIDTH * leftward_inphase)
    )
    revised_population = (
        population_multiplier
        * (1.0 - CLOCK_DELTA / DENSITY_LIFETIME - CLOCK_DELTA * GAIN_SLOPE_RATE * light_intensity)
        + TRANSVERSE_DIFFUS * transverse_curvature
        + 0.5 * GAIN_SLOPE_RATE * amplification_share
    )
    fresh_holeburn = holeburn_multiplier * (1.0 - CLOCK_DELTA / GRATING_LIFE) + COUPLING * (
        measured_rightward_quadrature * leftward_inphase
        - measured_rightward_inphase * leftward_quadrature
        + measured_leftward_quadrature * rightward_inphase
        - measured_leftward_inphase * rightward_quadrature
    )
    return (
        jnp.stack([revised_rightward_inphase, revised_rightward_quadrature]),
        jnp.stack([revised_leftward_inphase, revised_leftward_quadrature]),
        revised_population,
        fresh_holeburn,
    )


def per_device(
    ending_rightward_adjoint,
    ending_leftward_adjoint,
    ending_population_adjoint,
    ending_holeburn_adjoint,
    history_rightward,
    history_leftward,
    history_population,
    history_holeburn,
    segment_passive_attenuation,
):
    columns = ending_rightward_adjoint.shape[2]
    rows = ending_rightward_adjoint.shape[1]
    blocks = lax.axis_size("gz")
    position = lax.axis_index("gz")
    cells = rows * blocks
    zpos = (position * rows + jnp.arange(rows, dtype=jnp.int32)).astype(jnp.float32)
    scaling_factor = 1.0 + 2.0 * zpos / (cells - 1)
    rightward_multiplier, leftward_multiplier = (ending_rightward_adjoint, ending_leftward_adjoint)
    population_multiplier, holeburn_multiplier = (
        ending_population_adjoint,
        ending_holeburn_adjoint,
    )
    attenuation_factor = segment_passive_attenuation.astype(jnp.float32)
    shape_curve = jnp.zeros((columns,), jnp.float32)
    for moment_position in range(history_rightward.shape[0] - 1, -1, -1):
        shape_curve = shape_curve + jnp.sum(scaling_factor[:, None] * population_multiplier, axis=0)
        above = passed_along(rightward_multiplier[:, :1, :], "gz", -1)
        below = passed_along(leftward_multiplier[:, -1:, :], "gz", 1)
        top_row = jnp.where(
            position == blocks - 1, FRONT_FACET * leftward_multiplier[:, -1:, :], above
        )
        bottom_row = jnp.where(position == 0, REAR_FACET * rightward_multiplier[:, :1, :], below)
        lam_fwd = jnp.concatenate([rightward_multiplier[:, 1:, :], top_row], axis=1)
        lam_bwd = jnp.concatenate([bottom_row, leftward_multiplier[:, :-1, :]], axis=1)
        whole_fwd, whole_bwd = (
            lax.all_gather(lam_fwd, "gx", axis=2, tiled=True),
            lax.all_gather(lam_bwd, "gx", axis=2, tiled=True),
        )
        start = lax.axis_index("gx") * columns
        done_fwd, done_bwd = lateral_work((whole_fwd, whole_bwd))
        measured_rightward = lax.dynamic_slice_in_dim(done_fwd, start, columns, 2)
        measured_leftward = lax.dynamic_slice_in_dim(done_bwd, start, columns, 2)
        bordered_array = with_halo(population_multiplier, (("gx", 1),), 1)
        transverse_curvature = (
            bordered_array[:, 2:] + bordered_array[:, :-2] - 2.0 * population_multiplier
        )
        rightward_multiplier, leftward_multiplier, population_multiplier, holeburn_multiplier = (
            multiplier_revision(
                population_multiplier,
                holeburn_multiplier,
                measured_rightward,
                measured_leftward,
                history_rightward[moment_position].astype(jnp.float32),
                history_leftward[moment_position].astype(jnp.float32),
                history_population[moment_position].astype(jnp.float32),
                history_holeburn[moment_position].astype(jnp.float32),
                attenuation_factor,
                transverse_curvature,
            )
        )
    total = added_up(shape_curve, "gz")
    derivative_vector = CLOCK_DELTA * total / math.sqrt(cells)
    return (
        rightward_multiplier,
        leftward_multiplier,
        population_multiplier,
        holeburn_multiplier,
        derivative_vector,
    )

LANES = 128
TILE = 16
POWER = 12
STRETCH = 1211.0
SCALE_LANE = 8


def lateral_matrices(width, blocks):
    lanes = width // blocks
    k = np.arange(width)
    signed = np.where(k < width // 2, k, k - width).astype(np.float64)
    response = np.fft.ifft(np.exp(1j * signed * signed * (DIFF / (width / 2) ** 2)))
    step = np.arange(lanes)
    shift = lanes * np.arange(blocks)[:, None, None] + step[None, None, :] - step[None, :, None]
    kernels = np.fft.fft(response[shift % width], axis=0) / blocks
    top = np.concatenate([kernels.real, kernels.imag], axis=2)
    low = np.concatenate([-kernels.imag, kernels.real], axis=2)
    whole = np.concatenate([top, low], axis=1)
    first = whole.astype(ml_dtypes.bfloat16)
    rest = (whole - first.astype(np.float64)).astype(ml_dtypes.bfloat16)
    return np.stack([first, rest], axis=1)


def block_dft(values, sign):
    count = len(values)
    if count == 1:
        return values
    even = block_dft(values[0::2], sign)
    odd = block_dft(values[1::2], sign)
    out = [None] * count
    for k in range(count // 2):
        (er, ei), (wr, wi) = even[k], odd[k]
        if 4 * k == count:
            plus, minus = (er - wi, ei + wr), (er + wi, ei - wr)
            out[k], out[k + count // 2] = (plus, minus) if sign > 0 else (minus, plus)
            continue
        if k:
            c, s = math.cos(2 * math.pi * k / count), sign * math.sin(2 * math.pi * k / count)
            if 8 * k == count:
                wr, wi = (c * (wr - wi), c * (wr + wi)) if sign > 0 else (c * (wr + wi), c * (wi - wr))
            elif 8 * k == 3 * count:
                wr, wi = (c * (wr + wi), c * (wi - wr)) if sign > 0 else (c * (wr - wi), c * (wr + wi))
            else:
                wr, wi = c * wr - s * wi, c * wi + s * wr
        out[k] = (er + wr, ei + wi)
        out[k + count // 2] = (er - wr, ei - wi)
    return out


def lane(j):
    return pl.ds(pl.multiple_of(j * LANES, LANES), LANES)


def slab(j, rows):
    return pl.ds(pl.multiple_of(j * rows, rows), rows)


def fetch(pairs, sems, first=0):
    copies = [pltpu.make_async_copy(a, b, sems.at[first + i]) for i, (a, b) in enumerate(pairs)]
    for copy in copies:
        copy.start()
    return copies


def rows_of(info, rows, other):
    part = 1 - info[4] if other else info[4]
    return pl.ds(pl.multiple_of(part * rows, rows), rows)


def spread(field, work):
    rows = field.shape[1]
    blocks = work.shape[0]

    @pl.loop(0, rows // 8)
    def _(g):
        at = slab(g, 8)
        values = [
            (field[0, at, j * LANES : (j + 1) * LANES], field[1, at, j * LANES : (j + 1) * LANES])
            for j in range(blocks)
        ]
        for q, (re, im) in enumerate(block_dft(values, -1)):
            work[q, at, :LANES] = re
            work[q, at, LANES:] = im


def multiply(work, matrices):
    rows = work.shape[1]

    @pl.loop(0, work.shape[0], unroll=True)
    def _(q):
        value = work[q]
        first = value.astype(jnp.bfloat16)
        rest = (value - first.astype(jnp.float32)).astype(jnp.bfloat16)
        both = jnp.dot(
            jnp.concatenate([first, rest]), matrices[q, 0], preferred_element_type=jnp.float32
        )
        fine = jnp.dot(first, matrices[q, 1], preferred_element_type=jnp.float32)
        work[q] = both[:rows] + (both[rows:] + fine)


def gathered(work, at):
    values = [(work[q, at, :LANES], work[q, at, LANES:]) for q in range(work.shape[0])]
    return block_dft(values, 1)


def filtered(field, work, matrices, copy):
    spread(field, work)
    copy.wait()
    multiply(work, matrices)


def write_filtered(info, work, forward, backward, inner, outer):
    rows = work.shape[1] // 2
    for target, base, offset in ((forward, 0, 0), (backward, rows, 8)):

        @pl.loop(0, rows // 8)
        def _(g):
            here = pl.ds(pl.multiple_of(g * 8 + offset, 8), 8)
            for j, pair in enumerate(gathered(work, pl.ds(pl.multiple_of(g * 8 + base, 8), 8))):
                for part in range(2):
                    target[part, here, j * LANES : (j + 1) * LANES] = pair[part]

    low = info[4] == 0
    for part in range(2):
        first, last = forward[part, 0:1, :], backward[part, rows + 7 : rows + 8, :]
        inner[part : part + 1, :] = jnp.where(low, last, first)
        outer[part : part + 1, :] = jnp.where(low, first, last)


def size_of(largest):
    top = jnp.max(jnp.max(largest, axis=1, keepdims=True), axis=0, keepdims=True)
    return jnp.maximum(top, 1e-30).astype(jnp.bfloat16).astype(jnp.float32)


def encoded(value, size):
    unit = value * (STRETCH / size)
    square = unit * unit
    fourth = square * square
    return (fourth * fourth * square * (unit * jnp.abs(unit))).astype(jnp.bfloat16)


def decoded(code, size):
    value = code.astype(jnp.float32)
    root = jnp.exp2(jnp.log(jnp.abs(value)) * (1.0 / (POWER * math.log(2.0)))) * (size / STRETCH)
    return jnp.where(value < 0.0, -root, root)


def side_tile(columns, rows):
    index = lax.broadcasted_iota(jnp.int32, (rows, LANES), 1)
    tile = jnp.zeros((rows, LANES), jnp.float32)
    for at, column in columns:
        tile = jnp.where(index == at, column, tile)
    return tile.astype(jnp.bfloat16)


def sizes_in(tile, count):
    value = tile.astype(jnp.float32)
    return [value[0:1, SCALE_LANE + i : SCALE_LANE + i + 1] for i in range(count)]


def updated(fr, fi, br, bi, wave, population, hole, loss, carrier, grating, lap):
    rr, ri, lr, li = wave
    surplus = population - 1.0
    gain_re = 1.0 + 0.5 * (GAIN_SLOPE_RATE * surplus - loss)
    gain_im = (0.5 * GAIN_SLOPE_RATE * ALPHA_LINEWIDTH) * surplus
    joined = COUPLING * hole
    drive = (2.0 * CLOCK_DELTA * GAIN_SLOPE_RATE) * surplus * carrier
    mix = (2.0 * CLOCK_DELTA) * grating
    new_fr = gain_re * fr - gain_im * fi + joined * bi - drive * rr + mix * lr
    new_fi = gain_re * fi + gain_im * fr - joined * br - drive * ri + mix * li
    new_br = gain_re * br - gain_im * bi + joined * fi - drive * lr + mix * rr
    new_bi = gain_re * bi + gain_im * br - joined * fr - drive * li + mix * ri
    light = rr * rr + ri * ri + lr * lr + li * li
    share = (
        fr * (rr + ALPHA_LINEWIDTH * ri)
        + fi * (ri - ALPHA_LINEWIDTH * rr)
        + br * (lr + ALPHA_LINEWIDTH * li)
        + bi * (li - ALPHA_LINEWIDTH * lr)
    )
    new_carrier = (
        carrier * ((1.0 - CLOCK_DELTA / DENSITY_LIFETIME) - (CLOCK_DELTA * GAIN_SLOPE_RATE) * light)
        + TRANSVERSE_DIFFUS * lap
        + (0.5 * GAIN_SLOPE_RATE) * share
    )
    new_grating = grating * (1.0 - CLOCK_DELTA / GRATING_LIFE) + COUPLING * (
        fi * lr - fr * li + bi * rr - br * ri
    )
    return new_fr, new_fi, new_br, new_bi, new_carrier, new_grating


def curvature(left, mid, right, weight_left, weight_right):
    index = lax.broadcasted_iota(jnp.int32, mid.shape, 1)
    below = jnp.where(index == 0, pltpu.roll(left, 1, 1) * weight_left, pltpu.roll(mid, 1, 1))
    above = jnp.where(
        index == LANES - 1,
        pltpu.roll(right, LANES - 1, 1) * weight_right,
        pltpu.roll(mid, LANES - 1, 1),
    )
    return below + above - 2.0 * mid


def send_fields_kernel(info, forward, backward, out, fields, sems):
    rows, columns = fields.shape[2:]
    half = columns // LANES
    at = rows_of(info, rows, True)
    copies = fetch(
        [(ref.at[:, at, :], fields.at[f]) for f, ref in enumerate((forward, backward))], sems
    )
    sizes = []
    for f in range(2):
        copies[f].wait()
        largest = jnp.maximum(jnp.abs(fields[f, 0]), jnp.abs(fields[f, 1]))
        size = size_of(largest)
        sizes.append((SCALE_LANE + f, size))
        for part in range(2):
            put_tiles(out, (2 * f + part) * half, encoded(fields[f, part], size))
    out[4 * half * rows :, :] = side_tile(sizes, rows)


def put_tiles(out, first, value):
    rows, columns = value.shape
    for j in range(columns // LANES):
        at = (first + j) * rows
        out[at : at + rows, :] = value[:, j * LANES : (j + 1) * LANES]


def history_rows(forward, backward, population, hole, s, at):
    return [
        forward.at[s, 0, at, :], forward.at[s, 1, at, :], backward.at[s, 0, at, :],
        backward.at[s, 1, at, :], population.at[s, at, :], hole.at[s, at, :],
    ]


def into_rows(parts, target, first, rows):
    return [(part, target.at[pl.ds(first + i * rows, rows), :]) for i, part in enumerate(parts)]


def send_later_kernel(steps, info, forward, backward, population, hole, final, *refs):
    targets, sems = refs[:-1], refs[-1]
    rows = targets[0].shape[0] // 6
    history = (forward, backward, population, hole)
    pairs = []
    for i, s in enumerate(steps):
        for k, other in enumerate((True, False)):
            at = rows_of(info, rows, other)
            pairs += into_rows(history_rows(*history, s, at), targets[2 * i + k], 0, rows)
    pairs += into_rows(history_rows(*history, 0, pl.ds(0, 2 * rows)), final, 0, 2 * rows)
    for copy in fetch(pairs, sems):
        copy.wait()


def send_first_kernel(
    s, info, loss, carrier, grating, forward, backward, population, hole,
    own_loss, own, own_carrier, own_grating, out, states, sems,
):
    rows, columns = own_carrier.shape
    theirs, mine = rows_of(info, rows, True), rows_of(info, rows, False)
    history = (forward, backward, population, hole)
    copies = fetch(
        [(carrier.at[theirs, :], states.at[0]), (grating.at[theirs, :], states.at[1])]
        + into_rows([loss.at[theirs, :]], out, 0, rows)
        + into_rows(history_rows(*history, s, theirs), out, 3 * rows, rows)
        + [(loss.at[mine, :], own_loss), (carrier.at[mine, :], own_carrier)]
        + [(grating.at[mine, :], own_grating)]
        + into_rows(history_rows(*history, s, mine), own, 0, rows),
        sems,
    )
    for copy in copies[:2]:
        copy.wait()
    sizes = []
    for i in range(2):
        size = size_of(jnp.abs(states[i]))
        sizes.append(jnp.broadcast_to(size, (8, columns)))
        out[(1 + i) * rows : (2 + i) * rows, :] = encoded(states[i], size)
    out[9 * rows :, :] = jnp.concatenate(sizes).astype(jnp.bfloat16)
    for copy in copies[2:]:
        copy.wait()


def enter_kernel(
    info, forward, backward, other, source, tp, tq, inner, outer, field, work, matrices, sem, sems
):
    copy = pltpu.make_async_copy(source, matrices, sem)
    rows, width = field.shape[1] // 2, field.shape[2]
    columns = width // 2
    half = columns // LANES
    at = rows_of(info, rows, False)
    copies = fetch(
        [
            (ref.at[:, at, :], field.at[:, f * rows : (f + 1) * rows, :columns])
            for f, ref in enumerate((forward, backward))
        ],
        sems,
    )
    copy.start()
    sizes = sizes_in(other[4 * half * rows :, :], 2)
    for f in range(2):
        for part in range(2):

            @pl.loop(0, half, unroll=2)
            def _(j):
                code = other[slab((2 * f + part) * half + j, rows), :]
                field[part, f * rows : (f + 1) * rows, lane(half + j)] = decoded(code, sizes[f])

    for held in copies:
        held.wait()
    filtered(field, work, matrices, copy)
    write_filtered(info, work, tp, tq, inner, outer)


def rows_update(
    info, tp, tq, inner, outer, carrier, grating, own, other, own_loss, other_loss,
    field, new_carrier, new_grating, sums_in, sums, cells, last
):
    rows, width = carrier.shape
    half = width // LANES // 2
    columns = half * LANES
    mid = jnp.where(info[0] == 0, 1.0, 0.0)
    wrap = 1.0 - mid
    low = info[4] == 0
    is_first, is_last = info[1], info[2]
    row_index = lax.broadcasted_iota(jnp.int32, (TILE, LANES), 0)
    zero = jnp.zeros((8, LANES), jnp.float32)

    def step(jj, most):
        for side in range(2):
            j = jj + side * half
            here = lane(j)
            left_at = lane(jnp.where(j == 0, 2 * half - 1, j - 1))
            right_at = lane(jnp.where(j == 2 * half - 1, 0, j + 1))
            swapped = lane(jj + (1 - side) * half)
            weight_left = jnp.where(jj == 0, wrap if side == 0 else mid, 1.0)
            weight_right = jnp.where(jj == half - 1, mid if side == 0 else wrap, 1.0)
            total = zero
            for r in range(0, rows, TILE):
                at = slice(r, r + TILE)

                held, begin = (own, other)[side]

                def part_of(i):
                    tile = begin + i * rows + r
                    return held[tile : tile + TILE, lane(jj)].astype(jnp.float32)

                loss = (own_loss, other_loss)[side][at, lane(jj)].astype(jnp.float32)
                f = [tp[part, r + 1 : r + 1 + TILE, here] for part in range(2)]
                b = [tq[part, r + 7 : r + 7 + TILE, here] for part in range(2)]
                if r + TILE == rows:
                    for part in range(2):
                        facet = FRONT_FACET * tq[part, rows + 7 : rows + 8, here]
                        edge = jnp.where(
                            low, inner[part : part + 1, swapped], outer[part : part + 1, here]
                        )
                        edge = jnp.where(is_last, facet, edge)
                        f[part] = jnp.where(row_index == TILE - 1, edge, f[part])
                if r == 0:
                    for part in range(2):
                        facet = REAR_FACET * tp[part, 0:1, here]
                        edge = jnp.where(
                            low, outer[part : part + 1, here], inner[part : part + 1, swapped]
                        )
                        edge = jnp.where(is_first, facet, edge)
                        b[part] = jnp.where(row_index == 0, edge, b[part])
                c = carrier[at, here]
                lap = curvature(
                    carrier[at, left_at], c, carrier[at, right_at], weight_left, weight_right
                )
                out = updated(
                    *f, *b, [part_of(i) for i in range(4)], part_of(4), part_of(5), loss,
                    c, grating[at, here], lap,
                )
                field[0, r : r + TILE, here] = out[0]
                field[1, r : r + TILE, here] = out[1]
                field[0, rows + r : rows + r + TILE, here] = out[2]
                field[1, rows + r : rows + r + TILE, here] = out[3]
                new_carrier[at, here] = out[4]
                new_grating[at, here] = out[5]
                z = (info[3] + r + row_index).astype(jnp.float32)
                weighted = (1.0 + 2.0 * z / (cells - 1)) * ((c + out[4]) if last else c)
                for k in range(0, TILE, 8):
                    total = total + weighted[k : k + 8]
                if last and side == 1:
                    for k in range(0, TILE, 8):
                        most = (
                            jnp.maximum(most[0], jnp.abs(out[4][k : k + 8])),
                            jnp.maximum(most[1], jnp.abs(out[5][k : k + 8])),
                        )
            summed = jnp.sum(total, axis=0, keepdims=True)
            sums[:, here] = summed if sums_in is None else summed + sums_in[:, here]
        return most

    return lax.fori_loop(0, half, step, (zero, zero))


def first_step_kernel(
    cells, info, tp, tq, inner, outer, my_carrier, my_grating, loss, own, other, source,
    new_tp, new_tq, new_inner, new_outer, new_carrier, new_grating, sums,
    carrier, grating, field, work, matrices, sem,
):
    copy = pltpu.make_async_copy(source, matrices, sem)
    copy.start()
    rows, columns = my_carrier.shape
    half = columns // LANES
    sizes = other[9 * rows :, :LANES].astype(jnp.float32)
    sizes = [sizes[0:1, 0:1], sizes[8:9, 0:1]]
    for i, (whole, mine) in enumerate(((carrier, my_carrier), (grating, my_grating))):
        whole[:, :columns] = mine[...]

        @pl.loop(0, half, unroll=2)
        def _(j):
            whole[:, lane(half + j)] = decoded(
                other[(1 + i) * rows : (2 + i) * rows, lane(j)], sizes[i]
            )

    rows_update(
        info, tp, tq, inner, outer, carrier, grating, (own, 0), (other, 3 * rows), loss, other,
        field, new_carrier, new_grating, None, sums, cells, False,
    )
    filtered(field, work, matrices, copy)
    write_filtered(info, work, new_tp, new_tq, new_inner, new_outer)


def middle_step_kernel(
    cells, info, tp, tq, inner, outer, carrier, grating, loss, own, other, other_loss, sums_in,
    source, new_tp, new_tq, new_inner, new_outer, new_carrier, new_grating, sums,
    field, work, matrices, sem,
):
    copy = pltpu.make_async_copy(source, matrices, sem)
    copy.start()
    rows_update(
        info, tp, tq, inner, outer, carrier, grating, (own, 0), (other, 0), loss, other_loss,
        field, new_carrier, new_grating, sums_in, sums, cells, False,
    )
    filtered(field, work, matrices, copy)
    write_filtered(info, work, new_tp, new_tq, new_inner, new_outer)


def leave_kernel(
    cells, info, tp, tq, inner, outer, carrier, grating, loss, own, other, other_loss, sums_in,
    source, kept, kept_carrier, kept_grating, sides, sent, edge, shares,
    sums, new_carrier, new_grating, field, work, matrices, sem,
):
    copy = pltpu.make_async_copy(source, matrices, sem)
    copy.start()
    rows, width = carrier.shape
    columns = width // 2
    half = columns // LANES
    most = rows_update(
        info, tp, tq, inner, outer, carrier, grating, (own, 0), (other, 0), loss, other_loss,
        field, new_carrier, new_grating, sums_in, sums, cells, True,
    )
    mid = jnp.where(info[0] == 0, 1.0, 0.0)
    wrap = 1.0 - mid
    kept_carrier[...] = new_carrier[:, :columns]
    kept_grating[...] = new_grating[:, :columns]
    first, before = new_carrier[:, 0:1] * wrap, new_carrier[:, columns - 1 : columns] * mid
    after, final = new_carrier[:, columns : columns + 1] * mid, new_carrier[:, width - 1 :] * wrap
    sides[0] = jnp.broadcast_to(final, (rows, LANES))
    sides[1] = jnp.broadcast_to(after, (rows, LANES))
    pairs = []
    for at, value in ((0, before), (2, first)):
        coarse = value.astype(jnp.bfloat16).astype(jnp.float32)
        pairs += [(at, coarse), (at + 1, value - coarse)]
    for i, field_of in enumerate((new_carrier, new_grating)):
        size = size_of(most[i])
        pairs.append((SCALE_LANE + 2 + i, size))

        @pl.loop(0, half, unroll=2)
        def _(j):
            sent[slab((4 + i) * half + j, rows), :] = encoded(field_of[:, lane(half + j)], size)

    filtered(field, work, matrices, copy)
    zero = jnp.zeros((8, LANES), jnp.float32)
    for f in range(2):

        def unmix(g, most):
            at = pl.ds(pl.multiple_of(g * 8 + f * rows, 8), 8)
            for j, pair in enumerate(gathered(work, at)):
                for part in range(2):
                    if j < half:
                        kept[part, at, j * LANES : (j + 1) * LANES] = pair[part]
                    else:
                        work[j, at, part * LANES : (part + 1) * LANES] = pair[part]
                        most = jnp.maximum(most, jnp.abs(pair[part]))
            return most

        size = size_of(lax.fori_loop(0, rows // 8, unmix, zero))
        pairs.append((SCALE_LANE + f, size))

        @pl.loop(0, half, unroll=2)
        def _(j):
            for part in range(2):
                value = work[half + j, f * rows : (f + 1) * rows, part * LANES : (part + 1) * LANES]
                sent[slab((2 * f + part) * half + j, rows), :] = encoded(value, size)

    sent[6 * half * rows :, :] = side_tile(pairs, rows)
    low = info[4] == 0
    for part in range(2):
        lanes = slice(part * LANES, (part + 1) * LANES)
        edge[part : part + 1, :columns] = jnp.where(
            low, kept[part, 0:1, :], kept[part, 2 * rows - 1 : 2 * rows, :]
        )
        for j in range(half, 2 * half):
            edge[part : part + 1, j * LANES : (j + 1) * LANES] = jnp.where(
                low, work[j, 0:1, lanes], work[j, 2 * rows - 1 : 2 * rows, lanes]
            )
    tile = jnp.concatenate([sums[:, j * LANES : (j + 1) * LANES] for j in range(2 * half)])
    for i in range(shares.shape[0]):
        shares[i] = tile


def gather_kernel(info, partial, edge, mine, theirs):
    half = mine.shape[0]
    total = partial[0]
    for i in range(1, partial.shape[0]):
        total = total + partial[i]
    mine[...] = total[:half]
    theirs[:half] = total[half:]
    for part in range(2):
        for j in range(half):
            at = (1 + part) * half + j
            theirs[at : at + 1] = edge[part : part + 1, (half + j) * LANES : (half + j + 1) * LANES]


def final_kernel(
    cells, info, kept, kept_carrier, kept_grating, sides, came, edge, sums, theirs_in, loss, history,
    out_forward, out_backward, out_carrier, out_grating, out_sums,
    tp, tq, carrier, grating,
):
    rows, columns = kept_carrier.shape
    half = columns // LANES
    out_sums[...] = (sums[...] + theirs_in[:half]) * (CLOCK_DELTA / math.sqrt(cells))
    mine = info[4] * rows
    theirs = (1 - info[4]) * rows
    low = info[4] == 0
    extra = came[6 * half * rows :, :]
    size_forward, size_backward, size_carrier, size_grating = sizes_in(extra, 4)
    extra = extra.astype(jnp.float32)

    def at(start, offset, count):
        return pl.ds(pl.multiple_of(start + offset, 8), count)

    for part in range(2):
        tp[part, at(mine, 0, rows), :] = kept[part, :rows, :]
        tq[part, at(mine, 8, rows), :] = kept[part, rows:, :]
    carrier[at(mine, 0, rows), LANES : LANES + columns] = kept_carrier[...]
    carrier[at(mine, 0, rows), :LANES] = sides[0]
    carrier[at(mine, 0, rows), LANES + columns :] = sides[1]
    carrier[at(theirs, 0, rows), :LANES] = jnp.broadcast_to(
        extra[:, 0:1] + extra[:, 1:2], (rows, LANES)
    )
    carrier[at(theirs, 0, rows), LANES + columns :] = jnp.broadcast_to(
        extra[:, 2:3] + extra[:, 3:4], (rows, LANES)
    )
    grating[at(mine, 0, rows), :] = kept_grating[...]

    @pl.loop(0, half, unroll=2)
    def _(j):
        carrier[at(theirs, 0, rows), lane(1 + j)] = decoded(
            came[slab(4 * half + j, rows), :], size_carrier
        )
        grating[at(theirs, 0, rows), lane(j)] = decoded(
            came[slab(5 * half + j, rows), :], size_grating
        )
        for part in range(2):
            tp[part, at(theirs, 0, rows), lane(j)] = decoded(
                came[slab(part * half + j, rows), :], size_forward
            )
            tq[part, at(theirs, 8, rows), lane(j)] = decoded(
                came[slab((2 + part) * half + j, rows), :], size_backward
            )

    all_rows = 2 * rows
    for part in range(2):
        near = edge[part : part + 1, :columns]
        tiles = theirs_in[(1 + part) * half : (2 + part) * half, :]
        far = jnp.concatenate([tiles[j : j + 1] for j in range(half)], axis=1)
        next_edge = jnp.where(low, far, near)
        before_edge = jnp.where(low, near, far)
        front = FRONT_FACET * tq[part, all_rows + 7 : all_rows + 8, :]
        rear = REAR_FACET * tp[part, 0:1, :]
        tp[part, all_rows : all_rows + 1, :] = jnp.where(info[2], front, next_edge)
        tq[part, 7:8, :] = jnp.where(info[1], rear, before_edge)

    @pl.loop(0, half)
    def _(j):
        here = lane(j)
        for r in range(0, all_rows, TILE):
            row = slice(r, r + TILE)
            c = carrier[row, lane(j + 1)]
            lap = curvature(carrier[row, lane(j)], c, carrier[row, lane(j + 2)], 1.0, 1.0)
            parts = [
                history[i * all_rows + r : i * all_rows + r + TILE, here].astype(jnp.float32)
                for i in range(6)
            ]
            out = updated(
                tp[0, r + 1 : r + 1 + TILE, here], tp[1, r + 1 : r + 1 + TILE, here],
                tq[0, r + 7 : r + 7 + TILE, here], tq[1, r + 7 : r + 7 + TILE, here],
                parts[:4], parts[4], parts[5],
                loss[row, here].astype(jnp.float32), c, grating[row, here], lap,
            )
            out_forward[0, row, here] = out[0]
            out_forward[1, row, here] = out[1]
            out_backward[0, row, here] = out[2]
            out_backward[1, row, here] = out[3]
            out_carrier[row, here] = out[4]
            out_grating[row, here] = out[5]


def position(rows, whole):
    x, block, count = lax.axis_index("gx"), lax.axis_index("gz"), lax.axis_size("gz")
    high = lax.rem(x + block, 2)
    if whole:
        return x, block == 0, block == count - 1, block * rows, high
    place = 2 * block + high
    return x, place == 0, place == 2 * count - 1, place * rows, high


def whole_spec(shape):
    return pl.BlockSpec(shape, lambda i, n=len(shape): (0,) * n)


def call(name, kernel, rows, inputs, outputs, scratch, flops=0, grant=24, whole=False):
    arrays = [x[0] if isinstance(x, tuple) else x for x in inputs]
    specs = [x[1] if isinstance(x, tuple) else whole_spec(x.shape) for x in inputs]
    shapes = [jax.ShapeDtypeStruct(*out) for out in outputs]
    moved = sum(math.prod(s.shape) * s.dtype.itemsize for s in shapes)

    def body(*refs):
        kernel(position(rows, whole), *refs)

    return pl.pallas_call(
        body,
        grid=(1,),
        in_specs=specs,
        out_specs=[whole_spec(s.shape) for s in shapes],
        scratch_shapes=scratch,
        out_shape=shapes,
        compiler_params=pltpu.CompilerParams(vmem_limit_bytes=grant * 1024 * 1024),
        cost_estimate=pl.CostEstimate(
            flops=flops, bytes_accessed=moved + 4 * 1024 * 1024, transcendentals=0
        ),
        name=name,
    )(*arrays)


def per_pair(
    ending_rightward_adjoint,
    ending_leftward_adjoint,
    ending_population_adjoint,
    ending_holeburn_adjoint,
    history_rightward,
    history_leftward,
    history_population,
    history_holeburn,
    segment_passive_attenuation,
):
    cell_rows, columns = ending_population_adjoint.shape
    passes = history_population.shape[0]
    rows = cell_rows // 2
    half = columns // LANES
    blocks = 2 * half
    width = 2 * columns
    count = lax.axis_size("gz")
    cells = cell_rows * count
    x = lax.axis_index("gx")
    f32, bf16 = jnp.float32, jnp.bfloat16
    swap = [(0, 1), (1, 0)]
    in_place = pl.BlockSpec(memory_space=pltpu.HBM)

    def held(*arrays):
        return [(a, in_place) for a in arrays]

    def tiles(n):
        return ((n * rows, LANES), bf16)

    ends = held(ending_rightward_adjoint, ending_leftward_adjoint)
    planes = held(ending_population_adjoint, ending_holeburn_adjoint)
    history = held(history_rightward, history_leftward, history_population, history_holeburn)
    losses = held(segment_passive_attenuation)
    matrices = pltpu.with_memory_space_constraint(
        jnp.asarray(lateral_matrices(width, blocks)), pltpu.HBM
    )
    matrix_input = held(matrices)
    work = [
        pltpu.VMEM((blocks, 2 * rows, 2 * LANES), f32),
        pltpu.VMEM(matrices.shape, bf16),
        pltpu.SemaphoreType.DMA,
    ]
    field_scratch = pltpu.VMEM((2, 2 * rows, width), f32)
    state_out = [
        ((2, rows + 8, width), f32), ((2, rows + 8, width), f32), ((2, width), f32), ((2, width), f32),
    ]
    plane = ((rows, width), f32)
    plane_scratch = pltpu.VMEM((rows, width), f32)
    half_plane = ((rows, columns), f32)
    work_flops = 2 * 3 * 2 * rows * blocks * (2 * LANES) ** 2

    (coded,) = call(
        "send_fields", send_fields_kernel, rows, ends, [tiles(4 * half + 1)],
        [pltpu.VMEM((2, 2, rows, columns), f32), pltpu.SemaphoreType.DMA((2,))], grant=62,
    )
    other_fields = lax.ppermute(coded, "gx", swap)
    loss, own_first, my_carrier, my_grating, sent_first = call(
        "send_first", functools.partial(send_first_kernel, passes - 1), rows,
        [*losses, *planes, *history],
        [((rows, columns), bf16), ((6 * rows, columns), bf16), half_plane, half_plane,
         ((9 * rows + TILE, columns), bf16)],
        [pltpu.VMEM((2, rows, columns), f32), pltpu.SemaphoreType.DMA((18,))], grant=62,
    )
    steps = range(passes - 2, 0, -1)
    history_last, *later = call(
        "send_later", functools.partial(send_later_kernel, steps), rows, history,
        [((6 * cell_rows, columns), bf16)] + [((6 * rows, columns), bf16)] * (2 * len(steps)),
        [pltpu.SemaphoreType.DMA((12 * len(steps) + 6,))], grant=62,
    )
    sent_first, history_last, later, other_fields = lax.optimization_barrier(
        (sent_first, history_last, later, other_fields)
    )
    other_first = lax.ppermute(sent_first, "gx", swap)

    line = ("gz", "gx")
    neighbours = []
    for b in range(count - 1):
        top = (1 + b) % 2
        neighbours += [(2 * b + top, 2 * b + 2 + top), (2 * b + 2 + top, 2 * b + top)]

    def edges(inner, outer):
        outer = lax.ppermute(outer, line, neighbours)
        return lax.ppermute(inner, "gx", swap), outer

    tp, tq, inner, outer = call(
        "enter", enter_kernel, rows, [*ends, other_fields, *matrix_input],
        state_out, [field_scratch, *work, pltpu.SemaphoreType.DMA((2,))], work_flops,
    )
    inner, outer = edges(inner, outer)

    other_loss = (other_first, pl.BlockSpec((rows, columns), lambda i: (0, 0)))
    carrier = grating = sums = other = own = None
    for index, s in enumerate(range(passes - 1, 0, -1)):
        if index < len(steps):
            sent, own_next = later[2 * index : 2 * index + 2]
            sent, inner, outer = lax.optimization_barrier((sent, inner, outer))
            coming = lax.ppermute(sent, "gx", swap)
        shared = [tp, tq, inner, outer]
        if index == 0:
            tp, tq, inner, outer, carrier, grating, sums = call(
                "first_step", functools.partial(first_step_kernel, cells), rows,
                [*shared, my_carrier, my_grating, loss, own_first, other_first, *matrix_input],
                [*state_out, plane, plane, ((1, width), f32)],
                [plane_scratch, plane_scratch, field_scratch, *work], work_flops,
            )
        elif s > 1:
            tp, tq, inner, outer, carrier, grating, sums = call(
                "middle_step", functools.partial(middle_step_kernel, cells), rows,
                [*shared, carrier, grating, loss, own, other, other_loss, sums, *matrix_input],
                [*state_out, plane, plane, ((1, width), f32)],
                [field_scratch, *work], work_flops,
            )
        else:
            kept, kept_carrier, kept_grating, sides, sent, edge, shares = call(
                "leave", functools.partial(leave_kernel, cells), rows,
                [*shared, carrier, grating, loss, own, other, other_loss, sums, *matrix_input],
                [((2, 2 * rows, columns), f32), half_plane, half_plane, ((2, rows, LANES), f32),
                 tiles(6 * half + 1), ((2, width), f32), ((count, blocks, LANES), f32)],
                [pltpu.VMEM((1, width), f32), plane_scratch, plane_scratch, field_scratch, *work],
                work_flops,
            )
        if s > 1:
            inner, outer = edges(inner, outer)
            own, other = own_next, coming

    came = lax.ppermute(sent, "gx", swap)
    shares = lax.all_to_all(shares, "gz", 0, 0, tiled=True)
    edge = lax.ppermute(edge, line, neighbours)
    sums, theirs = call(
        "gather", gather_kernel, rows, [shares, edge],
        [((half, LANES), f32), ((3 * half, LANES), f32)], [],
    )
    theirs = lax.ppermute(theirs, "gx", swap)

    *outs, total = call(
        "final", functools.partial(final_kernel, cells), cell_rows,
        [kept, kept_carrier, kept_grating, sides, came, edge, sums, theirs,
         segment_passive_attenuation, history_last],
        [((2, cell_rows, columns), f32), ((2, cell_rows, columns), f32),
         ((cell_rows, columns), f32), ((cell_rows, columns), f32), ((half, LANES), f32)],
        [pltpu.VMEM((2, cell_rows + 8, columns), f32), pltpu.VMEM((2, cell_rows + 8, columns), f32),
         pltpu.VMEM((cell_rows, columns + 2 * LANES), f32), pltpu.VMEM((cell_rows, columns), f32)],
        whole=True,
    )
    return (*outs, total.reshape(columns))


def shared_by_pairs(mesh, arguments):
    population = arguments[6]
    passes, cells, width = population.shape
    rows, columns = cells // mesh.shape["gz"], width // mesh.shape["gx"]
    return (
        mesh.shape["gx"] == 2
        and passes >= 3
        and rows % (2 * TILE) == 0
        and columns % LANES == 0
        and (columns // LANES) & (columns // LANES - 1) == 0
        and width <= 4096
    )


def solution(mesh):
    def run(*arguments):
        body = per_pair if shared_by_pairs(mesh, arguments) else per_device
        return jax.shard_map(
            body,
            mesh=mesh,
            in_specs=(
                P(None, "gz", "gx"),
                P(None, "gz", "gx"),
                P("gz", "gx"),
                P("gz", "gx"),
                P(None, None, "gz", "gx"),
                P(None, None, "gz", "gx"),
                P(None, "gz", "gx"),
                P(None, "gz", "gx"),
                P("gz", "gx"),
            ),
            out_specs=(
                P(None, "gz", "gx"), P(None, "gz", "gx"), P("gz", "gx"), P("gz", "gx"), P("gx"),
            ),
            check_vma=False,
        )(*arguments)

    return run
```

```python
import functools
import math

import jax
import jax.numpy as jnp
import ml_dtypes
import numpy as np
from jax import lax
from jax.experimental import pallas as pl
from jax.experimental.pallas import tpu as pltpu
from jax.sharding import PartitionSpec as P

DIFF = 512


FRONT_FACET = 0.3
REAR_FACET = 0.9
GAIN_SLOPE_RATE = 0.3
ALPHA_LINEWIDTH = 2.0
COUPLING = 0.5
CLOCK_DELTA = 0.3
DENSITY_LIFETIME = 2.0
GRATING_LIFE = 0.75
TRANSVERSE_DIFFUS = 0.2


def passed_along(value, axis, steps):
    count = lax.axis_size(axis)
    initial, last = (max(0, -steps), min(count, count - steps))
    return lax.ppermute(value, axis, [(source, source + steps) for source in range(initial, last)])


def with_halo(block, sides, width):
    for axis, dim in sides:
        count = lax.axis_size(axis)
        forward = [(i, i + 1) for i in range(count - 1)]
        backward = [(target, source) for source, target in forward]
        low = lax.ppermute(
            lax.slice_in_dim(block, block.shape[dim] - width, None, axis=dim), axis, forward
        )
        high = lax.ppermute(lax.slice_in_dim(block, 0, width, axis=dim), axis, backward)
        block = jnp.concatenate([low, block, high], axis=dim)
    return block


def rotate(source_re, source_im, cosine, sine, form, sign):
    exact = lax.Precision.HIGHEST
    out_re = jnp.einsum(form, source_re, cosine, precision=exact) + sign * jnp.einsum(
        form, source_im, sine, precision=exact
    )
    out_im = jnp.einsum(form, source_im, cosine, precision=exact) - sign * jnp.einsum(
        form, source_re, sine, precision=exact
    )
    return (out_re, out_im)


def transform(stacked):
    count = stacked.shape[1]
    width = stacked.shape[2]
    second = min(128, width // 2)
    first = width // second
    two_pi = 2.0 * math.pi
    index_a = jnp.arange(first, dtype=jnp.int32)
    index_b = jnp.arange(second, dtype=jnp.int32)
    angle_a = two_pi * (index_a[:, None] * index_a[None, :] % first).astype(jnp.float32) / first
    angle_b = two_pi * (index_b[:, None] * index_b[None, :] % second).astype(jnp.float32) / second
    angle_t = two_pi * (index_a[:, None] * index_b[None, :] % width).astype(jnp.float32) / width
    cos_a, sin_a = (jnp.cos(angle_a), jnp.sin(angle_a))
    cos_b, sin_b = (jnp.cos(angle_b), jnp.sin(angle_b))
    cos_t, sin_t = (jnp.cos(angle_t), jnp.sin(angle_t))
    wavenum = index_a[:, None] + first * index_b[None, :]
    signed = jnp.where(wavenum < width // 2, wavenum, wavenum - width)
    phase = (signed * signed).astype(jnp.float32) * (DIFF / (width / 2) ** 2)
    cos_p, sin_p = (jnp.cos(phase), jnp.sin(phase))
    real_in = stacked[0].reshape(count, first, second)
    imag_in = stacked[1].reshape(count, first, second)
    step_re, step_im = rotate(real_in, imag_in, cos_a, sin_a, "nab,ak->nkb", 1.0)
    twist_re = step_re * cos_t + step_im * sin_t
    twist_im = step_im * cos_t - step_re * sin_t
    spec_re, spec_im = rotate(twist_re, twist_im, cos_b, sin_b, "nkb,bj->nkj", 1.0)
    moved_re = spec_re * cos_p - spec_im * sin_p
    moved_im = spec_re * sin_p + spec_im * cos_p
    back_re, back_im = rotate(moved_re, moved_im, cos_b, sin_b, "nkj,jb->nkb", -1.0)
    untw_re = back_re * cos_t - back_im * sin_t
    untw_im = back_im * cos_t + back_re * sin_t
    final_re, final_im = rotate(untw_re, untw_im, cos_a, sin_a, "nkb,ka->nab", -1.0)
    return jnp.stack([final_re.reshape(count, width), final_im.reshape(count, width)]) / width


def added_up(value, axis):
    count = lax.axis_size(axis)
    if count & (count - 1):
        return lax.psum(value, axis)
    reach = 1
    while reach < count:
        value = value + lax.ppermute(value, axis, [(i, i ^ reach) for i in range(count)])
        reach *= 2
    return value


def lateral_work(parts):
    return (transform(parts[0]), transform(parts[1]))


def multiplier_revision(
    population_multiplier,
    holeburn_multiplier,
    measured_rightward,
    measured_leftward,
    rightward_wave,
    leftward_wave,
    population_level,
    holeburn_magnitude,
    attenuation_factor,
    transverse_curvature,
):
    rightward_inphase, rightward_quadrature = (rightward_wave[0], rightward_wave[1])
    leftward_inphase, leftward_quadrature = (leftward_wave[0], leftward_wave[1])
    measured_rightward_inphase, measured_rightward_quadrature = (
        measured_rightward[0],
        measured_rightward[1],
    )
    measured_leftward_inphase, measured_leftward_quadrature = (
        measured_leftward[0],
        measured_leftward[1],
    )
    surplus_population = population_level - 1.0
    amplification_inphase = 1.0 + 0.5 * (GAIN_SLOPE_RATE * surplus_population - attenuation_factor)
    amplification_quadrature = 0.5 * GAIN_SLOPE_RATE * ALPHA_LINEWIDTH * surplus_population
    joined_waves = COUPLING * holeburn_magnitude
    population_derivative = (
        2.0 * CLOCK_DELTA * GAIN_SLOPE_RATE * surplus_population * population_multiplier
    )
    holeburn_derivative = 2.0 * CLOCK_DELTA * holeburn_multiplier
    revised_rightward_inphase = (
        amplification_inphase * measured_rightward_inphase
        - amplification_quadrature * measured_rightward_quadrature
        + joined_waves * measured_leftward_quadrature
        - population_derivative * rightward_inphase
        + holeburn_derivative * leftward_inphase
    )
    revised_rightward_quadrature = (
        amplification_inphase * measured_rightward_quadrature
        + amplification_quadrature * measured_rightward_inphase
        - joined_waves * measured_leftward_inphase
        - population_derivative * rightward_quadrature
        + holeburn_derivative * leftward_quadrature
    )
    revised_leftward_inphase = (
        amplification_inphase * measured_leftward_inphase
        - amplification_quadrature * measured_leftward_quadrature
        + joined_waves * measured_rightward_quadrature
        - population_derivative * leftward_inphase
        + holeburn_derivative * rightward_inphase
    )
    revised_leftward_quadrature = (
        amplification_inphase * measured_leftward_quadrature
        + amplification_quadrature * measured_leftward_inphase
        - joined_waves * measured_rightward_inphase
        - population_derivative * leftward_quadrature
        + holeburn_derivative * rightward_quadrature
    )
    light_intensity = (
        rightward_inphase * rightward_inphase
        + rightward_quadrature * rightward_quadrature
        + leftward_inphase * leftward_inphase
        + leftward_quadrature * leftward_quadrature
    )
    amplification_share = (
        measured_rightward_inphase * (rightward_inphase + ALPHA_LINEWIDTH * rightward_quadrature)
        + measured_rightward_quadrature
        * (rightward_quadrature - ALPHA_LINEWIDTH * rightward_inphase)
        + measured_leftward_inphase * (leftward_inphase + ALPHA_LINEWIDTH * leftward_quadrature)
        + measured_leftward_quadrature * (leftward_quadrature - ALPHA_LINEWIDTH * leftward_inphase)
    )
    revised_population = (
        population_multiplier
        * (1.0 - CLOCK_DELTA / DENSITY_LIFETIME - CLOCK_DELTA * GAIN_SLOPE_RATE * light_intensity)
        + TRANSVERSE_DIFFUS * transverse_curvature
        + 0.5 * GAIN_SLOPE_RATE * amplification_share
    )
    fresh_holeburn = holeburn_multiplier * (1.0 - CLOCK_DELTA / GRATING_LIFE) + COUPLING * (
        measured_rightward_quadrature * leftward_inphase
        - measured_rightward_inphase * leftward_quadrature
        + measured_leftward_quadrature * rightward_inphase
        - measured_leftward_inphase * rightward_quadrature
    )
    return (
        jnp.stack([revised_rightward_inphase, revised_rightward_quadrature]),
        jnp.stack([revised_leftward_inphase, revised_leftward_quadrature]),
        revised_population,
        fresh_holeburn,
    )


def per_device(
    ending_rightward_adjoint,
    ending_leftward_adjoint,
    ending_population_adjoint,
    ending_holeburn_adjoint,
    history_rightward,
    history_leftward,
    history_population,
    history_holeburn,
    segment_passive_attenuation,
):
    columns = ending_rightward_adjoint.shape[2]
    rows = ending_rightward_adjoint.shape[1]
    blocks = lax.axis_size("gz")
    position = lax.axis_index("gz")
    cells = rows * blocks
    zpos = (position * rows + jnp.arange(rows, dtype=jnp.int32)).astype(jnp.float32)
    scaling_factor = 1.0 + 2.0 * zpos / (cells - 1)
    rightward_multiplier, leftward_multiplier = (ending_rightward_adjoint, ending_leftward_adjoint)
    population_multiplier, holeburn_multiplier = (
        ending_population_adjoint,
        ending_holeburn_adjoint,
    )
    attenuation_factor = segment_passive_attenuation.astype(jnp.float32)
    shape_curve = jnp.zeros((columns,), jnp.float32)
    for moment_position in range(history_rightward.shape[0] - 1, -1, -1):
        shape_curve = shape_curve + jnp.sum(scaling_factor[:, None] * population_multiplier, axis=0)
        above = passed_along(rightward_multiplier[:, :1, :], "gz", -1)
        below = passed_along(leftward_multiplier[:, -1:, :], "gz", 1)
        top_row = jnp.where(
            position == blocks - 1, FRONT_FACET * leftward_multiplier[:, -1:, :], above
        )
        bottom_row = jnp.where(position == 0, REAR_FACET * rightward_multiplier[:, :1, :], below)
        lam_fwd = jnp.concatenate([rightward_multiplier[:, 1:, :], top_row], axis=1)
        lam_bwd = jnp.concatenate([bottom_row, leftward_multiplier[:, :-1, :]], axis=1)
        whole_fwd, whole_bwd = (
            lax.all_gather(lam_fwd, "gx", axis=2, tiled=True),
            lax.all_gather(lam_bwd, "gx", axis=2, tiled=True),
        )
        start = lax.axis_index("gx") * columns
        done_fwd, done_bwd = lateral_work((whole_fwd, whole_bwd))
        measured_rightward = lax.dynamic_slice_in_dim(done_fwd, start, columns, 2)
        measured_leftward = lax.dynamic_slice_in_dim(done_bwd, start, columns, 2)
        bordered_array = with_halo(population_multiplier, (("gx", 1),), 1)
        transverse_curvature = (
            bordered_array[:, 2:] + bordered_array[:, :-2] - 2.0 * population_multiplier
        )
        rightward_multiplier, leftward_multiplier, population_multiplier, holeburn_multiplier = (
            multiplier_revision(
                population_multiplier,
                holeburn_multiplier,
                measured_rightward,
                measured_leftward,
                history_rightward[moment_position].astype(jnp.float32),
                history_leftward[moment_position].astype(jnp.float32),
                history_population[moment_position].astype(jnp.float32),
                history_holeburn[moment_position].astype(jnp.float32),
                attenuation_factor,
                transverse_curvature,
            )
        )
    total = added_up(shape_curve, "gz")
    derivative_vector = CLOCK_DELTA * total / math.sqrt(cells)
    return (
        rightward_multiplier,
        leftward_multiplier,
        population_multiplier,
        holeburn_multiplier,
        derivative_vector,
    )

LANES = 128
TILE = 16
POWER = 12
STRETCH = 1211.0
SCALE_LANE = 8


def lateral_matrices(width, blocks):
    lanes = width // blocks
    k = np.arange(width)
    signed = np.where(k < width // 2, k, k - width).astype(np.float64)
    response = np.fft.ifft(np.exp(1j * signed * signed * (DIFF / (width / 2) ** 2)))
    step = np.arange(lanes)
    shift = lanes * np.arange(blocks)[:, None, None] + step[None, None, :] - step[None, :, None]
    kernels = np.fft.fft(response[shift % width], axis=0) / blocks
    top = np.concatenate([kernels.real, kernels.imag], axis=2)
    low = np.concatenate([-kernels.imag, kernels.real], axis=2)
    whole = np.concatenate([top, low], axis=1)
    first = whole.astype(ml_dtypes.bfloat16)
    rest = (whole - first.astype(np.float64)).astype(ml_dtypes.bfloat16)
    return np.stack([first, rest], axis=1)


def block_dft(values, sign):
    count = len(values)
    if count == 1:
        return values
    even = block_dft(values[0::2], sign)
    odd = block_dft(values[1::2], sign)
    out = [None] * count
    for k in range(count // 2):
        (er, ei), (wr, wi) = even[k], odd[k]
        if 4 * k == count:
            plus, minus = (er - wi, ei + wr), (er + wi, ei - wr)
            out[k], out[k + count // 2] = (plus, minus) if sign > 0 else (minus, plus)
            continue
        if k:
            c, s = math.cos(2 * math.pi * k / count), sign * math.sin(2 * math.pi * k / count)
            if 8 * k == count:
                wr, wi = (c * (wr - wi), c * (wr + wi)) if sign > 0 else (c * (wr + wi), c * (wi - wr))
            elif 8 * k == 3 * count:
                wr, wi = (c * (wr + wi), c * (wi - wr)) if sign > 0 else (c * (wr - wi), c * (wr + wi))
            else:
                wr, wi = c * wr - s * wi, c * wi + s * wr
        out[k] = (er + wr, ei + wi)
        out[k + count // 2] = (er - wr, ei - wi)
    return out


def lane(j):
    return pl.ds(pl.multiple_of(j * LANES, LANES), LANES)


def slab(j, rows):
    return pl.ds(pl.multiple_of(j * rows, rows), rows)


def fetch(pairs, sems, first=0):
    copies = [pltpu.make_async_copy(a, b, sems.at[first + i]) for i, (a, b) in enumerate(pairs)]
    for copy in copies:
        copy.start()
    return copies


def rows_of(info, rows, other):
    part = 1 - info[4] if other else info[4]
    return pl.ds(pl.multiple_of(part * rows, rows), rows)


def spread(field, work):
    rows = field.shape[1]
    blocks = work.shape[0]

    @pl.loop(0, rows // 8)
    def _(g):
        at = slab(g, 8)
        values = [
            (field[0, at, j * LANES : (j + 1) * LANES], field[1, at, j * LANES : (j + 1) * LANES])
            for j in range(blocks)
        ]
        for q, (re, im) in enumerate(block_dft(values, -1)):
            work[q, at, :LANES] = re
            work[q, at, LANES:] = im


def multiply(work, matrices):
    rows = work.shape[1]

    @pl.loop(0, work.shape[0], unroll=True)
    def _(q):
        value = work[q]
        first = value.astype(jnp.bfloat16)
        rest = (value - first.astype(jnp.float32)).astype(jnp.bfloat16)
        both = jnp.dot(
            jnp.concatenate([first, rest]), matrices[q, 0], preferred_element_type=jnp.float32
        )
        fine = jnp.dot(first, matrices[q, 1], preferred_element_type=jnp.float32)
        work[q] = both[:rows] + (both[rows:] + fine)


def gathered(work, at):
    values = [(work[q, at, :LANES], work[q, at, LANES:]) for q in range(work.shape[0])]
    return block_dft(values, 1)


def filtered(field, work, matrices, copy):
    spread(field, work)
    copy.wait()
    multiply(work, matrices)


def write_filtered(info, work, forward, backward, inner, outer):
    rows = work.shape[1] // 2
    for target, base, offset in ((forward, 0, 0), (backward, rows, 8)):

        @pl.loop(0, rows // 8)
        def _(g):
            here = pl.ds(pl.multiple_of(g * 8 + offset, 8), 8)
            for j, pair in enumerate(gathered(work, pl.ds(pl.multiple_of(g * 8 + base, 8), 8))):
                for part in range(2):
                    target[part, here, j * LANES : (j + 1) * LANES] = pair[part]

    low = info[4] == 0
    for part in range(2):
        first, last = forward[part, 0:1, :], backward[part, rows + 7 : rows + 8, :]
        inner[part : part + 1, :] = jnp.where(low, last, first)
        outer[part : part + 1, :] = jnp.where(low, first, last)


def size_of(largest):
    top = jnp.max(jnp.max(largest, axis=1, keepdims=True), axis=0, keepdims=True)
    return jnp.maximum(top, 1e-30).astype(jnp.bfloat16).astype(jnp.float32)


def encoded(value, size):
    unit = value * (STRETCH / size)
    square = unit * unit
    fourth = square * square
    return (fourth * fourth * square * (unit * jnp.abs(unit))).astype(jnp.bfloat16)


def decoded(code, size):
    value = code.astype(jnp.float32)
    root = jnp.exp2(jnp.log(jnp.abs(value)) * (1.0 / (POWER * math.log(2.0)))) * (size / STRETCH)
    return jnp.where(value < 0.0, -root, root)


def side_tile(columns, rows):
    index = lax.broadcasted_iota(jnp.int32, (rows, LANES), 1)
    tile = jnp.zeros((rows, LANES), jnp.float32)
    for at, column in columns:
        tile = jnp.where(index == at, column, tile)
    return tile.astype(jnp.bfloat16)


def sizes_in(tile, count):
    value = tile.astype(jnp.float32)
    return [value[0:1, SCALE_LANE + i : SCALE_LANE + i + 1] for i in range(count)]


def updated(fr, fi, br, bi, wave, population, hole, loss, carrier, grating, lap):
    rr, ri, lr, li = wave
    surplus = population - 1.0
    gain_re = 1.0 + 0.5 * (GAIN_SLOPE_RATE * surplus - loss)
    gain_im = (0.5 * GAIN_SLOPE_RATE * ALPHA_LINEWIDTH) * surplus
    joined = COUPLING * hole
    drive = (2.0 * CLOCK_DELTA * GAIN_SLOPE_RATE) * surplus * carrier
    mix = (2.0 * CLOCK_DELTA) * grating
    new_fr = gain_re * fr - gain_im * fi + joined * bi - drive * rr + mix * lr
    new_fi = gain_re * fi + gain_im * fr - joined * br - drive * ri + mix * li
    new_br = gain_re * br - gain_im * bi + joined * fi - drive * lr + mix * rr
    new_bi = gain_re * bi + gain_im * br - joined * fr - drive * li + mix * ri
    light = rr * rr + ri * ri + lr * lr + li * li
    share = (
        fr * (rr + ALPHA_LINEWIDTH * ri)
        + fi * (ri - ALPHA_LINEWIDTH * rr)
        + br * (lr + ALPHA_LINEWIDTH * li)
        + bi * (li - ALPHA_LINEWIDTH * lr)
    )
    new_carrier = (
        carrier * ((1.0 - CLOCK_DELTA / DENSITY_LIFETIME) - (CLOCK_DELTA * GAIN_SLOPE_RATE) * light)
        + TRANSVERSE_DIFFUS * lap
        + (0.5 * GAIN_SLOPE_RATE) * share
    )
    new_grating = grating * (1.0 - CLOCK_DELTA / GRATING_LIFE) + COUPLING * (
        fi * lr - fr * li + bi * rr - br * ri
    )
    return new_fr, new_fi, new_br, new_bi, new_carrier, new_grating


def curvature(left, mid, right, weight_left, weight_right):
    index = lax.broadcasted_iota(jnp.int32, mid.shape, 1)
    below = jnp.where(index == 0, pltpu.roll(left, 1, 1) * weight_left, pltpu.roll(mid, 1, 1))
    above = jnp.where(
        index == LANES - 1,
        pltpu.roll(right, LANES - 1, 1) * weight_right,
        pltpu.roll(mid, LANES - 1, 1),
    )
    return below + above - 2.0 * mid


def send_fields_kernel(info, forward, backward, out, fields, sems):
    rows, columns = fields.shape[2:]
    half = columns // LANES
    at = rows_of(info, rows, True)
    copies = fetch(
        [(ref.at[:, at, :], fields.at[f]) for f, ref in enumerate((forward, backward))], sems
    )
    sizes = []
    for f in range(2):
        copies[f].wait()
        largest = jnp.maximum(jnp.abs(fields[f, 0]), jnp.abs(fields[f, 1]))
        size = size_of(largest)
        sizes.append((SCALE_LANE + f, size))
        for part in range(2):
            put_tiles(out, (2 * f + part) * half, encoded(fields[f, part], size))
    out[4 * half * rows :, :] = side_tile(sizes, rows)


def put_tiles(out, first, value):
    rows, columns = value.shape
    for j in range(columns // LANES):
        at = (first + j) * rows
        out[at : at + rows, :] = value[:, j * LANES : (j + 1) * LANES]


def history_rows(forward, backward, population, hole, s, at):
    return [
        forward.at[s, 0, at, :], forward.at[s, 1, at, :], backward.at[s, 0, at, :],
        backward.at[s, 1, at, :], population.at[s, at, :], hole.at[s, at, :],
    ]


def into_rows(parts, target, first, rows):
    return [(part, target.at[pl.ds(first + i * rows, rows), :]) for i, part in enumerate(parts)]


def send_later_kernel(steps, info, forward, backward, population, hole, final, *refs):
    targets, sems = refs[:-1], refs[-1]
    rows = targets[0].shape[0] // 6
    history = (forward, backward, population, hole)
    pairs = []
    for i, s in enumerate(steps):
        for k, other in enumerate((True, False)):
            at = rows_of(info, rows, other)
            pairs += into_rows(history_rows(*history, s, at), targets[2 * i + k], 0, rows)
    pairs += into_rows(history_rows(*history, 0, pl.ds(0, 2 * rows)), final, 0, 2 * rows)
    for copy in fetch(pairs, sems):
        copy.wait()


def send_first_kernel(
    s, info, loss, carrier, grating, forward, backward, population, hole,
    own_loss, own, own_carrier, own_grating, out, states, sems,
):
    rows, columns = own_carrier.shape
    theirs, mine = rows_of(info, rows, True), rows_of(info, rows, False)
    history = (forward, backward, population, hole)
    copies = fetch(
        [(carrier.at[theirs, :], states.at[0]), (grating.at[theirs, :], states.at[1])]
        + into_rows([loss.at[theirs, :]], out, 0, rows)
        + into_rows(history_rows(*history, s, theirs), out, 3 * rows, rows)
        + [(loss.at[mine, :], own_loss), (carrier.at[mine, :], own_carrier)]
        + [(grating.at[mine, :], own_grating)]
        + into_rows(history_rows(*history, s, mine), own, 0, rows),
        sems,
    )
    for copy in copies[:2]:
        copy.wait()
    sizes = []
    for i in range(2):
        size = size_of(jnp.abs(states[i]))
        sizes.append(jnp.broadcast_to(size, (8, columns)))
        out[(1 + i) * rows : (2 + i) * rows, :] = encoded(states[i], size)
    out[9 * rows :, :] = jnp.concatenate(sizes).astype(jnp.bfloat16)
    for copy in copies[2:]:
        copy.wait()


def enter_kernel(
    info, forward, backward, other, source, tp, tq, inner, outer, field, work, matrices, sem, sems
):
    copy = pltpu.make_async_copy(source, matrices, sem)
    rows, width = field.shape[1] // 2, field.shape[2]
    columns = width // 2
    half = columns // LANES
    at = rows_of(info, rows, False)
    copies = fetch(
        [
            (ref.at[:, at, :], field.at[:, f * rows : (f + 1) * rows, :columns])
            for f, ref in enumerate((forward, backward))
        ],
        sems,
    )
    copy.start()
    sizes = sizes_in(other[4 * half * rows :, :], 2)
    for f in range(2):
        for part in range(2):

            @pl.loop(0, half, unroll=2)
            def _(j):
                code = other[slab((2 * f + part) * half + j, rows), :]
                field[part, f * rows : (f + 1) * rows, lane(half + j)] = decoded(code, sizes[f])

    for held in copies:
        held.wait()
    filtered(field, work, matrices, copy)
    write_filtered(info, work, tp, tq, inner, outer)


def rows_update(
    info, tp, tq, inner, outer, carrier, grating, own, other, own_loss, other_loss,
    field, new_carrier, new_grating, sums_in, sums, cells, last
):
    rows, width = carrier.shape
    half = width // LANES // 2
    columns = half * LANES
    mid = jnp.where(info[0] == 0, 1.0, 0.0)
    wrap = 1.0 - mid
    low = info[4] == 0
    is_first, is_last = info[1], info[2]
    row_index = lax.broadcasted_iota(jnp.int32, (TILE, LANES), 0)
    zero = jnp.zeros((8, LANES), jnp.float32)

    def step(jj, most):
        for side in range(2):
            j = jj + side * half
            here = lane(j)
            left_at = lane(jnp.where(j == 0, 2 * half - 1, j - 1))
            right_at = lane(jnp.where(j == 2 * half - 1, 0, j + 1))
            swapped = lane(jj + (1 - side) * half)
            weight_left = jnp.where(jj == 0, wrap if side == 0 else mid, 1.0)
            weight_right = jnp.where(jj == half - 1, mid if side == 0 else wrap, 1.0)
            total = zero
            for r in range(0, rows, TILE):
                at = slice(r, r + TILE)

                held, begin = (own, other)[side]

                def part_of(i):
                    tile = begin + i * rows + r
                    return held[tile : tile + TILE, lane(jj)].astype(jnp.float32)

                loss = (own_loss, other_loss)[side][at, lane(jj)].astype(jnp.float32)
                f = [tp[part, r + 1 : r + 1 + TILE, here] for part in range(2)]
                b = [tq[part, r + 7 : r + 7 + TILE, here] for part in range(2)]
                if r + TILE == rows:
                    for part in range(2):
                        facet = FRONT_FACET * tq[part, rows + 7 : rows + 8, here]
                        edge = jnp.where(
                            low, inner[part : part + 1, swapped], outer[part : part + 1, here]
                        )
                        edge = jnp.where(is_last, facet, edge)
                        f[part] = jnp.where(row_index == TILE - 1, edge, f[part])
                if r == 0:
                    for part in range(2):
                        facet = REAR_FACET * tp[part, 0:1, here]
                        edge = jnp.where(
                            low, outer[part : part + 1, here], inner[part : part + 1, swapped]
                        )
                        edge = jnp.where(is_first, facet, edge)
                        b[part] = jnp.where(row_index == 0, edge, b[part])
                c = carrier[at, here]
                lap = curvature(
                    carrier[at, left_at], c, carrier[at, right_at], weight_left, weight_right
                )
                out = updated(
                    *f, *b, [part_of(i) for i in range(4)], part_of(4), part_of(5), loss,
                    c, grating[at, here], lap,
                )
                field[0, r : r + TILE, here] = out[0]
                field[1, r : r + TILE, here] = out[1]
                field[0, rows + r : rows + r + TILE, here] = out[2]
                field[1, rows + r : rows + r + TILE, here] = out[3]
                new_carrier[at, here] = out[4]
                new_grating[at, here] = out[5]
                z = (info[3] + r + row_index).astype(jnp.float32)
                weighted = (1.0 + 2.0 * z / (cells - 1)) * ((c + out[4]) if last else c)
                for k in range(0, TILE, 8):
                    total = total + weighted[k : k + 8]
                if last and side == 1:
                    for k in range(0, TILE, 8):
                        most = (
                            jnp.maximum(most[0], jnp.abs(out[4][k : k + 8])),
                            jnp.maximum(most[1], jnp.abs(out[5][k : k + 8])),
                        )
            summed = jnp.sum(total, axis=0, keepdims=True)
            sums[:, here] = summed if sums_in is None else summed + sums_in[:, here]
        return most

    return lax.fori_loop(0, half, step, (zero, zero))


def first_step_kernel(
    cells, info, tp, tq, inner, outer, my_carrier, my_grating, loss, own, other, source,
    new_tp, new_tq, new_inner, new_outer, new_carrier, new_grating, sums,
    carrier, grating, field, work, matrices, sem,
):
    copy = pltpu.make_async_copy(source, matrices, sem)
    copy.start()
    rows, columns = my_carrier.shape
    half = columns // LANES
    sizes = other[9 * rows :, :LANES].astype(jnp.float32)
    sizes = [sizes[0:1, 0:1], sizes[8:9, 0:1]]
    for i, (whole, mine) in enumerate(((carrier, my_carrier), (grating, my_grating))):
        whole[:, :columns] = mine[...]

        @pl.loop(0, half, unroll=2)
        def _(j):
            whole[:, lane(half + j)] = decoded(
                other[(1 + i) * rows : (2 + i) * rows, lane(j)], sizes[i]
            )

    rows_update(
        info, tp, tq, inner, outer, carrier, grating, (own, 0), (other, 3 * rows), loss, other,
        field, new_carrier, new_grating, None, sums, cells, False,
    )
    filtered(field, work, matrices, copy)
    write_filtered(info, work, new_tp, new_tq, new_inner, new_outer)


def middle_step_kernel(
    cells, info, tp, tq, inner, outer, carrier, grating, loss, own, other, other_loss, sums_in,
    source, new_tp, new_tq, new_inner, new_outer, new_carrier, new_grating, sums,
    field, work, matrices, sem,
):
    copy = pltpu.make_async_copy(source, matrices, sem)
    copy.start()
    rows_update(
        info, tp, tq, inner, outer, carrier, grating, (own, 0), (other, 0), loss, other_loss,
        field, new_carrier, new_grating, sums_in, sums, cells, False,
    )
    filtered(field, work, matrices, copy)
    write_filtered(info, work, new_tp, new_tq, new_inner, new_outer)


def leave_kernel(
    cells, info, tp, tq, inner, outer, carrier, grating, loss, own, other, other_loss, sums_in,
    source, kept, kept_carrier, kept_grating, sides, sent, edge, shares,
    sums, new_carrier, new_grating, field, work, matrices, sem,
):
    copy = pltpu.make_async_copy(source, matrices, sem)
    copy.start()
    rows, width = carrier.shape
    columns = width // 2
    half = columns // LANES
    most = rows_update(
        info, tp, tq, inner, outer, carrier, grating, (own, 0), (other, 0), loss, other_loss,
        field, new_carrier, new_grating, sums_in, sums, cells, True,
    )
    mid = jnp.where(info[0] == 0, 1.0, 0.0)
    wrap = 1.0 - mid
    kept_carrier[...] = new_carrier[:, :columns]
    kept_grating[...] = new_grating[:, :columns]
    first, before = new_carrier[:, 0:1] * wrap, new_carrier[:, columns - 1 : columns] * mid
    after, final = new_carrier[:, columns : columns + 1] * mid, new_carrier[:, width - 1 :] * wrap
    sides[0] = jnp.broadcast_to(final, (rows, LANES))
    sides[1] = jnp.broadcast_to(after, (rows, LANES))
    pairs = []
    for at, value in ((0, before), (2, first)):
        coarse = value.astype(jnp.bfloat16).astype(jnp.float32)
        pairs += [(at, coarse), (at + 1, value - coarse)]
    for i, field_of in enumerate((new_carrier, new_grating)):
        size = size_of(most[i])
        pairs.append((SCALE_LANE + 2 + i, size))

        @pl.loop(0, half, unroll=2)
        def _(j):
            sent[slab((4 + i) * half + j, rows), :] = encoded(field_of[:, lane(half + j)], size)

    filtered(field, work, matrices, copy)
    zero = jnp.zeros((8, LANES), jnp.float32)
    for f in range(2):

        def unmix(g, most):
            at = pl.ds(pl.multiple_of(g * 8 + f * rows, 8), 8)
            for j, pair in enumerate(gathered(work, at)):
                for part in range(2):
                    if j < half:
                        kept[part, at, j * LANES : (j + 1) * LANES] = pair[part]
                    else:
                        work[j, at, part * LANES : (part + 1) * LANES] = pair[part]
                        most = jnp.maximum(most, jnp.abs(pair[part]))
            return most

        size = size_of(lax.fori_loop(0, rows // 8, unmix, zero))
        pairs.append((SCALE_LANE + f, size))

        @pl.loop(0, half, unroll=2)
        def _(j):
            for part in range(2):
                value = work[half + j, f * rows : (f + 1) * rows, part * LANES : (part + 1) * LANES]
                sent[slab((2 * f + part) * half + j, rows), :] = encoded(value, size)

    sent[6 * half * rows :, :] = side_tile(pairs, rows)
    low = info[4] == 0
    for part in range(2):
        lanes = slice(part * LANES, (part + 1) * LANES)
        edge[part : part + 1, :] = jnp.where(
            low, kept[part, 0:1, :], kept[part, 2 * rows - 1 : 2 * rows, :]
        )
        for j in range(half):
            edge[2 + part : 3 + part, j * LANES : (j + 1) * LANES] = jnp.where(
                low, work[half + j, 0:1, lanes], work[half + j, 2 * rows - 1 : 2 * rows, lanes]
            )
    tile = jnp.concatenate([sums[:, j * LANES : (j + 1) * LANES] for j in range(2 * half)])
    near, far = tile[:half], tile[half:]
    first = info[0] == 0
    to_first, to_second = jnp.where(first, near, far), jnp.where(first, far, near)
    for i in range(0, shares.shape[0], 2):
        shares[i] = to_first
        shares[i + 1] = to_second


def final_kernel(
    cells, info, kept, kept_carrier, kept_grating, sides, came, edge, other_edge, partial, loss, history,
    out_forward, out_backward, out_carrier, out_grating, out_sums,
    tp, tq, carrier, grating,
):
    rows, columns = kept_carrier.shape
    half = columns // LANES
    total = partial[0]
    for i in range(1, partial.shape[0]):
        total = total + partial[i]
    out_sums[...] = total * (CLOCK_DELTA / math.sqrt(cells))
    mine = info[4] * rows
    theirs = (1 - info[4]) * rows
    low = info[4] == 0
    extra = came[6 * half * rows :, :]
    size_forward, size_backward, size_carrier, size_grating = sizes_in(extra, 4)
    extra = extra.astype(jnp.float32)

    def at(start, offset, count):
        return pl.ds(pl.multiple_of(start + offset, 8), count)

    for part in range(2):
        tp[part, at(mine, 0, rows), :] = kept[part, :rows, :]
        tq[part, at(mine, 8, rows), :] = kept[part, rows:, :]
    carrier[at(mine, 0, rows), LANES : LANES + columns] = kept_carrier[...]
    carrier[at(mine, 0, rows), :LANES] = sides[0]
    carrier[at(mine, 0, rows), LANES + columns :] = sides[1]
    carrier[at(theirs, 0, rows), :LANES] = jnp.broadcast_to(
        extra[:, 0:1] + extra[:, 1:2], (rows, LANES)
    )
    carrier[at(theirs, 0, rows), LANES + columns :] = jnp.broadcast_to(
        extra[:, 2:3] + extra[:, 3:4], (rows, LANES)
    )
    grating[at(mine, 0, rows), :] = kept_grating[...]

    @pl.loop(0, half, unroll=2)
    def _(j):
        carrier[at(theirs, 0, rows), lane(1 + j)] = decoded(
            came[slab(4 * half + j, rows), :], size_carrier
        )
        grating[at(theirs, 0, rows), lane(j)] = decoded(
            came[slab(5 * half + j, rows), :], size_grating
        )
        for part in range(2):
            tp[part, at(theirs, 0, rows), lane(j)] = decoded(
                came[slab(part * half + j, rows), :], size_forward
            )
            tq[part, at(theirs, 8, rows), lane(j)] = decoded(
                came[slab((2 + part) * half + j, rows), :], size_backward
            )

    all_rows = 2 * rows
    for part in range(2):
        near = edge[part : part + 1, :]
        far = other_edge[2 + part : 3 + part, :]
        next_edge = jnp.where(low, far, near)
        before_edge = jnp.where(low, near, far)
        front = FRONT_FACET * tq[part, all_rows + 7 : all_rows + 8, :]
        rear = REAR_FACET * tp[part, 0:1, :]
        tp[part, all_rows : all_rows + 1, :] = jnp.where(info[2], front, next_edge)
        tq[part, 7:8, :] = jnp.where(info[1], rear, before_edge)

    @pl.loop(0, half)
    def _(j):
        here = lane(j)
        for r in range(0, all_rows, TILE):
            row = slice(r, r + TILE)
            c = carrier[row, lane(j + 1)]
            lap = curvature(carrier[row, lane(j)], c, carrier[row, lane(j + 2)], 1.0, 1.0)
            parts = [
                history[i * all_rows + r : i * all_rows + r + TILE, here].astype(jnp.float32)
                for i in range(6)
            ]
            out = updated(
                tp[0, r + 1 : r + 1 + TILE, here], tp[1, r + 1 : r + 1 + TILE, here],
                tq[0, r + 7 : r + 7 + TILE, here], tq[1, r + 7 : r + 7 + TILE, here],
                parts[:4], parts[4], parts[5],
                loss[row, here].astype(jnp.float32), c, grating[row, here], lap,
            )
            out_forward[0, row, here] = out[0]
            out_forward[1, row, here] = out[1]
            out_backward[0, row, here] = out[2]
            out_backward[1, row, here] = out[3]
            out_carrier[row, here] = out[4]
            out_grating[row, here] = out[5]


def position(rows, whole):
    x, block, count = lax.axis_index("gx"), lax.axis_index("gz"), lax.axis_size("gz")
    high = lax.rem(x + block, 2)
    if whole:
        return x, block == 0, block == count - 1, block * rows, high
    place = 2 * block + high
    return x, place == 0, place == 2 * count - 1, place * rows, high


def whole_spec(shape):
    return pl.BlockSpec(shape, lambda i, n=len(shape): (0,) * n)


def call(name, kernel, rows, inputs, outputs, scratch, flops=0, grant=24, whole=False):
    arrays = [x[0] if isinstance(x, tuple) else x for x in inputs]
    specs = [x[1] if isinstance(x, tuple) else whole_spec(x.shape) for x in inputs]
    shapes = [jax.ShapeDtypeStruct(*out) for out in outputs]
    moved = sum(math.prod(s.shape) * s.dtype.itemsize for s in shapes)

    def body(*refs):
        kernel(position(rows, whole), *refs)

    return pl.pallas_call(
        body,
        grid=(1,),
        in_specs=specs,
        out_specs=[whole_spec(s.shape) for s in shapes],
        scratch_shapes=scratch,
        out_shape=shapes,
        compiler_params=pltpu.CompilerParams(vmem_limit_bytes=grant * 1024 * 1024),
        cost_estimate=pl.CostEstimate(
            flops=flops, bytes_accessed=moved + 4 * 1024 * 1024, transcendentals=0
        ),
        name=name,
    )(*arrays)


def per_pair(
    ending_rightward_adjoint,
    ending_leftward_adjoint,
    ending_population_adjoint,
    ending_holeburn_adjoint,
    history_rightward,
    history_leftward,
    history_population,
    history_holeburn,
    segment_passive_attenuation,
):
    cell_rows, columns = ending_population_adjoint.shape
    passes = history_population.shape[0]
    rows = cell_rows // 2
    half = columns // LANES
    blocks = 2 * half
    width = 2 * columns
    count = lax.axis_size("gz")
    cells = cell_rows * count
    x = lax.axis_index("gx")
    f32, bf16 = jnp.float32, jnp.bfloat16
    swap = [(0, 1), (1, 0)]
    in_place = pl.BlockSpec(memory_space=pltpu.HBM)

    def held(*arrays):
        return [(a, in_place) for a in arrays]

    def tiles(n):
        return ((n * rows, LANES), bf16)

    ends = held(ending_rightward_adjoint, ending_leftward_adjoint)
    planes = held(ending_population_adjoint, ending_holeburn_adjoint)
    history = held(history_rightward, history_leftward, history_population, history_holeburn)
    losses = held(segment_passive_attenuation)
    matrices = pltpu.with_memory_space_constraint(
        jnp.asarray(lateral_matrices(width, blocks)), pltpu.HBM
    )
    matrix_input = held(matrices)
    work = [
        pltpu.VMEM((blocks, 2 * rows, 2 * LANES), f32),
        pltpu.VMEM(matrices.shape, bf16),
        pltpu.SemaphoreType.DMA,
    ]
    field_scratch = pltpu.VMEM((2, 2 * rows, width), f32)
    state_out = [
        ((2, rows + 8, width), f32), ((2, rows + 8, width), f32), ((2, width), f32), ((2, width), f32),
    ]
    plane = ((rows, width), f32)
    plane_scratch = pltpu.VMEM((rows, width), f32)
    half_plane = ((rows, columns), f32)
    work_flops = 2 * 3 * 2 * rows * blocks * (2 * LANES) ** 2

    (coded,) = call(
        "send_fields", send_fields_kernel, rows, ends, [tiles(4 * half + 1)],
        [pltpu.VMEM((2, 2, rows, columns), f32), pltpu.SemaphoreType.DMA((2,))], grant=62,
    )
    other_fields = lax.ppermute(coded, "gx", swap)
    loss, own_first, my_carrier, my_grating, sent_first = call(
        "send_first", functools.partial(send_first_kernel, passes - 1), rows,
        [*losses, *planes, *history],
        [((rows, columns), bf16), ((6 * rows, columns), bf16), half_plane, half_plane,
         ((9 * rows + TILE, columns), bf16)],
        [pltpu.VMEM((2, rows, columns), f32), pltpu.SemaphoreType.DMA((18,))], grant=62,
    )
    steps = range(passes - 2, 0, -1)
    history_last, *later = call(
        "send_later", functools.partial(send_later_kernel, steps), rows, history,
        [((6 * cell_rows, columns), bf16)] + [((6 * rows, columns), bf16)] * (2 * len(steps)),
        [pltpu.SemaphoreType.DMA((12 * len(steps) + 6,))], grant=62,
    )
    sent_first, history_last, later, other_fields = lax.optimization_barrier(
        (sent_first, history_last, later, other_fields)
    )
    other_first = lax.ppermute(sent_first, "gx", swap)

    line = ("gz", "gx")
    neighbours = []
    for b in range(count - 1):
        top = (1 + b) % 2
        neighbours += [(2 * b + top, 2 * b + 2 + top), (2 * b + 2 + top, 2 * b + top)]

    def edges(inner, outer):
        outer = lax.ppermute(outer, line, neighbours)
        return lax.ppermute(inner, "gx", swap), outer

    tp, tq, inner, outer = call(
        "enter", enter_kernel, rows, [*ends, other_fields, *matrix_input],
        state_out, [field_scratch, *work, pltpu.SemaphoreType.DMA((2,))], work_flops,
    )
    inner, outer = edges(inner, outer)

    other_loss = (other_first, pl.BlockSpec((rows, columns), lambda i: (0, 0)))
    carrier = grating = sums = other = own = None
    for index, s in enumerate(range(passes - 1, 0, -1)):
        if index < len(steps):
            sent, own_next = later[2 * index : 2 * index + 2]
            sent, inner, outer = lax.optimization_barrier((sent, inner, outer))
            coming = lax.ppermute(sent, "gx", swap)
        shared = [tp, tq, inner, outer]
        if index == 0:
            tp, tq, inner, outer, carrier, grating, sums = call(
                "first_step", functools.partial(first_step_kernel, cells), rows,
                [*shared, my_carrier, my_grating, loss, own_first, other_first, *matrix_input],
                [*state_out, plane, plane, ((1, width), f32)],
                [plane_scratch, plane_scratch, field_scratch, *work], work_flops,
            )
        elif s > 1:
            tp, tq, inner, outer, carrier, grating, sums = call(
                "middle_step", functools.partial(middle_step_kernel, cells), rows,
                [*shared, carrier, grating, loss, own, other, other_loss, sums, *matrix_input],
                [*state_out, plane, plane, ((1, width), f32)],
                [field_scratch, *work], work_flops,
            )
        else:
            kept, kept_carrier, kept_grating, sides, sent, edge, shares = call(
                "leave", functools.partial(leave_kernel, cells), rows,
                [*shared, carrier, grating, loss, own, other, other_loss, sums, *matrix_input],
                [((2, 2 * rows, columns), f32), half_plane, half_plane, ((2, rows, LANES), f32),
                 tiles(6 * half + 1), ((4, columns), f32), ((2 * count, half, LANES), f32)],
                [pltpu.VMEM((1, width), f32), plane_scratch, plane_scratch, field_scratch, *work],
                work_flops,
            )
        if s > 1:
            inner, outer = edges(inner, outer)
            own, other = own_next, coming

    came = lax.ppermute(sent, "gx", swap)
    edge = lax.ppermute(edge, line, neighbours)
    shares = lax.all_to_all(shares, line, 0, 0, tiled=True)
    other_edge = lax.ppermute(edge, "gx", swap)

    *outs, total = call(
        "final", functools.partial(final_kernel, cells), cell_rows,
        [kept, kept_carrier, kept_grating, sides, came, edge, other_edge, shares,
         segment_passive_attenuation, history_last],
        [((2, cell_rows, columns), f32), ((2, cell_rows, columns), f32),
         ((cell_rows, columns), f32), ((cell_rows, columns), f32), ((half, LANES), f32)],
        [pltpu.VMEM((2, cell_rows + 8, columns), f32), pltpu.VMEM((2, cell_rows + 8, columns), f32),
         pltpu.VMEM((cell_rows, columns + 2 * LANES), f32), pltpu.VMEM((cell_rows, columns), f32)],
        whole=True,
    )
    return (*outs, total.reshape(columns))


def shared_by_pairs(mesh, arguments):
    population = arguments[6]
    passes, cells, width = population.shape
    rows, columns = cells // mesh.shape["gz"], width // mesh.shape["gx"]
    return (
        mesh.shape["gx"] == 2
        and passes >= 3
        and rows % (2 * TILE) == 0
        and columns % LANES == 0
        and (columns // LANES) & (columns // LANES - 1) == 0
        and width <= 4096
    )


def solution(mesh):
    def run(*arguments):
        body = per_pair if shared_by_pairs(mesh, arguments) else per_device
        return jax.shard_map(
            body,
            mesh=mesh,
            in_specs=(
                P(None, "gz", "gx"),
                P(None, "gz", "gx"),
                P("gz", "gx"),
                P("gz", "gx"),
                P(None, None, "gz", "gx"),
                P(None, None, "gz", "gx"),
                P(None, "gz", "gx"),
                P(None, "gz", "gx"),
                P("gz", "gx"),
            ),
            out_specs=(
                P(None, "gz", "gx"), P(None, "gz", "gx"), P("gz", "gx"), P("gz", "gx"), P("gx"),
            ),
            check_vma=False,
        )(*arguments)

    return run
```

```python
import functools
import math

import jax
import jax.numpy as jnp
import ml_dtypes
import numpy as np
from jax import lax
from jax.experimental import pallas as pl
from jax.experimental.pallas import tpu as pltpu
from jax.sharding import PartitionSpec as P

DIFF = 512


FRONT_FACET = 0.3
REAR_FACET = 0.9
GAIN_SLOPE_RATE = 0.3
ALPHA_LINEWIDTH = 2.0
COUPLING = 0.5
CLOCK_DELTA = 0.3
DENSITY_LIFETIME = 2.0
GRATING_LIFE = 0.75
TRANSVERSE_DIFFUS = 0.2


def passed_along(value, axis, steps):
    count = lax.axis_size(axis)
    initial, last = (max(0, -steps), min(count, count - steps))
    return lax.ppermute(value, axis, [(source, source + steps) for source in range(initial, last)])


def with_halo(block, sides, width):
    for axis, dim in sides:
        count = lax.axis_size(axis)
        forward = [(i, i + 1) for i in range(count - 1)]
        backward = [(target, source) for source, target in forward]
        low = lax.ppermute(
            lax.slice_in_dim(block, block.shape[dim] - width, None, axis=dim), axis, forward
        )
        high = lax.ppermute(lax.slice_in_dim(block, 0, width, axis=dim), axis, backward)
        block = jnp.concatenate([low, block, high], axis=dim)
    return block


def rotate(source_re, source_im, cosine, sine, form, sign):
    exact = lax.Precision.HIGHEST
    out_re = jnp.einsum(form, source_re, cosine, precision=exact) + sign * jnp.einsum(
        form, source_im, sine, precision=exact
    )
    out_im = jnp.einsum(form, source_im, cosine, precision=exact) - sign * jnp.einsum(
        form, source_re, sine, precision=exact
    )
    return (out_re, out_im)


def transform(stacked):
    count = stacked.shape[1]
    width = stacked.shape[2]
    second = min(128, width // 2)
    first = width // second
    two_pi = 2.0 * math.pi
    index_a = jnp.arange(first, dtype=jnp.int32)
    index_b = jnp.arange(second, dtype=jnp.int32)
    angle_a = two_pi * (index_a[:, None] * index_a[None, :] % first).astype(jnp.float32) / first
    angle_b = two_pi * (index_b[:, None] * index_b[None, :] % second).astype(jnp.float32) / second
    angle_t = two_pi * (index_a[:, None] * index_b[None, :] % width).astype(jnp.float32) / width
    cos_a, sin_a = (jnp.cos(angle_a), jnp.sin(angle_a))
    cos_b, sin_b = (jnp.cos(angle_b), jnp.sin(angle_b))
    cos_t, sin_t = (jnp.cos(angle_t), jnp.sin(angle_t))
    wavenum = index_a[:, None] + first * index_b[None, :]
    signed = jnp.where(wavenum < width // 2, wavenum, wavenum - width)
    phase = (signed * signed).astype(jnp.float32) * (DIFF / (width / 2) ** 2)
    cos_p, sin_p = (jnp.cos(phase), jnp.sin(phase))
    real_in = stacked[0].reshape(count, first, second)
    imag_in = stacked[1].reshape(count, first, second)
    step_re, step_im = rotate(real_in, imag_in, cos_a, sin_a, "nab,ak->nkb", 1.0)
    twist_re = step_re * cos_t + step_im * sin_t
    twist_im = step_im * cos_t - step_re * sin_t
    spec_re, spec_im = rotate(twist_re, twist_im, cos_b, sin_b, "nkb,bj->nkj", 1.0)
    moved_re = spec_re * cos_p - spec_im * sin_p
    moved_im = spec_re * sin_p + spec_im * cos_p
    back_re, back_im = rotate(moved_re, moved_im, cos_b, sin_b, "nkj,jb->nkb", -1.0)
    untw_re = back_re * cos_t - back_im * sin_t
    untw_im = back_im * cos_t + back_re * sin_t
    final_re, final_im = rotate(untw_re, untw_im, cos_a, sin_a, "nkb,ka->nab", -1.0)
    return jnp.stack([final_re.reshape(count, width), final_im.reshape(count, width)]) / width


def added_up(value, axis):
    count = lax.axis_size(axis)
    if count & (count - 1):
        return lax.psum(value, axis)
    reach = 1
    while reach < count:
        value = value + lax.ppermute(value, axis, [(i, i ^ reach) for i in range(count)])
        reach *= 2
    return value


def lateral_work(parts):
    return (transform(parts[0]), transform(parts[1]))


def multiplier_revision(
    population_multiplier,
    holeburn_multiplier,
    measured_rightward,
    measured_leftward,
    rightward_wave,
    leftward_wave,
    population_level,
    holeburn_magnitude,
    attenuation_factor,
    transverse_curvature,
):
    rightward_inphase, rightward_quadrature = (rightward_wave[0], rightward_wave[1])
    leftward_inphase, leftward_quadrature = (leftward_wave[0], leftward_wave[1])
    measured_rightward_inphase, measured_rightward_quadrature = (
        measured_rightward[0],
        measured_rightward[1],
    )
    measured_leftward_inphase, measured_leftward_quadrature = (
        measured_leftward[0],
        measured_leftward[1],
    )
    surplus_population = population_level - 1.0
    amplification_inphase = 1.0 + 0.5 * (GAIN_SLOPE_RATE * surplus_population - attenuation_factor)
    amplification_quadrature = 0.5 * GAIN_SLOPE_RATE * ALPHA_LINEWIDTH * surplus_population
    joined_waves = COUPLING * holeburn_magnitude
    population_derivative = (
        2.0 * CLOCK_DELTA * GAIN_SLOPE_RATE * surplus_population * population_multiplier
    )
    holeburn_derivative = 2.0 * CLOCK_DELTA * holeburn_multiplier
    revised_rightward_inphase = (
        amplification_inphase * measured_rightward_inphase
        - amplification_quadrature * measured_rightward_quadrature
        + joined_waves * measured_leftward_quadrature
        - population_derivative * rightward_inphase
        + holeburn_derivative * leftward_inphase
    )
    revised_rightward_quadrature = (
        amplification_inphase * measured_rightward_quadrature
        + amplification_quadrature * measured_rightward_inphase
        - joined_waves * measured_leftward_inphase
        - population_derivative * rightward_quadrature
        + holeburn_derivative * leftward_quadrature
    )
    revised_leftward_inphase = (
        amplification_inphase * measured_leftward_inphase
        - amplification_quadrature * measured_leftward_quadrature
        + joined_waves * measured_rightward_quadrature
        - population_derivative * leftward_inphase
        + holeburn_derivative * rightward_inphase
    )
    revised_leftward_quadrature = (
        amplification_inphase * measured_leftward_quadrature
        + amplification_quadrature * measured_leftward_inphase
        - joined_waves * measured_rightward_inphase
        - population_derivative * leftward_quadrature
        + holeburn_derivative * rightward_quadrature
    )
    light_intensity = (
        rightward_inphase * rightward_inphase
        + rightward_quadrature * rightward_quadrature
        + leftward_inphase * leftward_inphase
        + leftward_quadrature * leftward_quadrature
    )
    amplification_share = (
        measured_rightward_inphase * (rightward_inphase + ALPHA_LINEWIDTH * rightward_quadrature)
        + measured_rightward_quadrature
        * (rightward_quadrature - ALPHA_LINEWIDTH * rightward_inphase)
        + measured_leftward_inphase * (leftward_inphase + ALPHA_LINEWIDTH * leftward_quadrature)
        + measured_leftward_quadrature * (leftward_quadrature - ALPHA_LINEWIDTH * leftward_inphase)
    )
    revised_population = (
        population_multiplier
        * (1.0 - CLOCK_DELTA / DENSITY_LIFETIME - CLOCK_DELTA * GAIN_SLOPE_RATE * light_intensity)
        + TRANSVERSE_DIFFUS * transverse_curvature
        + 0.5 * GAIN_SLOPE_RATE * amplification_share
    )
    fresh_holeburn = holeburn_multiplier * (1.0 - CLOCK_DELTA / GRATING_LIFE) + COUPLING * (
        measured_rightward_quadrature * leftward_inphase
        - measured_rightward_inphase * leftward_quadrature
        + measured_leftward_quadrature * rightward_inphase
        - measured_leftward_inphase * rightward_quadrature
    )
    return (
        jnp.stack([revised_rightward_inphase, revised_rightward_quadrature]),
        jnp.stack([revised_leftward_inphase, revised_leftward_quadrature]),
        revised_population,
        fresh_holeburn,
    )


def per_device(
    ending_rightward_adjoint,
    ending_leftward_adjoint,
    ending_population_adjoint,
    ending_holeburn_adjoint,
    history_rightward,
    history_leftward,
    history_population,
    history_holeburn,
    segment_passive_attenuation,
):
    columns = ending_rightward_adjoint.shape[2]
    rows = ending_rightward_adjoint.shape[1]
    blocks = lax.axis_size("gz")
    position = lax.axis_index("gz")
    cells = rows * blocks
    zpos = (position * rows + jnp.arange(rows, dtype=jnp.int32)).astype(jnp.float32)
    scaling_factor = 1.0 + 2.0 * zpos / (cells - 1)
    rightward_multiplier, leftward_multiplier = (ending_rightward_adjoint, ending_leftward_adjoint)
    population_multiplier, holeburn_multiplier = (
        ending_population_adjoint,
        ending_holeburn_adjoint,
    )
    attenuation_factor = segment_passive_attenuation.astype(jnp.float32)
    shape_curve = jnp.zeros((columns,), jnp.float32)
    for moment_position in range(history_rightward.shape[0] - 1, -1, -1):
        shape_curve = shape_curve + jnp.sum(scaling_factor[:, None] * population_multiplier, axis=0)
        above = passed_along(rightward_multiplier[:, :1, :], "gz", -1)
        below = passed_along(leftward_multiplier[:, -1:, :], "gz", 1)
        top_row = jnp.where(
            position == blocks - 1, FRONT_FACET * leftward_multiplier[:, -1:, :], above
        )
        bottom_row = jnp.where(position == 0, REAR_FACET * rightward_multiplier[:, :1, :], below)
        lam_fwd = jnp.concatenate([rightward_multiplier[:, 1:, :], top_row], axis=1)
        lam_bwd = jnp.concatenate([bottom_row, leftward_multiplier[:, :-1, :]], axis=1)
        whole_fwd, whole_bwd = (
            lax.all_gather(lam_fwd, "gx", axis=2, tiled=True),
            lax.all_gather(lam_bwd, "gx", axis=2, tiled=True),
        )
        start = lax.axis_index("gx") * columns
        done_fwd, done_bwd = lateral_work((whole_fwd, whole_bwd))
        measured_rightward = lax.dynamic_slice_in_dim(done_fwd, start, columns, 2)
        measured_leftward = lax.dynamic_slice_in_dim(done_bwd, start, columns, 2)
        bordered_array = with_halo(population_multiplier, (("gx", 1),), 1)
        transverse_curvature = (
            bordered_array[:, 2:] + bordered_array[:, :-2] - 2.0 * population_multiplier
        )
        rightward_multiplier, leftward_multiplier, population_multiplier, holeburn_multiplier = (
            multiplier_revision(
                population_multiplier,
                holeburn_multiplier,
                measured_rightward,
                measured_leftward,
                history_rightward[moment_position].astype(jnp.float32),
                history_leftward[moment_position].astype(jnp.float32),
                history_population[moment_position].astype(jnp.float32),
                history_holeburn[moment_position].astype(jnp.float32),
                attenuation_factor,
                transverse_curvature,
            )
        )
    total = added_up(shape_curve, "gz")
    derivative_vector = CLOCK_DELTA * total / math.sqrt(cells)
    return (
        rightward_multiplier,
        leftward_multiplier,
        population_multiplier,
        holeburn_multiplier,
        derivative_vector,
    )

LANES = 128
TILE = 16
POWER = 12
STRETCH = 1211.0
SCALE_LANE = 8


def lateral_matrices(width, blocks):
    lanes = width // blocks
    k = np.arange(width)
    signed = np.where(k < width // 2, k, k - width).astype(np.float64)
    response = np.fft.ifft(np.exp(1j * signed * signed * (DIFF / (width / 2) ** 2)))
    step = np.arange(lanes)
    shift = lanes * np.arange(blocks)[:, None, None] + step[None, None, :] - step[None, :, None]
    kernels = np.fft.fft(response[shift % width], axis=0) / blocks
    top = np.concatenate([kernels.real, kernels.imag], axis=2)
    low = np.concatenate([-kernels.imag, kernels.real], axis=2)
    whole = np.concatenate([top, low], axis=1)
    first = whole.astype(ml_dtypes.bfloat16)
    rest = (whole - first.astype(np.float64)).astype(ml_dtypes.bfloat16)
    return np.stack([first, rest], axis=1)


def block_dft(values, sign):
    count = len(values)
    if count == 1:
        return values
    even = block_dft(values[0::2], sign)
    odd = block_dft(values[1::2], sign)
    out = [None] * count
    for k in range(count // 2):
        (er, ei), (wr, wi) = even[k], odd[k]
        if 4 * k == count:
            plus, minus = (er - wi, ei + wr), (er + wi, ei - wr)
            out[k], out[k + count // 2] = (plus, minus) if sign > 0 else (minus, plus)
            continue
        if k:
            c, s = math.cos(2 * math.pi * k / count), sign * math.sin(2 * math.pi * k / count)
            if 8 * k == count:
                wr, wi = (c * (wr - wi), c * (wr + wi)) if sign > 0 else (c * (wr + wi), c * (wi - wr))
            elif 8 * k == 3 * count:
                wr, wi = (c * (wr + wi), c * (wi - wr)) if sign > 0 else (c * (wr - wi), c * (wr + wi))
            else:
                wr, wi = c * wr - s * wi, c * wi + s * wr
        out[k] = (er + wr, ei + wi)
        out[k + count // 2] = (er - wr, ei - wi)
    return out


def lane(j):
    return pl.ds(pl.multiple_of(j * LANES, LANES), LANES)


def slab(j, rows):
    return pl.ds(pl.multiple_of(j * rows, rows), rows)


def fetch(pairs, sems, first=0):
    copies = [pltpu.make_async_copy(a, b, sems.at[first + i]) for i, (a, b) in enumerate(pairs)]
    for copy in copies:
        copy.start()
    return copies


def rows_of(info, rows, other):
    part = 1 - info[4] if other else info[4]
    return pl.ds(pl.multiple_of(part * rows, rows), rows)


def spread(field, work):
    rows = field.shape[1]
    blocks = work.shape[0]

    @pl.loop(0, rows // 8)
    def _(g):
        at = slab(g, 8)
        values = [
            (field[0, at, j * LANES : (j + 1) * LANES], field[1, at, j * LANES : (j + 1) * LANES])
            for j in range(blocks)
        ]
        for q, (re, im) in enumerate(block_dft(values, -1)):
            work[q, at, :LANES] = re
            work[q, at, LANES:] = im


def multiply(work, matrices):
    rows = work.shape[1]

    @pl.loop(0, work.shape[0], unroll=True)
    def _(q):
        value = work[q]
        first = value.astype(jnp.bfloat16)
        rest = (value - first.astype(jnp.float32)).astype(jnp.bfloat16)
        both = jnp.dot(
            jnp.concatenate([first, rest]), matrices[q, 0], preferred_element_type=jnp.float32
        )
        fine = jnp.dot(first, matrices[q, 1], preferred_element_type=jnp.float32)
        work[q] = both[:rows] + (both[rows:] + fine)


def gathered(work, at):
    values = [(work[q, at, :LANES], work[q, at, LANES:]) for q in range(work.shape[0])]
    return block_dft(values, 1)


def filtered(field, work, matrices, copy):
    spread(field, work)
    copy.wait()
    multiply(work, matrices)


def write_filtered(info, work, forward, backward, inner, outer):
    rows = work.shape[1] // 2
    for target, base, offset in ((forward, 0, 0), (backward, rows, 8)):

        @pl.loop(0, rows // 8)
        def _(g):
            here = pl.ds(pl.multiple_of(g * 8 + offset, 8), 8)
            for j, pair in enumerate(gathered(work, pl.ds(pl.multiple_of(g * 8 + base, 8), 8))):
                for part in range(2):
                    target[part, here, j * LANES : (j + 1) * LANES] = pair[part]

    low = info[4] == 0
    for part in range(2):
        first, last = forward[part, 0:1, :], backward[part, rows + 7 : rows + 8, :]
        inner[part : part + 1, :] = jnp.where(low, last, first)
        outer[part : part + 1, :] = jnp.where(low, first, last)


def size_of(largest):
    top = jnp.max(jnp.max(largest, axis=1, keepdims=True), axis=0, keepdims=True)
    return jnp.maximum(top, 1e-30).astype(jnp.bfloat16).astype(jnp.float32)


def encoded(value, size):
    unit = value * (STRETCH / size)
    square = unit * unit
    fourth = square * square
    return (fourth * fourth * square * (unit * jnp.abs(unit))).astype(jnp.bfloat16)


def decoded(code, size):
    value = code.astype(jnp.float32)
    root = jnp.exp2(jnp.log(jnp.abs(value)) * (1.0 / (POWER * math.log(2.0)))) * (size / STRETCH)
    return jnp.where(value < 0.0, -root, root)


def side_tile(columns, rows):
    index = lax.broadcasted_iota(jnp.int32, (rows, LANES), 1)
    tile = jnp.zeros((rows, LANES), jnp.float32)
    for at, column in columns:
        tile = jnp.where(index == at, column, tile)
    return tile.astype(jnp.bfloat16)


def sizes_in(tile, count):
    value = tile.astype(jnp.float32)
    return [value[0:1, SCALE_LANE + i : SCALE_LANE + i + 1] for i in range(count)]


def updated(fr, fi, br, bi, wave, population, hole, loss, carrier, grating, lap):
    rr, ri, lr, li = wave
    surplus = population - 1.0
    gain_re = 1.0 + 0.5 * (GAIN_SLOPE_RATE * surplus - loss)
    gain_im = (0.5 * GAIN_SLOPE_RATE * ALPHA_LINEWIDTH) * surplus
    joined = COUPLING * hole
    drive = (2.0 * CLOCK_DELTA * GAIN_SLOPE_RATE) * surplus * carrier
    mix = (2.0 * CLOCK_DELTA) * grating
    new_fr = gain_re * fr - gain_im * fi + joined * bi - drive * rr + mix * lr
    new_fi = gain_re * fi + gain_im * fr - joined * br - drive * ri + mix * li
    new_br = gain_re * br - gain_im * bi + joined * fi - drive * lr + mix * rr
    new_bi = gain_re * bi + gain_im * br - joined * fr - drive * li + mix * ri
    light = rr * rr + ri * ri + lr * lr + li * li
    share = (
        fr * (rr + ALPHA_LINEWIDTH * ri)
        + fi * (ri - ALPHA_LINEWIDTH * rr)
        + br * (lr + ALPHA_LINEWIDTH * li)
        + bi * (li - ALPHA_LINEWIDTH * lr)
    )
    new_carrier = (
        carrier * ((1.0 - CLOCK_DELTA / DENSITY_LIFETIME) - (CLOCK_DELTA * GAIN_SLOPE_RATE) * light)
        + TRANSVERSE_DIFFUS * lap
        + (0.5 * GAIN_SLOPE_RATE) * share
    )
    new_grating = grating * (1.0 - CLOCK_DELTA / GRATING_LIFE) + COUPLING * (
        fi * lr - fr * li + bi * rr - br * ri
    )
    return new_fr, new_fi, new_br, new_bi, new_carrier, new_grating


def curvature(left, mid, right, weight_left, weight_right):
    index = lax.broadcasted_iota(jnp.int32, mid.shape, 1)
    below = jnp.where(index == 0, pltpu.roll(left, 1, 1) * weight_left, pltpu.roll(mid, 1, 1))
    above = jnp.where(
        index == LANES - 1,
        pltpu.roll(right, LANES - 1, 1) * weight_right,
        pltpu.roll(mid, LANES - 1, 1),
    )
    return below + above - 2.0 * mid


def send_fields_kernel(info, forward, backward, out, fields, sems):
    rows, columns = fields.shape[2:]
    half = columns // LANES
    at = rows_of(info, rows, True)
    copies = fetch(
        [(ref.at[:, at, :], fields.at[f]) for f, ref in enumerate((forward, backward))], sems
    )
    sizes = []
    for f in range(2):
        copies[f].wait()
        largest = jnp.maximum(jnp.abs(fields[f, 0]), jnp.abs(fields[f, 1]))
        size = size_of(largest)
        sizes.append((SCALE_LANE + f, size))
        for part in range(2):
            put_tiles(out, (2 * f + part) * half, encoded(fields[f, part], size))
    out[4 * half * rows :, :] = side_tile(sizes, rows)


def put_tiles(out, first, value):
    rows, columns = value.shape
    for j in range(columns // LANES):
        at = (first + j) * rows
        out[at : at + rows, :] = value[:, j * LANES : (j + 1) * LANES]


def history_rows(forward, backward, population, hole, s, at):
    return [
        forward.at[s, 0, at, :], forward.at[s, 1, at, :], backward.at[s, 0, at, :],
        backward.at[s, 1, at, :], population.at[s, at, :], hole.at[s, at, :],
    ]


def into_rows(parts, target, first, rows):
    return [(part, target.at[pl.ds(first + i * rows, rows), :]) for i, part in enumerate(parts)]


def send_later_kernel(steps, info, forward, backward, population, hole, final, *refs):
    targets, sems = refs[:-1], refs[-1]
    rows = targets[0].shape[0] // 6
    history = (forward, backward, population, hole)
    pairs = []
    for i, s in enumerate(steps):
        for k, other in enumerate((True, False)):
            at = rows_of(info, rows, other)
            pairs += into_rows(history_rows(*history, s, at), targets[2 * i + k], 0, rows)
    pairs += into_rows(history_rows(*history, 0, pl.ds(0, 2 * rows)), final, 0, 2 * rows)
    for copy in fetch(pairs, sems):
        copy.wait()


def send_first_kernel(
    s, info, loss, carrier, grating, forward, backward, population, hole,
    own_loss, own, own_carrier, own_grating, out, own_edge, states, ends, sems,
):
    rows, columns = own_carrier.shape
    theirs, mine = rows_of(info, rows, True), rows_of(info, rows, False)
    history = (forward, backward, population, hole)
    copies = fetch(
        [(carrier.at[theirs, :], states.at[0]), (grating.at[theirs, :], states.at[1])]
        + into_rows([loss.at[theirs, :]], out, 0, rows)
        + into_rows(history_rows(*history, s, theirs), out, 3 * rows, rows)
        + [(loss.at[mine, :], own_loss), (carrier.at[mine, :], own_carrier)]
        + [(grating.at[mine, :], own_grating)]
        + into_rows(history_rows(*history, s, mine), own, 0, rows)
        + [
            (part, ends.at[k, i])
            for k in range(2)
            for i, part in enumerate(
                history_rows(*history, 1, pl.ds(k * (2 * rows - TILE), TILE))
            )
        ],
        sems,
    )
    for copy in copies[:2]:
        copy.wait()
    sizes = []
    for i in range(2):
        size = size_of(jnp.abs(states[i]))
        sizes.append(jnp.broadcast_to(size, (1, columns)))
        out[(1 + i) * rows : (2 + i) * rows, :] = encoded(states[i], size)
    for copy in copies[2:]:
        copy.wait()
    low = info[4] == 0
    top = [ends[0, i].astype(jnp.float32)[:1] for i in range(6)]
    foot = [ends[1, i].astype(jnp.float32)[TILE - 1 :] for i in range(6)]
    own_edge[...] = jnp.concatenate([jnp.where(low, a, b) for a, b in zip(top, foot)])
    sizes += [jnp.where(low, b, a) for a, b in zip(top, foot)]
    sizes.append(jnp.zeros((TILE - 8, columns), jnp.float32))
    out[9 * rows :, :] = jnp.concatenate(sizes).astype(jnp.bfloat16)


def enter_kernel(
    info, forward, backward, other, source, tp, tq, inner, outer, field, work, matrices, sem, sems
):
    copy = pltpu.make_async_copy(source, matrices, sem)
    rows, width = field.shape[1] // 2, field.shape[2]
    columns = width // 2
    half = columns // LANES
    at = rows_of(info, rows, False)
    copies = fetch(
        [
            (ref.at[:, at, :], field.at[:, f * rows : (f + 1) * rows, :columns])
            for f, ref in enumerate((forward, backward))
        ],
        sems,
    )
    copy.start()
    sizes = sizes_in(other[4 * half * rows :, :], 2)
    for f in range(2):
        for part in range(2):

            @pl.loop(0, half, unroll=2)
            def _(j):
                code = other[slab((2 * f + part) * half + j, rows), :]
                field[part, f * rows : (f + 1) * rows, lane(half + j)] = decoded(code, sizes[f])

    for held in copies:
        held.wait()
    filtered(field, work, matrices, copy)
    write_filtered(info, work, tp, tq, inner, outer)


def rows_update(
    info, tp, tq, inner, outer, carrier, grating, own, other, own_loss, other_loss,
    field, new_carrier, new_grating, sums_in, sums, cells, last
):
    rows, width = carrier.shape
    half = width // LANES // 2
    columns = half * LANES
    mid = jnp.where(info[0] == 0, 1.0, 0.0)
    wrap = 1.0 - mid
    low = info[4] == 0
    is_first, is_last = info[1], info[2]
    row_index = lax.broadcasted_iota(jnp.int32, (TILE, LANES), 0)
    zero = jnp.zeros((8, LANES), jnp.float32)

    def step(jj, most):
        for side in range(2):
            j = jj + side * half
            here = lane(j)
            left_at = lane(jnp.where(j == 0, 2 * half - 1, j - 1))
            right_at = lane(jnp.where(j == 2 * half - 1, 0, j + 1))
            swapped = lane(jj + (1 - side) * half)
            weight_left = jnp.where(jj == 0, wrap if side == 0 else mid, 1.0)
            weight_right = jnp.where(jj == half - 1, mid if side == 0 else wrap, 1.0)
            total = zero
            for r in range(0, rows, TILE):
                at = slice(r, r + TILE)

                held, begin = (own, other)[side]

                def part_of(i):
                    tile = begin + i * rows + r
                    return held[tile : tile + TILE, lane(jj)].astype(jnp.float32)

                loss = (own_loss, other_loss)[side][at, lane(jj)].astype(jnp.float32)
                f = [tp[part, r + 1 : r + 1 + TILE, here] for part in range(2)]
                b = [tq[part, r + 7 : r + 7 + TILE, here] for part in range(2)]
                if r + TILE == rows:
                    for part in range(2):
                        facet = FRONT_FACET * tq[part, rows + 7 : rows + 8, here]
                        edge = jnp.where(
                            low, inner[part : part + 1, swapped], outer[part : part + 1, here]
                        )
                        edge = jnp.where(is_last, facet, edge)
                        f[part] = jnp.where(row_index == TILE - 1, edge, f[part])
                if r == 0:
                    for part in range(2):
                        facet = REAR_FACET * tp[part, 0:1, here]
                        edge = jnp.where(
                            low, outer[part : part + 1, here], inner[part : part + 1, swapped]
                        )
                        edge = jnp.where(is_first, facet, edge)
                        b[part] = jnp.where(row_index == 0, edge, b[part])
                c = carrier[at, here]
                lap = curvature(
                    carrier[at, left_at], c, carrier[at, right_at], weight_left, weight_right
                )
                out = updated(
                    *f, *b, [part_of(i) for i in range(4)], part_of(4), part_of(5), loss,
                    c, grating[at, here], lap,
                )
                field[0, r : r + TILE, here] = out[0]
                field[1, r : r + TILE, here] = out[1]
                field[0, rows + r : rows + r + TILE, here] = out[2]
                field[1, rows + r : rows + r + TILE, here] = out[3]
                new_carrier[at, here] = out[4]
                new_grating[at, here] = out[5]
                z = (info[3] + r + row_index).astype(jnp.float32)
                weighted = (1.0 + 2.0 * z / (cells - 1)) * ((c + out[4]) if last else c)
                for k in range(0, TILE, 8):
                    total = total + weighted[k : k + 8]
                if last and side == 1:
                    for k in range(0, TILE, 8):
                        most = (
                            jnp.maximum(most[0], jnp.abs(out[4][k : k + 8])),
                            jnp.maximum(most[1], jnp.abs(out[5][k : k + 8])),
                        )
            summed = jnp.sum(total, axis=0, keepdims=True)
            sums[:, here] = summed if sums_in is None else summed + sums_in[:, here]
        return most

    return lax.fori_loop(0, half, step, (zero, zero))


def first_step_kernel(
    cells, info, tp, tq, inner, outer, my_carrier, my_grating, loss, own, own_edge, other, source,
    new_tp, new_tq, new_inner, new_outer, new_carrier, new_grating, sums,
    carrier, grating, field, work, matrices, sem,
):
    copy = pltpu.make_async_copy(source, matrices, sem)
    copy.start()
    rows, columns = my_carrier.shape
    half = columns // LANES
    extra = other[9 * rows :, :].astype(jnp.float32)
    sizes = [extra[0:1, 0:1], extra[1:2, 0:1]]
    low = info[4] == 0
    new_outer[2:8, :columns] = own_edge[...]
    new_outer[2:8, columns:] = extra[2:8]
    for part, ref in ((0, loss), (1, other)):
        top = ref[:TILE, :].astype(jnp.float32)[:1]
        foot = ref[rows - TILE : rows, :].astype(jnp.float32)[TILE - 1 :]
        new_outer[8:9, part * columns : (part + 1) * columns] = jnp.where(low, top, foot)
    for i, (whole, mine) in enumerate(((carrier, my_carrier), (grating, my_grating))):
        whole[:, :columns] = mine[...]

        @pl.loop(0, half, unroll=2)
        def _(j):
            whole[:, lane(half + j)] = decoded(
                other[(1 + i) * rows : (2 + i) * rows, lane(j)], sizes[i]
            )

    rows_update(
        info, tp, tq, inner, outer, carrier, grating, (own, 0), (other, 3 * rows), loss, other,
        field, new_carrier, new_grating, None, sums, cells, False,
    )
    filtered(field, work, matrices, copy)
    write_filtered(info, work, new_tp, new_tq, new_inner, new_outer)


def middle_step_kernel(
    cells, info, tp, tq, inner, outer, carrier, grating, loss, own, other, other_loss, sums_in,
    source, new_tp, new_tq, new_inner, new_outer, new_carrier, new_grating, sums,
    field, work, matrices, sem,
):
    copy = pltpu.make_async_copy(source, matrices, sem)
    copy.start()
    rows_update(
        info, tp, tq, inner, outer, carrier, grating, (own, 0), (other, 0), loss, other_loss,
        field, new_carrier, new_grating, sums_in, sums, cells, False,
    )
    filtered(field, work, matrices, copy)
    write_filtered(info, work, new_tp, new_tq, new_inner, new_outer)
    rows = carrier.shape[0]
    low = info[4] == 0
    for part in range(2):
        new_outer[2 + part : 3 + part, :] = jnp.where(
            low, new_tp[part, 1:2, :], new_tq[part, rows + 6 : rows + 7, :]
        )
    for i, ref in enumerate((new_carrier, new_grating)):
        new_outer[4 + i : 5 + i, :] = jnp.where(low, ref[0:1, :], ref[rows - 1 : rows, :])


def row_beyond(info, tp, tq, outer, beyond):
    rows = tp.shape[1] - 8
    low = info[4] == 0
    xr, xi, carrier, grating = (outer[i : i + 1, :] for i in range(2, 6))
    yr, yi = (
        jnp.where(low, tp[part, 0:1, :], tq[part, rows + 7 : rows + 8, :]) for part in range(2)
    )
    rr, ri, lr, li, population, hole, loss = (beyond[i : i + 1, :] for i in range(2, 9))
    surplus = population - 1.0
    gain_re = 1.0 + 0.5 * (GAIN_SLOPE_RATE * surplus - loss)
    gain_im = (0.5 * GAIN_SLOPE_RATE * ALPHA_LINEWIDTH) * surplus
    joined = COUPLING * hole
    drive = (2.0 * CLOCK_DELTA * GAIN_SLOPE_RATE) * surplus * carrier
    mix = (2.0 * CLOCK_DELTA) * grating
    near_re, near_im = jnp.where(low, lr, rr), jnp.where(low, li, ri)
    far_re, far_im = jnp.where(low, rr, lr), jnp.where(low, ri, li)
    new_re = gain_re * xr - gain_im * xi + joined * yi - drive * near_re + mix * far_re
    new_im = gain_re * xi + gain_im * xr - joined * yr - drive * near_im + mix * far_im
    return new_re, new_im


def leave_kernel(
    cells, info, tp, tq, inner, outer, beyond, carrier, grating, loss, own, other, other_loss,
    sums_in, source, kept, kept_carrier, kept_grating, sides, sent, edge, shares,
    sums, new_carrier, new_grating, field, work, matrices, sem,
):
    copy = pltpu.make_async_copy(source, matrices, sem)
    copy.start()
    rows, width = carrier.shape
    columns = width // 2
    half = columns // LANES
    most = rows_update(
        info, tp, tq, inner, outer, carrier, grating, (own, 0), (other, 0), loss, other_loss,
        field, new_carrier, new_grating, sums_in, sums, cells, True,
    )
    mid = jnp.where(info[0] == 0, 1.0, 0.0)
    wrap = 1.0 - mid
    kept_carrier[...] = new_carrier[:, :columns]
    kept_grating[...] = new_grating[:, :columns]
    first, before = new_carrier[:, 0:1] * wrap, new_carrier[:, columns - 1 : columns] * mid
    after, final = new_carrier[:, columns : columns + 1] * mid, new_carrier[:, width - 1 :] * wrap
    sides[0] = jnp.broadcast_to(final, (rows, LANES))
    sides[1] = jnp.broadcast_to(after, (rows, LANES))
    pairs = []
    for at, value in ((0, before), (2, first)):
        coarse = value.astype(jnp.bfloat16).astype(jnp.float32)
        pairs += [(at, coarse), (at + 1, value - coarse)]
    for i, field_of in enumerate((new_carrier, new_grating)):
        size = size_of(most[i])
        pairs.append((SCALE_LANE + 2 + i, size))

        @pl.loop(0, half, unroll=2)
        def _(j):
            sent[slab((4 + i) * half + j, rows), :] = encoded(field_of[:, lane(half + j)], size)

    for part, value in enumerate(row_beyond(info, tp, tq, outer, beyond)):
        field[part, 2 * rows :, :] = jnp.broadcast_to(value, (8, width))
    filtered(field, work, matrices, copy)
    zero = jnp.zeros((8, LANES), jnp.float32)
    for f in range(2):

        def unmix(g, most):
            at = pl.ds(pl.multiple_of(g * 8 + f * rows, 8), 8)
            for j, pair in enumerate(gathered(work, at)):
                for part in range(2):
                    if j < half:
                        kept[part, at, j * LANES : (j + 1) * LANES] = pair[part]
                    else:
                        work[j, at, part * LANES : (part + 1) * LANES] = pair[part]
                        most = jnp.maximum(most, jnp.abs(pair[part]))
            return most

        size = size_of(lax.fori_loop(0, rows // 8, unmix, zero))
        pairs.append((SCALE_LANE + f, size))

        @pl.loop(0, half, unroll=2)
        def _(j):
            for part in range(2):
                value = work[half + j, f * rows : (f + 1) * rows, part * LANES : (part + 1) * LANES]
                sent[slab((2 * f + part) * half + j, rows), :] = encoded(value, size)

    ends = gathered(work, slice(2 * rows, 2 * rows + 8))
    for part in range(2):
        for j in range(half):
            edge[part : part + 1, j * LANES : (j + 1) * LANES] = ends[j][part][:1]
    far = jnp.concatenate([ends[j][part][:1] for part in range(2) for j in range(half, 2 * half)])
    size = size_of(jnp.abs(far))
    pairs.append((SCALE_LANE + 4, size))
    sent[6 * half * rows : (6 * half + 1) * rows, :] = side_tile(pairs, rows)
    spare = jnp.zeros((rows - 2 * half, LANES), jnp.float32)
    sent[(6 * half + 1) * rows :, :] = encoded(jnp.concatenate([far, spare]), size)
    tile = jnp.concatenate([sums[:, j * LANES : (j + 1) * LANES] for j in range(2 * half)])
    near, far = tile[:half], tile[half:]
    first = info[0] == 0
    to_first, to_second = jnp.where(first, near, far), jnp.where(first, far, near)
    for i in range(0, shares.shape[0], 2):
        shares[i] = to_first
        shares[i + 1] = to_second


def final_kernel(
    cells, info, kept, kept_carrier, kept_grating, sides, came, edge, partial, loss, history,
    out_forward, out_backward, out_carrier, out_grating, out_sums,
    tp, tq, carrier, grating,
):
    rows, columns = kept_carrier.shape
    half = columns // LANES
    total = partial[0]
    for i in range(1, partial.shape[0]):
        total = total + partial[i]
    out_sums[...] = total * (CLOCK_DELTA / math.sqrt(cells))
    mine = info[4] * rows
    theirs = (1 - info[4]) * rows
    low = info[4] == 0
    extra = came[6 * half * rows : (6 * half + 1) * rows, :]
    size_forward, size_backward, size_carrier, size_grating, size_edge = sizes_in(extra, 5)
    ends = decoded(came[(6 * half + 1) * rows :, :], size_edge)
    extra = extra.astype(jnp.float32)

    def at(start, offset, count):
        return pl.ds(pl.multiple_of(start + offset, 8), count)

    for part in range(2):
        tp[part, at(mine, 0, rows), :] = kept[part, :rows, :]
        tq[part, at(mine, 8, rows), :] = kept[part, rows:, :]
    carrier[at(mine, 0, rows), LANES : LANES + columns] = kept_carrier[...]
    carrier[at(mine, 0, rows), :LANES] = sides[0]
    carrier[at(mine, 0, rows), LANES + columns :] = sides[1]
    carrier[at(theirs, 0, rows), :LANES] = jnp.broadcast_to(
        extra[:, 0:1] + extra[:, 1:2], (rows, LANES)
    )
    carrier[at(theirs, 0, rows), LANES + columns :] = jnp.broadcast_to(
        extra[:, 2:3] + extra[:, 3:4], (rows, LANES)
    )
    grating[at(mine, 0, rows), :] = kept_grating[...]

    @pl.loop(0, half, unroll=2)
    def _(j):
        carrier[at(theirs, 0, rows), lane(1 + j)] = decoded(
            came[slab(4 * half + j, rows), :], size_carrier
        )
        grating[at(theirs, 0, rows), lane(j)] = decoded(
            came[slab(5 * half + j, rows), :], size_grating
        )
        for part in range(2):
            tp[part, at(theirs, 0, rows), lane(j)] = decoded(
                came[slab(part * half + j, rows), :], size_forward
            )
            tq[part, at(theirs, 8, rows), lane(j)] = decoded(
                came[slab((2 + part) * half + j, rows), :], size_backward
            )

    all_rows = 2 * rows
    for part in range(2):
        near = edge[part : part + 1, :]
        far = jnp.concatenate([ends[part * half + j : part * half + j + 1] for j in range(half)], axis=1)
        next_edge = jnp.where(low, far, near)
        before_edge = jnp.where(low, near, far)
        front = FRONT_FACET * tq[part, all_rows + 7 : all_rows + 8, :]
        rear = REAR_FACET * tp[part, 0:1, :]
        tp[part, all_rows : all_rows + 1, :] = jnp.where(info[2], front, next_edge)
        tq[part, 7:8, :] = jnp.where(info[1], rear, before_edge)

    @pl.loop(0, half)
    def _(j):
        here = lane(j)
        for r in range(0, all_rows, TILE):
            row = slice(r, r + TILE)
            c = carrier[row, lane(j + 1)]
            lap = curvature(carrier[row, lane(j)], c, carrier[row, lane(j + 2)], 1.0, 1.0)
            parts = [
                history[i * all_rows + r : i * all_rows + r + TILE, here].astype(jnp.float32)
                for i in range(6)
            ]
            out = updated(
                tp[0, r + 1 : r + 1 + TILE, here], tp[1, r + 1 : r + 1 + TILE, here],
                tq[0, r + 7 : r + 7 + TILE, here], tq[1, r + 7 : r + 7 + TILE, here],
                parts[:4], parts[4], parts[5],
                loss[row, here].astype(jnp.float32), c, grating[row, here], lap,
            )
            out_forward[0, row, here] = out[0]
            out_forward[1, row, here] = out[1]
            out_backward[0, row, here] = out[2]
            out_backward[1, row, here] = out[3]
            out_carrier[row, here] = out[4]
            out_grating[row, here] = out[5]


def position(rows, whole):
    x, block, count = lax.axis_index("gx"), lax.axis_index("gz"), lax.axis_size("gz")
    high = lax.rem(x + block, 2)
    if whole:
        return x, block == 0, block == count - 1, block * rows, high
    place = 2 * block + high
    return x, place == 0, place == 2 * count - 1, place * rows, high


def whole_spec(shape):
    return pl.BlockSpec(shape, lambda i, n=len(shape): (0,) * n)


def call(name, kernel, rows, inputs, outputs, scratch, flops=0, grant=24, whole=False):
    arrays = [x[0] if isinstance(x, tuple) else x for x in inputs]
    specs = [x[1] if isinstance(x, tuple) else whole_spec(x.shape) for x in inputs]
    shapes = [jax.ShapeDtypeStruct(*out) for out in outputs]
    moved = sum(math.prod(s.shape) * s.dtype.itemsize for s in shapes)

    def body(*refs):
        kernel(position(rows, whole), *refs)

    return pl.pallas_call(
        body,
        grid=(1,),
        in_specs=specs,
        out_specs=[whole_spec(s.shape) for s in shapes],
        scratch_shapes=scratch,
        out_shape=shapes,
        compiler_params=pltpu.CompilerParams(vmem_limit_bytes=grant * 1024 * 1024),
        cost_estimate=pl.CostEstimate(
            flops=flops, bytes_accessed=moved + 4 * 1024 * 1024, transcendentals=0
        ),
        name=name,
    )(*arrays)


def per_pair(
    ending_rightward_adjoint,
    ending_leftward_adjoint,
    ending_population_adjoint,
    ending_holeburn_adjoint,
    history_rightward,
    history_leftward,
    history_population,
    history_holeburn,
    segment_passive_attenuation,
):
    cell_rows, columns = ending_population_adjoint.shape
    passes = history_population.shape[0]
    rows = cell_rows // 2
    half = columns // LANES
    blocks = 2 * half
    width = 2 * columns
    count = lax.axis_size("gz")
    cells = cell_rows * count
    x = lax.axis_index("gx")
    f32, bf16 = jnp.float32, jnp.bfloat16
    swap = [(0, 1), (1, 0)]
    in_place = pl.BlockSpec(memory_space=pltpu.HBM)

    def held(*arrays):
        return [(a, in_place) for a in arrays]

    def tiles(n):
        return ((n * rows, LANES), bf16)

    ends = held(ending_rightward_adjoint, ending_leftward_adjoint)
    planes = held(ending_population_adjoint, ending_holeburn_adjoint)
    history = held(history_rightward, history_leftward, history_population, history_holeburn)
    losses = held(segment_passive_attenuation)
    matrices = pltpu.with_memory_space_constraint(
        jnp.asarray(lateral_matrices(width, blocks)), pltpu.HBM
    )
    matrix_input = held(matrices)
    work = [
        pltpu.VMEM((blocks, 2 * rows, 2 * LANES), f32),
        pltpu.VMEM(matrices.shape, bf16),
        pltpu.SemaphoreType.DMA,
    ]
    field_scratch = pltpu.VMEM((2, 2 * rows, width), f32)
    def state_out(outer_rows):
        state = ((2, rows + 8, width), f32)
        return [state, state, ((2, width), f32), ((outer_rows, width), f32)]

    plane = ((rows, width), f32)
    plane_scratch = pltpu.VMEM((rows, width), f32)
    half_plane = ((rows, columns), f32)
    work_flops = 2 * 3 * 2 * rows * blocks * (2 * LANES) ** 2

    (coded,) = call(
        "send_fields", send_fields_kernel, rows, ends, [tiles(4 * half + 1)],
        [pltpu.VMEM((2, 2, rows, columns), f32), pltpu.SemaphoreType.DMA((2,))], grant=62,
    )
    other_fields = lax.ppermute(coded, "gx", swap)
    loss, own_first, my_carrier, my_grating, sent_first, own_edge = call(
        "send_first", functools.partial(send_first_kernel, passes - 1), rows,
        [*losses, *planes, *history],
        [((rows, columns), bf16), ((6 * rows, columns), bf16), half_plane, half_plane,
         ((9 * rows + TILE, columns), bf16), ((6, columns), f32)],
        [pltpu.VMEM((2, rows, columns), f32), pltpu.VMEM((2, 6, TILE, columns), bf16),
         pltpu.SemaphoreType.DMA((30,))], grant=62,
    )
    steps = range(passes - 2, 0, -1)
    history_last, *later = call(
        "send_later", functools.partial(send_later_kernel, steps), rows, history,
        [((6 * cell_rows, columns), bf16)] + [((6 * rows, columns), bf16)] * (2 * len(steps)),
        [pltpu.SemaphoreType.DMA((12 * len(steps) + 6,))], grant=62,
    )
    sent_first, history_last, later, other_fields = lax.optimization_barrier(
        (sent_first, history_last, later, other_fields)
    )
    other_first = lax.ppermute(sent_first, "gx", swap)

    line = ("gz", "gx")
    neighbours = []
    for b in range(count - 1):
        top = (1 + b) % 2
        neighbours += [(2 * b + top, 2 * b + 2 + top), (2 * b + 2 + top, 2 * b + top)]

    def edges(inner, outer):
        outer = lax.ppermute(outer, line, neighbours)
        return lax.ppermute(inner, "gx", swap), outer

    tp, tq, inner, outer = call(
        "enter", enter_kernel, rows, [*ends, other_fields, *matrix_input],
        state_out(2), [field_scratch, *work, pltpu.SemaphoreType.DMA((2,))], work_flops,
    )
    inner, outer = edges(inner, outer)

    other_loss = (other_first, pl.BlockSpec((rows, columns), lambda i: (0, 0)))
    carrier = grating = sums = other = own = None
    for index, s in enumerate(range(passes - 1, 0, -1)):
        if index < len(steps):
            sent, own_next = later[2 * index : 2 * index + 2]
            sent, inner, outer = lax.optimization_barrier((sent, inner, outer))
            coming = lax.ppermute(sent, "gx", swap)
        shared = [tp, tq, inner, outer]
        if index == 0:
            tp, tq, inner, outer, carrier, grating, sums = call(
                "first_step", functools.partial(first_step_kernel, cells), rows,
                [*shared, my_carrier, my_grating, loss, own_first, own_edge, other_first,
                 *matrix_input],
                [*state_out(9), plane, plane, ((1, width), f32)],
                [plane_scratch, plane_scratch, field_scratch, *work], work_flops,
            )
        elif s > 1:
            tp, tq, inner, outer, carrier, grating, sums = call(
                "middle_step", functools.partial(middle_step_kernel, cells), rows,
                [*shared, carrier, grating, loss, own, other, other_loss, sums, *matrix_input],
                [*state_out(6), plane, plane, ((1, width), f32)],
                [field_scratch, *work], work_flops,
            )
        else:
            kept, kept_carrier, kept_grating, sides, sent, edge, shares = call(
                "leave", functools.partial(leave_kernel, cells), rows,
                [*shared, beyond, carrier, grating, loss, own, other, other_loss, sums, *matrix_input],
                [((2, 2 * rows, columns), f32), half_plane, half_plane, ((2, rows, LANES), f32),
                 tiles(6 * half + 2), ((2, columns), f32), ((2 * count, half, LANES), f32)],
                [pltpu.VMEM((1, width), f32), plane_scratch, plane_scratch,
                 pltpu.VMEM((2, 2 * rows + 8, width), f32),
                 pltpu.VMEM((blocks, 2 * rows + TILE, 2 * LANES), f32), *work[1:]],
                work_flops,
            )
        if s > 1:
            inner, outer = edges(inner, outer)
            own, other = own_next, coming
            if index == 0:
                beyond = outer

    came = lax.ppermute(sent, "gx", swap)
    shares = lax.all_to_all(shares, line, 0, 0, tiled=True)

    *outs, total = call(
        "final", functools.partial(final_kernel, cells), cell_rows,
        [kept, kept_carrier, kept_grating, sides, came, edge, shares,
         segment_passive_attenuation, history_last],
        [((2, cell_rows, columns), f32), ((2, cell_rows, columns), f32),
         ((cell_rows, columns), f32), ((cell_rows, columns), f32), ((half, LANES), f32)],
        [pltpu.VMEM((2, cell_rows + 8, columns), f32), pltpu.VMEM((2, cell_rows + 8, columns), f32),
         pltpu.VMEM((cell_rows, columns + 2 * LANES), f32), pltpu.VMEM((cell_rows, columns), f32)],
        whole=True,
    )
    return (*outs, total.reshape(columns))


def shared_by_pairs(mesh, arguments):
    population = arguments[6]
    passes, cells, width = population.shape
    rows, columns = cells // mesh.shape["gz"], width // mesh.shape["gx"]
    return (
        mesh.shape["gx"] == 2
        and passes >= 4
        and 4 * columns <= rows * LANES
        and rows % (2 * TILE) == 0
        and columns % LANES == 0
        and (columns // LANES) & (columns // LANES - 1) == 0
        and width <= 4096
    )


def solution(mesh):
    def run(*arguments):
        body = per_pair if shared_by_pairs(mesh, arguments) else per_device
        return jax.shard_map(
            body,
            mesh=mesh,
            in_specs=(
                P(None, "gz", "gx"),
                P(None, "gz", "gx"),
                P("gz", "gx"),
                P("gz", "gx"),
                P(None, None, "gz", "gx"),
                P(None, None, "gz", "gx"),
                P(None, "gz", "gx"),
                P(None, "gz", "gx"),
                P("gz", "gx"),
            ),
            out_specs=(
                P(None, "gz", "gx"), P(None, "gz", "gx"), P("gz", "gx"), P("gz", "gx"), P("gx"),
            ),
            check_vma=False,
        )(*arguments)

    return run
```

```python
import functools
import math

import jax
import jax.numpy as jnp
import ml_dtypes
import numpy as np
from jax import lax
from jax.experimental import pallas as pl
from jax.experimental.pallas import tpu as pltpu
from jax.sharding import PartitionSpec as P

DIFF = 512


FRONT_FACET = 0.3
REAR_FACET = 0.9
GAIN_SLOPE_RATE = 0.3
ALPHA_LINEWIDTH = 2.0
COUPLING = 0.5
CLOCK_DELTA = 0.3
DENSITY_LIFETIME = 2.0
GRATING_LIFE = 0.75
TRANSVERSE_DIFFUS = 0.2


def passed_along(value, axis, steps):
    count = lax.axis_size(axis)
    initial, last = (max(0, -steps), min(count, count - steps))
    return lax.ppermute(value, axis, [(source, source + steps) for source in range(initial, last)])


def with_halo(block, sides, width):
    for axis, dim in sides:
        count = lax.axis_size(axis)
        forward = [(i, i + 1) for i in range(count - 1)]
        backward = [(target, source) for source, target in forward]
        low = lax.ppermute(
            lax.slice_in_dim(block, block.shape[dim] - width, None, axis=dim), axis, forward
        )
        high = lax.ppermute(lax.slice_in_dim(block, 0, width, axis=dim), axis, backward)
        block = jnp.concatenate([low, block, high], axis=dim)
    return block


def rotate(source_re, source_im, cosine, sine, form, sign):
    exact = lax.Precision.HIGHEST
    out_re = jnp.einsum(form, source_re, cosine, precision=exact) + sign * jnp.einsum(
        form, source_im, sine, precision=exact
    )
    out_im = jnp.einsum(form, source_im, cosine, precision=exact) - sign * jnp.einsum(
        form, source_re, sine, precision=exact
    )
    return (out_re, out_im)


def transform(stacked):
    count = stacked.shape[1]
    width = stacked.shape[2]
    second = min(128, width // 2)
    first = width // second
    two_pi = 2.0 * math.pi
    index_a = jnp.arange(first, dtype=jnp.int32)
    index_b = jnp.arange(second, dtype=jnp.int32)
    angle_a = two_pi * (index_a[:, None] * index_a[None, :] % first).astype(jnp.float32) / first
    angle_b = two_pi * (index_b[:, None] * index_b[None, :] % second).astype(jnp.float32) / second
    angle_t = two_pi * (index_a[:, None] * index_b[None, :] % width).astype(jnp.float32) / width
    cos_a, sin_a = (jnp.cos(angle_a), jnp.sin(angle_a))
    cos_b, sin_b = (jnp.cos(angle_b), jnp.sin(angle_b))
    cos_t, sin_t = (jnp.cos(angle_t), jnp.sin(angle_t))
    wavenum = index_a[:, None] + first * index_b[None, :]
    signed = jnp.where(wavenum < width // 2, wavenum, wavenum - width)
    phase = (signed * signed).astype(jnp.float32) * (DIFF / (width / 2) ** 2)
    cos_p, sin_p = (jnp.cos(phase), jnp.sin(phase))
    real_in = stacked[0].reshape(count, first, second)
    imag_in = stacked[1].reshape(count, first, second)
    step_re, step_im = rotate(real_in, imag_in, cos_a, sin_a, "nab,ak->nkb", 1.0)
    twist_re = step_re * cos_t + step_im * sin_t
    twist_im = step_im * cos_t - step_re * sin_t
    spec_re, spec_im = rotate(twist_re, twist_im, cos_b, sin_b, "nkb,bj->nkj", 1.0)
    moved_re = spec_re * cos_p - spec_im * sin_p
    moved_im = spec_re * sin_p + spec_im * cos_p
    back_re, back_im = rotate(moved_re, moved_im, cos_b, sin_b, "nkj,jb->nkb", -1.0)
    untw_re = back_re * cos_t - back_im * sin_t
    untw_im = back_im * cos_t + back_re * sin_t
    final_re, final_im = rotate(untw_re, untw_im, cos_a, sin_a, "nkb,ka->nab", -1.0)
    return jnp.stack([final_re.reshape(count, width), final_im.reshape(count, width)]) / width


def added_up(value, axis):
    count = lax.axis_size(axis)
    if count & (count - 1):
        return lax.psum(value, axis)
    reach = 1
    while reach < count:
        value = value + lax.ppermute(value, axis, [(i, i ^ reach) for i in range(count)])
        reach *= 2
    return value


def lateral_work(parts):
    return (transform(parts[0]), transform(parts[1]))


def multiplier_revision(
    population_multiplier,
    holeburn_multiplier,
    measured_rightward,
    measured_leftward,
    rightward_wave,
    leftward_wave,
    population_level,
    holeburn_magnitude,
    attenuation_factor,
    transverse_curvature,
):
    rightward_inphase, rightward_quadrature = (rightward_wave[0], rightward_wave[1])
    leftward_inphase, leftward_quadrature = (leftward_wave[0], leftward_wave[1])
    measured_rightward_inphase, measured_rightward_quadrature = (
        measured_rightward[0],
        measured_rightward[1],
    )
    measured_leftward_inphase, measured_leftward_quadrature = (
        measured_leftward[0],
        measured_leftward[1],
    )
    surplus_population = population_level - 1.0
    amplification_inphase = 1.0 + 0.5 * (GAIN_SLOPE_RATE * surplus_population - attenuation_factor)
    amplification_quadrature = 0.5 * GAIN_SLOPE_RATE * ALPHA_LINEWIDTH * surplus_population
    joined_waves = COUPLING * holeburn_magnitude
    population_derivative = (
        2.0 * CLOCK_DELTA * GAIN_SLOPE_RATE * surplus_population * population_multiplier
    )
    holeburn_derivative = 2.0 * CLOCK_DELTA * holeburn_multiplier
    revised_rightward_inphase = (
        amplification_inphase * measured_rightward_inphase
        - amplification_quadrature * measured_rightward_quadrature
        + joined_waves * measured_leftward_quadrature
        - population_derivative * rightward_inphase
        + holeburn_derivative * leftward_inphase
    )
    revised_rightward_quadrature = (
        amplification_inphase * measured_rightward_quadrature
        + amplification_quadrature * measured_rightward_inphase
        - joined_waves * measured_leftward_inphase
        - population_derivative * rightward_quadrature
        + holeburn_derivative * leftward_quadrature
    )
    revised_leftward_inphase = (
        amplification_inphase * measured_leftward_inphase
        - amplification_quadrature * measured_leftward_quadrature
        + joined_waves * measured_rightward_quadrature
        - population_derivative * leftward_inphase
        + holeburn_derivative * rightward_inphase
    )
    revised_leftward_quadrature = (
        amplification_inphase * measured_leftward_quadrature
        + amplification_quadrature * measured_leftward_inphase
        - joined_waves * measured_rightward_inphase
        - population_derivative * leftward_quadrature
        + holeburn_derivative * rightward_quadrature
    )
    light_intensity = (
        rightward_inphase * rightward_inphase
        + rightward_quadrature * rightward_quadrature
        + leftward_inphase * leftward_inphase
        + leftward_quadrature * leftward_quadrature
    )
    amplification_share = (
        measured_rightward_inphase * (rightward_inphase + ALPHA_LINEWIDTH * rightward_quadrature)
        + measured_rightward_quadrature
        * (rightward_quadrature - ALPHA_LINEWIDTH * rightward_inphase)
        + measured_leftward_inphase * (leftward_inphase + ALPHA_LINEWIDTH * leftward_quadrature)
        + measured_leftward_quadrature * (leftward_quadrature - ALPHA_LINEWIDTH * leftward_inphase)
    )
    revised_population = (
        population_multiplier
        * (1.0 - CLOCK_DELTA / DENSITY_LIFETIME - CLOCK_DELTA * GAIN_SLOPE_RATE * light_intensity)
        + TRANSVERSE_DIFFUS * transverse_curvature
        + 0.5 * GAIN_SLOPE_RATE * amplification_share
    )
    fresh_holeburn = holeburn_multiplier * (1.0 - CLOCK_DELTA / GRATING_LIFE) + COUPLING * (
        measured_rightward_quadrature * leftward_inphase
        - measured_rightward_inphase * leftward_quadrature
        + measured_leftward_quadrature * rightward_inphase
        - measured_leftward_inphase * rightward_quadrature
    )
    return (
        jnp.stack([revised_rightward_inphase, revised_rightward_quadrature]),
        jnp.stack([revised_leftward_inphase, revised_leftward_quadrature]),
        revised_population,
        fresh_holeburn,
    )


def per_device(
    ending_rightward_adjoint,
    ending_leftward_adjoint,
    ending_population_adjoint,
    ending_holeburn_adjoint,
    history_rightward,
    history_leftward,
    history_population,
    history_holeburn,
    segment_passive_attenuation,
):
    columns = ending_rightward_adjoint.shape[2]
    rows = ending_rightward_adjoint.shape[1]
    blocks = lax.axis_size("gz")
    position = lax.axis_index("gz")
    cells = rows * blocks
    zpos = (position * rows + jnp.arange(rows, dtype=jnp.int32)).astype(jnp.float32)
    scaling_factor = 1.0 + 2.0 * zpos / (cells - 1)
    rightward_multiplier, leftward_multiplier = (ending_rightward_adjoint, ending_leftward_adjoint)
    population_multiplier, holeburn_multiplier = (
        ending_population_adjoint,
        ending_holeburn_adjoint,
    )
    attenuation_factor = segment_passive_attenuation.astype(jnp.float32)
    shape_curve = jnp.zeros((columns,), jnp.float32)
    for moment_position in range(history_rightward.shape[0] - 1, -1, -1):
        shape_curve = shape_curve + jnp.sum(scaling_factor[:, None] * population_multiplier, axis=0)
        above = passed_along(rightward_multiplier[:, :1, :], "gz", -1)
        below = passed_along(leftward_multiplier[:, -1:, :], "gz", 1)
        top_row = jnp.where(
            position == blocks - 1, FRONT_FACET * leftward_multiplier[:, -1:, :], above
        )
        bottom_row = jnp.where(position == 0, REAR_FACET * rightward_multiplier[:, :1, :], below)
        lam_fwd = jnp.concatenate([rightward_multiplier[:, 1:, :], top_row], axis=1)
        lam_bwd = jnp.concatenate([bottom_row, leftward_multiplier[:, :-1, :]], axis=1)
        whole_fwd, whole_bwd = (
            lax.all_gather(lam_fwd, "gx", axis=2, tiled=True),
            lax.all_gather(lam_bwd, "gx", axis=2, tiled=True),
        )
        start = lax.axis_index("gx") * columns
        done_fwd, done_bwd = lateral_work((whole_fwd, whole_bwd))
        measured_rightward = lax.dynamic_slice_in_dim(done_fwd, start, columns, 2)
        measured_leftward = lax.dynamic_slice_in_dim(done_bwd, start, columns, 2)
        bordered_array = with_halo(population_multiplier, (("gx", 1),), 1)
        transverse_curvature = (
            bordered_array[:, 2:] + bordered_array[:, :-2] - 2.0 * population_multiplier
        )
        rightward_multiplier, leftward_multiplier, population_multiplier, holeburn_multiplier = (
            multiplier_revision(
                population_multiplier,
                holeburn_multiplier,
                measured_rightward,
                measured_leftward,
                history_rightward[moment_position].astype(jnp.float32),
                history_leftward[moment_position].astype(jnp.float32),
                history_population[moment_position].astype(jnp.float32),
                history_holeburn[moment_position].astype(jnp.float32),
                attenuation_factor,
                transverse_curvature,
            )
        )
    total = added_up(shape_curve, "gz")
    derivative_vector = CLOCK_DELTA * total / math.sqrt(cells)
    return (
        rightward_multiplier,
        leftward_multiplier,
        population_multiplier,
        holeburn_multiplier,
        derivative_vector,
    )

LANES = 128
TILE = 16
POWER = 12
STRETCH = 1211.0
SCALE_LANE = 8


def lateral_matrices(width, blocks):
    lanes = width // blocks
    k = np.arange(width)
    signed = np.where(k < width // 2, k, k - width).astype(np.float64)
    response = np.fft.ifft(np.exp(1j * signed * signed * (DIFF / (width / 2) ** 2)))
    step = np.arange(lanes)
    shift = lanes * np.arange(blocks)[:, None, None] + step[None, None, :] - step[None, :, None]
    kernels = np.fft.fft(response[shift % width], axis=0) / blocks
    top = np.concatenate([kernels.real, kernels.imag], axis=2)
    low = np.concatenate([-kernels.imag, kernels.real], axis=2)
    whole = np.concatenate([top, low], axis=1)
    first = whole.astype(ml_dtypes.bfloat16)
    rest = (whole - first.astype(np.float64)).astype(ml_dtypes.bfloat16)
    return np.stack([first, rest], axis=1)


def block_dft(values, sign):
    count = len(values)
    if count == 1:
        return values
    even = block_dft(values[0::2], sign)
    odd = block_dft(values[1::2], sign)
    out = [None] * count
    for k in range(count // 2):
        (er, ei), (wr, wi) = even[k], odd[k]
        if 4 * k == count:
            plus, minus = (er - wi, ei + wr), (er + wi, ei - wr)
            out[k], out[k + count // 2] = (plus, minus) if sign > 0 else (minus, plus)
            continue
        if k:
            c, s = math.cos(2 * math.pi * k / count), sign * math.sin(2 * math.pi * k / count)
            if 8 * k == count:
                wr, wi = (c * (wr - wi), c * (wr + wi)) if sign > 0 else (c * (wr + wi), c * (wi - wr))
            elif 8 * k == 3 * count:
                wr, wi = (c * (wr + wi), c * (wi - wr)) if sign > 0 else (c * (wr - wi), c * (wr + wi))
            else:
                wr, wi = c * wr - s * wi, c * wi + s * wr
        out[k] = (er + wr, ei + wi)
        out[k + count // 2] = (er - wr, ei - wi)
    return out


def lane(j):
    return pl.ds(pl.multiple_of(j * LANES, LANES), LANES)


def slab(j, rows):
    return pl.ds(pl.multiple_of(j * rows, rows), rows)


def fetch(pairs, sems, first=0):
    copies = [pltpu.make_async_copy(a, b, sems.at[first + i]) for i, (a, b) in enumerate(pairs)]
    for copy in copies:
        copy.start()
    return copies


def rows_of(info, rows, other):
    part = 1 - info[4] if other else info[4]
    return pl.ds(pl.multiple_of(part * rows, rows), rows)


def spread(field, work):
    rows = field.shape[1]
    blocks = work.shape[0]

    @pl.loop(0, rows // 8)
    def _(g):
        at = slab(g, 8)
        values = [
            (field[0, at, j * LANES : (j + 1) * LANES], field[1, at, j * LANES : (j + 1) * LANES])
            for j in range(blocks)
        ]
        for q, (re, im) in enumerate(block_dft(values, -1)):
            work[q, at, :LANES] = re
            work[q, at, LANES:] = im


def multiply(work, matrices):
    rows = work.shape[1]

    @pl.loop(0, work.shape[0], unroll=True)
    def _(q):
        value = work[q]
        first = value.astype(jnp.bfloat16)
        rest = (value - first.astype(jnp.float32)).astype(jnp.bfloat16)
        both = jnp.dot(
            jnp.concatenate([first, rest]), matrices[q, 0], preferred_element_type=jnp.float32
        )
        fine = jnp.dot(first, matrices[q, 1], preferred_element_type=jnp.float32)
        work[q] = both[:rows] + (both[rows:] + fine)


def gathered(work, at):
    values = [(work[q, at, :LANES], work[q, at, LANES:]) for q in range(work.shape[0])]
    return block_dft(values, 1)


def filtered(field, work, matrices, copy):
    spread(field, work)
    copy.wait()
    multiply(work, matrices)


def write_filtered(info, work, forward, backward, inner, outer):
    rows = work.shape[1] // 2
    for target, base, offset in ((forward, 0, 0), (backward, rows, 8)):

        @pl.loop(0, rows // 8)
        def _(g):
            here = pl.ds(pl.multiple_of(g * 8 + offset, 8), 8)
            for j, pair in enumerate(gathered(work, pl.ds(pl.multiple_of(g * 8 + base, 8), 8))):
                for part in range(2):
                    target[part, here, j * LANES : (j + 1) * LANES] = pair[part]

    low = info[4] == 0
    for part in range(2):
        first, last = forward[part, 0:1, :], backward[part, rows + 7 : rows + 8, :]
        inner[part : part + 1, :] = jnp.where(low, last, first)
        outer[part : part + 1, :] = jnp.where(low, first, last)


def size_of(largest):
    top = jnp.max(jnp.max(largest, axis=1, keepdims=True), axis=0, keepdims=True)
    return jnp.maximum(top, 1e-30).astype(jnp.bfloat16).astype(jnp.float32)


def encoded(value, size):
    unit = value * (STRETCH / size)
    square = unit * unit
    fourth = square * square
    return (fourth * fourth * square * (unit * jnp.abs(unit))).astype(jnp.bfloat16)


def decoded(code, size):
    value = code.astype(jnp.float32)
    root = jnp.exp2(jnp.log(jnp.abs(value)) * (1.0 / (POWER * math.log(2.0)))) * (size / STRETCH)
    return jnp.where(value < 0.0, -root, root)


def side_tile(columns, rows):
    index = lax.broadcasted_iota(jnp.int32, (rows, LANES), 1)
    tile = jnp.zeros((rows, LANES), jnp.float32)
    for at, column in columns:
        tile = jnp.where(index == at, column, tile)
    return tile.astype(jnp.bfloat16)


def sizes_in(tile, count):
    value = tile.astype(jnp.float32)
    return [value[0:1, SCALE_LANE + i : SCALE_LANE + i + 1] for i in range(count)]


def updated(fr, fi, br, bi, wave, population, hole, loss, carrier, grating, lap):
    rr, ri, lr, li = wave
    surplus = population - 1.0
    gain_re = 1.0 + 0.5 * (GAIN_SLOPE_RATE * surplus - loss)
    gain_im = (0.5 * GAIN_SLOPE_RATE * ALPHA_LINEWIDTH) * surplus
    joined = COUPLING * hole
    drive = (2.0 * CLOCK_DELTA * GAIN_SLOPE_RATE) * surplus * carrier
    mix = (2.0 * CLOCK_DELTA) * grating
    new_fr = gain_re * fr - gain_im * fi + joined * bi - drive * rr + mix * lr
    new_fi = gain_re * fi + gain_im * fr - joined * br - drive * ri + mix * li
    new_br = gain_re * br - gain_im * bi + joined * fi - drive * lr + mix * rr
    new_bi = gain_re * bi + gain_im * br - joined * fr - drive * li + mix * ri
    light = rr * rr + ri * ri + lr * lr + li * li
    share = (
        fr * (rr + ALPHA_LINEWIDTH * ri)
        + fi * (ri - ALPHA_LINEWIDTH * rr)
        + br * (lr + ALPHA_LINEWIDTH * li)
        + bi * (li - ALPHA_LINEWIDTH * lr)
    )
    new_carrier = (
        carrier * ((1.0 - CLOCK_DELTA / DENSITY_LIFETIME) - (CLOCK_DELTA * GAIN_SLOPE_RATE) * light)
        + TRANSVERSE_DIFFUS * lap
        + (0.5 * GAIN_SLOPE_RATE) * share
    )
    new_grating = grating * (1.0 - CLOCK_DELTA / GRATING_LIFE) + COUPLING * (
        fi * lr - fr * li + bi * rr - br * ri
    )
    return new_fr, new_fi, new_br, new_bi, new_carrier, new_grating


def curvature(left, mid, right, weight_left, weight_right):
    index = lax.broadcasted_iota(jnp.int32, mid.shape, 1)
    below = jnp.where(index == 0, pltpu.roll(left, 1, 1) * weight_left, pltpu.roll(mid, 1, 1))
    above = jnp.where(
        index == LANES - 1,
        pltpu.roll(right, LANES - 1, 1) * weight_right,
        pltpu.roll(mid, LANES - 1, 1),
    )
    return below + above - 2.0 * mid


def send_fields_kernel(info, forward, backward, out, fields, sems):
    rows, columns = fields.shape[1:]
    half = columns // LANES
    at = rows_of(info, rows, True)
    copies = fetch(
        [
            (ref.at[part, at, :], fields.at[2 * f + part])
            for f, ref in enumerate((forward, backward))
            for part in range(2)
        ],
        sems,
    )
    sizes = []
    for i in range(4):
        copies[i].wait()
        size = size_of(jnp.abs(fields[i]))
        sizes.append((SCALE_LANE + i, size))
        put_tiles(out, i * half, encoded(fields[i], size))
    out[4 * half * rows :, :] = side_tile(sizes, rows)


def put_tiles(out, first, value):
    rows, columns = value.shape
    for j in range(columns // LANES):
        at = (first + j) * rows
        out[at : at + rows, :] = value[:, j * LANES : (j + 1) * LANES]


def history_rows(forward, backward, population, hole, s, at):
    return [
        forward.at[s, 0, at, :], forward.at[s, 1, at, :], backward.at[s, 0, at, :],
        backward.at[s, 1, at, :], population.at[s, at, :], hole.at[s, at, :],
    ]


def into_rows(parts, target, first, rows):
    return [(part, target.at[pl.ds(first + i * rows, rows), :]) for i, part in enumerate(parts)]


def send_later_kernel(steps, info, forward, backward, population, hole, final, *refs):
    targets, sems = refs[:-1], refs[-1]
    rows = targets[0].shape[0] // 6
    history = (forward, backward, population, hole)
    pairs = []
    for i, s in enumerate(steps):
        for k, other in enumerate((True, False)):
            at = rows_of(info, rows, other)
            pairs += into_rows(history_rows(*history, s, at), targets[2 * i + k], 0, rows)
    pairs += into_rows(history_rows(*history, 0, pl.ds(0, 2 * rows)), final, 0, 2 * rows)
    for copy in fetch(pairs, sems):
        copy.wait()


def send_first_kernel(
    s, info, loss, carrier, grating, forward, backward, population, hole,
    own_loss, own, own_carrier, own_grating, out, own_edge, states, ends, sems,
):
    rows, columns = own_carrier.shape
    theirs, mine = rows_of(info, rows, True), rows_of(info, rows, False)
    history = (forward, backward, population, hole)
    copies = fetch(
        [(carrier.at[theirs, :], states.at[0]), (grating.at[theirs, :], states.at[1])]
        + into_rows([loss.at[theirs, :]], out, 0, rows)
        + into_rows(history_rows(*history, s, theirs), out, 3 * rows, rows)
        + [(loss.at[mine, :], own_loss), (carrier.at[mine, :], own_carrier)]
        + [(grating.at[mine, :], own_grating)]
        + into_rows(history_rows(*history, s, mine), own, 0, rows)
        + [
            (part, ends.at[k, i])
            for k in range(2)
            for i, part in enumerate(
                history_rows(*history, 1, pl.ds(k * (2 * rows - TILE), TILE))
            )
        ],
        sems,
    )
    for copy in copies[:2]:
        copy.wait()
    sizes = []
    for i in range(2):
        size = size_of(jnp.abs(states[i]))
        sizes.append(jnp.broadcast_to(size, (1, columns)))
        out[(1 + i) * rows : (2 + i) * rows, :] = encoded(states[i], size)
    for copy in copies[2:]:
        copy.wait()
    low = info[4] == 0
    top = [ends[0, i].astype(jnp.float32)[:1] for i in range(6)]
    foot = [ends[1, i].astype(jnp.float32)[TILE - 1 :] for i in range(6)]
    own_edge[...] = jnp.concatenate([jnp.where(low, a, b) for a, b in zip(top, foot)])
    sizes += [jnp.where(low, b, a) for a, b in zip(top, foot)]
    sizes.append(jnp.zeros((TILE - 8, columns), jnp.float32))
    out[9 * rows :, :] = jnp.concatenate(sizes).astype(jnp.bfloat16)


def enter_kernel(
    info, forward, backward, other, source, tp, tq, inner, outer, field, work, matrices, sem, sems
):
    copy = pltpu.make_async_copy(source, matrices, sem)
    rows, width = field.shape[1] // 2, field.shape[2]
    columns = width // 2
    half = columns // LANES
    at = rows_of(info, rows, False)
    copies = fetch(
        [
            (ref.at[:, at, :], field.at[:, f * rows : (f + 1) * rows, :columns])
            for f, ref in enumerate((forward, backward))
        ],
        sems,
    )
    copy.start()
    sizes = sizes_in(other[4 * half * rows :, :], 4)
    for f in range(2):
        for part in range(2):

            @pl.loop(0, half, unroll=2)
            def _(j):
                code = other[slab((2 * f + part) * half + j, rows), :]
                field[part, f * rows : (f + 1) * rows, lane(half + j)] = decoded(
                    code, sizes[2 * f + part]
                )

    for held in copies:
        held.wait()
    filtered(field, work, matrices, copy)
    write_filtered(info, work, tp, tq, inner, outer)


def rows_update(
    info, tp, tq, inner, outer, carrier, grating, own, other, own_loss, other_loss,
    field, new_carrier, new_grating, sums_in, sums, cells, last
):
    rows, width = carrier.shape
    half = width // LANES // 2
    columns = half * LANES
    mid = jnp.where(info[0] == 0, 1.0, 0.0)
    wrap = 1.0 - mid
    low = info[4] == 0
    is_first, is_last = info[1], info[2]
    row_index = lax.broadcasted_iota(jnp.int32, (TILE, LANES), 0)
    zero = jnp.zeros((8, LANES), jnp.float32)

    def step(jj, most):
        for side in range(2):
            j = jj + side * half
            here = lane(j)
            left_at = lane(jnp.where(j == 0, 2 * half - 1, j - 1))
            right_at = lane(jnp.where(j == 2 * half - 1, 0, j + 1))
            swapped = lane(jj + (1 - side) * half)
            weight_left = jnp.where(jj == 0, wrap if side == 0 else mid, 1.0)
            weight_right = jnp.where(jj == half - 1, mid if side == 0 else wrap, 1.0)
            total = zero
            for r in range(0, rows, TILE):
                at = slice(r, r + TILE)

                held, begin = (own, other)[side]

                def part_of(i):
                    tile = begin + i * rows + r
                    return held[tile : tile + TILE, lane(jj)].astype(jnp.float32)

                loss = (own_loss, other_loss)[side][at, lane(jj)].astype(jnp.float32)
                f = [tp[part, r + 1 : r + 1 + TILE, here] for part in range(2)]
                b = [tq[part, r + 7 : r + 7 + TILE, here] for part in range(2)]
                if r + TILE == rows:
                    for part in range(2):
                        facet = FRONT_FACET * tq[part, rows + 7 : rows + 8, here]
                        edge = jnp.where(
                            low, inner[part : part + 1, swapped], outer[part : part + 1, here]
                        )
                        edge = jnp.where(is_last, facet, edge)
                        f[part] = jnp.where(row_index == TILE - 1, edge, f[part])
                if r == 0:
                    for part in range(2):
                        facet = REAR_FACET * tp[part, 0:1, here]
                        edge = jnp.where(
                            low, outer[part : part + 1, here], inner[part : part + 1, swapped]
                        )
                        edge = jnp.where(is_first, facet, edge)
                        b[part] = jnp.where(row_index == 0, edge, b[part])
                c = carrier[at, here]
                lap = curvature(
                    carrier[at, left_at], c, carrier[at, right_at], weight_left, weight_right
                )
                out = updated(
                    *f, *b, [part_of(i) for i in range(4)], part_of(4), part_of(5), loss,
                    c, grating[at, here], lap,
                )
                field[0, r : r + TILE, here] = out[0]
                field[1, r : r + TILE, here] = out[1]
                field[0, rows + r : rows + r + TILE, here] = out[2]
                field[1, rows + r : rows + r + TILE, here] = out[3]
                new_carrier[at, here] = out[4]
                new_grating[at, here] = out[5]
                z = (info[3] + r + row_index).astype(jnp.float32)
                weighted = (1.0 + 2.0 * z / (cells - 1)) * ((c + out[4]) if last else c)
                for k in range(0, TILE, 8):
                    total = total + weighted[k : k + 8]
                if last and side == 1:
                    for k in range(0, TILE, 8):
                        most = (
                            jnp.maximum(most[0], jnp.abs(out[4][k : k + 8])),
                            jnp.maximum(most[1], jnp.abs(out[5][k : k + 8])),
                        )
            summed = jnp.sum(total, axis=0, keepdims=True)
            sums[:, here] = summed if sums_in is None else summed + sums_in[:, here]
        return most

    return lax.fori_loop(0, half, step, (zero, zero))


def first_step_kernel(
    cells, info, tp, tq, inner, outer, my_carrier, my_grating, loss, own, own_edge, other, source,
    new_tp, new_tq, new_inner, new_outer, new_carrier, new_grating, sums,
    carrier, grating, field, work, matrices, sem,
):
    copy = pltpu.make_async_copy(source, matrices, sem)
    copy.start()
    rows, columns = my_carrier.shape
    half = columns // LANES
    extra = other[9 * rows :, :].astype(jnp.float32)
    sizes = [extra[0:1, 0:1], extra[1:2, 0:1]]
    low = info[4] == 0
    new_outer[2:8, :columns] = own_edge[...]
    new_outer[2:8, columns:] = extra[2:8]
    for part, ref in ((0, loss), (1, other)):
        top = ref[:TILE, :].astype(jnp.float32)[:1]
        foot = ref[rows - TILE : rows, :].astype(jnp.float32)[TILE - 1 :]
        new_outer[8:9, part * columns : (part + 1) * columns] = jnp.where(low, top, foot)
    for i, (whole, mine) in enumerate(((carrier, my_carrier), (grating, my_grating))):
        whole[:, :columns] = mine[...]

        @pl.loop(0, half, unroll=2)
        def _(j):
            whole[:, lane(half + j)] = decoded(
                other[(1 + i) * rows : (2 + i) * rows, lane(j)], sizes[i]
            )

    rows_update(
        info, tp, tq, inner, outer, carrier, grating, (own, 0), (other, 3 * rows), loss, other,
        field, new_carrier, new_grating, None, sums, cells, False,
    )
    filtered(field, work, matrices, copy)
    write_filtered(info, work, new_tp, new_tq, new_inner, new_outer)


def middle_step_kernel(
    cells, info, tp, tq, inner, outer, carrier, grating, loss, own, other, other_loss, sums_in,
    source, new_tp, new_tq, new_inner, new_outer, new_carrier, new_grating, sums,
    field, work, matrices, sem,
):
    copy = pltpu.make_async_copy(source, matrices, sem)
    copy.start()
    rows_update(
        info, tp, tq, inner, outer, carrier, grating, (own, 0), (other, 0), loss, other_loss,
        field, new_carrier, new_grating, sums_in, sums, cells, False,
    )
    filtered(field, work, matrices, copy)
    write_filtered(info, work, new_tp, new_tq, new_inner, new_outer)
    rows = carrier.shape[0]
    low = info[4] == 0
    for part in range(2):
        new_outer[2 + part : 3 + part, :] = jnp.where(
            low, new_tp[part, 1:2, :], new_tq[part, rows + 6 : rows + 7, :]
        )
    for i, ref in enumerate((new_carrier, new_grating)):
        new_outer[4 + i : 5 + i, :] = jnp.where(low, ref[0:1, :], ref[rows - 1 : rows, :])


def row_beyond(info, tp, tq, outer, beyond):
    rows = tp.shape[1] - 8
    low = info[4] == 0
    xr, xi, carrier, grating = (outer[i : i + 1, :] for i in range(2, 6))
    yr, yi = (
        jnp.where(low, tp[part, 0:1, :], tq[part, rows + 7 : rows + 8, :]) for part in range(2)
    )
    rr, ri, lr, li, population, hole, loss = (beyond[i : i + 1, :] for i in range(2, 9))
    surplus = population - 1.0
    gain_re = 1.0 + 0.5 * (GAIN_SLOPE_RATE * surplus - loss)
    gain_im = (0.5 * GAIN_SLOPE_RATE * ALPHA_LINEWIDTH) * surplus
    joined = COUPLING * hole
    drive = (2.0 * CLOCK_DELTA * GAIN_SLOPE_RATE) * surplus * carrier
    mix = (2.0 * CLOCK_DELTA) * grating
    near_re, near_im = jnp.where(low, lr, rr), jnp.where(low, li, ri)
    far_re, far_im = jnp.where(low, rr, lr), jnp.where(low, ri, li)
    new_re = gain_re * xr - gain_im * xi + joined * yi - drive * near_re + mix * far_re
    new_im = gain_re * xi + gain_im * xr - joined * yr - drive * near_im + mix * far_im
    return new_re, new_im


def leave_step_kernel(
    cells, info, tp, tq, inner, outer, beyond, carrier, grating, loss, own, other, other_loss,
    sums_in, field, kept_carrier, kept_grating, sides, sent, own_sums,
    sums, new_carrier, new_grating,
):
    rows, width = carrier.shape
    columns = width // 2
    half = columns // LANES
    most = rows_update(
        info, tp, tq, inner, outer, carrier, grating, (own, 0), (other, 0), loss, other_loss,
        field, new_carrier, new_grating, sums_in, sums, cells, True,
    )
    for part, value in enumerate(row_beyond(info, tp, tq, outer, beyond)):
        field[part, 2 * rows :, :] = jnp.broadcast_to(value, (8, width))
    mid = jnp.where(info[0] == 0, 1.0, 0.0)
    wrap = 1.0 - mid
    kept_carrier[...] = new_carrier[:, :columns]
    kept_grating[...] = new_grating[:, :columns]
    first, before = new_carrier[:, 0:1] * wrap, new_carrier[:, columns - 1 : columns] * mid
    after, final = new_carrier[:, columns : columns + 1] * mid, new_carrier[:, width - 1 :] * wrap
    sides[0] = jnp.broadcast_to(final, (rows, LANES))
    sides[1] = jnp.broadcast_to(after, (rows, LANES))
    pairs = []
    for at, value in ((0, before), (2, first)):
        coarse = value.astype(jnp.bfloat16).astype(jnp.float32)
        pairs += [(at, coarse), (at + 1, value - coarse)]
    for i, field_of in enumerate((new_carrier, new_grating)):
        size = size_of(most[i])
        pairs.append((SCALE_LANE + i, size))

        @pl.loop(0, half, unroll=2)
        def _(j):
            sent[slab(i * half + j, rows), :] = encoded(field_of[:, lane(half + j)], size)

    sent[2 * half * rows : (2 * half + 1) * rows, :] = side_tile(pairs, rows)
    own_sums[...] = jnp.concatenate([sums[:, j * LANES : (j + 1) * LANES] for j in range(half)])
    value = jnp.concatenate([sums[:, j * LANES : (j + 1) * LANES] for j in range(half, 2 * half)])
    parts = []
    for _ in range(3):
        parts.append(value.astype(jnp.bfloat16).astype(jnp.float32))
        value = value - parts[-1]
    parts.append(jnp.zeros((rows - 3 * half, LANES), jnp.float32))
    sent[(2 * half + 1) * rows :, :] = jnp.concatenate(parts).astype(jnp.bfloat16)


def fold_kernel(info, own_sums, came, shares):
    half = own_sums.shape[0]
    value = came[...].astype(jnp.float32)
    total = own_sums[...]
    for i in range(3):
        total = total + value[i * half : (i + 1) * half]
    for i in range(shares.shape[0]):
        shares[i] = total


def leave_filter_kernel(info, field, source, kept, sent, edge, work, matrices, sem):
    copy = pltpu.make_async_copy(source, matrices, sem)
    copy.start()
    rows, width = (field.shape[1] - 8) // 2, field.shape[2]
    half = width // LANES // 2
    filtered(field, work, matrices, copy)
    pairs = []
    zero = jnp.zeros((8, LANES), jnp.float32)
    for f in range(2):

        def unmix(g, most):
            at = pl.ds(pl.multiple_of(g * 8 + f * rows, 8), 8)
            for j, pair in enumerate(gathered(work, at)):
                for part in range(2):
                    if j < half:
                        kept[part, at, j * LANES : (j + 1) * LANES] = pair[part]
                    else:
                        work[j, at, part * LANES : (part + 1) * LANES] = pair[part]
                        most = jnp.maximum(most, jnp.abs(pair[part]))
            return most

        size = size_of(lax.fori_loop(0, rows // 8, unmix, zero))
        pairs.append((SCALE_LANE + f, size))

        @pl.loop(0, half, unroll=2)
        def _(j):
            for part in range(2):
                value = work[half + j, f * rows : (f + 1) * rows, part * LANES : (part + 1) * LANES]
                sent[slab((2 * f + part) * half + j, rows), :] = encoded(value, size)

    ends = gathered(work, slice(2 * rows, 2 * rows + 8))
    for part in range(2):
        for j in range(half):
            edge[part : part + 1, j * LANES : (j + 1) * LANES] = ends[j][part][:1]
    far = jnp.concatenate([ends[j][part][:1] for part in range(2) for j in range(half, 2 * half)])
    size = size_of(jnp.abs(far))
    pairs.append((SCALE_LANE + 2, size))
    sent[4 * half * rows : (4 * half + 1) * rows, :] = side_tile(pairs, rows)
    spare = jnp.zeros((rows - 2 * half, LANES), jnp.float32)
    sent[(4 * half + 1) * rows :, :] = encoded(jnp.concatenate([far, spare]), size)


def final_kernel(
    cells, info, kept, kept_carrier, kept_grating, sides, fields, pair, edge, partial, loss, history,
    out_forward, out_backward, out_carrier, out_grating, out_sums,
    tp, tq, carrier, grating,
):
    rows, columns = kept_carrier.shape
    half = columns // LANES
    total = partial[0]
    for i in range(1, partial.shape[0]):
        total = total + partial[i]
    out_sums[...] = total * (CLOCK_DELTA / math.sqrt(cells))
    mine = info[4] * rows
    theirs = (1 - info[4]) * rows
    low = info[4] == 0
    extra = pair[2 * half * rows : (2 * half + 1) * rows, :]
    size_carrier, size_grating = sizes_in(extra, 2)
    sizes = fields[4 * half * rows : (4 * half + 1) * rows, :]
    size_forward, size_backward, size_edge = sizes_in(sizes, 3)
    ends = decoded(fields[(4 * half + 1) * rows :, :], size_edge)
    extra = extra.astype(jnp.float32)

    def at(start, offset, count):
        return pl.ds(pl.multiple_of(start + offset, 8), count)

    for part in range(2):
        tp[part, at(mine, 0, rows), :] = kept[part, :rows, :]
        tq[part, at(mine, 8, rows), :] = kept[part, rows:, :]
    carrier[at(mine, 0, rows), LANES : LANES + columns] = kept_carrier[...]
    carrier[at(mine, 0, rows), :LANES] = sides[0]
    carrier[at(mine, 0, rows), LANES + columns :] = sides[1]
    carrier[at(theirs, 0, rows), :LANES] = jnp.broadcast_to(
        extra[:, 0:1] + extra[:, 1:2], (rows, LANES)
    )
    carrier[at(theirs, 0, rows), LANES + columns :] = jnp.broadcast_to(
        extra[:, 2:3] + extra[:, 3:4], (rows, LANES)
    )
    grating[at(mine, 0, rows), :] = kept_grating[...]

    @pl.loop(0, half, unroll=2)
    def _(j):
        carrier[at(theirs, 0, rows), lane(1 + j)] = decoded(
            pair[slab(j, rows), :], size_carrier
        )
        grating[at(theirs, 0, rows), lane(j)] = decoded(
            pair[slab(half + j, rows), :], size_grating
        )
        for part in range(2):
            tp[part, at(theirs, 0, rows), lane(j)] = decoded(
                fields[slab(part * half + j, rows), :], size_forward
            )
            tq[part, at(theirs, 8, rows), lane(j)] = decoded(
                fields[slab((2 + part) * half + j, rows), :], size_backward
            )

    all_rows = 2 * rows
    for part in range(2):
        near = edge[part : part + 1, :]
        far = jnp.concatenate([ends[part * half + j : part * half + j + 1] for j in range(half)], axis=1)
        next_edge = jnp.where(low, far, near)
        before_edge = jnp.where(low, near, far)
        front = FRONT_FACET * tq[part, all_rows + 7 : all_rows + 8, :]
        rear = REAR_FACET * tp[part, 0:1, :]
        tp[part, all_rows : all_rows + 1, :] = jnp.where(info[2], front, next_edge)
        tq[part, 7:8, :] = jnp.where(info[1], rear, before_edge)

    @pl.loop(0, half)
    def _(j):
        here = lane(j)
        for r in range(0, all_rows, TILE):
            row = slice(r, r + TILE)
            c = carrier[row, lane(j + 1)]
            lap = curvature(carrier[row, lane(j)], c, carrier[row, lane(j + 2)], 1.0, 1.0)
            parts = [
                history[i * all_rows + r : i * all_rows + r + TILE, here].astype(jnp.float32)
                for i in range(6)
            ]
            out = updated(
                tp[0, r + 1 : r + 1 + TILE, here], tp[1, r + 1 : r + 1 + TILE, here],
                tq[0, r + 7 : r + 7 + TILE, here], tq[1, r + 7 : r + 7 + TILE, here],
                parts[:4], parts[4], parts[5],
                loss[row, here].astype(jnp.float32), c, grating[row, here], lap,
            )
            out_forward[0, row, here] = out[0]
            out_forward[1, row, here] = out[1]
            out_backward[0, row, here] = out[2]
            out_backward[1, row, here] = out[3]
            out_carrier[row, here] = out[4]
            out_grating[row, here] = out[5]


def position(rows, whole):
    x, block, count = lax.axis_index("gx"), lax.axis_index("gz"), lax.axis_size("gz")
    high = lax.rem(x + block, 2)
    if whole:
        return x, block == 0, block == count - 1, block * rows, high
    place = 2 * block + high
    return x, place == 0, place == 2 * count - 1, place * rows, high


def whole_spec(shape):
    return pl.BlockSpec(shape, lambda i, n=len(shape): (0,) * n)


def call(name, kernel, rows, inputs, outputs, scratch, flops=0, grant=24, whole=False):
    arrays = [x[0] if isinstance(x, tuple) else x for x in inputs]
    specs = [x[1] if isinstance(x, tuple) else whole_spec(x.shape) for x in inputs]
    shapes = [jax.ShapeDtypeStruct(*out) for out in outputs]
    moved = sum(math.prod(s.shape) * s.dtype.itemsize for s in shapes)

    def body(*refs):
        kernel(position(rows, whole), *refs)

    return pl.pallas_call(
        body,
        grid=(1,),
        in_specs=specs,
        out_specs=[whole_spec(s.shape) for s in shapes],
        scratch_shapes=scratch,
        out_shape=shapes,
        compiler_params=pltpu.CompilerParams(vmem_limit_bytes=grant * 1024 * 1024),
        cost_estimate=pl.CostEstimate(
            flops=flops, bytes_accessed=moved + 4 * 1024 * 1024, transcendentals=0
        ),
        name=name,
    )(*arrays)


def per_pair(
    ending_rightward_adjoint,
    ending_leftward_adjoint,
    ending_population_adjoint,
    ending_holeburn_adjoint,
    history_rightward,
    history_leftward,
    history_population,
    history_holeburn,
    segment_passive_attenuation,
):
    cell_rows, columns = ending_population_adjoint.shape
    passes = history_population.shape[0]
    rows = cell_rows // 2
    half = columns // LANES
    blocks = 2 * half
    width = 2 * columns
    count = lax.axis_size("gz")
    cells = cell_rows * count
    x = lax.axis_index("gx")
    f32, bf16 = jnp.float32, jnp.bfloat16
    swap = [(0, 1), (1, 0)]
    in_place = pl.BlockSpec(memory_space=pltpu.HBM)

    def held(*arrays):
        return [(a, in_place) for a in arrays]

    def tiles(n):
        return ((n * rows, LANES), bf16)

    ends = held(ending_rightward_adjoint, ending_leftward_adjoint)
    planes = held(ending_population_adjoint, ending_holeburn_adjoint)
    history = held(history_rightward, history_leftward, history_population, history_holeburn)
    losses = held(segment_passive_attenuation)
    matrices = pltpu.with_memory_space_constraint(
        jnp.asarray(lateral_matrices(width, blocks)), pltpu.HBM
    )
    matrix_input = held(matrices)
    work = [
        pltpu.VMEM((blocks, 2 * rows, 2 * LANES), f32),
        pltpu.VMEM(matrices.shape, bf16),
        pltpu.SemaphoreType.DMA,
    ]
    field_scratch = pltpu.VMEM((2, 2 * rows, width), f32)
    def state_out(outer_rows):
        state = ((2, rows + 8, width), f32)
        return [state, state, ((2, width), f32), ((outer_rows, width), f32)]

    plane = ((rows, width), f32)
    plane_scratch = pltpu.VMEM((rows, width), f32)
    half_plane = ((rows, columns), f32)
    work_flops = 2 * 3 * 2 * rows * blocks * (2 * LANES) ** 2

    (coded,) = call(
        "send_fields", send_fields_kernel, rows, ends, [tiles(4 * half + 1)],
        [pltpu.VMEM((4, rows, columns), f32), pltpu.SemaphoreType.DMA((4,))], grant=62,
    )
    other_fields = lax.ppermute(coded, "gx", swap)
    loss, own_first, my_carrier, my_grating, sent_first, own_edge = call(
        "send_first", functools.partial(send_first_kernel, passes - 1), rows,
        [*losses, *planes, *history],
        [((rows, columns), bf16), ((6 * rows, columns), bf16), half_plane, half_plane,
         ((9 * rows + TILE, columns), bf16), ((6, columns), f32)],
        [pltpu.VMEM((2, rows, columns), f32), pltpu.VMEM((2, 6, TILE, columns), bf16),
         pltpu.SemaphoreType.DMA((30,))], grant=62,
    )
    steps = range(passes - 2, 0, -1)
    history_last, *later = call(
        "send_later", functools.partial(send_later_kernel, steps), rows, history,
        [((6 * cell_rows, columns), bf16)] + [((6 * rows, columns), bf16)] * (2 * len(steps)),
        [pltpu.SemaphoreType.DMA((12 * len(steps) + 6,))], grant=62,
    )
    sent_first, history_last, later, other_fields = lax.optimization_barrier(
        (sent_first, history_last, later, other_fields)
    )
    other_first = lax.ppermute(sent_first, "gx", swap)

    line = ("gz", "gx")
    neighbours = []
    for b in range(count - 1):
        top = (1 + b) % 2
        neighbours += [(2 * b + top, 2 * b + 2 + top), (2 * b + 2 + top, 2 * b + top)]

    def edges(inner, outer):
        outer = lax.ppermute(outer, line, neighbours)
        return lax.ppermute(inner, "gx", swap), outer

    tp, tq, inner, outer = call(
        "enter", enter_kernel, rows, [*ends, other_fields, *matrix_input],
        state_out(2), [field_scratch, *work, pltpu.SemaphoreType.DMA((2,))], work_flops,
    )
    inner, outer = edges(inner, outer)

    other_loss = (other_first, pl.BlockSpec((rows, columns), lambda i: (0, 0)))
    carrier = grating = sums = other = own = None
    for index, s in enumerate(range(passes - 1, 0, -1)):
        if index < len(steps):
            sent, own_next = later[2 * index : 2 * index + 2]
            sent, inner, outer = lax.optimization_barrier((sent, inner, outer))
            coming = lax.ppermute(sent, "gx", swap)
        shared = [tp, tq, inner, outer]
        if index == 0:
            tp, tq, inner, outer, carrier, grating, sums = call(
                "first_step", functools.partial(first_step_kernel, cells), rows,
                [*shared, my_carrier, my_grating, loss, own_first, own_edge, other_first,
                 *matrix_input],
                [*state_out(9), plane, plane, ((1, width), f32)],
                [plane_scratch, plane_scratch, field_scratch, *work], work_flops,
            )
        elif s > 1:
            tp, tq, inner, outer, carrier, grating, sums = call(
                "middle_step", functools.partial(middle_step_kernel, cells), rows,
                [*shared, carrier, grating, loss, own, other, other_loss, sums, *matrix_input],
                [*state_out(6), plane, plane, ((1, width), f32)],
                [field_scratch, *work], work_flops,
            )
        else:
            field, kept_carrier, kept_grating, sides, sent, sums = call(
                "leave_step", functools.partial(leave_step_kernel, cells), rows,
                [*shared, beyond, carrier, grating, loss, own, other, other_loss, sums],
                [((2, 2 * rows + 8, width), f32), half_plane, half_plane, ((2, rows, LANES), f32),
                 tiles(2 * half + 2), ((half, LANES), f32)],
                [pltpu.VMEM((1, width), f32), plane_scratch, plane_scratch],
            )
        if s > 1:
            inner, outer = edges(inner, outer)
            own, other = own_next, coming
            if index == 0:
                beyond = outer

    pair = lax.ppermute(sent, "gx", swap)
    kept, sent, edge = call(
        "leave_filter", leave_filter_kernel, rows, [field, *matrix_input],
        [((2, 2 * rows, columns), f32), tiles(4 * half + 2), ((2, columns), f32)],
        [pltpu.VMEM((blocks, 2 * rows + TILE, 2 * LANES), f32), *work[1:]], work_flops,
    )
    sent, pair = lax.optimization_barrier((sent, pair))
    fields = lax.ppermute(sent, "gx", swap)
    last_tile = pl.BlockSpec((rows, LANES), lambda i: (2 * half + 1, 0))
    (shares,) = call(
        "fold", fold_kernel, rows, [sums, (pair, last_tile)], [((count, half, LANES), f32)], [],
    )
    shares = lax.all_to_all(shares, "gz", 0, 0, tiled=True)

    *outs, total = call(
        "final", functools.partial(final_kernel, cells), cell_rows,
        [kept, kept_carrier, kept_grating, sides, fields, pair, edge, shares,
         segment_passive_attenuation, history_last],
        [((2, cell_rows, columns), f32), ((2, cell_rows, columns), f32),
         ((cell_rows, columns), f32), ((cell_rows, columns), f32), ((half, LANES), f32)],
        [pltpu.VMEM((2, cell_rows + 8, columns), f32), pltpu.VMEM((2, cell_rows + 8, columns), f32),
         pltpu.VMEM((cell_rows, columns + 2 * LANES), f32), pltpu.VMEM((cell_rows, columns), f32)],
        whole=True,
    )
    return (*outs, total.reshape(columns))


def shared_by_pairs(mesh, arguments):
    population = arguments[6]
    passes, cells, width = population.shape
    rows, columns = cells // mesh.shape["gz"], width // mesh.shape["gx"]
    return (
        mesh.shape["gx"] == 2
        and passes >= 4
        and 4 * columns <= rows // 2 * LANES
        and rows % (2 * TILE) == 0
        and columns % LANES == 0
        and (columns // LANES) & (columns // LANES - 1) == 0
        and width <= 4096
    )


def solution(mesh):
    def run(*arguments):
        body = per_pair if shared_by_pairs(mesh, arguments) else per_device
        return jax.shard_map(
            body,
            mesh=mesh,
            in_specs=(
                P(None, "gz", "gx"),
                P(None, "gz", "gx"),
                P("gz", "gx"),
                P("gz", "gx"),
                P(None, None, "gz", "gx"),
                P(None, None, "gz", "gx"),
                P(None, "gz", "gx"),
                P(None, "gz", "gx"),
                P("gz", "gx"),
            ),
            out_specs=(
                P(None, "gz", "gx"), P(None, "gz", "gx"), P("gz", "gx"), P("gz", "gx"), P("gx"),
            ),
            check_vma=False,
        )(*arguments)

    return run
```

```python
import functools
import math

import jax
import jax.numpy as jnp
import ml_dtypes
import numpy as np
from jax import lax
from jax.experimental import pallas as pl
from jax.experimental.pallas import tpu as pltpu
from jax.sharding import PartitionSpec as P

DIFF = 512


FRONT_FACET = 0.3
REAR_FACET = 0.9
GAIN_SLOPE_RATE = 0.3
ALPHA_LINEWIDTH = 2.0
COUPLING = 0.5
CLOCK_DELTA = 0.3
DENSITY_LIFETIME = 2.0
GRATING_LIFE = 0.75
TRANSVERSE_DIFFUS = 0.2


def passed_along(value, axis, steps):
    count = lax.axis_size(axis)
    initial, last = (max(0, -steps), min(count, count - steps))
    return lax.ppermute(value, axis, [(source, source + steps) for source in range(initial, last)])


def with_halo(block, sides, width):
    for axis, dim in sides:
        count = lax.axis_size(axis)
        forward = [(i, i + 1) for i in range(count - 1)]
        backward = [(target, source) for source, target in forward]
        low = lax.ppermute(
            lax.slice_in_dim(block, block.shape[dim] - width, None, axis=dim), axis, forward
        )
        high = lax.ppermute(lax.slice_in_dim(block, 0, width, axis=dim), axis, backward)
        block = jnp.concatenate([low, block, high], axis=dim)
    return block


def rotate(source_re, source_im, cosine, sine, form, sign):
    exact = lax.Precision.HIGHEST
    out_re = jnp.einsum(form, source_re, cosine, precision=exact) + sign * jnp.einsum(
        form, source_im, sine, precision=exact
    )
    out_im = jnp.einsum(form, source_im, cosine, precision=exact) - sign * jnp.einsum(
        form, source_re, sine, precision=exact
    )
    return (out_re, out_im)


def transform(stacked):
    count = stacked.shape[1]
    width = stacked.shape[2]
    second = min(128, width // 2)
    first = width // second
    two_pi = 2.0 * math.pi
    index_a = jnp.arange(first, dtype=jnp.int32)
    index_b = jnp.arange(second, dtype=jnp.int32)
    angle_a = two_pi * (index_a[:, None] * index_a[None, :] % first).astype(jnp.float32) / first
    angle_b = two_pi * (index_b[:, None] * index_b[None, :] % second).astype(jnp.float32) / second
    angle_t = two_pi * (index_a[:, None] * index_b[None, :] % width).astype(jnp.float32) / width
    cos_a, sin_a = (jnp.cos(angle_a), jnp.sin(angle_a))
    cos_b, sin_b = (jnp.cos(angle_b), jnp.sin(angle_b))
    cos_t, sin_t = (jnp.cos(angle_t), jnp.sin(angle_t))
    wavenum = index_a[:, None] + first * index_b[None, :]
    signed = jnp.where(wavenum < width // 2, wavenum, wavenum - width)
    phase = (signed * signed).astype(jnp.float32) * (DIFF / (width / 2) ** 2)
    cos_p, sin_p = (jnp.cos(phase), jnp.sin(phase))
    real_in = stacked[0].reshape(count, first, second)
    imag_in = stacked[1].reshape(count, first, second)
    step_re, step_im = rotate(real_in, imag_in, cos_a, sin_a, "nab,ak->nkb", 1.0)
    twist_re = step_re * cos_t + step_im * sin_t
    twist_im = step_im * cos_t - step_re * sin_t
    spec_re, spec_im = rotate(twist_re, twist_im, cos_b, sin_b, "nkb,bj->nkj", 1.0)
    moved_re = spec_re * cos_p - spec_im * sin_p
    moved_im = spec_re * sin_p + spec_im * cos_p
    back_re, back_im = rotate(moved_re, moved_im, cos_b, sin_b, "nkj,jb->nkb", -1.0)
    untw_re = back_re * cos_t - back_im * sin_t
    untw_im = back_im * cos_t + back_re * sin_t
    final_re, final_im = rotate(untw_re, untw_im, cos_a, sin_a, "nkb,ka->nab", -1.0)
    return jnp.stack([final_re.reshape(count, width), final_im.reshape(count, width)]) / width


def added_up(value, axis):
    count = lax.axis_size(axis)
    if count & (count - 1):
        return lax.psum(value, axis)
    reach = 1
    while reach < count:
        value = value + lax.ppermute(value, axis, [(i, i ^ reach) for i in range(count)])
        reach *= 2
    return value


def lateral_work(parts):
    return (transform(parts[0]), transform(parts[1]))


def multiplier_revision(
    population_multiplier,
    holeburn_multiplier,
    measured_rightward,
    measured_leftward,
    rightward_wave,
    leftward_wave,
    population_level,
    holeburn_magnitude,
    attenuation_factor,
    transverse_curvature,
):
    rightward_inphase, rightward_quadrature = (rightward_wave[0], rightward_wave[1])
    leftward_inphase, leftward_quadrature = (leftward_wave[0], leftward_wave[1])
    measured_rightward_inphase, measured_rightward_quadrature = (
        measured_rightward[0],
        measured_rightward[1],
    )
    measured_leftward_inphase, measured_leftward_quadrature = (
        measured_leftward[0],
        measured_leftward[1],
    )
    surplus_population = population_level - 1.0
    amplification_inphase = 1.0 + 0.5 * (GAIN_SLOPE_RATE * surplus_population - attenuation_factor)
    amplification_quadrature = 0.5 * GAIN_SLOPE_RATE * ALPHA_LINEWIDTH * surplus_population
    joined_waves = COUPLING * holeburn_magnitude
    population_derivative = (
        2.0 * CLOCK_DELTA * GAIN_SLOPE_RATE * surplus_population * population_multiplier
    )
    holeburn_derivative = 2.0 * CLOCK_DELTA * holeburn_multiplier
    revised_rightward_inphase = (
        amplification_inphase * measured_rightward_inphase
        - amplification_quadrature * measured_rightward_quadrature
        + joined_waves * measured_leftward_quadrature
        - population_derivative * rightward_inphase
        + holeburn_derivative * leftward_inphase
    )
    revised_rightward_quadrature = (
        amplification_inphase * measured_rightward_quadrature
        + amplification_quadrature * measured_rightward_inphase
        - joined_waves * measured_leftward_inphase
        - population_derivative * rightward_quadrature
        + holeburn_derivative * leftward_quadrature
    )
    revised_leftward_inphase = (
        amplification_inphase * measured_leftward_inphase
        - amplification_quadrature * measured_leftward_quadrature
        + joined_waves * measured_rightward_quadrature
        - population_derivative * leftward_inphase
        + holeburn_derivative * rightward_inphase
    )
    revised_leftward_quadrature = (
        amplification_inphase * measured_leftward_quadrature
        + amplification_quadrature * measured_leftward_inphase
        - joined_waves * measured_rightward_inphase
        - population_derivative * leftward_quadrature
        + holeburn_derivative * rightward_quadrature
    )
    light_intensity = (
        rightward_inphase * rightward_inphase
        + rightward_quadrature * rightward_quadrature
        + leftward_inphase * leftward_inphase
        + leftward_quadrature * leftward_quadrature
    )
    amplification_share = (
        measured_rightward_inphase * (rightward_inphase + ALPHA_LINEWIDTH * rightward_quadrature)
        + measured_rightward_quadrature
        * (rightward_quadrature - ALPHA_LINEWIDTH * rightward_inphase)
        + measured_leftward_inphase * (leftward_inphase + ALPHA_LINEWIDTH * leftward_quadrature)
        + measured_leftward_quadrature * (leftward_quadrature - ALPHA_LINEWIDTH * leftward_inphase)
    )
    revised_population = (
        population_multiplier
        * (1.0 - CLOCK_DELTA / DENSITY_LIFETIME - CLOCK_DELTA * GAIN_SLOPE_RATE * light_intensity)
        + TRANSVERSE_DIFFUS * transverse_curvature
        + 0.5 * GAIN_SLOPE_RATE * amplification_share
    )
    fresh_holeburn = holeburn_multiplier * (1.0 - CLOCK_DELTA / GRATING_LIFE) + COUPLING * (
        measured_rightward_quadrature * leftward_inphase
        - measured_rightward_inphase * leftward_quadrature
        + measured_leftward_quadrature * rightward_inphase
        - measured_leftward_inphase * rightward_quadrature
    )
    return (
        jnp.stack([revised_rightward_inphase, revised_rightward_quadrature]),
        jnp.stack([revised_leftward_inphase, revised_leftward_quadrature]),
        revised_population,
        fresh_holeburn,
    )


def per_device(
    ending_rightward_adjoint,
    ending_leftward_adjoint,
    ending_population_adjoint,
    ending_holeburn_adjoint,
    history_rightward,
    history_leftward,
    history_population,
    history_holeburn,
    segment_passive_attenuation,
):
    columns = ending_rightward_adjoint.shape[2]
    rows = ending_rightward_adjoint.shape[1]
    blocks = lax.axis_size("gz")
    position = lax.axis_index("gz")
    cells = rows * blocks
    zpos = (position * rows + jnp.arange(rows, dtype=jnp.int32)).astype(jnp.float32)
    scaling_factor = 1.0 + 2.0 * zpos / (cells - 1)
    rightward_multiplier, leftward_multiplier = (ending_rightward_adjoint, ending_leftward_adjoint)
    population_multiplier, holeburn_multiplier = (
        ending_population_adjoint,
        ending_holeburn_adjoint,
    )
    attenuation_factor = segment_passive_attenuation.astype(jnp.float32)
    shape_curve = jnp.zeros((columns,), jnp.float32)
    for moment_position in range(history_rightward.shape[0] - 1, -1, -1):
        shape_curve = shape_curve + jnp.sum(scaling_factor[:, None] * population_multiplier, axis=0)
        above = passed_along(rightward_multiplier[:, :1, :], "gz", -1)
        below = passed_along(leftward_multiplier[:, -1:, :], "gz", 1)
        top_row = jnp.where(
            position == blocks - 1, FRONT_FACET * leftward_multiplier[:, -1:, :], above
        )
        bottom_row = jnp.where(position == 0, REAR_FACET * rightward_multiplier[:, :1, :], below)
        lam_fwd = jnp.concatenate([rightward_multiplier[:, 1:, :], top_row], axis=1)
        lam_bwd = jnp.concatenate([bottom_row, leftward_multiplier[:, :-1, :]], axis=1)
        whole_fwd, whole_bwd = (
            lax.all_gather(lam_fwd, "gx", axis=2, tiled=True),
            lax.all_gather(lam_bwd, "gx", axis=2, tiled=True),
        )
        start = lax.axis_index("gx") * columns
        done_fwd, done_bwd = lateral_work((whole_fwd, whole_bwd))
        measured_rightward = lax.dynamic_slice_in_dim(done_fwd, start, columns, 2)
        measured_leftward = lax.dynamic_slice_in_dim(done_bwd, start, columns, 2)
        bordered_array = with_halo(population_multiplier, (("gx", 1),), 1)
        transverse_curvature = (
            bordered_array[:, 2:] + bordered_array[:, :-2] - 2.0 * population_multiplier
        )
        rightward_multiplier, leftward_multiplier, population_multiplier, holeburn_multiplier = (
            multiplier_revision(
                population_multiplier,
                holeburn_multiplier,
                measured_rightward,
                measured_leftward,
                history_rightward[moment_position].astype(jnp.float32),
                history_leftward[moment_position].astype(jnp.float32),
                history_population[moment_position].astype(jnp.float32),
                history_holeburn[moment_position].astype(jnp.float32),
                attenuation_factor,
                transverse_curvature,
            )
        )
    total = added_up(shape_curve, "gz")
    derivative_vector = CLOCK_DELTA * total / math.sqrt(cells)
    return (
        rightward_multiplier,
        leftward_multiplier,
        population_multiplier,
        holeburn_multiplier,
        derivative_vector,
    )

LANES = 128
TILE = 16
POWER = 12
STRETCH = 1211.0
SCALE_LANE = 8


def lateral_matrices(width, blocks):
    lanes = width // blocks
    k = np.arange(width)
    signed = np.where(k < width // 2, k, k - width).astype(np.float64)
    response = np.fft.ifft(np.exp(1j * signed * signed * (DIFF / (width / 2) ** 2)))
    step = np.arange(lanes)
    shift = lanes * np.arange(blocks)[:, None, None] + step[None, None, :] - step[None, :, None]
    kernels = np.fft.fft(response[shift % width], axis=0) / blocks
    top = np.concatenate([kernels.real, kernels.imag], axis=2)
    low = np.concatenate([-kernels.imag, kernels.real], axis=2)
    whole = np.concatenate([top, low], axis=1)
    first = whole.astype(ml_dtypes.bfloat16)
    rest = (whole - first.astype(np.float64)).astype(ml_dtypes.bfloat16)
    return np.stack([first, rest], axis=1)


def block_dft(values, sign):
    count = len(values)
    if count == 1:
        return values
    even = block_dft(values[0::2], sign)
    odd = block_dft(values[1::2], sign)
    out = [None] * count
    for k in range(count // 2):
        (er, ei), (wr, wi) = even[k], odd[k]
        if 4 * k == count:
            plus, minus = (er - wi, ei + wr), (er + wi, ei - wr)
            out[k], out[k + count // 2] = (plus, minus) if sign > 0 else (minus, plus)
            continue
        if k:
            c, s = math.cos(2 * math.pi * k / count), sign * math.sin(2 * math.pi * k / count)
            if 8 * k == count:
                wr, wi = (c * (wr - wi), c * (wr + wi)) if sign > 0 else (c * (wr + wi), c * (wi - wr))
            elif 8 * k == 3 * count:
                wr, wi = (c * (wr + wi), c * (wi - wr)) if sign > 0 else (c * (wr - wi), c * (wr + wi))
            else:
                wr, wi = c * wr - s * wi, c * wi + s * wr
        out[k] = (er + wr, ei + wi)
        out[k + count // 2] = (er - wr, ei - wi)
    return out


def lane(j):
    return pl.ds(pl.multiple_of(j * LANES, LANES), LANES)


def slab(j, rows):
    return pl.ds(pl.multiple_of(j * rows, rows), rows)


def fetch(pairs, sems, first=0):
    copies = [pltpu.make_async_copy(a, b, sems.at[first + i]) for i, (a, b) in enumerate(pairs)]
    for copy in copies:
        copy.start()
    return copies


def rows_of(info, rows, other):
    part = 1 - info[4] if other else info[4]
    return pl.ds(pl.multiple_of(part * rows, rows), rows)


def spread(field, work):
    rows = field.shape[1]
    blocks = work.shape[0]

    @pl.loop(0, rows // 8)
    def _(g):
        at = slab(g, 8)
        values = [
            (field[0, at, j * LANES : (j + 1) * LANES], field[1, at, j * LANES : (j + 1) * LANES])
            for j in range(blocks)
        ]
        for q, (re, im) in enumerate(block_dft(values, -1)):
            work[q, at, :LANES] = re
            work[q, at, LANES:] = im


def multiply(work, matrices):
    rows = work.shape[1]

    @pl.loop(0, work.shape[0], unroll=True)
    def _(q):
        value = work[q]
        first = value.astype(jnp.bfloat16)
        rest = (value - first.astype(jnp.float32)).astype(jnp.bfloat16)
        both = jnp.dot(
            jnp.concatenate([first, rest]), matrices[q, 0], preferred_element_type=jnp.float32
        )
        fine = jnp.dot(first, matrices[q, 1], preferred_element_type=jnp.float32)
        work[q] = both[:rows] + (both[rows:] + fine)


def gathered(work, at):
    values = [(work[q, at, :LANES], work[q, at, LANES:]) for q in range(work.shape[0])]
    return block_dft(values, 1)


def filtered(field, work, matrices, copy):
    spread(field, work)
    copy.wait()
    multiply(work, matrices)


def write_filtered(info, work, forward, backward, inner, outer):
    rows = work.shape[1] // 2
    for target, base, offset in ((forward, 0, 0), (backward, rows, 8)):

        @pl.loop(0, rows // 8)
        def _(g):
            here = pl.ds(pl.multiple_of(g * 8 + offset, 8), 8)
            for j, pair in enumerate(gathered(work, pl.ds(pl.multiple_of(g * 8 + base, 8), 8))):
                for part in range(2):
                    target[part, here, j * LANES : (j + 1) * LANES] = pair[part]

    low = info[4] == 0
    for part in range(2):
        first, last = forward[part, 0:1, :], backward[part, rows + 7 : rows + 8, :]
        inner[part : part + 1, :] = jnp.where(low, last, first)
        outer[part : part + 1, :] = jnp.where(low, first, last)


def size_of(largest):
    top = jnp.max(jnp.max(largest, axis=1, keepdims=True), axis=0, keepdims=True)
    return jnp.maximum(top, 1e-30).astype(jnp.bfloat16).astype(jnp.float32)


def encoded(value, size):
    unit = value * (STRETCH / size)
    square = unit * unit
    fourth = square * square
    return (fourth * fourth * square * (unit * jnp.abs(unit))).astype(jnp.bfloat16)


def decoded(code, size):
    value = code.astype(jnp.float32)
    root = jnp.exp2(jnp.log(jnp.abs(value)) * (1.0 / (POWER * math.log(2.0)))) * (size / STRETCH)
    return jnp.where(value < 0.0, -root, root)


def side_tile(columns, rows):
    index = lax.broadcasted_iota(jnp.int32, (rows, LANES), 1)
    tile = jnp.zeros((rows, LANES), jnp.float32)
    for at, column in columns:
        tile = jnp.where(index == at, column, tile)
    return tile.astype(jnp.bfloat16)


def sizes_in(tile, count):
    value = tile.astype(jnp.float32)
    return [value[0:1, SCALE_LANE + i : SCALE_LANE + i + 1] for i in range(count)]


def updated(fr, fi, br, bi, wave, population, hole, loss, carrier, grating, lap):
    rr, ri, lr, li = wave
    surplus = population - 1.0
    gain_re = 1.0 + 0.5 * (GAIN_SLOPE_RATE * surplus - loss)
    gain_im = (0.5 * GAIN_SLOPE_RATE * ALPHA_LINEWIDTH) * surplus
    joined = COUPLING * hole
    drive = (2.0 * CLOCK_DELTA * GAIN_SLOPE_RATE) * surplus * carrier
    mix = (2.0 * CLOCK_DELTA) * grating
    new_fr = gain_re * fr - gain_im * fi + joined * bi - drive * rr + mix * lr
    new_fi = gain_re * fi + gain_im * fr - joined * br - drive * ri + mix * li
    new_br = gain_re * br - gain_im * bi + joined * fi - drive * lr + mix * rr
    new_bi = gain_re * bi + gain_im * br - joined * fr - drive * li + mix * ri
    light = rr * rr + ri * ri + lr * lr + li * li
    share = (
        fr * (rr + ALPHA_LINEWIDTH * ri)
        + fi * (ri - ALPHA_LINEWIDTH * rr)
        + br * (lr + ALPHA_LINEWIDTH * li)
        + bi * (li - ALPHA_LINEWIDTH * lr)
    )
    new_carrier = (
        carrier * ((1.0 - CLOCK_DELTA / DENSITY_LIFETIME) - (CLOCK_DELTA * GAIN_SLOPE_RATE) * light)
        + TRANSVERSE_DIFFUS * lap
        + (0.5 * GAIN_SLOPE_RATE) * share
    )
    new_grating = grating * (1.0 - CLOCK_DELTA / GRATING_LIFE) + COUPLING * (
        fi * lr - fr * li + bi * rr - br * ri
    )
    return new_fr, new_fi, new_br, new_bi, new_carrier, new_grating


def curvature(left, mid, right, weight_left, weight_right):
    index = lax.broadcasted_iota(jnp.int32, mid.shape, 1)
    below = jnp.where(index == 0, pltpu.roll(left, 1, 1) * weight_left, pltpu.roll(mid, 1, 1))
    above = jnp.where(
        index == LANES - 1,
        pltpu.roll(right, LANES - 1, 1) * weight_right,
        pltpu.roll(mid, LANES - 1, 1),
    )
    return below + above - 2.0 * mid


def send_fields_kernel(info, forward, backward, out, fields, sems):
    rows, columns = fields.shape[2:]
    half = columns // LANES
    at = rows_of(info, rows, True)
    copies = fetch(
        [(ref.at[:, at, :], fields.at[f]) for f, ref in enumerate((forward, backward))], sems
    )
    sizes = []
    for f in range(2):
        copies[f].wait()
        largest = jnp.maximum(jnp.abs(fields[f, 0]), jnp.abs(fields[f, 1]))
        size = size_of(largest)
        sizes.append((SCALE_LANE + f, size))
        for part in range(2):
            put_tiles(out, (2 * f + part) * half, encoded(fields[f, part], size))
    out[4 * half * rows :, :] = side_tile(sizes, rows)


def put_tiles(out, first, value):
    rows, columns = value.shape
    for j in range(columns // LANES):
        at = (first + j) * rows
        out[at : at + rows, :] = value[:, j * LANES : (j + 1) * LANES]


def history_rows(forward, backward, population, hole, s, at):
    return [
        forward.at[s, 0, at, :], forward.at[s, 1, at, :], backward.at[s, 0, at, :],
        backward.at[s, 1, at, :], population.at[s, at, :], hole.at[s, at, :],
    ]


def into_rows(parts, target, first, rows):
    return [(part, target.at[pl.ds(first + i * rows, rows), :]) for i, part in enumerate(parts)]


def send_later_kernel(steps, info, forward, backward, population, hole, final, *refs):
    targets, sems = refs[:-1], refs[-1]
    rows = targets[0].shape[0] // 6
    history = (forward, backward, population, hole)
    pairs = []
    for i, s in enumerate(steps):
        for k, other in enumerate((True, False)):
            at = rows_of(info, rows, other)
            pairs += into_rows(history_rows(*history, s, at), targets[2 * i + k], 0, rows)
    pairs += into_rows(history_rows(*history, 0, pl.ds(0, 2 * rows)), final, 0, 2 * rows)
    for copy in fetch(pairs, sems):
        copy.wait()


def send_first_kernel(
    s, info, loss, carrier, grating, forward, backward, population, hole,
    own_loss, own, own_carrier, own_grating, out, own_edge, states, ends, sems,
):
    rows, columns = own_carrier.shape
    theirs, mine = rows_of(info, rows, True), rows_of(info, rows, False)
    history = (forward, backward, population, hole)
    copies = fetch(
        [(carrier.at[theirs, :], states.at[0]), (grating.at[theirs, :], states.at[1])]
        + into_rows([loss.at[theirs, :]], out, 0, rows)
        + into_rows(history_rows(*history, s, theirs), out, 3 * rows, rows)
        + [(loss.at[mine, :], own_loss), (carrier.at[mine, :], own_carrier)]
        + [(grating.at[mine, :], own_grating)]
        + into_rows(history_rows(*history, s, mine), own, 0, rows)
        + [
            (part, ends.at[k, i])
            for k in range(2)
            for i, part in enumerate(
                history_rows(*history, 1, pl.ds(k * (2 * rows - TILE), TILE))
            )
        ],
        sems,
    )
    for copy in copies[:2]:
        copy.wait()
    sizes = []
    for i in range(2):
        size = size_of(jnp.abs(states[i]))
        sizes.append(jnp.broadcast_to(size, (1, columns)))
        out[(1 + i) * rows : (2 + i) * rows, :] = encoded(states[i], size)
    for copy in copies[2:]:
        copy.wait()
    low = info[4] == 0
    top = [ends[0, i].astype(jnp.float32)[:1] for i in range(6)]
    foot = [ends[1, i].astype(jnp.float32)[TILE - 1 :] for i in range(6)]
    own_edge[...] = jnp.concatenate([jnp.where(low, a, b) for a, b in zip(top, foot)])
    sizes += [jnp.where(low, b, a) for a, b in zip(top, foot)]
    sizes.append(jnp.zeros((TILE - 8, columns), jnp.float32))
    out[9 * rows :, :] = jnp.concatenate(sizes).astype(jnp.bfloat16)


def enter_kernel(
    info, forward, backward, other, source, tp, tq, inner, outer, field, work, matrices, sem, sems
):
    copy = pltpu.make_async_copy(source, matrices, sem)
    rows, width = field.shape[1] // 2, field.shape[2]
    columns = width // 2
    half = columns // LANES
    at = rows_of(info, rows, False)
    copies = fetch(
        [
            (ref.at[:, at, :], field.at[:, f * rows : (f + 1) * rows, :columns])
            for f, ref in enumerate((forward, backward))
        ],
        sems,
    )
    copy.start()
    sizes = sizes_in(other[4 * half * rows :, :], 2)
    for f in range(2):
        for part in range(2):

            @pl.loop(0, half, unroll=2)
            def _(j):
                code = other[slab((2 * f + part) * half + j, rows), :]
                field[part, f * rows : (f + 1) * rows, lane(half + j)] = decoded(code, sizes[f])

    for held in copies:
        held.wait()
    filtered(field, work, matrices, copy)
    write_filtered(info, work, tp, tq, inner, outer)


def rows_update(
    info, tp, tq, inner, outer, carrier, grating, own, other, own_loss, other_loss,
    field, new_carrier, new_grating, sums_in, sums, cells, last
):
    rows, width = carrier.shape
    half = width // LANES // 2
    columns = half * LANES
    mid = jnp.where(info[0] == 0, 1.0, 0.0)
    wrap = 1.0 - mid
    low = info[4] == 0
    is_first, is_last = info[1], info[2]
    row_index = lax.broadcasted_iota(jnp.int32, (TILE, LANES), 0)
    zero = jnp.zeros((8, LANES), jnp.float32)

    def step(jj, most):
        for side in range(2):
            j = jj + side * half
            here = lane(j)
            left_at = lane(jnp.where(j == 0, 2 * half - 1, j - 1))
            right_at = lane(jnp.where(j == 2 * half - 1, 0, j + 1))
            swapped = lane(jj + (1 - side) * half)
            weight_left = jnp.where(jj == 0, wrap if side == 0 else mid, 1.0)
            weight_right = jnp.where(jj == half - 1, mid if side == 0 else wrap, 1.0)
            total = zero
            for r in range(0, rows, TILE):
                at = slice(r, r + TILE)

                held, begin = (own, other)[side]

                def part_of(i):
                    tile = begin + i * rows + r
                    return held[tile : tile + TILE, lane(jj)].astype(jnp.float32)

                loss = (own_loss, other_loss)[side][at, lane(jj)].astype(jnp.float32)
                f = [tp[part, r + 1 : r + 1 + TILE, here] for part in range(2)]
                b = [tq[part, r + 7 : r + 7 + TILE, here] for part in range(2)]
                if r + TILE == rows:
                    for part in range(2):
                        facet = FRONT_FACET * tq[part, rows + 7 : rows + 8, here]
                        edge = jnp.where(
                            low, inner[part : part + 1, swapped], outer[part : part + 1, here]
                        )
                        edge = jnp.where(is_last, facet, edge)
                        f[part] = jnp.where(row_index == TILE - 1, edge, f[part])
                if r == 0:
                    for part in range(2):
                        facet = REAR_FACET * tp[part, 0:1, here]
                        edge = jnp.where(
                            low, outer[part : part + 1, here], inner[part : part + 1, swapped]
                        )
                        edge = jnp.where(is_first, facet, edge)
                        b[part] = jnp.where(row_index == 0, edge, b[part])
                c = carrier[at, here]
                lap = curvature(
                    carrier[at, left_at], c, carrier[at, right_at], weight_left, weight_right
                )
                out = updated(
                    *f, *b, [part_of(i) for i in range(4)], part_of(4), part_of(5), loss,
                    c, grating[at, here], lap,
                )
                field[0, r : r + TILE, here] = out[0]
                field[1, r : r + TILE, here] = out[1]
                field[0, rows + r : rows + r + TILE, here] = out[2]
                field[1, rows + r : rows + r + TILE, here] = out[3]
                new_carrier[at, here] = out[4]
                new_grating[at, here] = out[5]
                z = (info[3] + r + row_index).astype(jnp.float32)
                weighted = (1.0 + 2.0 * z / (cells - 1)) * ((c + out[4]) if last else c)
                for k in range(0, TILE, 8):
                    total = total + weighted[k : k + 8]
                if last and side == 1:
                    for k in range(0, TILE, 8):
                        most = (
                            jnp.maximum(most[0], jnp.abs(out[4][k : k + 8])),
                            jnp.maximum(most[1], jnp.abs(out[5][k : k + 8])),
                        )
            summed = jnp.sum(total, axis=0, keepdims=True)
            sums[:, here] = summed if sums_in is None else summed + sums_in[:, here]
        return most

    return lax.fori_loop(0, half, step, (zero, zero))


def first_step_kernel(
    cells, info, tp, tq, inner, outer, my_carrier, my_grating, loss, own, own_edge, other, source,
    new_tp, new_tq, new_inner, new_outer, new_carrier, new_grating, sums,
    carrier, grating, field, work, matrices, sem,
):
    copy = pltpu.make_async_copy(source, matrices, sem)
    copy.start()
    rows, columns = my_carrier.shape
    half = columns // LANES
    extra = other[9 * rows :, :].astype(jnp.float32)
    sizes = [extra[0:1, 0:1], extra[1:2, 0:1]]
    low = info[4] == 0
    new_outer[2:8, :columns] = own_edge[...]
    new_outer[2:8, columns:] = extra[2:8]
    for part, ref in ((0, loss), (1, other)):
        top = ref[:TILE, :].astype(jnp.float32)[:1]
        foot = ref[rows - TILE : rows, :].astype(jnp.float32)[TILE - 1 :]
        new_outer[8:9, part * columns : (part + 1) * columns] = jnp.where(low, top, foot)
    for i, (whole, mine) in enumerate(((carrier, my_carrier), (grating, my_grating))):
        whole[:, :columns] = mine[...]

        @pl.loop(0, half, unroll=2)
        def _(j):
            whole[:, lane(half + j)] = decoded(
                other[(1 + i) * rows : (2 + i) * rows, lane(j)], sizes[i]
            )

    rows_update(
        info, tp, tq, inner, outer, carrier, grating, (own, 0), (other, 3 * rows), loss, other,
        field, new_carrier, new_grating, None, sums, cells, False,
    )
    filtered(field, work, matrices, copy)
    write_filtered(info, work, new_tp, new_tq, new_inner, new_outer)


def middle_step_kernel(
    cells, info, tp, tq, inner, outer, carrier, grating, loss, own, other, other_loss, sums_in,
    source, new_tp, new_tq, new_inner, new_outer, new_carrier, new_grating, sums,
    field, work, matrices, sem,
):
    copy = pltpu.make_async_copy(source, matrices, sem)
    copy.start()
    rows_update(
        info, tp, tq, inner, outer, carrier, grating, (own, 0), (other, 0), loss, other_loss,
        field, new_carrier, new_grating, sums_in, sums, cells, False,
    )
    filtered(field, work, matrices, copy)
    write_filtered(info, work, new_tp, new_tq, new_inner, new_outer)
    rows = carrier.shape[0]
    low = info[4] == 0
    for part in range(2):
        new_outer[2 + part : 3 + part, :] = jnp.where(
            low, new_tp[part, 1:2, :], new_tq[part, rows + 6 : rows + 7, :]
        )
    for i, ref in enumerate((new_carrier, new_grating)):
        new_outer[4 + i : 5 + i, :] = jnp.where(low, ref[0:1, :], ref[rows - 1 : rows, :])


def row_beyond(info, tp, tq, outer, beyond):
    rows = tp.shape[1] - 8
    low = info[4] == 0
    xr, xi, carrier, grating = (outer[i : i + 1, :] for i in range(2, 6))
    yr, yi = (
        jnp.where(low, tp[part, 0:1, :], tq[part, rows + 7 : rows + 8, :]) for part in range(2)
    )
    rr, ri, lr, li, population, hole, loss = (beyond[i : i + 1, :] for i in range(2, 9))
    surplus = population - 1.0
    gain_re = 1.0 + 0.5 * (GAIN_SLOPE_RATE * surplus - loss)
    gain_im = (0.5 * GAIN_SLOPE_RATE * ALPHA_LINEWIDTH) * surplus
    joined = COUPLING * hole
    drive = (2.0 * CLOCK_DELTA * GAIN_SLOPE_RATE) * surplus * carrier
    mix = (2.0 * CLOCK_DELTA) * grating
    near_re, near_im = jnp.where(low, lr, rr), jnp.where(low, li, ri)
    far_re, far_im = jnp.where(low, rr, lr), jnp.where(low, ri, li)
    new_re = gain_re * xr - gain_im * xi + joined * yi - drive * near_re + mix * far_re
    new_im = gain_re * xi + gain_im * xr - joined * yr - drive * near_im + mix * far_im
    return new_re, new_im


def leave_kernel(
    cells, info, tp, tq, inner, outer, beyond, carrier, grating, loss, own, other, other_loss,
    sums_in, source, kept, kept_carrier, kept_grating, sides, sent, edge, shares,
    sums, new_carrier, new_grating, field, work, matrices, sem,
):
    copy = pltpu.make_async_copy(source, matrices, sem)
    copy.start()
    rows, width = carrier.shape
    columns = width // 2
    half = columns // LANES
    most = rows_update(
        info, tp, tq, inner, outer, carrier, grating, (own, 0), (other, 0), loss, other_loss,
        field, new_carrier, new_grating, sums_in, sums, cells, True,
    )
    mid = jnp.where(info[0] == 0, 1.0, 0.0)
    wrap = 1.0 - mid
    kept_carrier[...] = new_carrier[:, :columns]
    kept_grating[...] = new_grating[:, :columns]
    first, before = new_carrier[:, 0:1] * wrap, new_carrier[:, columns - 1 : columns] * mid
    after, final = new_carrier[:, columns : columns + 1] * mid, new_carrier[:, width - 1 :] * wrap
    sides[0] = jnp.broadcast_to(final, (rows, LANES))
    sides[1] = jnp.broadcast_to(after, (rows, LANES))
    pairs = []
    for at, value in ((0, before), (2, first)):
        coarse = value.astype(jnp.bfloat16).astype(jnp.float32)
        pairs += [(at, coarse), (at + 1, value - coarse)]
    for i, field_of in enumerate((new_carrier, new_grating)):
        size = size_of(most[i])
        pairs.append((SCALE_LANE + 2 + i, size))

        @pl.loop(0, half, unroll=2)
        def _(j):
            sent[slab((4 + i) * half + j, rows), :] = encoded(field_of[:, lane(half + j)], size)

    for part, value in enumerate(row_beyond(info, tp, tq, outer, beyond)):
        field[part, 2 * rows :, :] = jnp.broadcast_to(value, (8, width))
    filtered(field, work, matrices, copy)
    zero = jnp.zeros((8, LANES), jnp.float32)
    for f in range(2):

        def unmix(g, most):
            at = pl.ds(pl.multiple_of(g * 8 + f * rows, 8), 8)
            for j, pair in enumerate(gathered(work, at)):
                for part in range(2):
                    if j < half:
                        kept[part, at, j * LANES : (j + 1) * LANES] = pair[part]
                    else:
                        work[j, at, part * LANES : (part + 1) * LANES] = pair[part]
                        most = jnp.maximum(most, jnp.abs(pair[part]))
            return most

        size = size_of(lax.fori_loop(0, rows // 8, unmix, zero))
        pairs.append((SCALE_LANE + f, size))

        @pl.loop(0, half, unroll=2)
        def _(j):
            for part in range(2):
                value = work[half + j, f * rows : (f + 1) * rows, part * LANES : (part + 1) * LANES]
                sent[slab((2 * f + part) * half + j, rows), :] = encoded(value, size)

    ends = gathered(work, slice(2 * rows, 2 * rows + 8))
    for part in range(2):
        for j in range(half):
            edge[part : part + 1, j * LANES : (j + 1) * LANES] = ends[j][part][:1]
    far = jnp.concatenate([ends[j][part][:1] for part in range(2) for j in range(half, 2 * half)])
    size = size_of(jnp.abs(far))
    pairs.append((SCALE_LANE + 4, size))
    sent[6 * half * rows : (6 * half + 1) * rows, :] = side_tile(pairs, rows)
    spare = jnp.zeros((rows - 2 * half, LANES), jnp.float32)
    sent[(6 * half + 1) * rows :, :] = encoded(jnp.concatenate([far, spare]), size)
    tile = jnp.concatenate([sums[:, j * LANES : (j + 1) * LANES] for j in range(2 * half)])
    near, far = tile[:half], tile[half:]
    first = info[0] == 0
    to_first, to_second = jnp.where(first, near, far), jnp.where(first, far, near)
    for i in range(0, shares.shape[0], 2):
        shares[i] = to_first
        shares[i + 1] = to_second


def total_kernel(cells, info, partial, out):
    total = partial[0]
    for i in range(1, partial.shape[0]):
        total = total + partial[i]
    out[...] = total * (CLOCK_DELTA / math.sqrt(cells))


def final_kernel(
    info, kept, kept_carrier, kept_grating, sides, came, edge, loss, history,
    out_forward, out_backward, out_carrier, out_grating,
    tp, tq, carrier, grating,
):
    rows, columns = kept_carrier.shape
    half = columns // LANES
    mine = info[4] * rows
    theirs = (1 - info[4]) * rows
    low = info[4] == 0
    extra = came[6 * half * rows : (6 * half + 1) * rows, :]
    size_forward, size_backward, size_carrier, size_grating, size_edge = sizes_in(extra, 5)
    ends = decoded(came[(6 * half + 1) * rows :, :], size_edge)
    extra = extra.astype(jnp.float32)

    def at(start, offset, count):
        return pl.ds(pl.multiple_of(start + offset, 8), count)

    for part in range(2):
        tp[part, at(mine, 0, rows), :] = kept[part, :rows, :]
        tq[part, at(mine, 8, rows), :] = kept[part, rows:, :]
    carrier[at(mine, 0, rows), LANES : LANES + columns] = kept_carrier[...]
    carrier[at(mine, 0, rows), :LANES] = sides[0]
    carrier[at(mine, 0, rows), LANES + columns :] = sides[1]
    carrier[at(theirs, 0, rows), :LANES] = jnp.broadcast_to(
        extra[:, 0:1] + extra[:, 1:2], (rows, LANES)
    )
    carrier[at(theirs, 0, rows), LANES + columns :] = jnp.broadcast_to(
        extra[:, 2:3] + extra[:, 3:4], (rows, LANES)
    )
    grating[at(mine, 0, rows), :] = kept_grating[...]

    @pl.loop(0, half, unroll=2)
    def _(j):
        carrier[at(theirs, 0, rows), lane(1 + j)] = decoded(
            came[slab(4 * half + j, rows), :], size_carrier
        )
        grating[at(theirs, 0, rows), lane(j)] = decoded(
            came[slab(5 * half + j, rows), :], size_grating
        )
        for part in range(2):
            tp[part, at(theirs, 0, rows), lane(j)] = decoded(
                came[slab(part * half + j, rows), :], size_forward
            )
            tq[part, at(theirs, 8, rows), lane(j)] = decoded(
                came[slab((2 + part) * half + j, rows), :], size_backward
            )

    all_rows = 2 * rows
    for part in range(2):
        near = edge[part : part + 1, :]
        far = jnp.concatenate([ends[part * half + j : part * half + j + 1] for j in range(half)], axis=1)
        next_edge = jnp.where(low, far, near)
        before_edge = jnp.where(low, near, far)
        front = FRONT_FACET * tq[part, all_rows + 7 : all_rows + 8, :]
        rear = REAR_FACET * tp[part, 0:1, :]
        tp[part, all_rows : all_rows + 1, :] = jnp.where(info[2], front, next_edge)
        tq[part, 7:8, :] = jnp.where(info[1], rear, before_edge)

    @pl.loop(0, half)
    def _(j):
        here = lane(j)
        for r in range(0, all_rows, TILE):
            row = slice(r, r + TILE)
            c = carrier[row, lane(j + 1)]
            lap = curvature(carrier[row, lane(j)], c, carrier[row, lane(j + 2)], 1.0, 1.0)
            parts = [
                history[i * all_rows + r : i * all_rows + r + TILE, here].astype(jnp.float32)
                for i in range(6)
            ]
            out = updated(
                tp[0, r + 1 : r + 1 + TILE, here], tp[1, r + 1 : r + 1 + TILE, here],
                tq[0, r + 7 : r + 7 + TILE, here], tq[1, r + 7 : r + 7 + TILE, here],
                parts[:4], parts[4], parts[5],
                loss[row, here].astype(jnp.float32), c, grating[row, here], lap,
            )
            out_forward[0, row, here] = out[0]
            out_forward[1, row, here] = out[1]
            out_backward[0, row, here] = out[2]
            out_backward[1, row, here] = out[3]
            out_carrier[row, here] = out[4]
            out_grating[row, here] = out[5]


def position(rows, whole):
    x, block, count = lax.axis_index("gx"), lax.axis_index("gz"), lax.axis_size("gz")
    high = lax.rem(x + block, 2)
    if whole:
        return x, block == 0, block == count - 1, block * rows, high
    place = 2 * block + high
    return x, place == 0, place == 2 * count - 1, place * rows, high


def whole_spec(shape):
    return pl.BlockSpec(shape, lambda i, n=len(shape): (0,) * n)


def call(name, kernel, rows, inputs, outputs, scratch, flops=0, grant=24, whole=False):
    arrays = [x[0] if isinstance(x, tuple) else x for x in inputs]
    specs = [x[1] if isinstance(x, tuple) else whole_spec(x.shape) for x in inputs]
    shapes = [jax.ShapeDtypeStruct(*out) for out in outputs]
    moved = sum(math.prod(s.shape) * s.dtype.itemsize for s in shapes)

    def body(*refs):
        kernel(position(rows, whole), *refs)

    return pl.pallas_call(
        body,
        grid=(1,),
        in_specs=specs,
        out_specs=[whole_spec(s.shape) for s in shapes],
        scratch_shapes=scratch,
        out_shape=shapes,
        compiler_params=pltpu.CompilerParams(vmem_limit_bytes=grant * 1024 * 1024),
        cost_estimate=pl.CostEstimate(
            flops=flops, bytes_accessed=moved + 4 * 1024 * 1024, transcendentals=0
        ),
        name=name,
    )(*arrays)


def per_pair(
    ending_rightward_adjoint,
    ending_leftward_adjoint,
    ending_population_adjoint,
    ending_holeburn_adjoint,
    history_rightward,
    history_leftward,
    history_population,
    history_holeburn,
    segment_passive_attenuation,
):
    cell_rows, columns = ending_population_adjoint.shape
    passes = history_population.shape[0]
    rows = cell_rows // 2
    half = columns // LANES
    blocks = 2 * half
    width = 2 * columns
    count = lax.axis_size("gz")
    cells = cell_rows * count
    x = lax.axis_index("gx")
    f32, bf16 = jnp.float32, jnp.bfloat16
    swap = [(0, 1), (1, 0)]
    in_place = pl.BlockSpec(memory_space=pltpu.HBM)

    def held(*arrays):
        return [(a, in_place) for a in arrays]

    def tiles(n):
        return ((n * rows, LANES), bf16)

    ends = held(ending_rightward_adjoint, ending_leftward_adjoint)
    planes = held(ending_population_adjoint, ending_holeburn_adjoint)
    history = held(history_rightward, history_leftward, history_population, history_holeburn)
    losses = held(segment_passive_attenuation)
    matrices = pltpu.with_memory_space_constraint(
        jnp.asarray(lateral_matrices(width, blocks)), pltpu.HBM
    )
    matrix_input = held(matrices)
    work = [
        pltpu.VMEM((blocks, 2 * rows, 2 * LANES), f32),
        pltpu.VMEM(matrices.shape, bf16),
        pltpu.SemaphoreType.DMA,
    ]
    field_scratch = pltpu.VMEM((2, 2 * rows, width), f32)
    def state_out(outer_rows):
        state = ((2, rows + 8, width), f32)
        return [state, state, ((2, width), f32), ((outer_rows, width), f32)]

    plane = ((rows, width), f32)
    plane_scratch = pltpu.VMEM((rows, width), f32)
    half_plane = ((rows, columns), f32)
    work_flops = 2 * 3 * 2 * rows * blocks * (2 * LANES) ** 2

    (coded,) = call(
        "send_fields", send_fields_kernel, rows, ends, [tiles(4 * half + 1)],
        [pltpu.VMEM((2, 2, rows, columns), f32), pltpu.SemaphoreType.DMA((2,))], grant=62,
    )
    other_fields = lax.ppermute(coded, "gx", swap)
    loss, own_first, my_carrier, my_grating, sent_first, own_edge = call(
        "send_first", functools.partial(send_first_kernel, passes - 1), rows,
        [*losses, *planes, *history],
        [((rows, columns), bf16), ((6 * rows, columns), bf16), half_plane, half_plane,
         ((9 * rows + TILE, columns), bf16), ((6, columns), f32)],
        [pltpu.VMEM((2, rows, columns), f32), pltpu.VMEM((2, 6, TILE, columns), bf16),
         pltpu.SemaphoreType.DMA((30,))], grant=62,
    )
    steps = range(passes - 2, 0, -1)
    history_last, *later = call(
        "send_later", functools.partial(send_later_kernel, steps), rows, history,
        [((6 * cell_rows, columns), bf16)] + [((6 * rows, columns), bf16)] * (2 * len(steps)),
        [pltpu.SemaphoreType.DMA((12 * len(steps) + 6,))], grant=62,
    )
    sent_first, history_last, later, other_fields = lax.optimization_barrier(
        (sent_first, history_last, later, other_fields)
    )
    other_first = lax.ppermute(sent_first, "gx", swap)

    line = ("gz", "gx")
    neighbours = []
    for b in range(count - 1):
        top = (1 + b) % 2
        neighbours += [(2 * b + top, 2 * b + 2 + top), (2 * b + 2 + top, 2 * b + top)]

    def edges(inner, outer):
        outer = lax.ppermute(outer, line, neighbours)
        return lax.ppermute(inner, "gx", swap), outer

    tp, tq, inner, outer = call(
        "enter", enter_kernel, rows, [*ends, other_fields, *matrix_input],
        state_out(2), [field_scratch, *work, pltpu.SemaphoreType.DMA((2,))], work_flops,
    )
    inner, outer = edges(inner, outer)

    other_loss = (other_first, pl.BlockSpec((rows, columns), lambda i: (0, 0)))
    carrier = grating = sums = other = own = None
    for index, s in enumerate(range(passes - 1, 0, -1)):
        if index < len(steps):
            sent, own_next = later[2 * index : 2 * index + 2]
            sent, inner, outer = lax.optimization_barrier((sent, inner, outer))
            coming = lax.ppermute(sent, "gx", swap)
        shared = [tp, tq, inner, outer]
        if index == 0:
            tp, tq, inner, outer, carrier, grating, sums = call(
                "first_step", functools.partial(first_step_kernel, cells), rows,
                [*shared, my_carrier, my_grating, loss, own_first, own_edge, other_first,
                 *matrix_input],
                [*state_out(9), plane, plane, ((1, width), f32)],
                [plane_scratch, plane_scratch, field_scratch, *work], work_flops,
            )
        elif s > 1:
            tp, tq, inner, outer, carrier, grating, sums = call(
                "middle_step", functools.partial(middle_step_kernel, cells), rows,
                [*shared, carrier, grating, loss, own, other, other_loss, sums, *matrix_input],
                [*state_out(6), plane, plane, ((1, width), f32)],
                [field_scratch, *work], work_flops,
            )
        else:
            kept, kept_carrier, kept_grating, sides, sent, edge, shares = call(
                "leave", functools.partial(leave_kernel, cells), rows,
                [*shared, beyond, carrier, grating, loss, own, other, other_loss, sums, *matrix_input],
                [((2, 2 * rows, columns), f32), half_plane, half_plane, ((2, rows, LANES), f32),
                 tiles(6 * half + 2), ((2, columns), f32), ((2 * count, half, LANES), f32)],
                [pltpu.VMEM((1, width), f32), plane_scratch, plane_scratch,
                 pltpu.VMEM((2, 2 * rows + 8, width), f32),
                 pltpu.VMEM((blocks, 2 * rows + TILE, 2 * LANES), f32), *work[1:]],
                work_flops,
            )
        if s > 1:
            inner, outer = edges(inner, outer)
            own, other = own_next, coming
            if index == 0:
                beyond = outer

    came = lax.ppermute(sent, "gx", swap)
    shares = lax.all_to_all(shares, line, 0, 0, tiled=True)

    outs = call(
        "final", final_kernel, cell_rows,
        [kept, kept_carrier, kept_grating, sides, came, edge,
         segment_passive_attenuation, history_last],
        [((2, cell_rows, columns), f32), ((2, cell_rows, columns), f32),
         ((cell_rows, columns), f32), ((cell_rows, columns), f32)],
        [pltpu.VMEM((2, cell_rows + 8, columns), f32), pltpu.VMEM((2, cell_rows + 8, columns), f32),
         pltpu.VMEM((cell_rows, columns + 2 * LANES), f32), pltpu.VMEM((cell_rows, columns), f32)],
        whole=True,
    )
    shares, *outs = lax.optimization_barrier((shares, *outs))
    (total,) = call(
        "total", functools.partial(total_kernel, cells), rows, [shares], [((half, LANES), f32)], [],
    )
    return (*outs, total.reshape(columns))


def shared_by_pairs(mesh, arguments):
    population = arguments[6]
    passes, cells, width = population.shape
    rows, columns = cells // mesh.shape["gz"], width // mesh.shape["gx"]
    return (
        mesh.shape["gx"] == 2
        and passes >= 4
        and 4 * columns <= rows * LANES
        and rows % (2 * TILE) == 0
        and columns % LANES == 0
        and (columns // LANES) & (columns // LANES - 1) == 0
        and width <= 4096
    )


def solution(mesh):
    def run(*arguments):
        body = per_pair if shared_by_pairs(mesh, arguments) else per_device
        return jax.shard_map(
            body,
            mesh=mesh,
            in_specs=(
                P(None, "gz", "gx"),
                P(None, "gz", "gx"),
                P("gz", "gx"),
                P("gz", "gx"),
                P(None, None, "gz", "gx"),
                P(None, None, "gz", "gx"),
                P(None, "gz", "gx"),
                P(None, "gz", "gx"),
                P("gz", "gx"),
            ),
            out_specs=(
                P(None, "gz", "gx"), P(None, "gz", "gx"), P("gz", "gx"), P("gz", "gx"), P("gx"),
            ),
            check_vma=False,
        )(*arguments)

    return run
```

```python
import functools
import math

import jax
import jax.numpy as jnp
import ml_dtypes
import numpy as np
from jax import lax
from jax.experimental import pallas as pl
from jax.experimental.pallas import tpu as pltpu
from jax.sharding import PartitionSpec as P

DIFF = 512


FRONT_FACET = 0.3
REAR_FACET = 0.9
GAIN_SLOPE_RATE = 0.3
ALPHA_LINEWIDTH = 2.0
COUPLING = 0.5
CLOCK_DELTA = 0.3
DENSITY_LIFETIME = 2.0
GRATING_LIFE = 0.75
TRANSVERSE_DIFFUS = 0.2


def passed_along(value, axis, steps):
    count = lax.axis_size(axis)
    initial, last = (max(0, -steps), min(count, count - steps))
    return lax.ppermute(value, axis, [(source, source + steps) for source in range(initial, last)])


def with_halo(block, sides, width):
    for axis, dim in sides:
        count = lax.axis_size(axis)
        forward = [(i, i + 1) for i in range(count - 1)]
        backward = [(target, source) for source, target in forward]
        low = lax.ppermute(
            lax.slice_in_dim(block, block.shape[dim] - width, None, axis=dim), axis, forward
        )
        high = lax.ppermute(lax.slice_in_dim(block, 0, width, axis=dim), axis, backward)
        block = jnp.concatenate([low, block, high], axis=dim)
    return block


def rotate(source_re, source_im, cosine, sine, form, sign):
    exact = lax.Precision.HIGHEST
    out_re = jnp.einsum(form, source_re, cosine, precision=exact) + sign * jnp.einsum(
        form, source_im, sine, precision=exact
    )
    out_im = jnp.einsum(form, source_im, cosine, precision=exact) - sign * jnp.einsum(
        form, source_re, sine, precision=exact
    )
    return (out_re, out_im)


def transform(stacked):
    count = stacked.shape[1]
    width = stacked.shape[2]
    second = min(128, width // 2)
    first = width // second
    two_pi = 2.0 * math.pi
    index_a = jnp.arange(first, dtype=jnp.int32)
    index_b = jnp.arange(second, dtype=jnp.int32)
    angle_a = two_pi * (index_a[:, None] * index_a[None, :] % first).astype(jnp.float32) / first
    angle_b = two_pi * (index_b[:, None] * index_b[None, :] % second).astype(jnp.float32) / second
    angle_t = two_pi * (index_a[:, None] * index_b[None, :] % width).astype(jnp.float32) / width
    cos_a, sin_a = (jnp.cos(angle_a), jnp.sin(angle_a))
    cos_b, sin_b = (jnp.cos(angle_b), jnp.sin(angle_b))
    cos_t, sin_t = (jnp.cos(angle_t), jnp.sin(angle_t))
    wavenum = index_a[:, None] + first * index_b[None, :]
    signed = jnp.where(wavenum < width // 2, wavenum, wavenum - width)
    phase = (signed * signed).astype(jnp.float32) * (DIFF / (width / 2) ** 2)
    cos_p, sin_p = (jnp.cos(phase), jnp.sin(phase))
    real_in = stacked[0].reshape(count, first, second)
    imag_in = stacked[1].reshape(count, first, second)
    step_re, step_im = rotate(real_in, imag_in, cos_a, sin_a, "nab,ak->nkb", 1.0)
    twist_re = step_re * cos_t + step_im * sin_t
    twist_im = step_im * cos_t - step_re * sin_t
    spec_re, spec_im = rotate(twist_re, twist_im, cos_b, sin_b, "nkb,bj->nkj", 1.0)
    moved_re = spec_re * cos_p - spec_im * sin_p
    moved_im = spec_re * sin_p + spec_im * cos_p
    back_re, back_im = rotate(moved_re, moved_im, cos_b, sin_b, "nkj,jb->nkb", -1.0)
    untw_re = back_re * cos_t - back_im * sin_t
    untw_im = back_im * cos_t + back_re * sin_t
    final_re, final_im = rotate(untw_re, untw_im, cos_a, sin_a, "nkb,ka->nab", -1.0)
    return jnp.stack([final_re.reshape(count, width), final_im.reshape(count, width)]) / width


def added_up(value, axis):
    count = lax.axis_size(axis)
    if count & (count - 1):
        return lax.psum(value, axis)
    reach = 1
    while reach < count:
        value = value + lax.ppermute(value, axis, [(i, i ^ reach) for i in range(count)])
        reach *= 2
    return value


def lateral_work(parts):
    return (transform(parts[0]), transform(parts[1]))


def multiplier_revision(
    population_multiplier,
    holeburn_multiplier,
    measured_rightward,
    measured_leftward,
    rightward_wave,
    leftward_wave,
    population_level,
    holeburn_magnitude,
    attenuation_factor,
    transverse_curvature,
):
    rightward_inphase, rightward_quadrature = (rightward_wave[0], rightward_wave[1])
    leftward_inphase, leftward_quadrature = (leftward_wave[0], leftward_wave[1])
    measured_rightward_inphase, measured_rightward_quadrature = (
        measured_rightward[0],
        measured_rightward[1],
    )
    measured_leftward_inphase, measured_leftward_quadrature = (
        measured_leftward[0],
        measured_leftward[1],
    )
    surplus_population = population_level - 1.0
    amplification_inphase = 1.0 + 0.5 * (GAIN_SLOPE_RATE * surplus_population - attenuation_factor)
    amplification_quadrature = 0.5 * GAIN_SLOPE_RATE * ALPHA_LINEWIDTH * surplus_population
    joined_waves = COUPLING * holeburn_magnitude
    population_derivative = (
        2.0 * CLOCK_DELTA * GAIN_SLOPE_RATE * surplus_population * population_multiplier
    )
    holeburn_derivative = 2.0 * CLOCK_DELTA * holeburn_multiplier
    revised_rightward_inphase = (
        amplification_inphase * measured_rightward_inphase
        - amplification_quadrature * measured_rightward_quadrature
        + joined_waves * measured_leftward_quadrature
        - population_derivative * rightward_inphase
        + holeburn_derivative * leftward_inphase
    )
    revised_rightward_quadrature = (
        amplification_inphase * measured_rightward_quadrature
        + amplification_quadrature * measured_rightward_inphase
        - joined_waves * measured_leftward_inphase
        - population_derivative * rightward_quadrature
        + holeburn_derivative * leftward_quadrature
    )
    revised_leftward_inphase = (
        amplification_inphase * measured_leftward_inphase
        - amplification_quadrature * measured_leftward_quadrature
        + joined_waves * measured_rightward_quadrature
        - population_derivative * leftward_inphase
        + holeburn_derivative * rightward_inphase
    )
    revised_leftward_quadrature = (
        amplification_inphase * measured_leftward_quadrature
        + amplification_quadrature * measured_leftward_inphase
        - joined_waves * measured_rightward_inphase
        - population_derivative * leftward_quadrature
        + holeburn_derivative * rightward_quadrature
    )
    light_intensity = (
        rightward_inphase * rightward_inphase
        + rightward_quadrature * rightward_quadrature
        + leftward_inphase * leftward_inphase
        + leftward_quadrature * leftward_quadrature
    )
    amplification_share = (
        measured_rightward_inphase * (rightward_inphase + ALPHA_LINEWIDTH * rightward_quadrature)
        + measured_rightward_quadrature
        * (rightward_quadrature - ALPHA_LINEWIDTH * rightward_inphase)
        + measured_leftward_inphase * (leftward_inphase + ALPHA_LINEWIDTH * leftward_quadrature)
        + measured_leftward_quadrature * (leftward_quadrature - ALPHA_LINEWIDTH * leftward_inphase)
    )
    revised_population = (
        population_multiplier
        * (1.0 - CLOCK_DELTA / DENSITY_LIFETIME - CLOCK_DELTA * GAIN_SLOPE_RATE * light_intensity)
        + TRANSVERSE_DIFFUS * transverse_curvature
        + 0.5 * GAIN_SLOPE_RATE * amplification_share
    )
    fresh_holeburn = holeburn_multiplier * (1.0 - CLOCK_DELTA / GRATING_LIFE) + COUPLING * (
        measured_rightward_quadrature * leftward_inphase
        - measured_rightward_inphase * leftward_quadrature
        + measured_leftward_quadrature * rightward_inphase
        - measured_leftward_inphase * rightward_quadrature
    )
    return (
        jnp.stack([revised_rightward_inphase, revised_rightward_quadrature]),
        jnp.stack([revised_leftward_inphase, revised_leftward_quadrature]),
        revised_population,
        fresh_holeburn,
    )


def per_device(
    ending_rightward_adjoint,
    ending_leftward_adjoint,
    ending_population_adjoint,
    ending_holeburn_adjoint,
    history_rightward,
    history_leftward,
    history_population,
    history_holeburn,
    segment_passive_attenuation,
):
    columns = ending_rightward_adjoint.shape[2]
    rows = ending_rightward_adjoint.shape[1]
    blocks = lax.axis_size("gz")
    position = lax.axis_index("gz")
    cells = rows * blocks
    zpos = (position * rows + jnp.arange(rows, dtype=jnp.int32)).astype(jnp.float32)
    scaling_factor = 1.0 + 2.0 * zpos / (cells - 1)
    rightward_multiplier, leftward_multiplier = (ending_rightward_adjoint, ending_leftward_adjoint)
    population_multiplier, holeburn_multiplier = (
        ending_population_adjoint,
        ending_holeburn_adjoint,
    )
    attenuation_factor = segment_passive_attenuation.astype(jnp.float32)
    shape_curve = jnp.zeros((columns,), jnp.float32)
    for moment_position in range(history_rightward.shape[0] - 1, -1, -1):
        shape_curve = shape_curve + jnp.sum(scaling_factor[:, None] * population_multiplier, axis=0)
        above = passed_along(rightward_multiplier[:, :1, :], "gz", -1)
        below = passed_along(leftward_multiplier[:, -1:, :], "gz", 1)
        top_row = jnp.where(
            position == blocks - 1, FRONT_FACET * leftward_multiplier[:, -1:, :], above
        )
        bottom_row = jnp.where(position == 0, REAR_FACET * rightward_multiplier[:, :1, :], below)
        lam_fwd = jnp.concatenate([rightward_multiplier[:, 1:, :], top_row], axis=1)
        lam_bwd = jnp.concatenate([bottom_row, leftward_multiplier[:, :-1, :]], axis=1)
        whole_fwd, whole_bwd = (
            lax.all_gather(lam_fwd, "gx", axis=2, tiled=True),
            lax.all_gather(lam_bwd, "gx", axis=2, tiled=True),
        )
        start = lax.axis_index("gx") * columns
        done_fwd, done_bwd = lateral_work((whole_fwd, whole_bwd))
        measured_rightward = lax.dynamic_slice_in_dim(done_fwd, start, columns, 2)
        measured_leftward = lax.dynamic_slice_in_dim(done_bwd, start, columns, 2)
        bordered_array = with_halo(population_multiplier, (("gx", 1),), 1)
        transverse_curvature = (
            bordered_array[:, 2:] + bordered_array[:, :-2] - 2.0 * population_multiplier
        )
        rightward_multiplier, leftward_multiplier, population_multiplier, holeburn_multiplier = (
            multiplier_revision(
                population_multiplier,
                holeburn_multiplier,
                measured_rightward,
                measured_leftward,
                history_rightward[moment_position].astype(jnp.float32),
                history_leftward[moment_position].astype(jnp.float32),
                history_population[moment_position].astype(jnp.float32),
                history_holeburn[moment_position].astype(jnp.float32),
                attenuation_factor,
                transverse_curvature,
            )
        )
    total = added_up(shape_curve, "gz")
    derivative_vector = CLOCK_DELTA * total / math.sqrt(cells)
    return (
        rightward_multiplier,
        leftward_multiplier,
        population_multiplier,
        holeburn_multiplier,
        derivative_vector,
    )

LANES = 128
TILE = 16
POWER = 12
STRETCH = 1211.0
SCALE_LANE = 8


def lateral_matrices(width, blocks):
    lanes = width // blocks
    k = np.arange(width)
    signed = np.where(k < width // 2, k, k - width).astype(np.float64)
    response = np.fft.ifft(np.exp(1j * signed * signed * (DIFF / (width / 2) ** 2)))
    step = np.arange(lanes)
    shift = lanes * np.arange(blocks)[:, None, None] + step[None, None, :] - step[None, :, None]
    kernels = np.fft.fft(response[shift % width], axis=0) / blocks
    top = np.concatenate([kernels.real, kernels.imag], axis=2)
    low = np.concatenate([-kernels.imag, kernels.real], axis=2)
    whole = np.concatenate([top, low], axis=1)
    first = whole.astype(ml_dtypes.bfloat16)
    rest = (whole - first.astype(np.float64)).astype(ml_dtypes.bfloat16)
    return np.stack([first, rest], axis=1)


def block_dft(values, sign):
    count = len(values)
    if count == 1:
        return values
    even = block_dft(values[0::2], sign)
    odd = block_dft(values[1::2], sign)
    out = [None] * count
    for k in range(count // 2):
        (er, ei), (wr, wi) = even[k], odd[k]
        if 4 * k == count:
            plus, minus = (er - wi, ei + wr), (er + wi, ei - wr)
            out[k], out[k + count // 2] = (plus, minus) if sign > 0 else (minus, plus)
            continue
        if k:
            c, s = math.cos(2 * math.pi * k / count), sign * math.sin(2 * math.pi * k / count)
            if 8 * k == count:
                wr, wi = (c * (wr - wi), c * (wr + wi)) if sign > 0 else (c * (wr + wi), c * (wi - wr))
            elif 8 * k == 3 * count:
                wr, wi = (c * (wr + wi), c * (wi - wr)) if sign > 0 else (c * (wr - wi), c * (wr + wi))
            else:
                wr, wi = c * wr - s * wi, c * wi + s * wr
        out[k] = (er + wr, ei + wi)
        out[k + count // 2] = (er - wr, ei - wi)
    return out


def lane(j):
    return pl.ds(pl.multiple_of(j * LANES, LANES), LANES)


def slab(j, rows):
    return pl.ds(pl.multiple_of(j * rows, rows), rows)


def fetch(pairs, sems, first=0):
    copies = [pltpu.make_async_copy(a, b, sems.at[first + i]) for i, (a, b) in enumerate(pairs)]
    for copy in copies:
        copy.start()
    return copies


def rows_of(info, rows, other):
    part = 1 - info[4] if other else info[4]
    return pl.ds(pl.multiple_of(part * rows, rows), rows)


def spread(field, work):
    rows = field.shape[1]
    blocks = work.shape[0]

    @pl.loop(0, rows // 8)
    def _(g):
        at = slab(g, 8)
        values = [
            (field[0, at, j * LANES : (j + 1) * LANES], field[1, at, j * LANES : (j + 1) * LANES])
            for j in range(blocks)
        ]
        for q, (re, im) in enumerate(block_dft(values, -1)):
            work[q, at, :LANES] = re
            work[q, at, LANES:] = im


def multiply(work, matrices):
    rows = work.shape[1]

    @pl.loop(0, work.shape[0], unroll=True)
    def _(q):
        value = work[q]
        first = value.astype(jnp.bfloat16)
        rest = (value - first.astype(jnp.float32)).astype(jnp.bfloat16)
        both = jnp.dot(
            jnp.concatenate([first, rest]), matrices[q, 0], preferred_element_type=jnp.float32
        )
        fine = jnp.dot(first, matrices[q, 1], preferred_element_type=jnp.float32)
        work[q] = both[:rows] + (both[rows:] + fine)


def gathered(work, at):
    values = [(work[q, at, :LANES], work[q, at, LANES:]) for q in range(work.shape[0])]
    return block_dft(values, 1)


def filtered(field, work, matrices, copy):
    spread(field, work)
    copy.wait()
    multiply(work, matrices)


def write_filtered(info, work, forward, backward, inner, outer):
    rows = work.shape[1] // 2
    for target, base, offset in ((forward, 0, 0), (backward, rows, 8)):

        @pl.loop(0, rows // 8)
        def _(g):
            here = pl.ds(pl.multiple_of(g * 8 + offset, 8), 8)
            for j, pair in enumerate(gathered(work, pl.ds(pl.multiple_of(g * 8 + base, 8), 8))):
                for part in range(2):
                    target[part, here, j * LANES : (j + 1) * LANES] = pair[part]

    low = info[4] == 0
    for part in range(2):
        first, last = forward[part, 0:1, :], backward[part, rows + 7 : rows + 8, :]
        inner[part : part + 1, :] = jnp.where(low, last, first)
        outer[part : part + 1, :] = jnp.where(low, first, last)


def size_of(largest):
    top = jnp.max(jnp.max(largest, axis=1, keepdims=True), axis=0, keepdims=True)
    return jnp.maximum(top, 1e-30).astype(jnp.bfloat16).astype(jnp.float32)


def encoded(value, size):
    unit = value * (STRETCH / size)
    square = unit * unit
    fourth = square * square
    return (fourth * fourth * square * (unit * jnp.abs(unit))).astype(jnp.bfloat16)


def decoded(code, size):
    value = code.astype(jnp.float32)
    root = jnp.exp2(jnp.log(jnp.abs(value)) * (1.0 / (POWER * math.log(2.0)))) * (size / STRETCH)
    return jnp.where(value < 0.0, -root, root)


def side_tile(columns, rows):
    index = lax.broadcasted_iota(jnp.int32, (rows, LANES), 1)
    tile = jnp.zeros((rows, LANES), jnp.float32)
    for at, column in columns:
        tile = jnp.where(index == at, column, tile)
    return tile.astype(jnp.bfloat16)


def sizes_in(tile, count):
    value = tile.astype(jnp.float32)
    return [value[0:1, SCALE_LANE + i : SCALE_LANE + i + 1] for i in range(count)]


def updated(fr, fi, br, bi, wave, population, hole, loss, carrier, grating, lap):
    rr, ri, lr, li = wave
    surplus = population - 1.0
    gain_re = 1.0 + 0.5 * (GAIN_SLOPE_RATE * surplus - loss)
    gain_im = (0.5 * GAIN_SLOPE_RATE * ALPHA_LINEWIDTH) * surplus
    joined = COUPLING * hole
    drive = (2.0 * CLOCK_DELTA * GAIN_SLOPE_RATE) * surplus * carrier
    mix = (2.0 * CLOCK_DELTA) * grating
    new_fr = gain_re * fr - gain_im * fi + joined * bi - drive * rr + mix * lr
    new_fi = gain_re * fi + gain_im * fr - joined * br - drive * ri + mix * li
    new_br = gain_re * br - gain_im * bi + joined * fi - drive * lr + mix * rr
    new_bi = gain_re * bi + gain_im * br - joined * fr - drive * li + mix * ri
    light = rr * rr + ri * ri + lr * lr + li * li
    share = (
        fr * (rr + ALPHA_LINEWIDTH * ri)
        + fi * (ri - ALPHA_LINEWIDTH * rr)
        + br * (lr + ALPHA_LINEWIDTH * li)
        + bi * (li - ALPHA_LINEWIDTH * lr)
    )
    new_carrier = (
        carrier * ((1.0 - CLOCK_DELTA / DENSITY_LIFETIME) - (CLOCK_DELTA * GAIN_SLOPE_RATE) * light)
        + TRANSVERSE_DIFFUS * lap
        + (0.5 * GAIN_SLOPE_RATE) * share
    )
    new_grating = grating * (1.0 - CLOCK_DELTA / GRATING_LIFE) + COUPLING * (
        fi * lr - fr * li + bi * rr - br * ri
    )
    return new_fr, new_fi, new_br, new_bi, new_carrier, new_grating


def curvature(left, mid, right, weight_left, weight_right):
    index = lax.broadcasted_iota(jnp.int32, mid.shape, 1)
    below = jnp.where(index == 0, pltpu.roll(left, 1, 1) * weight_left, pltpu.roll(mid, 1, 1))
    above = jnp.where(
        index == LANES - 1,
        pltpu.roll(right, LANES - 1, 1) * weight_right,
        pltpu.roll(mid, LANES - 1, 1),
    )
    return below + above - 2.0 * mid


def send_fields_kernel(info, forward, backward, out, fields, sems):
    rows, columns = fields.shape[2:]
    half = columns // LANES
    at = rows_of(info, rows, True)
    copies = fetch(
        [(ref.at[:, at, :], fields.at[f]) for f, ref in enumerate((forward, backward))], sems
    )
    sizes = []
    for f in range(2):
        copies[f].wait()
        largest = jnp.maximum(jnp.abs(fields[f, 0]), jnp.abs(fields[f, 1]))
        size = size_of(largest)
        sizes.append((SCALE_LANE + f, size))
        for part in range(2):
            put_tiles(out, (2 * f + part) * half, encoded(fields[f, part], size))
    out[4 * half * rows :, :] = side_tile(sizes, rows)


def put_tiles(out, first, value):
    rows, columns = value.shape
    for j in range(columns // LANES):
        at = (first + j) * rows
        out[at : at + rows, :] = value[:, j * LANES : (j + 1) * LANES]


def history_rows(forward, backward, population, hole, s, at):
    return [
        forward.at[s, 0, at, :], forward.at[s, 1, at, :], backward.at[s, 0, at, :],
        backward.at[s, 1, at, :], population.at[s, at, :], hole.at[s, at, :],
    ]


def into_rows(parts, target, first, rows):
    return [(part, target.at[pl.ds(first + i * rows, rows), :]) for i, part in enumerate(parts)]


def send_later_kernel(steps, info, forward, backward, population, hole, final, *refs):
    targets, sems = refs[:-1], refs[-1]
    rows = targets[0].shape[0] // 6
    history = (forward, backward, population, hole)
    pairs = []
    for i, s in enumerate(steps):
        for k, other in enumerate((True, False)):
            at = rows_of(info, rows, other)
            pairs += into_rows(history_rows(*history, s, at), targets[2 * i + k], 0, rows)
    pairs += into_rows(history_rows(*history, 0, pl.ds(0, 2 * rows)), final, 0, 2 * rows)
    for copy in fetch(pairs, sems):
        copy.wait()


def send_first_kernel(
    s, info, loss, carrier, grating, forward, backward, population, hole,
    own_loss, own, own_carrier, own_grating, out, own_edge, states, ends, sems,
):
    rows, columns = own_carrier.shape
    theirs, mine = rows_of(info, rows, True), rows_of(info, rows, False)
    history = (forward, backward, population, hole)
    copies = fetch(
        [(carrier.at[theirs, :], states.at[0]), (grating.at[theirs, :], states.at[1])]
        + into_rows([loss.at[theirs, :]], out, 0, rows)
        + into_rows(history_rows(*history, s, theirs), out, 3 * rows, rows)
        + [(loss.at[mine, :], own_loss), (carrier.at[mine, :], own_carrier)]
        + [(grating.at[mine, :], own_grating)]
        + into_rows(history_rows(*history, s, mine), own, 0, rows)
        + [
            (part, ends.at[k, i])
            for k in range(2)
            for i, part in enumerate(
                history_rows(*history, 1, pl.ds(k * (2 * rows - TILE), TILE))
            )
        ],
        sems,
    )
    for copy in copies[:2]:
        copy.wait()
    sizes = []
    for i in range(2):
        size = size_of(jnp.abs(states[i]))
        sizes.append(jnp.broadcast_to(size, (1, columns)))
        out[(1 + i) * rows : (2 + i) * rows, :] = encoded(states[i], size)
    for copy in copies[2:]:
        copy.wait()
    low = info[4] == 0
    top = [ends[0, i].astype(jnp.float32)[:1] for i in range(6)]
    foot = [ends[1, i].astype(jnp.float32)[TILE - 1 :] for i in range(6)]
    own_edge[...] = jnp.concatenate([jnp.where(low, a, b) for a, b in zip(top, foot)])
    sizes += [jnp.where(low, b, a) for a, b in zip(top, foot)]
    sizes.append(jnp.zeros((TILE - 8, columns), jnp.float32))
    out[9 * rows :, :] = jnp.concatenate(sizes).astype(jnp.bfloat16)


def enter_kernel(
    info, forward, backward, other, source, tp, tq, inner, outer, field, work, matrices, sem, sems
):
    copy = pltpu.make_async_copy(source, matrices, sem)
    rows, width = field.shape[1] // 2, field.shape[2]
    columns = width // 2
    half = columns // LANES
    at = rows_of(info, rows, False)
    copies = fetch(
        [
            (ref.at[:, at, :], field.at[:, f * rows : (f + 1) * rows, :columns])
            for f, ref in enumerate((forward, backward))
        ],
        sems,
    )
    copy.start()
    sizes = sizes_in(other[4 * half * rows :, :], 2)
    for f in range(2):
        for part in range(2):

            @pl.loop(0, half, unroll=2)
            def _(j):
                code = other[slab((2 * f + part) * half + j, rows), :]
                field[part, f * rows : (f + 1) * rows, lane(half + j)] = decoded(code, sizes[f])

    for held in copies:
        held.wait()
    filtered(field, work, matrices, copy)
    write_filtered(info, work, tp, tq, inner, outer)


def rows_update(
    info, tp, tq, inner, outer, carrier, grating, own, other, own_loss, other_loss,
    field, new_carrier, new_grating, sums_in, sums, cells, last
):
    rows, width = carrier.shape
    half = width // LANES // 2
    columns = half * LANES
    mid = jnp.where(info[0] == 0, 1.0, 0.0)
    wrap = 1.0 - mid
    low = info[4] == 0
    is_first, is_last = info[1], info[2]
    row_index = lax.broadcasted_iota(jnp.int32, (TILE, LANES), 0)
    zero = jnp.zeros((8, LANES), jnp.float32)

    def step(jj, most):
        for side in range(2):
            j = jj + side * half
            here = lane(j)
            left_at = lane(jnp.where(j == 0, 2 * half - 1, j - 1))
            right_at = lane(jnp.where(j == 2 * half - 1, 0, j + 1))
            swapped = lane(jj + (1 - side) * half)
            weight_left = jnp.where(jj == 0, wrap if side == 0 else mid, 1.0)
            weight_right = jnp.where(jj == half - 1, mid if side == 0 else wrap, 1.0)
            total = zero
            for r in range(0, rows, TILE):
                at = slice(r, r + TILE)

                held, begin = (own, other)[side]

                def part_of(i):
                    tile = begin + i * rows + r
                    return held[tile : tile + TILE, lane(jj)].astype(jnp.float32)

                loss = (own_loss, other_loss)[side][at, lane(jj)].astype(jnp.float32)
                f = [tp[part, r + 1 : r + 1 + TILE, here] for part in range(2)]
                b = [tq[part, r + 7 : r + 7 + TILE, here] for part in range(2)]
                if r + TILE == rows:
                    for part in range(2):
                        facet = FRONT_FACET * tq[part, rows + 7 : rows + 8, here]
                        edge = jnp.where(
                            low, inner[part : part + 1, swapped], outer[part : part + 1, here]
                        )
                        edge = jnp.where(is_last, facet, edge)
                        f[part] = jnp.where(row_index == TILE - 1, edge, f[part])
                if r == 0:
                    for part in range(2):
                        facet = REAR_FACET * tp[part, 0:1, here]
                        edge = jnp.where(
                            low, outer[part : part + 1, here], inner[part : part + 1, swapped]
                        )
                        edge = jnp.where(is_first, facet, edge)
                        b[part] = jnp.where(row_index == 0, edge, b[part])
                c = carrier[at, here]
                lap = curvature(
                    carrier[at, left_at], c, carrier[at, right_at], weight_left, weight_right
                )
                out = updated(
                    *f, *b, [part_of(i) for i in range(4)], part_of(4), part_of(5), loss,
                    c, grating[at, here], lap,
                )
                field[0, r : r + TILE, here] = out[0]
                field[1, r : r + TILE, here] = out[1]
                field[0, rows + r : rows + r + TILE, here] = out[2]
                field[1, rows + r : rows + r + TILE, here] = out[3]
                new_carrier[at, here] = out[4]
                new_grating[at, here] = out[5]
                z = (info[3] + r + row_index).astype(jnp.float32)
                weighted = (1.0 + 2.0 * z / (cells - 1)) * ((c + out[4]) if last else c)
                for k in range(0, TILE, 8):
                    total = total + weighted[k : k + 8]
                if last and side == 1:
                    for k in range(0, TILE, 8):
                        most = (
                            jnp.maximum(most[0], jnp.abs(out[4][k : k + 8])),
                            jnp.maximum(most[1], jnp.abs(out[5][k : k + 8])),
                        )
            summed = jnp.sum(total, axis=0, keepdims=True)
            sums[:, here] = summed if sums_in is None else summed + sums_in[:, here]
        return most

    return lax.fori_loop(0, half, step, (zero, zero))


def first_step_kernel(
    cells, info, tp, tq, inner, outer, my_carrier, my_grating, loss, own, own_edge, other, source,
    new_tp, new_tq, new_inner, new_outer, new_carrier, new_grating, sums,
    carrier, grating, field, work, matrices, sem,
):
    copy = pltpu.make_async_copy(source, matrices, sem)
    copy.start()
    rows, columns = my_carrier.shape
    half = columns // LANES
    extra = other[9 * rows :, :].astype(jnp.float32)
    sizes = [extra[0:1, 0:1], extra[1:2, 0:1]]
    new_outer[2:8, :columns] = own_edge[...]
    new_outer[2:8, columns:] = extra[2:8]
    for i, (whole, mine) in enumerate(((carrier, my_carrier), (grating, my_grating))):
        whole[:, :columns] = mine[...]

        @pl.loop(0, half, unroll=2)
        def _(j):
            whole[:, lane(half + j)] = decoded(
                other[(1 + i) * rows : (2 + i) * rows, lane(j)], sizes[i]
            )

    rows_update(
        info, tp, tq, inner, outer, carrier, grating, (own, 0), (other, 3 * rows), loss, other,
        field, new_carrier, new_grating, None, sums, cells, False,
    )
    filtered(field, work, matrices, copy)
    write_filtered(info, work, new_tp, new_tq, new_inner, new_outer)


def middle_step_kernel(
    cells, info, tp, tq, inner, outer, carrier, grating, loss, own, other, other_loss, sums_in,
    source, new_tp, new_tq, new_inner, new_outer, new_carrier, new_grating, sums,
    field, work, matrices, sem,
):
    copy = pltpu.make_async_copy(source, matrices, sem)
    copy.start()
    rows_update(
        info, tp, tq, inner, outer, carrier, grating, (own, 0), (other, 0), loss, other_loss,
        field, new_carrier, new_grating, sums_in, sums, cells, False,
    )
    filtered(field, work, matrices, copy)
    write_filtered(info, work, new_tp, new_tq, new_inner, new_outer)
    rows = carrier.shape[0]
    low = info[4] == 0
    for part in range(2):
        new_outer[2 + part : 3 + part, :] = jnp.where(
            low, new_tp[part, 1:2, :], new_tq[part, rows + 6 : rows + 7, :]
        )
    for i, ref in enumerate((new_carrier, new_grating)):
        new_outer[4 + i : 5 + i, :] = jnp.where(low, ref[0:1, :], ref[rows - 1 : rows, :])
    columns = loss.shape[1]
    for part, ref in enumerate((loss, other_loss)):
        top = ref[:TILE, :].astype(jnp.float32)[:1]
        foot = ref[rows - TILE :, :].astype(jnp.float32)[TILE - 1 :]
        new_outer[6:7, part * columns : (part + 1) * columns] = jnp.where(low, top, foot)


def row_beyond(info, tp, tq, outer, beyond):
    rows = tp.shape[1] - 8
    low = info[4] == 0
    xr, xi, carrier, grating = (outer[i : i + 1, :] for i in range(2, 6))
    yr, yi = (
        jnp.where(low, tp[part, 0:1, :], tq[part, rows + 7 : rows + 8, :]) for part in range(2)
    )
    rr, ri, lr, li, population, hole = (beyond[i : i + 1, :] for i in range(2, 8))
    loss = outer[6:7, :]
    surplus = population - 1.0
    gain_re = 1.0 + 0.5 * (GAIN_SLOPE_RATE * surplus - loss)
    gain_im = (0.5 * GAIN_SLOPE_RATE * ALPHA_LINEWIDTH) * surplus
    joined = COUPLING * hole
    drive = (2.0 * CLOCK_DELTA * GAIN_SLOPE_RATE) * surplus * carrier
    mix = (2.0 * CLOCK_DELTA) * grating
    near_re, near_im = jnp.where(low, lr, rr), jnp.where(low, li, ri)
    far_re, far_im = jnp.where(low, rr, lr), jnp.where(low, ri, li)
    new_re = gain_re * xr - gain_im * xi + joined * yi - drive * near_re + mix * far_re
    new_im = gain_re * xi + gain_im * xr - joined * yr - drive * near_im + mix * far_im
    return new_re, new_im


def leave_step_kernel(
    cells, info, tp, tq, inner, outer, beyond, carrier, grating, loss, own, other, other_loss,
    sums_in, source, field, kept_carrier, kept_grating, sides, sent, shares, matrices,
    sums, new_carrier, new_grating, sem,
):
    copy = pltpu.make_async_copy(source, matrices, sem)
    copy.start()
    rows, width = carrier.shape
    columns = width // 2
    half = columns // LANES
    most = rows_update(
        info, tp, tq, inner, outer, carrier, grating, (own, 0), (other, 0), loss, other_loss,
        field, new_carrier, new_grating, sums_in, sums, cells, True,
    )
    for part, value in enumerate(row_beyond(info, tp, tq, outer, beyond)):
        field[part, 2 * rows :, :] = jnp.broadcast_to(value, (8, width))
    mid = jnp.where(info[0] == 0, 1.0, 0.0)
    wrap = 1.0 - mid
    kept_carrier[...] = new_carrier[:, :columns]
    kept_grating[...] = new_grating[:, :columns]
    first, before = new_carrier[:, 0:1] * wrap, new_carrier[:, columns - 1 : columns] * mid
    after, final = new_carrier[:, columns : columns + 1] * mid, new_carrier[:, width - 1 :] * wrap
    sides[0] = jnp.broadcast_to(final, (rows, LANES))
    sides[1] = jnp.broadcast_to(after, (rows, LANES))
    pairs = []
    for at, value in ((0, before), (2, first)):
        coarse = value.astype(jnp.bfloat16).astype(jnp.float32)
        pairs += [(at, coarse), (at + 1, value - coarse)]
    for i, field_of in enumerate((new_carrier, new_grating)):
        size = size_of(most[i])
        pairs.append((SCALE_LANE + i, size))

        @pl.loop(0, half, unroll=2)
        def _(j):
            sent[slab(i * half + j, rows), :] = encoded(field_of[:, lane(half + j)], size)

    sent[2 * half * rows :, :] = side_tile(pairs, rows)
    tile = jnp.concatenate([sums[:, j * LANES : (j + 1) * LANES] for j in range(2 * half)])
    near, far = tile[:half], tile[half:]
    low = info[0] == 0
    to_first, to_second = jnp.where(low, near, far), jnp.where(low, far, near)
    for i in range(0, shares.shape[0], 2):
        shares[i] = to_first
        shares[i + 1] = to_second
    copy.wait()


def leave_filter_kernel(info, field, matrices, kept, sent, edge, work):
    rows, width = (field.shape[1] - 8) // 2, field.shape[2]
    half = width // LANES // 2
    spread(field, work)
    multiply(work, matrices)
    pairs = []
    zero = jnp.zeros((8, LANES), jnp.float32)
    for f in range(2):

        def unmix(g, most):
            at = pl.ds(pl.multiple_of(g * 8 + f * rows, 8), 8)
            for j, pair in enumerate(gathered(work, at)):
                for part in range(2):
                    if j < half:
                        kept[part, at, j * LANES : (j + 1) * LANES] = pair[part]
                    else:
                        work[j, at, part * LANES : (part + 1) * LANES] = pair[part]
                        most = jnp.maximum(most, jnp.abs(pair[part]))
            return most

        size = size_of(lax.fori_loop(0, rows // 8, unmix, zero))
        pairs.append((SCALE_LANE + f, size))

        @pl.loop(0, half, unroll=2)
        def _(j):
            for part in range(2):
                value = work[half + j, f * rows : (f + 1) * rows, part * LANES : (part + 1) * LANES]
                sent[slab((2 * f + part) * half + j, rows), :] = encoded(value, size)

    ends = gathered(work, slice(2 * rows, 2 * rows + 8))
    for part in range(2):
        for j in range(half):
            edge[part : part + 1, j * LANES : (j + 1) * LANES] = ends[j][part][:1]
    far = jnp.concatenate([ends[j][part][:1] for part in range(2) for j in range(half, 2 * half)])
    size = size_of(jnp.abs(far))
    pairs.append((SCALE_LANE + 2, size))
    sent[4 * half * rows : (4 * half + 1) * rows, :] = side_tile(pairs, rows)
    spare = jnp.zeros((rows - 2 * half, LANES), jnp.float32)
    sent[(4 * half + 1) * rows :, :] = encoded(jnp.concatenate([far, spare]), size)


def total_kernel(cells, info, partial, out):
    total = partial[0]
    for i in range(1, partial.shape[0]):
        total = total + partial[i]
    out[...] = total * (CLOCK_DELTA / math.sqrt(cells))


def final_kernel(
    info, kept, kept_carrier, kept_grating, sides, fields, pair, edge, loss, history,
    out_forward, out_backward, out_carrier, out_grating,
    tp, tq, carrier, grating,
):
    rows, columns = kept_carrier.shape
    half = columns // LANES
    mine = info[4] * rows
    theirs = (1 - info[4]) * rows
    low = info[4] == 0
    extra = pair[2 * half * rows :, :]
    size_carrier, size_grating = sizes_in(extra, 2)
    sizes = fields[4 * half * rows : (4 * half + 1) * rows, :]
    size_forward, size_backward, size_edge = sizes_in(sizes, 3)
    ends = decoded(fields[(4 * half + 1) * rows :, :], size_edge)
    extra = extra.astype(jnp.float32)

    def at(start, offset, count):
        return pl.ds(pl.multiple_of(start + offset, 8), count)

    for part in range(2):
        tp[part, at(mine, 0, rows), :] = kept[part, :rows, :]
        tq[part, at(mine, 8, rows), :] = kept[part, rows:, :]
    carrier[at(mine, 0, rows), LANES : LANES + columns] = kept_carrier[...]
    carrier[at(mine, 0, rows), :LANES] = sides[0]
    carrier[at(mine, 0, rows), LANES + columns :] = sides[1]
    carrier[at(theirs, 0, rows), :LANES] = jnp.broadcast_to(
        extra[:, 0:1] + extra[:, 1:2], (rows, LANES)
    )
    carrier[at(theirs, 0, rows), LANES + columns :] = jnp.broadcast_to(
        extra[:, 2:3] + extra[:, 3:4], (rows, LANES)
    )
    grating[at(mine, 0, rows), :] = kept_grating[...]

    @pl.loop(0, half, unroll=2)
    def _(j):
        carrier[at(theirs, 0, rows), lane(1 + j)] = decoded(
            pair[slab(j, rows), :], size_carrier
        )
        grating[at(theirs, 0, rows), lane(j)] = decoded(
            pair[slab(half + j, rows), :], size_grating
        )
        for part in range(2):
            tp[part, at(theirs, 0, rows), lane(j)] = decoded(
                fields[slab(part * half + j, rows), :], size_forward
            )
            tq[part, at(theirs, 8, rows), lane(j)] = decoded(
                fields[slab((2 + part) * half + j, rows), :], size_backward
            )

    all_rows = 2 * rows
    for part in range(2):
        near = edge[part : part + 1, :]
        far = jnp.concatenate([ends[part * half + j : part * half + j + 1] for j in range(half)], axis=1)
        next_edge = jnp.where(low, far, near)
        before_edge = jnp.where(low, near, far)
        front = FRONT_FACET * tq[part, all_rows + 7 : all_rows + 8, :]
        rear = REAR_FACET * tp[part, 0:1, :]
        tp[part, all_rows : all_rows + 1, :] = jnp.where(info[2], front, next_edge)
        tq[part, 7:8, :] = jnp.where(info[1], rear, before_edge)

    @pl.loop(0, half)
    def _(j):
        here = lane(j)
        for r in range(0, all_rows, TILE):
            row = slice(r, r + TILE)
            c = carrier[row, lane(j + 1)]
            lap = curvature(carrier[row, lane(j)], c, carrier[row, lane(j + 2)], 1.0, 1.0)
            parts = [
                history[i * all_rows + r : i * all_rows + r + TILE, here].astype(jnp.float32)
                for i in range(6)
            ]
            out = updated(
                tp[0, r + 1 : r + 1 + TILE, here], tp[1, r + 1 : r + 1 + TILE, here],
                tq[0, r + 7 : r + 7 + TILE, here], tq[1, r + 7 : r + 7 + TILE, here],
                parts[:4], parts[4], parts[5],
                loss[row, here].astype(jnp.float32), c, grating[row, here], lap,
            )
            out_forward[0, row, here] = out[0]
            out_forward[1, row, here] = out[1]
            out_backward[0, row, here] = out[2]
            out_backward[1, row, here] = out[3]
            out_carrier[row, here] = out[4]
            out_grating[row, here] = out[5]


def position(rows, whole):
    x, block, count = lax.axis_index("gx"), lax.axis_index("gz"), lax.axis_size("gz")
    high = lax.rem(x + block, 2)
    if whole:
        return x, block == 0, block == count - 1, block * rows, high
    place = 2 * block + high
    return x, place == 0, place == 2 * count - 1, place * rows, high


def whole_spec(shape):
    return pl.BlockSpec(shape, lambda i, n=len(shape): (0,) * n)


def call(name, kernel, rows, inputs, outputs, scratch, flops=0, grant=24, whole=False):
    arrays = [x[0] if isinstance(x, tuple) else x for x in inputs]
    specs = [x[1] if isinstance(x, tuple) else whole_spec(x.shape) for x in inputs]
    shapes = [jax.ShapeDtypeStruct(*out) for out in outputs]
    moved = sum(math.prod(s.shape) * s.dtype.itemsize for s in shapes)

    def body(*refs):
        kernel(position(rows, whole), *refs)

    return pl.pallas_call(
        body,
        grid=(1,),
        in_specs=specs,
        out_specs=[whole_spec(s.shape) for s in shapes],
        scratch_shapes=scratch,
        out_shape=shapes,
        compiler_params=pltpu.CompilerParams(vmem_limit_bytes=grant * 1024 * 1024),
        cost_estimate=pl.CostEstimate(
            flops=flops, bytes_accessed=moved + 4 * 1024 * 1024, transcendentals=0
        ),
        name=name,
    )(*arrays)


def per_pair(
    ending_rightward_adjoint,
    ending_leftward_adjoint,
    ending_population_adjoint,
    ending_holeburn_adjoint,
    history_rightward,
    history_leftward,
    history_population,
    history_holeburn,
    segment_passive_attenuation,
):
    cell_rows, columns = ending_population_adjoint.shape
    passes = history_population.shape[0]
    rows = cell_rows // 2
    half = columns // LANES
    blocks = 2 * half
    width = 2 * columns
    count = lax.axis_size("gz")
    cells = cell_rows * count
    x = lax.axis_index("gx")
    f32, bf16 = jnp.float32, jnp.bfloat16
    swap = [(0, 1), (1, 0)]
    in_place = pl.BlockSpec(memory_space=pltpu.HBM)

    def held(*arrays):
        return [(a, in_place) for a in arrays]

    def tiles(n):
        return ((n * rows, LANES), bf16)

    ends = held(ending_rightward_adjoint, ending_leftward_adjoint)
    planes = held(ending_population_adjoint, ending_holeburn_adjoint)
    history = held(history_rightward, history_leftward, history_population, history_holeburn)
    losses = held(segment_passive_attenuation)
    matrices = pltpu.with_memory_space_constraint(
        jnp.asarray(lateral_matrices(width, blocks)), pltpu.HBM
    )
    matrix_input = held(matrices)
    work = [
        pltpu.VMEM((blocks, 2 * rows, 2 * LANES), f32),
        pltpu.VMEM(matrices.shape, bf16),
        pltpu.SemaphoreType.DMA,
    ]
    field_scratch = pltpu.VMEM((2, 2 * rows, width), f32)
    def state_out(outer_rows):
        state = ((2, rows + 8, width), f32)
        return [state, state, ((2, width), f32), ((outer_rows, width), f32)]

    plane = ((rows, width), f32)
    plane_scratch = pltpu.VMEM((rows, width), f32)
    half_plane = ((rows, columns), f32)
    work_flops = 2 * 3 * 2 * rows * blocks * (2 * LANES) ** 2

    (coded,) = call(
        "send_fields", send_fields_kernel, rows, ends, [tiles(4 * half + 1)],
        [pltpu.VMEM((2, 2, rows, columns), f32), pltpu.SemaphoreType.DMA((2,))], grant=62,
    )
    other_fields = lax.ppermute(coded, "gx", swap)
    loss, own_first, my_carrier, my_grating, sent_first, own_edge = call(
        "send_first", functools.partial(send_first_kernel, passes - 1), rows,
        [*losses, *planes, *history],
        [((rows, columns), bf16), ((6 * rows, columns), bf16), half_plane, half_plane,
         ((9 * rows + TILE, columns), bf16), ((6, columns), f32)],
        [pltpu.VMEM((2, rows, columns), f32), pltpu.VMEM((2, 6, TILE, columns), bf16),
         pltpu.SemaphoreType.DMA((30,))], grant=62,
    )
    steps = range(passes - 2, 0, -1)
    history_last, *later = call(
        "send_later", functools.partial(send_later_kernel, steps), rows, history,
        [((6 * cell_rows, columns), bf16)] + [((6 * rows, columns), bf16)] * (2 * len(steps)),
        [pltpu.SemaphoreType.DMA((12 * len(steps) + 6,))], grant=62,
    )
    sent_first, history_last, later, other_fields = lax.optimization_barrier(
        (sent_first, history_last, later, other_fields)
    )
    other_first = lax.ppermute(sent_first, "gx", swap)

    line = ("gz", "gx")
    neighbours = []
    for b in range(count - 1):
        top = (1 + b) % 2
        neighbours += [(2 * b + top, 2 * b + 2 + top), (2 * b + 2 + top, 2 * b + top)]

    def edges(inner, outer):
        outer = lax.ppermute(outer, line, neighbours)
        return lax.ppermute(inner, "gx", swap), outer

    tp, tq, inner, outer = call(
        "enter", enter_kernel, rows, [*ends, other_fields, *matrix_input],
        state_out(2), [field_scratch, *work, pltpu.SemaphoreType.DMA((2,))], work_flops,
    )
    inner, outer = edges(inner, outer)

    other_loss = (other_first, pl.BlockSpec((rows, columns), lambda i: (0, 0)))
    carrier = grating = sums = other = own = None
    for index, s in enumerate(range(passes - 1, 0, -1)):
        if index < len(steps):
            sent, own_next = later[2 * index : 2 * index + 2]
            sent, inner, outer = lax.optimization_barrier((sent, inner, outer))
            coming = lax.ppermute(sent, "gx", swap)
        shared = [tp, tq, inner, outer]
        if index == 0:
            tp, tq, inner, outer, carrier, grating, sums = call(
                "first_step", functools.partial(first_step_kernel, cells), rows,
                [*shared, my_carrier, my_grating, loss, own_first, own_edge, other_first,
                 *matrix_input],
                [*state_out(8), plane, plane, ((1, width), f32)],
                [plane_scratch, plane_scratch, field_scratch, *work], work_flops,
            )
        elif s > 1:
            tp, tq, inner, outer, carrier, grating, sums = call(
                "middle_step", functools.partial(middle_step_kernel, cells), rows,
                [*shared, carrier, grating, loss, own, other, other_loss, sums, *matrix_input],
                [*state_out(7), plane, plane, ((1, width), f32)],
                [field_scratch, *work], work_flops,
            )
        else:
            field, kept_carrier, kept_grating, sides, sent, shares, fetched = call(
                "leave_step", functools.partial(leave_step_kernel, cells), rows,
                [*shared, beyond, carrier, grating, loss, own, other, other_loss, sums, *matrix_input],
                [((2, 2 * rows + 8, width), f32), half_plane, half_plane, ((2, rows, LANES), f32),
                 tiles(2 * half + 1), ((2 * count, half, LANES), f32), (matrices.shape, bf16)],
                [pltpu.VMEM((1, width), f32), plane_scratch, plane_scratch,
                 pltpu.SemaphoreType.DMA],
            )
        if s > 1:
            inner, outer = edges(inner, outer)
            own, other = own_next, coming
            if index == 0:
                beyond = outer

    pair = lax.ppermute(sent, "gx", swap)
    kept, sent, edge = call(
        "leave_filter", leave_filter_kernel, rows, [field, fetched],
        [((2, 2 * rows, columns), f32), tiles(4 * half + 2), ((2, columns), f32)],
        [pltpu.VMEM((blocks, 2 * rows + TILE, 2 * LANES), f32)], work_flops,
    )
    sent, pair, shares = lax.optimization_barrier((sent, pair, shares))
    fields = lax.ppermute(sent, "gx", swap)
    shares = lax.all_to_all(shares, line, 0, 0, tiled=True)

    outs = call(
        "final", final_kernel, cell_rows,
        [kept, kept_carrier, kept_grating, sides, fields, pair, edge,
         segment_passive_attenuation, history_last],
        [((2, cell_rows, columns), f32), ((2, cell_rows, columns), f32),
         ((cell_rows, columns), f32), ((cell_rows, columns), f32)],
        [pltpu.VMEM((2, cell_rows + 8, columns), f32), pltpu.VMEM((2, cell_rows + 8, columns), f32),
         pltpu.VMEM((cell_rows, columns + 2 * LANES), f32), pltpu.VMEM((cell_rows, columns), f32)],
        whole=True,
    )
    shares, *outs = lax.optimization_barrier((shares, *outs))
    (total,) = call(
        "total", functools.partial(total_kernel, cells), rows, [shares], [((half, LANES), f32)], [],
    )
    return (*outs, total.reshape(columns))


def shared_by_pairs(mesh, arguments):
    population = arguments[6]
    passes, cells, width = population.shape
    rows, columns = cells // mesh.shape["gz"], width // mesh.shape["gx"]
    return (
        mesh.shape["gx"] == 2
        and passes >= 4
        and 4 * columns <= rows * LANES
        and rows % (2 * TILE) == 0
        and columns % LANES == 0
        and (columns // LANES) & (columns // LANES - 1) == 0
        and width <= 4096
    )


def solution(mesh):
    def run(*arguments):
        body = per_pair if shared_by_pairs(mesh, arguments) else per_device
        return jax.shard_map(
            body,
            mesh=mesh,
            in_specs=(
                P(None, "gz", "gx"),
                P(None, "gz", "gx"),
                P("gz", "gx"),
                P("gz", "gx"),
                P(None, None, "gz", "gx"),
                P(None, None, "gz", "gx"),
                P(None, "gz", "gx"),
                P(None, "gz", "gx"),
                P("gz", "gx"),
            ),
            out_specs=(
                P(None, "gz", "gx"), P(None, "gz", "gx"), P("gz", "gx"), P("gz", "gx"), P("gx"),
            ),
            check_vma=False,
        )(*arguments)

    return run
```

```python
import functools
import math

import jax
import jax.numpy as jnp
import ml_dtypes
import numpy as np
from jax import lax
from jax.experimental import pallas as pl
from jax.experimental.pallas import tpu as pltpu
from jax.sharding import PartitionSpec as P

DIFF = 512


FRONT_FACET = 0.3
REAR_FACET = 0.9
GAIN_SLOPE_RATE = 0.3
ALPHA_LINEWIDTH = 2.0
COUPLING = 0.5
CLOCK_DELTA = 0.3
DENSITY_LIFETIME = 2.0
GRATING_LIFE = 0.75
TRANSVERSE_DIFFUS = 0.2


def passed_along(value, axis, steps):
    count = lax.axis_size(axis)
    initial, last = (max(0, -steps), min(count, count - steps))
    return lax.ppermute(value, axis, [(source, source + steps) for source in range(initial, last)])


def with_halo(block, sides, width):
    for axis, dim in sides:
        count = lax.axis_size(axis)
        forward = [(i, i + 1) for i in range(count - 1)]
        backward = [(target, source) for source, target in forward]
        low = lax.ppermute(
            lax.slice_in_dim(block, block.shape[dim] - width, None, axis=dim), axis, forward
        )
        high = lax.ppermute(lax.slice_in_dim(block, 0, width, axis=dim), axis, backward)
        block = jnp.concatenate([low, block, high], axis=dim)
    return block


def rotate(source_re, source_im, cosine, sine, form, sign):
    exact = lax.Precision.HIGHEST
    out_re = jnp.einsum(form, source_re, cosine, precision=exact) + sign * jnp.einsum(
        form, source_im, sine, precision=exact
    )
    out_im = jnp.einsum(form, source_im, cosine, precision=exact) - sign * jnp.einsum(
        form, source_re, sine, precision=exact
    )
    return (out_re, out_im)


def transform(stacked):
    count = stacked.shape[1]
    width = stacked.shape[2]
    second = min(128, width // 2)
    first = width // second
    two_pi = 2.0 * math.pi
    index_a = jnp.arange(first, dtype=jnp.int32)
    index_b = jnp.arange(second, dtype=jnp.int32)
    angle_a = two_pi * (index_a[:, None] * index_a[None, :] % first).astype(jnp.float32) / first
    angle_b = two_pi * (index_b[:, None] * index_b[None, :] % second).astype(jnp.float32) / second
    angle_t = two_pi * (index_a[:, None] * index_b[None, :] % width).astype(jnp.float32) / width
    cos_a, sin_a = (jnp.cos(angle_a), jnp.sin(angle_a))
    cos_b, sin_b = (jnp.cos(angle_b), jnp.sin(angle_b))
    cos_t, sin_t = (jnp.cos(angle_t), jnp.sin(angle_t))
    wavenum = index_a[:, None] + first * index_b[None, :]
    signed = jnp.where(wavenum < width // 2, wavenum, wavenum - width)
    phase = (signed * signed).astype(jnp.float32) * (DIFF / (width / 2) ** 2)
    cos_p, sin_p = (jnp.cos(phase), jnp.sin(phase))
    real_in = stacked[0].reshape(count, first, second)
    imag_in = stacked[1].reshape(count, first, second)
    step_re, step_im = rotate(real_in, imag_in, cos_a, sin_a, "nab,ak->nkb", 1.0)
    twist_re = step_re * cos_t + step_im * sin_t
    twist_im = step_im * cos_t - step_re * sin_t
    spec_re, spec_im = rotate(twist_re, twist_im, cos_b, sin_b, "nkb,bj->nkj", 1.0)
    moved_re = spec_re * cos_p - spec_im * sin_p
    moved_im = spec_re * sin_p + spec_im * cos_p
    back_re, back_im = rotate(moved_re, moved_im, cos_b, sin_b, "nkj,jb->nkb", -1.0)
    untw_re = back_re * cos_t - back_im * sin_t
    untw_im = back_im * cos_t + back_re * sin_t
    final_re, final_im = rotate(untw_re, untw_im, cos_a, sin_a, "nkb,ka->nab", -1.0)
    return jnp.stack([final_re.reshape(count, width), final_im.reshape(count, width)]) / width


def added_up(value, axis):
    count = lax.axis_size(axis)
    if count & (count - 1):
        return lax.psum(value, axis)
    reach = 1
    while reach < count:
        value = value + lax.ppermute(value, axis, [(i, i ^ reach) for i in range(count)])
        reach *= 2
    return value


def lateral_work(parts):
    return (transform(parts[0]), transform(parts[1]))


def multiplier_revision(
    population_multiplier,
    holeburn_multiplier,
    measured_rightward,
    measured_leftward,
    rightward_wave,
    leftward_wave,
    population_level,
    holeburn_magnitude,
    attenuation_factor,
    transverse_curvature,
):
    rightward_inphase, rightward_quadrature = (rightward_wave[0], rightward_wave[1])
    leftward_inphase, leftward_quadrature = (leftward_wave[0], leftward_wave[1])
    measured_rightward_inphase, measured_rightward_quadrature = (
        measured_rightward[0],
        measured_rightward[1],
    )
    measured_leftward_inphase, measured_leftward_quadrature = (
        measured_leftward[0],
        measured_leftward[1],
    )
    surplus_population = population_level - 1.0
    amplification_inphase = 1.0 + 0.5 * (GAIN_SLOPE_RATE * surplus_population - attenuation_factor)
    amplification_quadrature = 0.5 * GAIN_SLOPE_RATE * ALPHA_LINEWIDTH * surplus_population
    joined_waves = COUPLING * holeburn_magnitude
    population_derivative = (
        2.0 * CLOCK_DELTA * GAIN_SLOPE_RATE * surplus_population * population_multiplier
    )
    holeburn_derivative = 2.0 * CLOCK_DELTA * holeburn_multiplier
    revised_rightward_inphase = (
        amplification_inphase * measured_rightward_inphase
        - amplification_quadrature * measured_rightward_quadrature
        + joined_waves * measured_leftward_quadrature
        - population_derivative * rightward_inphase
        + holeburn_derivative * leftward_inphase
    )
    revised_rightward_quadrature = (
        amplification_inphase * measured_rightward_quadrature
        + amplification_quadrature * measured_rightward_inphase
        - joined_waves * measured_leftward_inphase
        - population_derivative * rightward_quadrature
        + holeburn_derivative * leftward_quadrature
    )
    revised_leftward_inphase = (
        amplification_inphase * measured_leftward_inphase
        - amplification_quadrature * measured_leftward_quadrature
        + joined_waves * measured_rightward_quadrature
        - population_derivative * leftward_inphase
        + holeburn_derivative * rightward_inphase
    )
    revised_leftward_quadrature = (
        amplification_inphase * measured_leftward_quadrature
        + amplification_quadrature * measured_leftward_inphase
        - joined_waves * measured_rightward_inphase
        - population_derivative * leftward_quadrature
        + holeburn_derivative * rightward_quadrature
    )
    light_intensity = (
        rightward_inphase * rightward_inphase
        + rightward_quadrature * rightward_quadrature
        + leftward_inphase * leftward_inphase
        + leftward_quadrature * leftward_quadrature
    )
    amplification_share = (
        measured_rightward_inphase * (rightward_inphase + ALPHA_LINEWIDTH * rightward_quadrature)
        + measured_rightward_quadrature
        * (rightward_quadrature - ALPHA_LINEWIDTH * rightward_inphase)
        + measured_leftward_inphase * (leftward_inphase + ALPHA_LINEWIDTH * leftward_quadrature)
        + measured_leftward_quadrature * (leftward_quadrature - ALPHA_LINEWIDTH * leftward_inphase)
    )
    revised_population = (
        population_multiplier
        * (1.0 - CLOCK_DELTA / DENSITY_LIFETIME - CLOCK_DELTA * GAIN_SLOPE_RATE * light_intensity)
        + TRANSVERSE_DIFFUS * transverse_curvature
        + 0.5 * GAIN_SLOPE_RATE * amplification_share
    )
    fresh_holeburn = holeburn_multiplier * (1.0 - CLOCK_DELTA / GRATING_LIFE) + COUPLING * (
        measured_rightward_quadrature * leftward_inphase
        - measured_rightward_inphase * leftward_quadrature
        + measured_leftward_quadrature * rightward_inphase
        - measured_leftward_inphase * rightward_quadrature
    )
    return (
        jnp.stack([revised_rightward_inphase, revised_rightward_quadrature]),
        jnp.stack([revised_leftward_inphase, revised_leftward_quadrature]),
        revised_population,
        fresh_holeburn,
    )


def per_device(
    ending_rightward_adjoint,
    ending_leftward_adjoint,
    ending_population_adjoint,
    ending_holeburn_adjoint,
    history_rightward,
    history_leftward,
    history_population,
    history_holeburn,
    segment_passive_attenuation,
):
    columns = ending_rightward_adjoint.shape[2]
    rows = ending_rightward_adjoint.shape[1]
    blocks = lax.axis_size("gz")
    position = lax.axis_index("gz")
    cells = rows * blocks
    zpos = (position * rows + jnp.arange(rows, dtype=jnp.int32)).astype(jnp.float32)
    scaling_factor = 1.0 + 2.0 * zpos / (cells - 1)
    rightward_multiplier, leftward_multiplier = (ending_rightward_adjoint, ending_leftward_adjoint)
    population_multiplier, holeburn_multiplier = (
        ending_population_adjoint,
        ending_holeburn_adjoint,
    )
    attenuation_factor = segment_passive_attenuation.astype(jnp.float32)
    shape_curve = jnp.zeros((columns,), jnp.float32)
    for moment_position in range(history_rightward.shape[0] - 1, -1, -1):
        shape_curve = shape_curve + jnp.sum(scaling_factor[:, None] * population_multiplier, axis=0)
        above = passed_along(rightward_multiplier[:, :1, :], "gz", -1)
        below = passed_along(leftward_multiplier[:, -1:, :], "gz", 1)
        top_row = jnp.where(
            position == blocks - 1, FRONT_FACET * leftward_multiplier[:, -1:, :], above
        )
        bottom_row = jnp.where(position == 0, REAR_FACET * rightward_multiplier[:, :1, :], below)
        lam_fwd = jnp.concatenate([rightward_multiplier[:, 1:, :], top_row], axis=1)
        lam_bwd = jnp.concatenate([bottom_row, leftward_multiplier[:, :-1, :]], axis=1)
        whole_fwd, whole_bwd = (
            lax.all_gather(lam_fwd, "gx", axis=2, tiled=True),
            lax.all_gather(lam_bwd, "gx", axis=2, tiled=True),
        )
        start = lax.axis_index("gx") * columns
        done_fwd, done_bwd = lateral_work((whole_fwd, whole_bwd))
        measured_rightward = lax.dynamic_slice_in_dim(done_fwd, start, columns, 2)
        measured_leftward = lax.dynamic_slice_in_dim(done_bwd, start, columns, 2)
        bordered_array = with_halo(population_multiplier, (("gx", 1),), 1)
        transverse_curvature = (
            bordered_array[:, 2:] + bordered_array[:, :-2] - 2.0 * population_multiplier
        )
        rightward_multiplier, leftward_multiplier, population_multiplier, holeburn_multiplier = (
            multiplier_revision(
                population_multiplier,
                holeburn_multiplier,
                measured_rightward,
                measured_leftward,
                history_rightward[moment_position].astype(jnp.float32),
                history_leftward[moment_position].astype(jnp.float32),
                history_population[moment_position].astype(jnp.float32),
                history_holeburn[moment_position].astype(jnp.float32),
                attenuation_factor,
                transverse_curvature,
            )
        )
    total = added_up(shape_curve, "gz")
    derivative_vector = CLOCK_DELTA * total / math.sqrt(cells)
    return (
        rightward_multiplier,
        leftward_multiplier,
        population_multiplier,
        holeburn_multiplier,
        derivative_vector,
    )

LANES = 128
TILE = 16
POWER = 12
STRETCH = 1211.0
SCALE_LANE = 8


def lateral_matrices(width, blocks):
    lanes = width // blocks
    k = np.arange(width)
    signed = np.where(k < width // 2, k, k - width).astype(np.float64)
    response = np.fft.ifft(np.exp(1j * signed * signed * (DIFF / (width / 2) ** 2)))
    step = np.arange(lanes)
    shift = lanes * np.arange(blocks)[:, None, None] + step[None, None, :] - step[None, :, None]
    kernels = np.fft.fft(response[shift % width], axis=0) / blocks
    top = np.concatenate([kernels.real, kernels.imag], axis=2)
    low = np.concatenate([-kernels.imag, kernels.real], axis=2)
    whole = np.concatenate([top, low], axis=1)
    first = whole.astype(ml_dtypes.bfloat16)
    rest = (whole - first.astype(np.float64)).astype(ml_dtypes.bfloat16)
    return np.stack([first, rest], axis=1)


def block_dft(values, sign):
    count = len(values)
    if count == 1:
        return values
    even = block_dft(values[0::2], sign)
    odd = block_dft(values[1::2], sign)
    out = [None] * count
    for k in range(count // 2):
        (er, ei), (wr, wi) = even[k], odd[k]
        if 4 * k == count:
            plus, minus = (er - wi, ei + wr), (er + wi, ei - wr)
            out[k], out[k + count // 2] = (plus, minus) if sign > 0 else (minus, plus)
            continue
        if k:
            c, s = math.cos(2 * math.pi * k / count), sign * math.sin(2 * math.pi * k / count)
            if 8 * k == count:
                wr, wi = (c * (wr - wi), c * (wr + wi)) if sign > 0 else (c * (wr + wi), c * (wi - wr))
            elif 8 * k == 3 * count:
                wr, wi = (c * (wr + wi), c * (wi - wr)) if sign > 0 else (c * (wr - wi), c * (wr + wi))
            else:
                wr, wi = c * wr - s * wi, c * wi + s * wr
        out[k] = (er + wr, ei + wi)
        out[k + count // 2] = (er - wr, ei - wi)
    return out


def lane(j):
    return pl.ds(pl.multiple_of(j * LANES, LANES), LANES)


def slab(j, rows):
    return pl.ds(pl.multiple_of(j * rows, rows), rows)


def fetch(pairs, sems, first=0):
    copies = [pltpu.make_async_copy(a, b, sems.at[first + i]) for i, (a, b) in enumerate(pairs)]
    for copy in copies:
        copy.start()
    return copies


def rows_of(info, rows, other):
    part = 1 - info[4] if other else info[4]
    return pl.ds(pl.multiple_of(part * rows, rows), rows)


def spread(field, work):
    rows = field.shape[1]
    blocks = work.shape[0]

    @pl.loop(0, rows // 8)
    def _(g):
        at = slab(g, 8)
        values = [
            (field[0, at, j * LANES : (j + 1) * LANES], field[1, at, j * LANES : (j + 1) * LANES])
            for j in range(blocks)
        ]
        for q, (re, im) in enumerate(block_dft(values, -1)):
            work[q, at, :LANES] = re
            work[q, at, LANES:] = im


def fetch_matrices(source, matrices, sem):
    count = matrices.shape[0] // 2
    parts = [pl.ds(i * count, count) for i in range(2)]
    return fetch([(source.at[part], matrices.at[part]) for part in parts], sem)


def multiply(work, matrices, copies):
    rows = work.shape[1]
    count = work.shape[0] // len(copies)
    for i, copy in enumerate(copies):
        copy.wait()

        @pl.loop(i * count, (i + 1) * count, unroll=True)
        def _(q):
            value = work[q]
            first = value.astype(jnp.bfloat16)
            rest = (value - first.astype(jnp.float32)).astype(jnp.bfloat16)
            both = jnp.dot(
                jnp.concatenate([first, rest]), matrices[q, 0], preferred_element_type=jnp.float32
            )
            fine = jnp.dot(first, matrices[q, 1], preferred_element_type=jnp.float32)
            work[q] = both[:rows] + (both[rows:] + fine)


def gathered(work, at):
    values = [(work[q, at, :LANES], work[q, at, LANES:]) for q in range(work.shape[0])]
    return block_dft(values, 1)


def filtered(field, work, matrices, copies):
    spread(field, work)
    multiply(work, matrices, copies)


def write_filtered(info, work, forward, backward, inner, outer):
    rows = work.shape[1] // 2
    for target, base, offset in ((forward, 0, 0), (backward, rows, 8)):

        @pl.loop(0, rows // 8)
        def _(g):
            here = pl.ds(pl.multiple_of(g * 8 + offset, 8), 8)
            for j, pair in enumerate(gathered(work, pl.ds(pl.multiple_of(g * 8 + base, 8), 8))):
                for part in range(2):
                    target[part, here, j * LANES : (j + 1) * LANES] = pair[part]

    low = info[4] == 0
    for part in range(2):
        first, last = forward[part, 0:1, :], backward[part, rows + 7 : rows + 8, :]
        inner[part : part + 1, :] = jnp.where(low, last, first)
        outer[part : part + 1, :] = jnp.where(low, first, last)


def size_of(largest):
    top = jnp.max(jnp.max(largest, axis=1, keepdims=True), axis=0, keepdims=True)
    return jnp.maximum(top, 1e-30).astype(jnp.bfloat16).astype(jnp.float32)


def encoded(value, size):
    unit = value * (STRETCH / size)
    square = unit * unit
    fourth = square * square
    return (fourth * fourth * square * (unit * jnp.abs(unit))).astype(jnp.bfloat16)


def decoded(code, size):
    value = code.astype(jnp.float32)
    root = jnp.exp2(jnp.log(jnp.abs(value)) * (1.0 / (POWER * math.log(2.0)))) * (size / STRETCH)
    return jnp.where(value < 0.0, -root, root)


def side_tile(columns, rows):
    index = lax.broadcasted_iota(jnp.int32, (rows, LANES), 1)
    tile = jnp.zeros((rows, LANES), jnp.float32)
    for at, column in columns:
        tile = jnp.where(index == at, column, tile)
    return tile.astype(jnp.bfloat16)


def sizes_in(tile, count):
    value = tile.astype(jnp.float32)
    return [value[0:1, SCALE_LANE + i : SCALE_LANE + i + 1] for i in range(count)]


def updated(fr, fi, br, bi, wave, population, hole, loss, carrier, grating, lap):
    rr, ri, lr, li = wave
    surplus = population - 1.0
    gain_re = 1.0 + 0.5 * (GAIN_SLOPE_RATE * surplus - loss)
    gain_im = (0.5 * GAIN_SLOPE_RATE * ALPHA_LINEWIDTH) * surplus
    joined = COUPLING * hole
    drive = (2.0 * CLOCK_DELTA * GAIN_SLOPE_RATE) * surplus * carrier
    mix = (2.0 * CLOCK_DELTA) * grating
    new_fr = gain_re * fr - gain_im * fi + joined * bi - drive * rr + mix * lr
    new_fi = gain_re * fi + gain_im * fr - joined * br - drive * ri + mix * li
    new_br = gain_re * br - gain_im * bi + joined * fi - drive * lr + mix * rr
    new_bi = gain_re * bi + gain_im * br - joined * fr - drive * li + mix * ri
    light = rr * rr + ri * ri + lr * lr + li * li
    share = (
        fr * (rr + ALPHA_LINEWIDTH * ri)
        + fi * (ri - ALPHA_LINEWIDTH * rr)
        + br * (lr + ALPHA_LINEWIDTH * li)
        + bi * (li - ALPHA_LINEWIDTH * lr)
    )
    new_carrier = (
        carrier * ((1.0 - CLOCK_DELTA / DENSITY_LIFETIME) - (CLOCK_DELTA * GAIN_SLOPE_RATE) * light)
        + TRANSVERSE_DIFFUS * lap
        + (0.5 * GAIN_SLOPE_RATE) * share
    )
    new_grating = grating * (1.0 - CLOCK_DELTA / GRATING_LIFE) + COUPLING * (
        fi * lr - fr * li + bi * rr - br * ri
    )
    return new_fr, new_fi, new_br, new_bi, new_carrier, new_grating


def curvature(left, mid, right, weight_left, weight_right):
    index = lax.broadcasted_iota(jnp.int32, mid.shape, 1)
    below = jnp.where(index == 0, pltpu.roll(left, 1, 1) * weight_left, pltpu.roll(mid, 1, 1))
    above = jnp.where(
        index == LANES - 1,
        pltpu.roll(right, LANES - 1, 1) * weight_right,
        pltpu.roll(mid, LANES - 1, 1),
    )
    return below + above - 2.0 * mid


def send_fields_kernel(info, forward, backward, out, fields, sems):
    rows, columns = fields.shape[2:]
    half = columns // LANES
    at = rows_of(info, rows, True)
    copies = fetch(
        [(ref.at[:, at, :], fields.at[f]) for f, ref in enumerate((forward, backward))], sems
    )
    sizes = []
    for f in range(2):
        copies[f].wait()
        largest = jnp.maximum(jnp.abs(fields[f, 0]), jnp.abs(fields[f, 1]))
        size = size_of(largest)
        sizes.append((SCALE_LANE + f, size))
        for part in range(2):
            put_tiles(out, (2 * f + part) * half, encoded(fields[f, part], size))
    out[4 * half * rows :, :] = side_tile(sizes, rows)


def put_tiles(out, first, value):
    rows, columns = value.shape
    for j in range(columns // LANES):
        at = (first + j) * rows
        out[at : at + rows, :] = value[:, j * LANES : (j + 1) * LANES]


def history_rows(forward, backward, population, hole, s, at):
    return [
        forward.at[s, 0, at, :], forward.at[s, 1, at, :], backward.at[s, 0, at, :],
        backward.at[s, 1, at, :], population.at[s, at, :], hole.at[s, at, :],
    ]


def into_rows(parts, target, first, rows):
    return [(part, target.at[pl.ds(first + i * rows, rows), :]) for i, part in enumerate(parts)]


def send_later_kernel(steps, info, forward, backward, population, hole, final, *refs):
    targets, sems = refs[:-1], refs[-1]
    rows = targets[0].shape[0] // 6
    history = (forward, backward, population, hole)
    pairs = []
    for i, s in enumerate(steps):
        for k, other in enumerate((True, False)):
            at = rows_of(info, rows, other)
            pairs += into_rows(history_rows(*history, s, at), targets[2 * i + k], 0, rows)
    pairs += into_rows(history_rows(*history, 0, pl.ds(0, 2 * rows)), final, 0, 2 * rows)
    for copy in fetch(pairs, sems):
        copy.wait()


def send_first_kernel(
    s, info, loss, carrier, grating, forward, backward, population, hole,
    own_loss, own, own_carrier, own_grating, out, own_edge, states, ends, sems,
):
    rows, columns = own_carrier.shape
    theirs, mine = rows_of(info, rows, True), rows_of(info, rows, False)
    history = (forward, backward, population, hole)
    copies = fetch(
        [(carrier.at[theirs, :], states.at[0]), (grating.at[theirs, :], states.at[1])]
        + into_rows([loss.at[theirs, :]], out, 0, rows)
        + into_rows(history_rows(*history, s, theirs), out, 3 * rows, rows)
        + [(loss.at[mine, :], own_loss), (carrier.at[mine, :], own_carrier)]
        + [(grating.at[mine, :], own_grating)]
        + into_rows(history_rows(*history, s, mine), own, 0, rows)
        + [
            (part, ends.at[k, i])
            for k in range(2)
            for i, part in enumerate(
                history_rows(*history, 1, pl.ds(k * (2 * rows - TILE), TILE))
            )
        ],
        sems,
    )
    for copy in copies[:2]:
        copy.wait()
    sizes = []
    for i in range(2):
        size = size_of(jnp.abs(states[i]))
        sizes.append(jnp.broadcast_to(size, (1, columns)))
        out[(1 + i) * rows : (2 + i) * rows, :] = encoded(states[i], size)
    for copy in copies[2:]:
        copy.wait()
    low = info[4] == 0
    top = [ends[0, i].astype(jnp.float32)[:1] for i in range(6)]
    foot = [ends[1, i].astype(jnp.float32)[TILE - 1 :] for i in range(6)]
    own_edge[...] = jnp.concatenate([jnp.where(low, a, b) for a, b in zip(top, foot)])
    sizes += [jnp.where(low, b, a) for a, b in zip(top, foot)]
    sizes.append(jnp.zeros((TILE - 8, columns), jnp.float32))
    out[9 * rows :, :] = jnp.concatenate(sizes).astype(jnp.bfloat16)


def enter_kernel(
    info, forward, backward, other, source, tp, tq, inner, outer, field, work, matrices, sem, sems
):
    rows, width = field.shape[1] // 2, field.shape[2]
    columns = width // 2
    half = columns // LANES
    at = rows_of(info, rows, False)
    copies = fetch(
        [
            (ref.at[:, at, :], field.at[:, f * rows : (f + 1) * rows, :columns])
            for f, ref in enumerate((forward, backward))
        ],
        sems,
    )
    matrix_copies = fetch_matrices(source, matrices, sem)
    sizes = sizes_in(other[4 * half * rows :, :], 2)
    for f in range(2):
        for part in range(2):

            @pl.loop(0, half, unroll=2)
            def _(j):
                code = other[slab((2 * f + part) * half + j, rows), :]
                field[part, f * rows : (f + 1) * rows, lane(half + j)] = decoded(code, sizes[f])

    for held in copies:
        held.wait()
    filtered(field, work, matrices, matrix_copies)
    write_filtered(info, work, tp, tq, inner, outer)


def rows_update(
    info, tp, tq, inner, outer, carrier, grating, own, other, own_loss, other_loss,
    field, new_carrier, new_grating, sums_in, sums, cells, last
):
    rows, width = carrier.shape
    half = width // LANES // 2
    columns = half * LANES
    mid = jnp.where(info[0] == 0, 1.0, 0.0)
    wrap = 1.0 - mid
    low = info[4] == 0
    is_first, is_last = info[1], info[2]
    row_index = lax.broadcasted_iota(jnp.int32, (TILE, LANES), 0)
    zero = jnp.zeros((8, LANES), jnp.float32)

    def step(jj, most):
        for side in range(2):
            j = jj + side * half
            here = lane(j)
            left_at = lane(jnp.where(j == 0, 2 * half - 1, j - 1))
            right_at = lane(jnp.where(j == 2 * half - 1, 0, j + 1))
            swapped = lane(jj + (1 - side) * half)
            weight_left = jnp.where(jj == 0, wrap if side == 0 else mid, 1.0)
            weight_right = jnp.where(jj == half - 1, mid if side == 0 else wrap, 1.0)
            total = zero
            for r in range(0, rows, TILE):
                at = slice(r, r + TILE)

                held, begin = (own, other)[side]

                def part_of(i):
                    tile = begin + i * rows + r
                    return held[tile : tile + TILE, lane(jj)].astype(jnp.float32)

                loss = (own_loss, other_loss)[side][at, lane(jj)].astype(jnp.float32)
                f = [tp[part, r + 1 : r + 1 + TILE, here] for part in range(2)]
                b = [tq[part, r + 7 : r + 7 + TILE, here] for part in range(2)]
                if r + TILE == rows:
                    for part in range(2):
                        facet = FRONT_FACET * tq[part, rows + 7 : rows + 8, here]
                        edge = jnp.where(
                            low, inner[part : part + 1, swapped], outer[part : part + 1, here]
                        )
                        edge = jnp.where(is_last, facet, edge)
                        f[part] = jnp.where(row_index == TILE - 1, edge, f[part])
                if r == 0:
                    for part in range(2):
                        facet = REAR_FACET * tp[part, 0:1, here]
                        edge = jnp.where(
                            low, outer[part : part + 1, here], inner[part : part + 1, swapped]
                        )
                        edge = jnp.where(is_first, facet, edge)
                        b[part] = jnp.where(row_index == 0, edge, b[part])
                c = carrier[at, here]
                lap = curvature(
                    carrier[at, left_at], c, carrier[at, right_at], weight_left, weight_right
                )
                out = updated(
                    *f, *b, [part_of(i) for i in range(4)], part_of(4), part_of(5), loss,
                    c, grating[at, here], lap,
                )
                field[0, r : r + TILE, here] = out[0]
                field[1, r : r + TILE, here] = out[1]
                field[0, rows + r : rows + r + TILE, here] = out[2]
                field[1, rows + r : rows + r + TILE, here] = out[3]
                new_carrier[at, here] = out[4]
                new_grating[at, here] = out[5]
                z = (info[3] + r + row_index).astype(jnp.float32)
                weighted = (1.0 + 2.0 * z / (cells - 1)) * ((c + out[4]) if last else c)
                for k in range(0, TILE, 8):
                    total = total + weighted[k : k + 8]
                if last and side == 1:
                    for k in range(0, TILE, 8):
                        most = (
                            jnp.maximum(most[0], jnp.abs(out[4][k : k + 8])),
                            jnp.maximum(most[1], jnp.abs(out[5][k : k + 8])),
                        )
            summed = jnp.sum(total, axis=0, keepdims=True)
            sums[:, here] = summed if sums_in is None else summed + sums_in[:, here]
        return most

    return lax.fori_loop(0, half, step, (zero, zero))


def first_step_kernel(
    cells, info, tp, tq, inner, outer, my_carrier, my_grating, loss, own, own_edge, other, source,
    new_tp, new_tq, new_inner, new_outer, new_carrier, new_grating, sums,
    carrier, grating, field, work, matrices, sem,
):
    matrix_copies = fetch_matrices(source, matrices, sem)
    rows, columns = my_carrier.shape
    half = columns // LANES
    extra = other[9 * rows :, :].astype(jnp.float32)
    sizes = [extra[0:1, 0:1], extra[1:2, 0:1]]
    new_outer[2:8, :columns] = own_edge[...]
    new_outer[2:8, columns:] = extra[2:8]
    for i, (whole, mine) in enumerate(((carrier, my_carrier), (grating, my_grating))):
        whole[:, :columns] = mine[...]

        @pl.loop(0, half, unroll=2)
        def _(j):
            whole[:, lane(half + j)] = decoded(
                other[(1 + i) * rows : (2 + i) * rows, lane(j)], sizes[i]
            )

    rows_update(
        info, tp, tq, inner, outer, carrier, grating, (own, 0), (other, 3 * rows), loss, other,
        field, new_carrier, new_grating, None, sums, cells, False,
    )
    filtered(field, work, matrices, matrix_copies)
    write_filtered(info, work, new_tp, new_tq, new_inner, new_outer)


def middle_step_kernel(
    cells, info, tp, tq, inner, outer, carrier, grating, loss, own, other, other_loss, sums_in,
    source, new_tp, new_tq, new_inner, new_outer, new_carrier, new_grating, sums,
    field, work, matrices, sem,
):
    matrix_copies = fetch_matrices(source, matrices, sem)
    rows_update(
        info, tp, tq, inner, outer, carrier, grating, (own, 0), (other, 0), loss, other_loss,
        field, new_carrier, new_grating, sums_in, sums, cells, False,
    )
    filtered(field, work, matrices, matrix_copies)
    write_filtered(info, work, new_tp, new_tq, new_inner, new_outer)
    rows = carrier.shape[0]
    low = info[4] == 0
    for part in range(2):
        new_outer[2 + part : 3 + part, :] = jnp.where(
            low, new_tp[part, 1:2, :], new_tq[part, rows + 6 : rows + 7, :]
        )
    for i, ref in enumerate((new_carrier, new_grating)):
        new_outer[4 + i : 5 + i, :] = jnp.where(low, ref[0:1, :], ref[rows - 1 : rows, :])
    columns = loss.shape[1]
    for part, ref in enumerate((loss, other_loss)):
        top = ref[:TILE, :].astype(jnp.float32)[:1]
        foot = ref[rows - TILE :, :].astype(jnp.float32)[TILE - 1 :]
        new_outer[6:7, part * columns : (part + 1) * columns] = jnp.where(low, top, foot)


def row_beyond(info, tp, tq, outer, beyond):
    rows = tp.shape[1] - 8
    low = info[4] == 0
    xr, xi, carrier, grating = (outer[i : i + 1, :] for i in range(2, 6))
    yr, yi = (
        jnp.where(low, tp[part, 0:1, :], tq[part, rows + 7 : rows + 8, :]) for part in range(2)
    )
    rr, ri, lr, li, population, hole = (beyond[i : i + 1, :] for i in range(2, 8))
    loss = outer[6:7, :]
    surplus = population - 1.0
    gain_re = 1.0 + 0.5 * (GAIN_SLOPE_RATE * surplus - loss)
    gain_im = (0.5 * GAIN_SLOPE_RATE * ALPHA_LINEWIDTH) * surplus
    joined = COUPLING * hole
    drive = (2.0 * CLOCK_DELTA * GAIN_SLOPE_RATE) * surplus * carrier
    mix = (2.0 * CLOCK_DELTA) * grating
    near_re, near_im = jnp.where(low, lr, rr), jnp.where(low, li, ri)
    far_re, far_im = jnp.where(low, rr, lr), jnp.where(low, ri, li)
    new_re = gain_re * xr - gain_im * xi + joined * yi - drive * near_re + mix * far_re
    new_im = gain_re * xi + gain_im * xr - joined * yr - drive * near_im + mix * far_im
    return new_re, new_im


def leave_kernel(
    cells, info, tp, tq, inner, outer, beyond, carrier, grating, loss, own, other, other_loss,
    sums_in, source, kept, kept_carrier, kept_grating, sides, sent, edge, shares,
    sums, new_carrier, new_grating, field, work, matrices, sem,
):
    matrix_copies = fetch_matrices(source, matrices, sem)
    rows, width = carrier.shape
    columns = width // 2
    half = columns // LANES
    most = rows_update(
        info, tp, tq, inner, outer, carrier, grating, (own, 0), (other, 0), loss, other_loss,
        field, new_carrier, new_grating, sums_in, sums, cells, True,
    )
    mid = jnp.where(info[0] == 0, 1.0, 0.0)
    wrap = 1.0 - mid
    kept_carrier[...] = new_carrier[:, :columns]
    kept_grating[...] = new_grating[:, :columns]
    first, before = new_carrier[:, 0:1] * wrap, new_carrier[:, columns - 1 : columns] * mid
    after, final = new_carrier[:, columns : columns + 1] * mid, new_carrier[:, width - 1 :] * wrap
    sides[0] = jnp.broadcast_to(final, (rows, LANES))
    sides[1] = jnp.broadcast_to(after, (rows, LANES))
    pairs = []
    for at, value in ((0, before), (2, first)):
        coarse = value.astype(jnp.bfloat16).astype(jnp.float32)
        pairs += [(at, coarse), (at + 1, value - coarse)]
    for i, field_of in enumerate((new_carrier, new_grating)):
        size = size_of(most[i])
        pairs.append((SCALE_LANE + 2 + i, size))

        @pl.loop(0, half, unroll=2)
        def _(j):
            sent[slab((4 + i) * half + j, rows), :] = encoded(field_of[:, lane(half + j)], size)

    for part, value in enumerate(row_beyond(info, tp, tq, outer, beyond)):
        field[part, 2 * rows :, :] = jnp.broadcast_to(value, (8, width))
    filtered(field, work, matrices, matrix_copies)
    zero = jnp.zeros((8, LANES), jnp.float32)
    for f in range(2):

        def unmix(g, most):
            at = pl.ds(pl.multiple_of(g * 8 + f * rows, 8), 8)
            for j, pair in enumerate(gathered(work, at)):
                for part in range(2):
                    if j < half:
                        kept[part, at, j * LANES : (j + 1) * LANES] = pair[part]
                    else:
                        work[j, at, part * LANES : (part + 1) * LANES] = pair[part]
                        most = jnp.maximum(most, jnp.abs(pair[part]))
            return most

        size = size_of(lax.fori_loop(0, rows // 8, unmix, zero))
        pairs.append((SCALE_LANE + f, size))

        @pl.loop(0, half, unroll=2)
        def _(j):
            for part in range(2):
                value = work[half + j, f * rows : (f + 1) * rows, part * LANES : (part + 1) * LANES]
                sent[slab((2 * f + part) * half + j, rows), :] = encoded(value, size)

    ends = gathered(work, slice(2 * rows, 2 * rows + 8))
    for part in range(2):
        for j in range(half):
            edge[part : part + 1, j * LANES : (j + 1) * LANES] = ends[j][part][:1]
    far = jnp.concatenate([ends[j][part][:1] for part in range(2) for j in range(half, 2 * half)])
    size = size_of(jnp.abs(far))
    pairs.append((SCALE_LANE + 4, size))
    sent[6 * half * rows : (6 * half + 1) * rows, :] = side_tile(pairs, rows)
    spare = jnp.zeros((rows - 2 * half, LANES), jnp.float32)
    sent[(6 * half + 1) * rows :, :] = encoded(jnp.concatenate([far, spare]), size)
    tile = jnp.concatenate([sums[:, j * LANES : (j + 1) * LANES] for j in range(2 * half)])
    near, far = tile[:half], tile[half:]
    first = info[0] == 0
    to_first, to_second = jnp.where(first, near, far), jnp.where(first, far, near)
    for i in range(0, shares.shape[0], 2):
        shares[i] = to_first
        shares[i + 1] = to_second


def total_kernel(cells, info, partial, out):
    total = partial[0]
    for i in range(1, partial.shape[0]):
        total = total + partial[i]
    out[...] = total * (CLOCK_DELTA / math.sqrt(cells))


def final_kernel(
    info, kept, kept_carrier, kept_grating, sides, came, edge, loss_in, history_in,
    forward_out, backward_out, carrier_out, grating_out,
    tp, tq, carrier, grating, loss, history, out_forward, out_backward, out_carrier, out_grating,
    sems, out_sems,
):
    rows, columns = kept_carrier.shape
    half = columns // LANES
    copies = fetch([(loss_in, loss), (history_in, history)], sems)
    mine = info[4] * rows
    theirs = (1 - info[4]) * rows
    low = info[4] == 0
    extra = came[6 * half * rows : (6 * half + 1) * rows, :]
    size_forward, size_backward, size_carrier, size_grating, size_edge = sizes_in(extra, 5)
    ends = decoded(came[(6 * half + 1) * rows :, :], size_edge)
    extra = extra.astype(jnp.float32)

    def at(start, offset, count):
        return pl.ds(pl.multiple_of(start + offset, 8), count)

    for part in range(2):
        tp[part, at(mine, 0, rows), :] = kept[part, :rows, :]
        tq[part, at(mine, 8, rows), :] = kept[part, rows:, :]
    carrier[at(mine, 0, rows), LANES : LANES + columns] = kept_carrier[...]
    carrier[at(mine, 0, rows), :LANES] = sides[0]
    carrier[at(mine, 0, rows), LANES + columns :] = sides[1]
    carrier[at(theirs, 0, rows), :LANES] = jnp.broadcast_to(
        extra[:, 0:1] + extra[:, 1:2], (rows, LANES)
    )
    carrier[at(theirs, 0, rows), LANES + columns :] = jnp.broadcast_to(
        extra[:, 2:3] + extra[:, 3:4], (rows, LANES)
    )
    grating[at(mine, 0, rows), :] = kept_grating[...]

    @pl.loop(0, half, unroll=2)
    def _(j):
        carrier[at(theirs, 0, rows), lane(1 + j)] = decoded(
            came[slab(4 * half + j, rows), :], size_carrier
        )
        grating[at(theirs, 0, rows), lane(j)] = decoded(
            came[slab(5 * half + j, rows), :], size_grating
        )
        for part in range(2):
            tp[part, at(theirs, 0, rows), lane(j)] = decoded(
                came[slab(part * half + j, rows), :], size_forward
            )
            tq[part, at(theirs, 8, rows), lane(j)] = decoded(
                came[slab((2 + part) * half + j, rows), :], size_backward
            )

    all_rows = 2 * rows
    for part in range(2):
        near = edge[part : part + 1, :]
        far = jnp.concatenate([ends[part * half + j : part * half + j + 1] for j in range(half)], axis=1)
        next_edge = jnp.where(low, far, near)
        before_edge = jnp.where(low, near, far)
        front = FRONT_FACET * tq[part, all_rows + 7 : all_rows + 8, :]
        rear = REAR_FACET * tp[part, 0:1, :]
        tp[part, all_rows : all_rows + 1, :] = jnp.where(info[2], front, next_edge)
        tq[part, 7:8, :] = jnp.where(info[1], rear, before_edge)

    for copy in copies:
        copy.wait()

    def results(j):
        pairs = [
            (out_forward.at[:, :, lane(j)], forward_out.at[:, :, lane(j)]),
            (out_backward.at[:, :, lane(j)], backward_out.at[:, :, lane(j)]),
            (out_carrier.at[:, lane(j)], carrier_out.at[:, lane(j)]),
            (out_grating.at[:, lane(j)], grating_out.at[:, lane(j)]),
        ]
        return [
            pltpu.make_async_copy(a, b, out_sems.at[j, i]) for i, (a, b) in enumerate(pairs)
        ]

    @pl.loop(0, half)
    def _(j):
        here = lane(j)
        for r in range(0, all_rows, TILE):
            row = slice(r, r + TILE)
            c = carrier[row, lane(j + 1)]
            lap = curvature(carrier[row, lane(j)], c, carrier[row, lane(j + 2)], 1.0, 1.0)
            parts = [
                history[i * all_rows + r : i * all_rows + r + TILE, here].astype(jnp.float32)
                for i in range(6)
            ]
            out = updated(
                tp[0, r + 1 : r + 1 + TILE, here], tp[1, r + 1 : r + 1 + TILE, here],
                tq[0, r + 7 : r + 7 + TILE, here], tq[1, r + 7 : r + 7 + TILE, here],
                parts[:4], parts[4], parts[5],
                loss[row, here].astype(jnp.float32), c, grating[row, here], lap,
            )
            out_forward[0, row, here] = out[0]
            out_forward[1, row, here] = out[1]
            out_backward[0, row, here] = out[2]
            out_backward[1, row, here] = out[3]
            out_carrier[row, here] = out[4]
            out_grating[row, here] = out[5]
        for copy in results(j):
            copy.start()

    @pl.loop(0, half)
    def _(j):
        for copy in results(j):
            copy.wait()


def position(rows, whole):
    x, block, count = lax.axis_index("gx"), lax.axis_index("gz"), lax.axis_size("gz")
    high = lax.rem(x + block, 2)
    if whole:
        return x, block == 0, block == count - 1, block * rows, high
    place = 2 * block + high
    return x, place == 0, place == 2 * count - 1, place * rows, high


def whole_spec(shape):
    return pl.BlockSpec(shape, lambda i, n=len(shape): (0,) * n)


def call(name, kernel, rows, inputs, outputs, scratch, flops=0, grant=24, whole=False, in_place=False):
    arrays = [x[0] if isinstance(x, tuple) else x for x in inputs]
    specs = [x[1] if isinstance(x, tuple) else whole_spec(x.shape) for x in inputs]
    shapes = [jax.ShapeDtypeStruct(*out) for out in outputs]
    moved = sum(math.prod(s.shape) * s.dtype.itemsize for s in shapes)

    def body(*refs):
        kernel(position(rows, whole), *refs)

    return pl.pallas_call(
        body,
        grid=(1,),
        in_specs=specs,
        out_specs=[
            pl.BlockSpec(memory_space=pltpu.HBM) if in_place else whole_spec(s.shape) for s in shapes
        ],
        scratch_shapes=scratch,
        out_shape=shapes,
        compiler_params=pltpu.CompilerParams(vmem_limit_bytes=grant * 1024 * 1024),
        cost_estimate=pl.CostEstimate(
            flops=flops, bytes_accessed=moved + 4 * 1024 * 1024, transcendentals=0
        ),
        name=name,
    )(*arrays)


def per_pair(
    ending_rightward_adjoint,
    ending_leftward_adjoint,
    ending_population_adjoint,
    ending_holeburn_adjoint,
    history_rightward,
    history_leftward,
    history_population,
    history_holeburn,
    segment_passive_attenuation,
):
    cell_rows, columns = ending_population_adjoint.shape
    passes = history_population.shape[0]
    rows = cell_rows // 2
    half = columns // LANES
    blocks = 2 * half
    width = 2 * columns
    count = lax.axis_size("gz")
    cells = cell_rows * count
    x = lax.axis_index("gx")
    f32, bf16 = jnp.float32, jnp.bfloat16
    swap = [(0, 1), (1, 0)]
    in_place = pl.BlockSpec(memory_space=pltpu.HBM)

    def held(*arrays):
        return [(a, in_place) for a in arrays]

    def tiles(n):
        return ((n * rows, LANES), bf16)

    ends = held(ending_rightward_adjoint, ending_leftward_adjoint)
    planes = held(ending_population_adjoint, ending_holeburn_adjoint)
    history = held(history_rightward, history_leftward, history_population, history_holeburn)
    losses = held(segment_passive_attenuation)
    matrices = pltpu.with_memory_space_constraint(
        jnp.asarray(lateral_matrices(width, blocks)), pltpu.HBM
    )
    matrix_input = held(matrices)
    work = [
        pltpu.VMEM((blocks, 2 * rows, 2 * LANES), f32),
        pltpu.VMEM(matrices.shape, bf16),
        pltpu.SemaphoreType.DMA((2,)),
    ]
    field_scratch = pltpu.VMEM((2, 2 * rows, width), f32)
    def state_out(outer_rows):
        state = ((2, rows + 8, width), f32)
        return [state, state, ((2, width), f32), ((outer_rows, width), f32)]

    plane = ((rows, width), f32)
    plane_scratch = pltpu.VMEM((rows, width), f32)
    half_plane = ((rows, columns), f32)
    work_flops = 2 * 3 * 2 * rows * blocks * (2 * LANES) ** 2

    (coded,) = call(
        "send_fields", send_fields_kernel, rows, ends, [tiles(4 * half + 1)],
        [pltpu.VMEM((2, 2, rows, columns), f32), pltpu.SemaphoreType.DMA((2,))], grant=62,
    )
    other_fields = lax.ppermute(coded, "gx", swap)
    loss, own_first, my_carrier, my_grating, sent_first, own_edge = call(
        "send_first", functools.partial(send_first_kernel, passes - 1), rows,
        [*losses, *planes, *history],
        [((rows, columns), bf16), ((6 * rows, columns), bf16), half_plane, half_plane,
         ((9 * rows + TILE, columns), bf16), ((6, columns), f32)],
        [pltpu.VMEM((2, rows, columns), f32), pltpu.VMEM((2, 6, TILE, columns), bf16),
         pltpu.SemaphoreType.DMA((30,))], grant=62,
    )
    steps = range(passes - 2, 0, -1)
    history_last, *later = call(
        "send_later", functools.partial(send_later_kernel, steps), rows, history,
        [((6 * cell_rows, columns), bf16)] + [((6 * rows, columns), bf16)] * (2 * len(steps)),
        [pltpu.SemaphoreType.DMA((12 * len(steps) + 6,))], grant=62,
    )
    sent_first, history_last, later, other_fields = lax.optimization_barrier(
        (sent_first, history_last, later, other_fields)
    )
    other_first = lax.ppermute(sent_first, "gx", swap)

    line = ("gz", "gx")
    neighbours = []
    for b in range(count - 1):
        top = (1 + b) % 2
        neighbours += [(2 * b + top, 2 * b + 2 + top), (2 * b + 2 + top, 2 * b + top)]

    def edges(inner, outer):
        outer = lax.ppermute(outer, line, neighbours)
        return lax.ppermute(inner, "gx", swap), outer

    tp, tq, inner, outer = call(
        "enter", enter_kernel, rows, [*ends, other_fields, *matrix_input],
        state_out(2), [field_scratch, *work, pltpu.SemaphoreType.DMA((2,))], work_flops,
    )
    inner, outer = edges(inner, outer)

    other_loss = (other_first, pl.BlockSpec((rows, columns), lambda i: (0, 0)))
    carrier = grating = sums = other = own = None
    for index, s in enumerate(range(passes - 1, 0, -1)):
        if index < len(steps):
            sent, own_next = later[2 * index : 2 * index + 2]
            sent, inner, outer = lax.optimization_barrier((sent, inner, outer))
            coming = lax.ppermute(sent, "gx", swap)
        shared = [tp, tq, inner, outer]
        if index == 0:
            tp, tq, inner, outer, carrier, grating, sums = call(
                "first_step", functools.partial(first_step_kernel, cells), rows,
                [*shared, my_carrier, my_grating, loss, own_first, own_edge, other_first,
                 *matrix_input],
                [*state_out(8), plane, plane, ((1, width), f32)],
                [plane_scratch, plane_scratch, field_scratch, *work], work_flops,
            )
        elif s > 1:
            tp, tq, inner, outer, carrier, grating, sums = call(
                "middle_step", functools.partial(middle_step_kernel, cells), rows,
                [*shared, carrier, grating, loss, own, other, other_loss, sums, *matrix_input],
                [*state_out(7), plane, plane, ((1, width), f32)],
                [field_scratch, *work], work_flops,
            )
        else:
            kept, kept_carrier, kept_grating, sides, sent, edge, shares = call(
                "leave", functools.partial(leave_kernel, cells), rows,
                [*shared, beyond, carrier, grating, loss, own, other, other_loss, sums, *matrix_input],
                [((2, 2 * rows, columns), f32), half_plane, half_plane, ((2, rows, LANES), f32),
                 tiles(6 * half + 2), ((2, columns), f32), ((2 * count, half, LANES), f32)],
                [pltpu.VMEM((1, width), f32), plane_scratch, plane_scratch,
                 pltpu.VMEM((2, 2 * rows + 8, width), f32),
                 pltpu.VMEM((blocks, 2 * rows + TILE, 2 * LANES), f32), *work[1:]],
                work_flops,
            )
        if s > 1:
            inner, outer = edges(inner, outer)
            own, other = own_next, coming
            if index == 0:
                beyond = outer

    came = lax.ppermute(sent, "gx", swap)
    shares = lax.all_to_all(shares, line, 0, 0, tiled=True)

    outs = call(
        "final", final_kernel, cell_rows,
        [kept, kept_carrier, kept_grating, sides, came, edge,
         *(held(*(pltpu.with_memory_space_constraint(a, pltpu.HBM) for a in
                  (segment_passive_attenuation, history_last))))],
        [((2, cell_rows, columns), f32), ((2, cell_rows, columns), f32),
         ((cell_rows, columns), f32), ((cell_rows, columns), f32)],
        [pltpu.VMEM((2, cell_rows + 8, columns), f32), pltpu.VMEM((2, cell_rows + 8, columns), f32),
         pltpu.VMEM((cell_rows, columns + 2 * LANES), f32), pltpu.VMEM((cell_rows, columns), f32),
         pltpu.VMEM((cell_rows, columns), bf16), pltpu.VMEM((6 * cell_rows, columns), bf16),
         pltpu.VMEM((2, cell_rows, columns), f32), pltpu.VMEM((2, cell_rows, columns), f32),
         pltpu.VMEM((cell_rows, columns), f32), pltpu.VMEM((cell_rows, columns), f32),
         pltpu.SemaphoreType.DMA((2,)), pltpu.SemaphoreType.DMA((half, 4))],
        whole=True, in_place=True,
    )
    shares, *outs = lax.optimization_barrier((shares, *outs))
    (total,) = call(
        "total", functools.partial(total_kernel, cells), rows, [shares], [((half, LANES), f32)], [],
    )
    return (*outs, total.reshape(columns))


def shared_by_pairs(mesh, arguments):
    population = arguments[6]
    passes, cells, width = population.shape
    rows, columns = cells // mesh.shape["gz"], width // mesh.shape["gx"]
    return (
        mesh.shape["gx"] == 2
        and passes >= 4
        and 4 * columns <= rows * LANES
        and rows % (2 * TILE) == 0
        and columns % LANES == 0
        and (columns // LANES) & (columns // LANES - 1) == 0
        and width <= 4096
    )


def solution(mesh):
    def run(*arguments):
        body = per_pair if shared_by_pairs(mesh, arguments) else per_device
        return jax.shard_map(
            body,
            mesh=mesh,
            in_specs=(
                P(None, "gz", "gx"),
                P(None, "gz", "gx"),
                P("gz", "gx"),
                P("gz", "gx"),
                P(None, None, "gz", "gx"),
                P(None, None, "gz", "gx"),
                P(None, "gz", "gx"),
                P(None, "gz", "gx"),
                P("gz", "gx"),
            ),
            out_specs=(
                P(None, "gz", "gx"), P(None, "gz", "gx"), P("gz", "gx"), P("gz", "gx"), P("gx"),
            ),
            check_vma=False,
        )(*arguments)

    return run
```

```python
import functools
import math

import jax
import jax.numpy as jnp
import ml_dtypes
import numpy as np
from jax import lax
from jax.experimental import pallas as pl
from jax.experimental.pallas import tpu as pltpu
from jax.sharding import PartitionSpec as P

DIFF = 512


FRONT_FACET = 0.3
REAR_FACET = 0.9
GAIN_SLOPE_RATE = 0.3
ALPHA_LINEWIDTH = 2.0
COUPLING = 0.5
CLOCK_DELTA = 0.3
DENSITY_LIFETIME = 2.0
GRATING_LIFE = 0.75
TRANSVERSE_DIFFUS = 0.2


def passed_along(value, axis, steps):
    count = lax.axis_size(axis)
    initial, last = (max(0, -steps), min(count, count - steps))
    return lax.ppermute(value, axis, [(source, source + steps) for source in range(initial, last)])


def with_halo(block, sides, width):
    for axis, dim in sides:
        count = lax.axis_size(axis)
        forward = [(i, i + 1) for i in range(count - 1)]
        backward = [(target, source) for source, target in forward]
        low = lax.ppermute(
            lax.slice_in_dim(block, block.shape[dim] - width, None, axis=dim), axis, forward
        )
        high = lax.ppermute(lax.slice_in_dim(block, 0, width, axis=dim), axis, backward)
        block = jnp.concatenate([low, block, high], axis=dim)
    return block


def rotate(source_re, source_im, cosine, sine, form, sign):
    exact = lax.Precision.HIGHEST
    out_re = jnp.einsum(form, source_re, cosine, precision=exact) + sign * jnp.einsum(
        form, source_im, sine, precision=exact
    )
    out_im = jnp.einsum(form, source_im, cosine, precision=exact) - sign * jnp.einsum(
        form, source_re, sine, precision=exact
    )
    return (out_re, out_im)


def transform(stacked):
    count = stacked.shape[1]
    width = stacked.shape[2]
    second = min(128, width // 2)
    first = width // second
    two_pi = 2.0 * math.pi
    index_a = jnp.arange(first, dtype=jnp.int32)
    index_b = jnp.arange(second, dtype=jnp.int32)
    angle_a = two_pi * (index_a[:, None] * index_a[None, :] % first).astype(jnp.float32) / first
    angle_b = two_pi * (index_b[:, None] * index_b[None, :] % second).astype(jnp.float32) / second
    angle_t = two_pi * (index_a[:, None] * index_b[None, :] % width).astype(jnp.float32) / width
    cos_a, sin_a = (jnp.cos(angle_a), jnp.sin(angle_a))
    cos_b, sin_b = (jnp.cos(angle_b), jnp.sin(angle_b))
    cos_t, sin_t = (jnp.cos(angle_t), jnp.sin(angle_t))
    wavenum = index_a[:, None] + first * index_b[None, :]
    signed = jnp.where(wavenum < width // 2, wavenum, wavenum - width)
    phase = (signed * signed).astype(jnp.float32) * (DIFF / (width / 2) ** 2)
    cos_p, sin_p = (jnp.cos(phase), jnp.sin(phase))
    real_in = stacked[0].reshape(count, first, second)
    imag_in = stacked[1].reshape(count, first, second)
    step_re, step_im = rotate(real_in, imag_in, cos_a, sin_a, "nab,ak->nkb", 1.0)
    twist_re = step_re * cos_t + step_im * sin_t
    twist_im = step_im * cos_t - step_re * sin_t
    spec_re, spec_im = rotate(twist_re, twist_im, cos_b, sin_b, "nkb,bj->nkj", 1.0)
    moved_re = spec_re * cos_p - spec_im * sin_p
    moved_im = spec_re * sin_p + spec_im * cos_p
    back_re, back_im = rotate(moved_re, moved_im, cos_b, sin_b, "nkj,jb->nkb", -1.0)
    untw_re = back_re * cos_t - back_im * sin_t
    untw_im = back_im * cos_t + back_re * sin_t
    final_re, final_im = rotate(untw_re, untw_im, cos_a, sin_a, "nkb,ka->nab", -1.0)
    return jnp.stack([final_re.reshape(count, width), final_im.reshape(count, width)]) / width


def added_up(value, axis):
    count = lax.axis_size(axis)
    if count & (count - 1):
        return lax.psum(value, axis)
    reach = 1
    while reach < count:
        value = value + lax.ppermute(value, axis, [(i, i ^ reach) for i in range(count)])
        reach *= 2
    return value


def lateral_work(parts):
    return (transform(parts[0]), transform(parts[1]))


def multiplier_revision(
    population_multiplier,
    holeburn_multiplier,
    measured_rightward,
    measured_leftward,
    rightward_wave,
    leftward_wave,
    population_level,
    holeburn_magnitude,
    attenuation_factor,
    transverse_curvature,
):
    rightward_inphase, rightward_quadrature = (rightward_wave[0], rightward_wave[1])
    leftward_inphase, leftward_quadrature = (leftward_wave[0], leftward_wave[1])
    measured_rightward_inphase, measured_rightward_quadrature = (
        measured_rightward[0],
        measured_rightward[1],
    )
    measured_leftward_inphase, measured_leftward_quadrature = (
        measured_leftward[0],
        measured_leftward[1],
    )
    surplus_population = population_level - 1.0
    amplification_inphase = 1.0 + 0.5 * (GAIN_SLOPE_RATE * surplus_population - attenuation_factor)
    amplification_quadrature = 0.5 * GAIN_SLOPE_RATE * ALPHA_LINEWIDTH * surplus_population
    joined_waves = COUPLING * holeburn_magnitude
    population_derivative = (
        2.0 * CLOCK_DELTA * GAIN_SLOPE_RATE * surplus_population * population_multiplier
    )
    holeburn_derivative = 2.0 * CLOCK_DELTA * holeburn_multiplier
    revised_rightward_inphase = (
        amplification_inphase * measured_rightward_inphase
        - amplification_quadrature * measured_rightward_quadrature
        + joined_waves * measured_leftward_quadrature
        - population_derivative * rightward_inphase
        + holeburn_derivative * leftward_inphase
    )
    revised_rightward_quadrature = (
        amplification_inphase * measured_rightward_quadrature
        + amplification_quadrature * measured_rightward_inphase
        - joined_waves * measured_leftward_inphase
        - population_derivative * rightward_quadrature
        + holeburn_derivative * leftward_quadrature
    )
    revised_leftward_inphase = (
        amplification_inphase * measured_leftward_inphase
        - amplification_quadrature * measured_leftward_quadrature
        + joined_waves * measured_rightward_quadrature
        - population_derivative * leftward_inphase
        + holeburn_derivative * rightward_inphase
    )
    revised_leftward_quadrature = (
        amplification_inphase * measured_leftward_quadrature
        + amplification_quadrature * measured_leftward_inphase
        - joined_waves * measured_rightward_inphase
        - population_derivative * leftward_quadrature
        + holeburn_derivative * rightward_quadrature
    )
    light_intensity = (
        rightward_inphase * rightward_inphase
        + rightward_quadrature * rightward_quadrature
        + leftward_inphase * leftward_inphase
        + leftward_quadrature * leftward_quadrature
    )
    amplification_share = (
        measured_rightward_inphase * (rightward_inphase + ALPHA_LINEWIDTH * rightward_quadrature)
        + measured_rightward_quadrature
        * (rightward_quadrature - ALPHA_LINEWIDTH * rightward_inphase)
        + measured_leftward_inphase * (leftward_inphase + ALPHA_LINEWIDTH * leftward_quadrature)
        + measured_leftward_quadrature * (leftward_quadrature - ALPHA_LINEWIDTH * leftward_inphase)
    )
    revised_population = (
        population_multiplier
        * (1.0 - CLOCK_DELTA / DENSITY_LIFETIME - CLOCK_DELTA * GAIN_SLOPE_RATE * light_intensity)
        + TRANSVERSE_DIFFUS * transverse_curvature
        + 0.5 * GAIN_SLOPE_RATE * amplification_share
    )
    fresh_holeburn = holeburn_multiplier * (1.0 - CLOCK_DELTA / GRATING_LIFE) + COUPLING * (
        measured_rightward_quadrature * leftward_inphase
        - measured_rightward_inphase * leftward_quadrature
        + measured_leftward_quadrature * rightward_inphase
        - measured_leftward_inphase * rightward_quadrature
    )
    return (
        jnp.stack([revised_rightward_inphase, revised_rightward_quadrature]),
        jnp.stack([revised_leftward_inphase, revised_leftward_quadrature]),
        revised_population,
        fresh_holeburn,
    )


def per_device(
    ending_rightward_adjoint,
    ending_leftward_adjoint,
    ending_population_adjoint,
    ending_holeburn_adjoint,
    history_rightward,
    history_leftward,
    history_population,
    history_holeburn,
    segment_passive_attenuation,
):
    columns = ending_rightward_adjoint.shape[2]
    rows = ending_rightward_adjoint.shape[1]
    blocks = lax.axis_size("gz")
    position = lax.axis_index("gz")
    cells = rows * blocks
    zpos = (position * rows + jnp.arange(rows, dtype=jnp.int32)).astype(jnp.float32)
    scaling_factor = 1.0 + 2.0 * zpos / (cells - 1)
    rightward_multiplier, leftward_multiplier = (ending_rightward_adjoint, ending_leftward_adjoint)
    population_multiplier, holeburn_multiplier = (
        ending_population_adjoint,
        ending_holeburn_adjoint,
    )
    attenuation_factor = segment_passive_attenuation.astype(jnp.float32)
    shape_curve = jnp.zeros((columns,), jnp.float32)
    for moment_position in range(history_rightward.shape[0] - 1, -1, -1):
        shape_curve = shape_curve + jnp.sum(scaling_factor[:, None] * population_multiplier, axis=0)
        above = passed_along(rightward_multiplier[:, :1, :], "gz", -1)
        below = passed_along(leftward_multiplier[:, -1:, :], "gz", 1)
        top_row = jnp.where(
            position == blocks - 1, FRONT_FACET * leftward_multiplier[:, -1:, :], above
        )
        bottom_row = jnp.where(position == 0, REAR_FACET * rightward_multiplier[:, :1, :], below)
        lam_fwd = jnp.concatenate([rightward_multiplier[:, 1:, :], top_row], axis=1)
        lam_bwd = jnp.concatenate([bottom_row, leftward_multiplier[:, :-1, :]], axis=1)
        whole_fwd, whole_bwd = (
            lax.all_gather(lam_fwd, "gx", axis=2, tiled=True),
            lax.all_gather(lam_bwd, "gx", axis=2, tiled=True),
        )
        start = lax.axis_index("gx") * columns
        done_fwd, done_bwd = lateral_work((whole_fwd, whole_bwd))
        measured_rightward = lax.dynamic_slice_in_dim(done_fwd, start, columns, 2)
        measured_leftward = lax.dynamic_slice_in_dim(done_bwd, start, columns, 2)
        bordered_array = with_halo(population_multiplier, (("gx", 1),), 1)
        transverse_curvature = (
            bordered_array[:, 2:] + bordered_array[:, :-2] - 2.0 * population_multiplier
        )
        rightward_multiplier, leftward_multiplier, population_multiplier, holeburn_multiplier = (
            multiplier_revision(
                population_multiplier,
                holeburn_multiplier,
                measured_rightward,
                measured_leftward,
                history_rightward[moment_position].astype(jnp.float32),
                history_leftward[moment_position].astype(jnp.float32),
                history_population[moment_position].astype(jnp.float32),
                history_holeburn[moment_position].astype(jnp.float32),
                attenuation_factor,
                transverse_curvature,
            )
        )
    total = added_up(shape_curve, "gz")
    derivative_vector = CLOCK_DELTA * total / math.sqrt(cells)
    return (
        rightward_multiplier,
        leftward_multiplier,
        population_multiplier,
        holeburn_multiplier,
        derivative_vector,
    )

LANES = 128
TILE = 16
POWER = 12
STRETCH = 1211.0
SCALE_LANE = 8


def lateral_matrices(width, blocks):
    lanes = width // blocks
    k = np.arange(width)
    signed = np.where(k < width // 2, k, k - width).astype(np.float64)
    response = np.fft.ifft(np.exp(1j * signed * signed * (DIFF / (width / 2) ** 2)))
    step = np.arange(lanes)
    shift = lanes * np.arange(blocks)[:, None, None] + step[None, None, :] - step[None, :, None]
    kernels = np.fft.fft(response[shift % width], axis=0) / blocks
    top = np.concatenate([kernels.real, kernels.imag], axis=2)
    low = np.concatenate([-kernels.imag, kernels.real], axis=2)
    whole = np.concatenate([top, low], axis=1)
    first = whole.astype(ml_dtypes.bfloat16)
    rest = (whole - first.astype(np.float64)).astype(ml_dtypes.bfloat16)
    return np.stack([first, rest], axis=1)


def block_dft(values, sign):
    count = len(values)
    if count == 1:
        return values
    even = block_dft(values[0::2], sign)
    odd = block_dft(values[1::2], sign)
    out = [None] * count
    for k in range(count // 2):
        (er, ei), (wr, wi) = even[k], odd[k]
        if 4 * k == count:
            plus, minus = (er - wi, ei + wr), (er + wi, ei - wr)
            out[k], out[k + count // 2] = (plus, minus) if sign > 0 else (minus, plus)
            continue
        if k:
            c, s = math.cos(2 * math.pi * k / count), sign * math.sin(2 * math.pi * k / count)
            if 8 * k == count:
                wr, wi = (c * (wr - wi), c * (wr + wi)) if sign > 0 else (c * (wr + wi), c * (wi - wr))
            elif 8 * k == 3 * count:
                wr, wi = (c * (wr + wi), c * (wi - wr)) if sign > 0 else (c * (wr - wi), c * (wr + wi))
            else:
                wr, wi = c * wr - s * wi, c * wi + s * wr
        out[k] = (er + wr, ei + wi)
        out[k + count // 2] = (er - wr, ei - wi)
    return out


def lane(j):
    return pl.ds(pl.multiple_of(j * LANES, LANES), LANES)


def slab(j, rows):
    return pl.ds(pl.multiple_of(j * rows, rows), rows)


def fetch(pairs, sems, first=0):
    copies = [pltpu.make_async_copy(a, b, sems.at[first + i]) for i, (a, b) in enumerate(pairs)]
    for copy in copies:
        copy.start()
    return copies


def rows_of(info, rows, other):
    part = 1 - info[4] if other else info[4]
    return pl.ds(pl.multiple_of(part * rows, rows), rows)


def spread(field, work):
    rows = field.shape[1]
    blocks = work.shape[0]

    @pl.loop(0, rows // 8)
    def _(g):
        at = slab(g, 8)
        values = [
            (field[0, at, j * LANES : (j + 1) * LANES], field[1, at, j * LANES : (j + 1) * LANES])
            for j in range(blocks)
        ]
        for q, (re, im) in enumerate(block_dft(values, -1)):
            work[q, at, :LANES] = re
            work[q, at, LANES:] = im


def fetch_matrices(source, matrices, sem):
    count = matrices.shape[0] // 2
    parts = [pl.ds(i * count, count) for i in range(2)]
    return fetch([(source.at[part], matrices.at[part]) for part in parts], sem)


def multiply(work, matrices, copies):
    rows = work.shape[1]
    count = work.shape[0] // len(copies)
    for i, copy in enumerate(copies):
        copy.wait()

        @pl.loop(i * count, (i + 1) * count, unroll=True)
        def _(q):
            value = work[q]
            first = value.astype(jnp.bfloat16)
            rest = (value - first.astype(jnp.float32)).astype(jnp.bfloat16)
            both = jnp.dot(
                jnp.concatenate([first, rest]), matrices[q, 0], preferred_element_type=jnp.float32
            )
            fine = jnp.dot(first, matrices[q, 1], preferred_element_type=jnp.float32)
            work[q] = both[:rows] + (both[rows:] + fine)


def gathered(work, at):
    values = [(work[q, at, :LANES], work[q, at, LANES:]) for q in range(work.shape[0])]
    return block_dft(values, 1)


def filtered(field, work, matrices, copies):
    spread(field, work)
    multiply(work, matrices, copies)


def write_filtered(info, work, forward, backward, inner, outer):
    rows = work.shape[1] // 2
    for target, base, offset in ((forward, 0, 0), (backward, rows, 8)):

        @pl.loop(0, rows // 8)
        def _(g):
            here = pl.ds(pl.multiple_of(g * 8 + offset, 8), 8)
            for j, pair in enumerate(gathered(work, pl.ds(pl.multiple_of(g * 8 + base, 8), 8))):
                for part in range(2):
                    target[part, here, j * LANES : (j + 1) * LANES] = pair[part]

    low = info[4] == 0
    for part in range(2):
        first, last = forward[part, 0:1, :], backward[part, rows + 7 : rows + 8, :]
        inner[part : part + 1, :] = jnp.where(low, last, first)
        outer[part : part + 1, :] = jnp.where(low, first, last)


def size_of(largest):
    top = jnp.max(jnp.max(largest, axis=1, keepdims=True), axis=0, keepdims=True)
    return jnp.maximum(top, 1e-30).astype(jnp.bfloat16).astype(jnp.float32)


def encoded(value, size):
    unit = value * (STRETCH / size)
    square = unit * unit
    fourth = square * square
    return (fourth * fourth * square * (unit * jnp.abs(unit))).astype(jnp.bfloat16)


def decoded(code, size):
    value = code.astype(jnp.float32)
    root = jnp.exp2(jnp.log(jnp.abs(value)) * (1.0 / (POWER * math.log(2.0)))) * (size / STRETCH)
    return jnp.where(value < 0.0, -root, root)


def side_tile(columns, rows):
    index = lax.broadcasted_iota(jnp.int32, (rows, LANES), 1)
    tile = jnp.zeros((rows, LANES), jnp.float32)
    for at, column in columns:
        tile = jnp.where(index == at, column, tile)
    return tile.astype(jnp.bfloat16)


def sizes_in(tile, count):
    value = tile.astype(jnp.float32)
    return [value[0:1, SCALE_LANE + i : SCALE_LANE + i + 1] for i in range(count)]


def updated(fr, fi, br, bi, wave, population, hole, loss, carrier, grating, lap):
    rr, ri, lr, li = wave
    surplus = population - 1.0
    gain_re = 1.0 + 0.5 * (GAIN_SLOPE_RATE * surplus - loss)
    gain_im = (0.5 * GAIN_SLOPE_RATE * ALPHA_LINEWIDTH) * surplus
    joined = COUPLING * hole
    drive = (2.0 * CLOCK_DELTA * GAIN_SLOPE_RATE) * surplus * carrier
    mix = (2.0 * CLOCK_DELTA) * grating
    new_fr = gain_re * fr - gain_im * fi + joined * bi - drive * rr + mix * lr
    new_fi = gain_re * fi + gain_im * fr - joined * br - drive * ri + mix * li
    new_br = gain_re * br - gain_im * bi + joined * fi - drive * lr + mix * rr
    new_bi = gain_re * bi + gain_im * br - joined * fr - drive * li + mix * ri
    light = rr * rr + ri * ri + lr * lr + li * li
    share = (
        fr * (rr + ALPHA_LINEWIDTH * ri)
        + fi * (ri - ALPHA_LINEWIDTH * rr)
        + br * (lr + ALPHA_LINEWIDTH * li)
        + bi * (li - ALPHA_LINEWIDTH * lr)
    )
    new_carrier = (
        carrier * ((1.0 - CLOCK_DELTA / DENSITY_LIFETIME) - (CLOCK_DELTA * GAIN_SLOPE_RATE) * light)
        + TRANSVERSE_DIFFUS * lap
        + (0.5 * GAIN_SLOPE_RATE) * share
    )
    new_grating = grating * (1.0 - CLOCK_DELTA / GRATING_LIFE) + COUPLING * (
        fi * lr - fr * li + bi * rr - br * ri
    )
    return new_fr, new_fi, new_br, new_bi, new_carrier, new_grating


def curvature(left, mid, right, weight_left, weight_right):
    index = lax.broadcasted_iota(jnp.int32, mid.shape, 1)
    below = jnp.where(index == 0, pltpu.roll(left, 1, 1) * weight_left, pltpu.roll(mid, 1, 1))
    above = jnp.where(
        index == LANES - 1,
        pltpu.roll(right, LANES - 1, 1) * weight_right,
        pltpu.roll(mid, LANES - 1, 1),
    )
    return below + above - 2.0 * mid


def send_fields_kernel(info, forward, backward, out, fields, sems):
    rows, columns = fields.shape[2:]
    half = columns // LANES
    at = rows_of(info, rows, True)
    copies = fetch(
        [(ref.at[:, at, :], fields.at[f]) for f, ref in enumerate((forward, backward))], sems
    )
    sizes = []
    for f in range(2):
        copies[f].wait()
        largest = jnp.maximum(jnp.abs(fields[f, 0]), jnp.abs(fields[f, 1]))
        size = size_of(largest)
        sizes.append((SCALE_LANE + f, size))
        for part in range(2):
            put_tiles(out, (2 * f + part) * half, encoded(fields[f, part], size))
    out[4 * half * rows :, :] = side_tile(sizes, rows)


def put_tiles(out, first, value):
    rows, columns = value.shape
    for j in range(columns // LANES):
        at = (first + j) * rows
        out[at : at + rows, :] = value[:, j * LANES : (j + 1) * LANES]


def history_rows(forward, backward, population, hole, s, at):
    return [
        forward.at[s, 0, at, :], forward.at[s, 1, at, :], backward.at[s, 0, at, :],
        backward.at[s, 1, at, :], population.at[s, at, :], hole.at[s, at, :],
    ]


def into_rows(parts, target, first, rows):
    return [(part, target.at[pl.ds(first + i * rows, rows), :]) for i, part in enumerate(parts)]


def send_later_kernel(steps, info, forward, backward, population, hole, final, *refs):
    targets, sems = refs[:-1], refs[-1]
    rows = targets[0].shape[0] // 6
    history = (forward, backward, population, hole)
    pairs = []
    for i, s in enumerate(steps):
        for k, other in enumerate((True, False)):
            at = rows_of(info, rows, other)
            pairs += into_rows(history_rows(*history, s, at), targets[2 * i + k], 0, rows)
    pairs += into_rows(history_rows(*history, 0, pl.ds(0, 2 * rows)), final, 0, 2 * rows)
    for copy in fetch(pairs, sems):
        copy.wait()


def send_first_kernel(
    s, info, loss, carrier, grating, forward, backward, population, hole,
    own_loss, own, own_carrier, own_grating, out, own_edge, states, ends, sems,
):
    rows, columns = own_carrier.shape
    theirs, mine = rows_of(info, rows, True), rows_of(info, rows, False)
    history = (forward, backward, population, hole)
    copies = fetch(
        [(carrier.at[theirs, :], states.at[0]), (grating.at[theirs, :], states.at[1])]
        + into_rows([loss.at[theirs, :]], out, 0, rows)
        + into_rows(history_rows(*history, s, theirs), out, 3 * rows, rows)
        + [(loss.at[mine, :], own_loss), (carrier.at[mine, :], own_carrier)]
        + [(grating.at[mine, :], own_grating)]
        + into_rows(history_rows(*history, s, mine), own, 0, rows)
        + [
            (part, ends.at[k, i])
            for k in range(2)
            for i, part in enumerate(
                history_rows(*history, 1, pl.ds(k * (2 * rows - TILE), TILE))
            )
        ],
        sems,
    )
    for copy in copies[:2]:
        copy.wait()
    sizes = []
    for i in range(2):
        size = size_of(jnp.abs(states[i]))
        sizes.append(jnp.broadcast_to(size, (1, columns)))
        out[(1 + i) * rows : (2 + i) * rows, :] = encoded(states[i], size)
    for copy in copies[2:]:
        copy.wait()
    low = info[4] == 0
    top = [ends[0, i].astype(jnp.float32)[:1] for i in range(6)]
    foot = [ends[1, i].astype(jnp.float32)[TILE - 1 :] for i in range(6)]
    own_edge[...] = jnp.concatenate([jnp.where(low, a, b) for a, b in zip(top, foot)])
    sizes += [jnp.where(low, b, a) for a, b in zip(top, foot)]
    sizes.append(jnp.zeros((TILE - 8, columns), jnp.float32))
    out[9 * rows :, :] = jnp.concatenate(sizes).astype(jnp.bfloat16)


def enter_kernel(
    info, forward, backward, other, source, tp, tq, inner, outer, field, work, matrices, sem, sems
):
    rows, width = field.shape[1] // 2, field.shape[2]
    columns = width // 2
    half = columns // LANES
    at = rows_of(info, rows, False)
    copies = fetch(
        [
            (ref.at[:, at, :], field.at[:, f * rows : (f + 1) * rows, :columns])
            for f, ref in enumerate((forward, backward))
        ],
        sems,
    )
    matrix_copies = fetch_matrices(source, matrices, sem)
    sizes = sizes_in(other[4 * half * rows :, :], 2)
    for f in range(2):
        for part in range(2):

            @pl.loop(0, half, unroll=2)
            def _(j):
                code = other[slab((2 * f + part) * half + j, rows), :]
                field[part, f * rows : (f + 1) * rows, lane(half + j)] = decoded(code, sizes[f])

    for held in copies:
        held.wait()
    filtered(field, work, matrices, matrix_copies)
    write_filtered(info, work, tp, tq, inner, outer)


def rows_update(
    info, tp, tq, inner, outer, carrier, grating, own, other, own_loss, other_loss,
    field, new_carrier, new_grating, sums_in, sums, cells, last
):
    rows, width = carrier.shape
    half = width // LANES // 2
    columns = half * LANES
    mid = jnp.where(info[0] == 0, 1.0, 0.0)
    wrap = 1.0 - mid
    low = info[4] == 0
    is_first, is_last = info[1], info[2]
    row_index = lax.broadcasted_iota(jnp.int32, (TILE, LANES), 0)
    zero = jnp.zeros((8, LANES), jnp.float32)

    def step(jj, most):
        for side in range(2):
            j = jj + side * half
            here = lane(j)
            left_at = lane(jnp.where(j == 0, 2 * half - 1, j - 1))
            right_at = lane(jnp.where(j == 2 * half - 1, 0, j + 1))
            swapped = lane(jj + (1 - side) * half)
            weight_left = jnp.where(jj == 0, wrap if side == 0 else mid, 1.0)
            weight_right = jnp.where(jj == half - 1, mid if side == 0 else wrap, 1.0)
            total = zero
            for r in range(0, rows, TILE):
                at = slice(r, r + TILE)

                held, begin = (own, other)[side]

                def part_of(i):
                    tile = begin + i * rows + r
                    return held[tile : tile + TILE, lane(jj)].astype(jnp.float32)

                loss = (own_loss, other_loss)[side][at, lane(jj)].astype(jnp.float32)
                f = [tp[part, r + 1 : r + 1 + TILE, here] for part in range(2)]
                b = [tq[part, r + 7 : r + 7 + TILE, here] for part in range(2)]
                if r + TILE == rows:
                    for part in range(2):
                        facet = FRONT_FACET * tq[part, rows + 7 : rows + 8, here]
                        edge = jnp.where(
                            low, inner[part : part + 1, swapped], outer[part : part + 1, here]
                        )
                        edge = jnp.where(is_last, facet, edge)
                        f[part] = jnp.where(row_index == TILE - 1, edge, f[part])
                if r == 0:
                    for part in range(2):
                        facet = REAR_FACET * tp[part, 0:1, here]
                        edge = jnp.where(
                            low, outer[part : part + 1, here], inner[part : part + 1, swapped]
                        )
                        edge = jnp.where(is_first, facet, edge)
                        b[part] = jnp.where(row_index == 0, edge, b[part])
                c = carrier[at, here]
                lap = curvature(
                    carrier[at, left_at], c, carrier[at, right_at], weight_left, weight_right
                )
                out = updated(
                    *f, *b, [part_of(i) for i in range(4)], part_of(4), part_of(5), loss,
                    c, grating[at, here], lap,
                )
                field[0, r : r + TILE, here] = out[0]
                field[1, r : r + TILE, here] = out[1]
                field[0, rows + r : rows + r + TILE, here] = out[2]
                field[1, rows + r : rows + r + TILE, here] = out[3]
                new_carrier[at, here] = out[4]
                new_grating[at, here] = out[5]
                z = (info[3] + r + row_index).astype(jnp.float32)
                weighted = (1.0 + 2.0 * z / (cells - 1)) * ((c + out[4]) if last else c)
                for k in range(0, TILE, 8):
                    total = total + weighted[k : k + 8]
                if last and side == 1:
                    for k in range(0, TILE, 8):
                        most = (
                            jnp.maximum(most[0], jnp.abs(out[4][k : k + 8])),
                            jnp.maximum(most[1], jnp.abs(out[5][k : k + 8])),
                        )
            summed = jnp.sum(total, axis=0, keepdims=True)
            sums[:, here] = summed if sums_in is None else summed + sums_in[:, here]
        return most

    return lax.fori_loop(0, half, step, (zero, zero))


def first_step_kernel(
    cells, info, tp, tq, inner, outer, my_carrier, my_grating, loss, own, own_edge, other, source,
    new_tp, new_tq, new_inner, new_outer, new_carrier, new_grating, sums,
    carrier, grating, field, work, matrices, sem,
):
    matrix_copies = fetch_matrices(source, matrices, sem)
    rows, columns = my_carrier.shape
    half = columns // LANES
    extra = other[9 * rows :, :].astype(jnp.float32)
    sizes = [extra[0:1, 0:1], extra[1:2, 0:1]]
    new_outer[2:8, :columns] = own_edge[...]
    new_outer[2:8, columns:] = extra[2:8]
    for i, (whole, mine) in enumerate(((carrier, my_carrier), (grating, my_grating))):
        whole[:, :columns] = mine[...]

        @pl.loop(0, half, unroll=2)
        def _(j):
            whole[:, lane(half + j)] = decoded(
                other[(1 + i) * rows : (2 + i) * rows, lane(j)], sizes[i]
            )

    rows_update(
        info, tp, tq, inner, outer, carrier, grating, (own, 0), (other, 3 * rows), loss, other,
        field, new_carrier, new_grating, None, sums, cells, False,
    )
    filtered(field, work, matrices, matrix_copies)
    write_filtered(info, work, new_tp, new_tq, new_inner, new_outer)


def middle_step_kernel(
    cells, info, tp, tq, inner, outer, carrier, grating, loss, own, other, other_loss, sums_in,
    source, new_tp, new_tq, new_inner, new_outer, new_carrier, new_grating, sums,
    field, work, matrices, sem,
):
    matrix_copies = fetch_matrices(source, matrices, sem)
    rows_update(
        info, tp, tq, inner, outer, carrier, grating, (own, 0), (other, 0), loss, other_loss,
        field, new_carrier, new_grating, sums_in, sums, cells, False,
    )
    filtered(field, work, matrices, matrix_copies)
    write_filtered(info, work, new_tp, new_tq, new_inner, new_outer)
    rows = carrier.shape[0]
    low = info[4] == 0
    for part in range(2):
        new_outer[2 + part : 3 + part, :] = jnp.where(
            low, new_tp[part, 1:2, :], new_tq[part, rows + 6 : rows + 7, :]
        )
    for i, ref in enumerate((new_carrier, new_grating)):
        new_outer[4 + i : 5 + i, :] = jnp.where(low, ref[0:1, :], ref[rows - 1 : rows, :])
    columns = loss.shape[1]
    for part, ref in enumerate((loss, other_loss)):
        top = ref[:TILE, :].astype(jnp.float32)[:1]
        foot = ref[rows - TILE :, :].astype(jnp.float32)[TILE - 1 :]
        new_outer[6:7, part * columns : (part + 1) * columns] = jnp.where(low, top, foot)


def row_beyond(info, tp, tq, outer, beyond):
    rows = tp.shape[1] - 8
    low = info[4] == 0
    xr, xi, carrier, grating = (outer[i : i + 1, :] for i in range(2, 6))
    yr, yi = (
        jnp.where(low, tp[part, 0:1, :], tq[part, rows + 7 : rows + 8, :]) for part in range(2)
    )
    rr, ri, lr, li, population, hole = (beyond[i : i + 1, :] for i in range(2, 8))
    loss = outer[6:7, :]
    surplus = population - 1.0
    gain_re = 1.0 + 0.5 * (GAIN_SLOPE_RATE * surplus - loss)
    gain_im = (0.5 * GAIN_SLOPE_RATE * ALPHA_LINEWIDTH) * surplus
    joined = COUPLING * hole
    drive = (2.0 * CLOCK_DELTA * GAIN_SLOPE_RATE) * surplus * carrier
    mix = (2.0 * CLOCK_DELTA) * grating
    near_re, near_im = jnp.where(low, lr, rr), jnp.where(low, li, ri)
    far_re, far_im = jnp.where(low, rr, lr), jnp.where(low, ri, li)
    new_re = gain_re * xr - gain_im * xi + joined * yi - drive * near_re + mix * far_re
    new_im = gain_re * xi + gain_im * xr - joined * yr - drive * near_im + mix * far_im
    return new_re, new_im


def leave_kernel(
    cells, info, tp, tq, inner, outer, beyond, carrier, grating, loss, own, other, other_loss,
    sums_in, source, kept, kept_carrier, kept_grating, sides, sent, edge, shares,
    sums, new_carrier, new_grating, field, work, matrices, sem,
):
    matrix_copies = fetch_matrices(source, matrices, sem)
    rows, width = carrier.shape
    columns = width // 2
    half = columns // LANES
    most = rows_update(
        info, tp, tq, inner, outer, carrier, grating, (own, 0), (other, 0), loss, other_loss,
        field, new_carrier, new_grating, sums_in, sums, cells, True,
    )
    mid = jnp.where(info[0] == 0, 1.0, 0.0)
    wrap = 1.0 - mid
    kept_carrier[...] = new_carrier[:, :columns]
    kept_grating[...] = new_grating[:, :columns]
    first, before = new_carrier[:, 0:1] * wrap, new_carrier[:, columns - 1 : columns] * mid
    after, final = new_carrier[:, columns : columns + 1] * mid, new_carrier[:, width - 1 :] * wrap
    sides[0] = jnp.broadcast_to(final, (rows, LANES))
    sides[1] = jnp.broadcast_to(after, (rows, LANES))
    pairs = []
    for at, value in ((0, before), (2, first)):
        coarse = value.astype(jnp.bfloat16).astype(jnp.float32)
        pairs += [(at, coarse), (at + 1, value - coarse)]
    for i, field_of in enumerate((new_carrier, new_grating)):
        size = size_of(most[i])
        pairs.append((SCALE_LANE + 2 + i, size))

        @pl.loop(0, half, unroll=2)
        def _(j):
            sent[slab((4 + i) * half + j, rows), :] = encoded(field_of[:, lane(half + j)], size)

    for part, value in enumerate(row_beyond(info, tp, tq, outer, beyond)):
        field[part, 2 * rows :, :] = jnp.broadcast_to(value, (8, width))
    filtered(field, work, matrices, matrix_copies)
    zero = jnp.zeros((8, LANES), jnp.float32)
    for f in range(2):

        def unmix(g, most):
            at = pl.ds(pl.multiple_of(g * 8 + f * rows, 8), 8)
            for j, pair in enumerate(gathered(work, at)):
                for part in range(2):
                    if j < half:
                        kept[part, at, j * LANES : (j + 1) * LANES] = pair[part]
                    else:
                        work[j, at, part * LANES : (part + 1) * LANES] = pair[part]
                        most = jnp.maximum(most, jnp.abs(pair[part]))
            return most

        size = size_of(lax.fori_loop(0, rows // 8, unmix, zero))
        pairs.append((SCALE_LANE + f, size))

        @pl.loop(0, half, unroll=2)
        def _(j):
            for part in range(2):
                value = work[half + j, f * rows : (f + 1) * rows, part * LANES : (part + 1) * LANES]
                sent[slab((2 * f + part) * half + j, rows), :] = encoded(value, size)

    ends = gathered(work, slice(2 * rows, 2 * rows + 8))
    for part in range(2):
        for j in range(half):
            edge[part : part + 1, j * LANES : (j + 1) * LANES] = ends[j][part][:1]
    far = jnp.concatenate([ends[j][part][:1] for part in range(2) for j in range(half, 2 * half)])
    size = size_of(jnp.abs(far))
    pairs.append((SCALE_LANE + 4, size))
    sent[6 * half * rows : (6 * half + 1) * rows, :] = side_tile(pairs, rows)
    spare = jnp.zeros((rows - 2 * half, LANES), jnp.float32)
    sent[(6 * half + 1) * rows :, :] = encoded(jnp.concatenate([far, spare]), size)
    tile = jnp.concatenate([sums[:, j * LANES : (j + 1) * LANES] for j in range(2 * half)])
    near, far = tile[:half], tile[half:]
    first = info[0] == 0
    to_first, to_second = jnp.where(first, near, far), jnp.where(first, far, near)
    shares[0] = to_first
    shares[1] = to_second


def spread_kernel(info, shares, out):
    for i in range(out.shape[0]):
        out[i] = shares[i % 2]


def total_kernel(cells, info, partial, out):
    total = partial[0]
    for i in range(1, partial.shape[0]):
        total = total + partial[i]
    out[...] = total * (CLOCK_DELTA / math.sqrt(cells))


def final_kernel(
    info, kept, kept_carrier, kept_grating, sides, came, edge, loss, history,
    out_forward, out_backward, out_carrier, out_grating,
    tp, tq, carrier, grating,
):
    rows, columns = kept_carrier.shape
    half = columns // LANES
    mine = info[4] * rows
    theirs = (1 - info[4]) * rows
    low = info[4] == 0
    extra = came[6 * half * rows : (6 * half + 1) * rows, :]
    size_forward, size_backward, size_carrier, size_grating, size_edge = sizes_in(extra, 5)
    ends = decoded(came[(6 * half + 1) * rows :, :], size_edge)
    extra = extra.astype(jnp.float32)

    def at(start, offset, count):
        return pl.ds(pl.multiple_of(start + offset, 8), count)

    for part in range(2):
        tp[part, at(mine, 0, rows), :] = kept[part, :rows, :]
        tq[part, at(mine, 8, rows), :] = kept[part, rows:, :]
    carrier[at(mine, 0, rows), LANES : LANES + columns] = kept_carrier[...]
    carrier[at(mine, 0, rows), :LANES] = sides[0]
    carrier[at(mine, 0, rows), LANES + columns :] = sides[1]
    carrier[at(theirs, 0, rows), :LANES] = jnp.broadcast_to(
        extra[:, 0:1] + extra[:, 1:2], (rows, LANES)
    )
    carrier[at(theirs, 0, rows), LANES + columns :] = jnp.broadcast_to(
        extra[:, 2:3] + extra[:, 3:4], (rows, LANES)
    )
    grating[at(mine, 0, rows), :] = kept_grating[...]

    @pl.loop(0, half, unroll=2)
    def _(j):
        carrier[at(theirs, 0, rows), lane(1 + j)] = decoded(
            came[slab(4 * half + j, rows), :], size_carrier
        )
        grating[at(theirs, 0, rows), lane(j)] = decoded(
            came[slab(5 * half + j, rows), :], size_grating
        )
        for part in range(2):
            tp[part, at(theirs, 0, rows), lane(j)] = decoded(
                came[slab(part * half + j, rows), :], size_forward
            )
            tq[part, at(theirs, 8, rows), lane(j)] = decoded(
                came[slab((2 + part) * half + j, rows), :], size_backward
            )

    all_rows = 2 * rows
    for part in range(2):
        near = edge[part : part + 1, :]
        far = jnp.concatenate([ends[part * half + j : part * half + j + 1] for j in range(half)], axis=1)
        next_edge = jnp.where(low, far, near)
        before_edge = jnp.where(low, near, far)
        front = FRONT_FACET * tq[part, all_rows + 7 : all_rows + 8, :]
        rear = REAR_FACET * tp[part, 0:1, :]
        tp[part, all_rows : all_rows + 1, :] = jnp.where(info[2], front, next_edge)
        tq[part, 7:8, :] = jnp.where(info[1], rear, before_edge)

    @pl.loop(0, half)
    def _(j):
        here = lane(j)
        for r in range(0, all_rows, TILE):
            row = slice(r, r + TILE)
            c = carrier[row, lane(j + 1)]
            lap = curvature(carrier[row, lane(j)], c, carrier[row, lane(j + 2)], 1.0, 1.0)
            parts = [
                history[i * all_rows + r : i * all_rows + r + TILE, here].astype(jnp.float32)
                for i in range(6)
            ]
            out = updated(
                tp[0, r + 1 : r + 1 + TILE, here], tp[1, r + 1 : r + 1 + TILE, here],
                tq[0, r + 7 : r + 7 + TILE, here], tq[1, r + 7 : r + 7 + TILE, here],
                parts[:4], parts[4], parts[5],
                loss[row, here].astype(jnp.float32), c, grating[row, here], lap,
            )
            out_forward[0, row, here] = out[0]
            out_forward[1, row, here] = out[1]
            out_backward[0, row, here] = out[2]
            out_backward[1, row, here] = out[3]
            out_carrier[row, here] = out[4]
            out_grating[row, here] = out[5]


def position(rows, whole):
    x, block, count = lax.axis_index("gx"), lax.axis_index("gz"), lax.axis_size("gz")
    high = lax.rem(x + block, 2)
    if whole:
        return x, block == 0, block == count - 1, block * rows, high
    place = 2 * block + high
    return x, place == 0, place == 2 * count - 1, place * rows, high


def whole_spec(shape):
    return pl.BlockSpec(shape, lambda i, n=len(shape): (0,) * n)


def call(name, kernel, rows, inputs, outputs, scratch, flops=0, grant=24, whole=False):
    arrays = [x[0] if isinstance(x, tuple) else x for x in inputs]
    specs = [x[1] if isinstance(x, tuple) else whole_spec(x.shape) for x in inputs]
    shapes = [jax.ShapeDtypeStruct(*out) for out in outputs]
    moved = sum(math.prod(s.shape) * s.dtype.itemsize for s in shapes)

    def body(*refs):
        kernel(position(rows, whole), *refs)

    return pl.pallas_call(
        body,
        grid=(1,),
        in_specs=specs,
        out_specs=[whole_spec(s.shape) for s in shapes],
        scratch_shapes=scratch,
        out_shape=shapes,
        compiler_params=pltpu.CompilerParams(vmem_limit_bytes=grant * 1024 * 1024),
        cost_estimate=pl.CostEstimate(
            flops=flops, bytes_accessed=moved + 4 * 1024 * 1024, transcendentals=0
        ),
        name=name,
    )(*arrays)


def per_pair(
    ending_rightward_adjoint,
    ending_leftward_adjoint,
    ending_population_adjoint,
    ending_holeburn_adjoint,
    history_rightward,
    history_leftward,
    history_population,
    history_holeburn,
    segment_passive_attenuation,
):
    cell_rows, columns = ending_population_adjoint.shape
    passes = history_population.shape[0]
    rows = cell_rows // 2
    half = columns // LANES
    blocks = 2 * half
    width = 2 * columns
    count = lax.axis_size("gz")
    cells = cell_rows * count
    x = lax.axis_index("gx")
    f32, bf16 = jnp.float32, jnp.bfloat16
    swap = [(0, 1), (1, 0)]
    in_place = pl.BlockSpec(memory_space=pltpu.HBM)

    def held(*arrays):
        return [(a, in_place) for a in arrays]

    def tiles(n):
        return ((n * rows, LANES), bf16)

    ends = held(ending_rightward_adjoint, ending_leftward_adjoint)
    planes = held(ending_population_adjoint, ending_holeburn_adjoint)
    history = held(history_rightward, history_leftward, history_population, history_holeburn)
    losses = held(segment_passive_attenuation)
    matrices = pltpu.with_memory_space_constraint(
        jnp.asarray(lateral_matrices(width, blocks)), pltpu.HBM
    )
    matrix_input = held(matrices)
    work = [
        pltpu.VMEM((blocks, 2 * rows, 2 * LANES), f32),
        pltpu.VMEM(matrices.shape, bf16),
        pltpu.SemaphoreType.DMA((2,)),
    ]
    field_scratch = pltpu.VMEM((2, 2 * rows, width), f32)
    def state_out(outer_rows):
        state = ((2, rows + 8, width), f32)
        return [state, state, ((2, width), f32), ((outer_rows, width), f32)]

    plane = ((rows, width), f32)
    plane_scratch = pltpu.VMEM((rows, width), f32)
    half_plane = ((rows, columns), f32)
    work_flops = 2 * 3 * 2 * rows * blocks * (2 * LANES) ** 2

    (coded,) = call(
        "send_fields", send_fields_kernel, rows, ends, [tiles(4 * half + 1)],
        [pltpu.VMEM((2, 2, rows, columns), f32), pltpu.SemaphoreType.DMA((2,))], grant=62,
    )
    other_fields = lax.ppermute(coded, "gx", swap)
    loss, own_first, my_carrier, my_grating, sent_first, own_edge = call(
        "send_first", functools.partial(send_first_kernel, passes - 1), rows,
        [*losses, *planes, *history],
        [((rows, columns), bf16), ((6 * rows, columns), bf16), half_plane, half_plane,
         ((9 * rows + TILE, columns), bf16), ((6, columns), f32)],
        [pltpu.VMEM((2, rows, columns), f32), pltpu.VMEM((2, 6, TILE, columns), bf16),
         pltpu.SemaphoreType.DMA((30,))], grant=62,
    )
    steps = range(passes - 2, 0, -1)
    history_last, *later = call(
        "send_later", functools.partial(send_later_kernel, steps), rows, history,
        [((6 * cell_rows, columns), bf16)] + [((6 * rows, columns), bf16)] * (2 * len(steps)),
        [pltpu.SemaphoreType.DMA((12 * len(steps) + 6,))], grant=62,
    )
    sent_first, history_last, later, other_fields = lax.optimization_barrier(
        (sent_first, history_last, later, other_fields)
    )
    other_first = lax.ppermute(sent_first, "gx", swap)

    line = ("gz", "gx")
    neighbours = []
    for b in range(count - 1):
        top = (1 + b) % 2
        neighbours += [(2 * b + top, 2 * b + 2 + top), (2 * b + 2 + top, 2 * b + top)]

    def edges(inner, outer):
        outer = lax.ppermute(outer, line, neighbours)
        return lax.ppermute(inner, "gx", swap), outer

    tp, tq, inner, outer = call(
        "enter", enter_kernel, rows, [*ends, other_fields, *matrix_input],
        state_out(2), [field_scratch, *work, pltpu.SemaphoreType.DMA((2,))], work_flops,
    )
    inner, outer = edges(inner, outer)

    other_loss = (other_first, pl.BlockSpec((rows, columns), lambda i: (0, 0)))
    carrier = grating = sums = other = own = None
    for index, s in enumerate(range(passes - 1, 0, -1)):
        if index < len(steps):
            sent, own_next = later[2 * index : 2 * index + 2]
            sent, inner, outer = lax.optimization_barrier((sent, inner, outer))
            coming = lax.ppermute(sent, "gx", swap)
        shared = [tp, tq, inner, outer]
        if index == 0:
            tp, tq, inner, outer, carrier, grating, sums = call(
                "first_step", functools.partial(first_step_kernel, cells), rows,
                [*shared, my_carrier, my_grating, loss, own_first, own_edge, other_first,
                 *matrix_input],
                [*state_out(8), plane, plane, ((1, width), f32)],
                [plane_scratch, plane_scratch, field_scratch, *work], work_flops,
            )
        elif s > 1:
            tp, tq, inner, outer, carrier, grating, sums = call(
                "middle_step", functools.partial(middle_step_kernel, cells), rows,
                [*shared, carrier, grating, loss, own, other, other_loss, sums, *matrix_input],
                [*state_out(7), plane, plane, ((1, width), f32)],
                [field_scratch, *work], work_flops,
            )
        else:
            kept, kept_carrier, kept_grating, sides, sent, edge, shares = call(
                "leave", functools.partial(leave_kernel, cells), rows,
                [*shared, beyond, carrier, grating, loss, own, other, other_loss, sums, *matrix_input],
                [((2, 2 * rows, columns), f32), half_plane, half_plane, ((2, rows, LANES), f32),
                 tiles(6 * half + 2), ((2, columns), f32), ((2, half, LANES), f32)],
                [pltpu.VMEM((1, width), f32), plane_scratch, plane_scratch,
                 pltpu.VMEM((2, 2 * rows + 8, width), f32),
                 pltpu.VMEM((blocks, 2 * rows + TILE, 2 * LANES), f32), *work[1:]],
                work_flops,
            )
        if s > 1:
            inner, outer = edges(inner, outer)
            own, other = own_next, coming
            if index == 0:
                beyond = outer

    came = lax.ppermute(sent, "gx", swap)
    (shares,) = call(
        "spread", spread_kernel, rows, [shares], [((2 * count, half, LANES), f32)], [],
    )
    shares = lax.all_to_all(shares, line, 0, 0, tiled=True)

    outs = call(
        "final", final_kernel, cell_rows,
        [kept, kept_carrier, kept_grating, sides, came, edge,
         segment_passive_attenuation, history_last],
        [((2, cell_rows, columns), f32), ((2, cell_rows, columns), f32),
         ((cell_rows, columns), f32), ((cell_rows, columns), f32)],
        [pltpu.VMEM((2, cell_rows + 8, columns), f32), pltpu.VMEM((2, cell_rows + 8, columns), f32),
         pltpu.VMEM((cell_rows, columns + 2 * LANES), f32), pltpu.VMEM((cell_rows, columns), f32)],
        whole=True,
    )
    shares, *outs = lax.optimization_barrier((shares, *outs))
    (total,) = call(
        "total", functools.partial(total_kernel, cells), rows, [shares], [((half, LANES), f32)], [],
    )
    return (*outs, total.reshape(columns))


def shared_by_pairs(mesh, arguments):
    population = arguments[6]
    passes, cells, width = population.shape
    rows, columns = cells // mesh.shape["gz"], width // mesh.shape["gx"]
    return (
        mesh.shape["gx"] == 2
        and passes >= 4
        and 4 * columns <= rows * LANES
        and rows % (2 * TILE) == 0
        and columns % LANES == 0
        and (columns // LANES) & (columns // LANES - 1) == 0
        and width <= 4096
    )


def solution(mesh):
    def run(*arguments):
        body = per_pair if shared_by_pairs(mesh, arguments) else per_device
        return jax.shard_map(
            body,
            mesh=mesh,
            in_specs=(
                P(None, "gz", "gx"),
                P(None, "gz", "gx"),
                P("gz", "gx"),
                P("gz", "gx"),
                P(None, None, "gz", "gx"),
                P(None, None, "gz", "gx"),
                P(None, "gz", "gx"),
                P(None, "gz", "gx"),
                P("gz", "gx"),
            ),
            out_specs=(
                P(None, "gz", "gx"), P(None, "gz", "gx"), P("gz", "gx"), P("gz", "gx"), P("gx"),
            ),
            check_vma=False,
        )(*arguments)

    return run
```

```python
import functools
import math

import jax
import jax.numpy as jnp
import ml_dtypes
import numpy as np
from jax import lax
from jax.experimental import pallas as pl
from jax.experimental.pallas import tpu as pltpu
from jax.sharding import PartitionSpec as P

DIFF = 512


FRONT_FACET = 0.3
REAR_FACET = 0.9
GAIN_SLOPE_RATE = 0.3
ALPHA_LINEWIDTH = 2.0
COUPLING = 0.5
CLOCK_DELTA = 0.3
DENSITY_LIFETIME = 2.0
GRATING_LIFE = 0.75
TRANSVERSE_DIFFUS = 0.2


def passed_along(value, axis, steps):
    count = lax.axis_size(axis)
    initial, last = (max(0, -steps), min(count, count - steps))
    return lax.ppermute(value, axis, [(source, source + steps) for source in range(initial, last)])


def with_halo(block, sides, width):
    for axis, dim in sides:
        count = lax.axis_size(axis)
        forward = [(i, i + 1) for i in range(count - 1)]
        backward = [(target, source) for source, target in forward]
        low = lax.ppermute(
            lax.slice_in_dim(block, block.shape[dim] - width, None, axis=dim), axis, forward
        )
        high = lax.ppermute(lax.slice_in_dim(block, 0, width, axis=dim), axis, backward)
        block = jnp.concatenate([low, block, high], axis=dim)
    return block


def rotate(source_re, source_im, cosine, sine, form, sign):
    exact = lax.Precision.HIGHEST
    out_re = jnp.einsum(form, source_re, cosine, precision=exact) + sign * jnp.einsum(
        form, source_im, sine, precision=exact
    )
    out_im = jnp.einsum(form, source_im, cosine, precision=exact) - sign * jnp.einsum(
        form, source_re, sine, precision=exact
    )
    return (out_re, out_im)


def transform(stacked):
    count = stacked.shape[1]
    width = stacked.shape[2]
    second = min(128, width // 2)
    first = width // second
    two_pi = 2.0 * math.pi
    index_a = jnp.arange(first, dtype=jnp.int32)
    index_b = jnp.arange(second, dtype=jnp.int32)
    angle_a = two_pi * (index_a[:, None] * index_a[None, :] % first).astype(jnp.float32) / first
    angle_b = two_pi * (index_b[:, None] * index_b[None, :] % second).astype(jnp.float32) / second
    angle_t = two_pi * (index_a[:, None] * index_b[None, :] % width).astype(jnp.float32) / width
    cos_a, sin_a = (jnp.cos(angle_a), jnp.sin(angle_a))
    cos_b, sin_b = (jnp.cos(angle_b), jnp.sin(angle_b))
    cos_t, sin_t = (jnp.cos(angle_t), jnp.sin(angle_t))
    wavenum = index_a[:, None] + first * index_b[None, :]
    signed = jnp.where(wavenum < width // 2, wavenum, wavenum - width)
    phase = (signed * signed).astype(jnp.float32) * (DIFF / (width / 2) ** 2)
    cos_p, sin_p = (jnp.cos(phase), jnp.sin(phase))
    real_in = stacked[0].reshape(count, first, second)
    imag_in = stacked[1].reshape(count, first, second)
    step_re, step_im = rotate(real_in, imag_in, cos_a, sin_a, "nab,ak->nkb", 1.0)
    twist_re = step_re * cos_t + step_im * sin_t
    twist_im = step_im * cos_t - step_re * sin_t
    spec_re, spec_im = rotate(twist_re, twist_im, cos_b, sin_b, "nkb,bj->nkj", 1.0)
    moved_re = spec_re * cos_p - spec_im * sin_p
    moved_im = spec_re * sin_p + spec_im * cos_p
    back_re, back_im = rotate(moved_re, moved_im, cos_b, sin_b, "nkj,jb->nkb", -1.0)
    untw_re = back_re * cos_t - back_im * sin_t
    untw_im = back_im * cos_t + back_re * sin_t
    final_re, final_im = rotate(untw_re, untw_im, cos_a, sin_a, "nkb,ka->nab", -1.0)
    return jnp.stack([final_re.reshape(count, width), final_im.reshape(count, width)]) / width


def added_up(value, axis):
    count = lax.axis_size(axis)
    if count & (count - 1):
        return lax.psum(value, axis)
    reach = 1
    while reach < count:
        value = value + lax.ppermute(value, axis, [(i, i ^ reach) for i in range(count)])
        reach *= 2
    return value


def lateral_work(parts):
    return (transform(parts[0]), transform(parts[1]))


def multiplier_revision(
    population_multiplier,
    holeburn_multiplier,
    measured_rightward,
    measured_leftward,
    rightward_wave,
    leftward_wave,
    population_level,
    holeburn_magnitude,
    attenuation_factor,
    transverse_curvature,
):
    rightward_inphase, rightward_quadrature = (rightward_wave[0], rightward_wave[1])
    leftward_inphase, leftward_quadrature = (leftward_wave[0], leftward_wave[1])
    measured_rightward_inphase, measured_rightward_quadrature = (
        measured_rightward[0],
        measured_rightward[1],
    )
    measured_leftward_inphase, measured_leftward_quadrature = (
        measured_leftward[0],
        measured_leftward[1],
    )
    surplus_population = population_level - 1.0
    amplification_inphase = 1.0 + 0.5 * (GAIN_SLOPE_RATE * surplus_population - attenuation_factor)
    amplification_quadrature = 0.5 * GAIN_SLOPE_RATE * ALPHA_LINEWIDTH * surplus_population
    joined_waves = COUPLING * holeburn_magnitude
    population_derivative = (
        2.0 * CLOCK_DELTA * GAIN_SLOPE_RATE * surplus_population * population_multiplier
    )
    holeburn_derivative = 2.0 * CLOCK_DELTA * holeburn_multiplier
    revised_rightward_inphase = (
        amplification_inphase * measured_rightward_inphase
        - amplification_quadrature * measured_rightward_quadrature
        + joined_waves * measured_leftward_quadrature
        - population_derivative * rightward_inphase
        + holeburn_derivative * leftward_inphase
    )
    revised_rightward_quadrature = (
        amplification_inphase * measured_rightward_quadrature
        + amplification_quadrature * measured_rightward_inphase
        - joined_waves * measured_leftward_inphase
        - population_derivative * rightward_quadrature
        + holeburn_derivative * leftward_quadrature
    )
    revised_leftward_inphase = (
        amplification_inphase * measured_leftward_inphase
        - amplification_quadrature * measured_leftward_quadrature
        + joined_waves * measured_rightward_quadrature
        - population_derivative * leftward_inphase
        + holeburn_derivative * rightward_inphase
    )
    revised_leftward_quadrature = (
        amplification_inphase * measured_leftward_quadrature
        + amplification_quadrature * measured_leftward_inphase
        - joined_waves * measured_rightward_inphase
        - population_derivative * leftward_quadrature
        + holeburn_derivative * rightward_quadrature
    )
    light_intensity = (
        rightward_inphase * rightward_inphase
        + rightward_quadrature * rightward_quadrature
        + leftward_inphase * leftward_inphase
        + leftward_quadrature * leftward_quadrature
    )
    amplification_share = (
        measured_rightward_inphase * (rightward_inphase + ALPHA_LINEWIDTH * rightward_quadrature)
        + measured_rightward_quadrature
        * (rightward_quadrature - ALPHA_LINEWIDTH * rightward_inphase)
        + measured_leftward_inphase * (leftward_inphase + ALPHA_LINEWIDTH * leftward_quadrature)
        + measured_leftward_quadrature * (leftward_quadrature - ALPHA_LINEWIDTH * leftward_inphase)
    )
    revised_population = (
        population_multiplier
        * (1.0 - CLOCK_DELTA / DENSITY_LIFETIME - CLOCK_DELTA * GAIN_SLOPE_RATE * light_intensity)
        + TRANSVERSE_DIFFUS * transverse_curvature
        + 0.5 * GAIN_SLOPE_RATE * amplification_share
    )
    fresh_holeburn = holeburn_multiplier * (1.0 - CLOCK_DELTA / GRATING_LIFE) + COUPLING * (
        measured_rightward_quadrature * leftward_inphase
        - measured_rightward_inphase * leftward_quadrature
        + measured_leftward_quadrature * rightward_inphase
        - measured_leftward_inphase * rightward_quadrature
    )
    return (
        jnp.stack([revised_rightward_inphase, revised_rightward_quadrature]),
        jnp.stack([revised_leftward_inphase, revised_leftward_quadrature]),
        revised_population,
        fresh_holeburn,
    )


def per_device(
    ending_rightward_adjoint,
    ending_leftward_adjoint,
    ending_population_adjoint,
    ending_holeburn_adjoint,
    history_rightward,
    history_leftward,
    history_population,
    history_holeburn,
    segment_passive_attenuation,
):
    columns = ending_rightward_adjoint.shape[2]
    rows = ending_rightward_adjoint.shape[1]
    blocks = lax.axis_size("gz")
    position = lax.axis_index("gz")
    cells = rows * blocks
    zpos = (position * rows + jnp.arange(rows, dtype=jnp.int32)).astype(jnp.float32)
    scaling_factor = 1.0 + 2.0 * zpos / (cells - 1)
    rightward_multiplier, leftward_multiplier = (ending_rightward_adjoint, ending_leftward_adjoint)
    population_multiplier, holeburn_multiplier = (
        ending_population_adjoint,
        ending_holeburn_adjoint,
    )
    attenuation_factor = segment_passive_attenuation.astype(jnp.float32)
    shape_curve = jnp.zeros((columns,), jnp.float32)
    for moment_position in range(history_rightward.shape[0] - 1, -1, -1):
        shape_curve = shape_curve + jnp.sum(scaling_factor[:, None] * population_multiplier, axis=0)
        above = passed_along(rightward_multiplier[:, :1, :], "gz", -1)
        below = passed_along(leftward_multiplier[:, -1:, :], "gz", 1)
        top_row = jnp.where(
            position == blocks - 1, FRONT_FACET * leftward_multiplier[:, -1:, :], above
        )
        bottom_row = jnp.where(position == 0, REAR_FACET * rightward_multiplier[:, :1, :], below)
        lam_fwd = jnp.concatenate([rightward_multiplier[:, 1:, :], top_row], axis=1)
        lam_bwd = jnp.concatenate([bottom_row, leftward_multiplier[:, :-1, :]], axis=1)
        whole_fwd, whole_bwd = (
            lax.all_gather(lam_fwd, "gx", axis=2, tiled=True),
            lax.all_gather(lam_bwd, "gx", axis=2, tiled=True),
        )
        start = lax.axis_index("gx") * columns
        done_fwd, done_bwd = lateral_work((whole_fwd, whole_bwd))
        measured_rightward = lax.dynamic_slice_in_dim(done_fwd, start, columns, 2)
        measured_leftward = lax.dynamic_slice_in_dim(done_bwd, start, columns, 2)
        bordered_array = with_halo(population_multiplier, (("gx", 1),), 1)
        transverse_curvature = (
            bordered_array[:, 2:] + bordered_array[:, :-2] - 2.0 * population_multiplier
        )
        rightward_multiplier, leftward_multiplier, population_multiplier, holeburn_multiplier = (
            multiplier_revision(
                population_multiplier,
                holeburn_multiplier,
                measured_rightward,
                measured_leftward,
                history_rightward[moment_position].astype(jnp.float32),
                history_leftward[moment_position].astype(jnp.float32),
                history_population[moment_position].astype(jnp.float32),
                history_holeburn[moment_position].astype(jnp.float32),
                attenuation_factor,
                transverse_curvature,
            )
        )
    total = added_up(shape_curve, "gz")
    derivative_vector = CLOCK_DELTA * total / math.sqrt(cells)
    return (
        rightward_multiplier,
        leftward_multiplier,
        population_multiplier,
        holeburn_multiplier,
        derivative_vector,
    )

LANES = 128
TILE = 16
POWER = 12
STRETCH = 1211.0
SCALE_LANE = 8


def lateral_matrices(width, blocks):
    lanes = width // blocks
    k = np.arange(width)
    signed = np.where(k < width // 2, k, k - width).astype(np.float64)
    response = np.fft.ifft(np.exp(1j * signed * signed * (DIFF / (width / 2) ** 2)))
    step = np.arange(lanes)
    shift = lanes * np.arange(blocks)[:, None, None] + step[None, None, :] - step[None, :, None]
    kernels = np.fft.fft(response[shift % width], axis=0) / blocks
    top = np.concatenate([kernels.real, kernels.imag], axis=2)
    low = np.concatenate([-kernels.imag, kernels.real], axis=2)
    whole = np.concatenate([top, low], axis=1)
    first = whole.astype(ml_dtypes.bfloat16)
    rest = (whole - first.astype(np.float64)).astype(ml_dtypes.bfloat16)
    return np.stack([first, rest], axis=1)


def block_dft(values, sign):
    count = len(values)
    if count == 1:
        return values
    even = block_dft(values[0::2], sign)
    odd = block_dft(values[1::2], sign)
    out = [None] * count
    for k in range(count // 2):
        (er, ei), (wr, wi) = even[k], odd[k]
        if 4 * k == count:
            plus, minus = (er - wi, ei + wr), (er + wi, ei - wr)
            out[k], out[k + count // 2] = (plus, minus) if sign > 0 else (minus, plus)
            continue
        if k:
            c, s = math.cos(2 * math.pi * k / count), sign * math.sin(2 * math.pi * k / count)
            if 8 * k == count:
                wr, wi = (c * (wr - wi), c * (wr + wi)) if sign > 0 else (c * (wr + wi), c * (wi - wr))
            elif 8 * k == 3 * count:
                wr, wi = (c * (wr + wi), c * (wi - wr)) if sign > 0 else (c * (wr - wi), c * (wr + wi))
            else:
                wr, wi = c * wr - s * wi, c * wi + s * wr
        out[k] = (er + wr, ei + wi)
        out[k + count // 2] = (er - wr, ei - wi)
    return out


def lane(j):
    return pl.ds(pl.multiple_of(j * LANES, LANES), LANES)


def slab(j, rows):
    return pl.ds(pl.multiple_of(j * rows, rows), rows)


def fetch(pairs, sems, first=0):
    copies = [pltpu.make_async_copy(a, b, sems.at[first + i]) for i, (a, b) in enumerate(pairs)]
    for copy in copies:
        copy.start()
    return copies


def rows_of(info, rows, other):
    part = 1 - info[4] if other else info[4]
    return pl.ds(pl.multiple_of(part * rows, rows), rows)


def spread(field, work):
    rows = field.shape[1]
    blocks = work.shape[0]

    @pl.loop(0, rows // 8)
    def _(g):
        at = slab(g, 8)
        values = [
            (field[0, at, j * LANES : (j + 1) * LANES], field[1, at, j * LANES : (j + 1) * LANES])
            for j in range(blocks)
        ]
        for q, (re, im) in enumerate(block_dft(values, -1)):
            work[q, at, :LANES] = re
            work[q, at, LANES:] = im


def fetch_matrices(source, matrices, sem):
    count = matrices.shape[0] // 2
    parts = [pl.ds(i * count, count) for i in range(2)]
    return fetch([(source.at[part], matrices.at[part]) for part in parts], sem)


def multiply(work, matrices, copies):
    rows = work.shape[1]
    count = work.shape[0] // len(copies)
    for i, copy in enumerate(copies):
        copy.wait()

        @pl.loop(i * count, (i + 1) * count, unroll=True)
        def _(q):
            value = work[q]
            first = value.astype(jnp.bfloat16)
            rest = (value - first.astype(jnp.float32)).astype(jnp.bfloat16)
            both = jnp.dot(
                jnp.concatenate([first, rest]), matrices[q, 0], preferred_element_type=jnp.float32
            )
            fine = jnp.dot(first, matrices[q, 1], preferred_element_type=jnp.float32)
            work[q] = both[:rows] + (both[rows:] + fine)


def gathered(work, at):
    values = [(work[q, at, :LANES], work[q, at, LANES:]) for q in range(work.shape[0])]
    return block_dft(values, 1)


def filtered(field, work, matrices, copies):
    spread(field, work)
    multiply(work, matrices, copies)


def write_filtered(info, work, forward, backward, inner, outer):
    rows = work.shape[1] // 2
    for target, base, offset in ((forward, 0, 0), (backward, rows, 8)):

        @pl.loop(0, rows // 8)
        def _(g):
            here = pl.ds(pl.multiple_of(g * 8 + offset, 8), 8)
            for j, pair in enumerate(gathered(work, pl.ds(pl.multiple_of(g * 8 + base, 8), 8))):
                for part in range(2):
                    target[part, here, j * LANES : (j + 1) * LANES] = pair[part]

    low = info[4] == 0
    for part in range(2):
        first, last = forward[part, 0:1, :], backward[part, rows + 7 : rows + 8, :]
        inner[part : part + 1, :] = jnp.where(low, last, first)
        outer[part : part + 1, :] = jnp.where(low, first, last)


def size_of(largest):
    top = jnp.max(jnp.max(largest, axis=1, keepdims=True), axis=0, keepdims=True)
    return jnp.maximum(top, 1e-30).astype(jnp.bfloat16).astype(jnp.float32)


def encoded(value, size):
    unit = value * (STRETCH / size)
    square = unit * unit
    fourth = square * square
    return (fourth * fourth * square * (unit * jnp.abs(unit))).astype(jnp.bfloat16)


def decoded(code, size):
    value = code.astype(jnp.float32)
    root = jnp.exp2(jnp.log(jnp.abs(value)) * (1.0 / (POWER * math.log(2.0)))) * (size / STRETCH)
    return jnp.where(value < 0.0, -root, root)


def side_tile(columns, rows):
    index = lax.broadcasted_iota(jnp.int32, (rows, LANES), 1)
    tile = jnp.zeros((rows, LANES), jnp.float32)
    for at, column in columns:
        tile = jnp.where(index == at, column, tile)
    return tile.astype(jnp.bfloat16)


def sizes_in(tile, count):
    value = tile.astype(jnp.float32)
    return [value[0:1, SCALE_LANE + i : SCALE_LANE + i + 1] for i in range(count)]


def updated(fr, fi, br, bi, wave, population, hole, loss, carrier, grating, lap):
    rr, ri, lr, li = wave
    surplus = population - 1.0
    gain_re = 1.0 + 0.5 * (GAIN_SLOPE_RATE * surplus - loss)
    gain_im = (0.5 * GAIN_SLOPE_RATE * ALPHA_LINEWIDTH) * surplus
    joined = COUPLING * hole
    drive = (2.0 * CLOCK_DELTA * GAIN_SLOPE_RATE) * surplus * carrier
    mix = (2.0 * CLOCK_DELTA) * grating
    new_fr = gain_re * fr - gain_im * fi + joined * bi - drive * rr + mix * lr
    new_fi = gain_re * fi + gain_im * fr - joined * br - drive * ri + mix * li
    new_br = gain_re * br - gain_im * bi + joined * fi - drive * lr + mix * rr
    new_bi = gain_re * bi + gain_im * br - joined * fr - drive * li + mix * ri
    light = rr * rr + ri * ri + lr * lr + li * li
    share = (
        fr * (rr + ALPHA_LINEWIDTH * ri)
        + fi * (ri - ALPHA_LINEWIDTH * rr)
        + br * (lr + ALPHA_LINEWIDTH * li)
        + bi * (li - ALPHA_LINEWIDTH * lr)
    )
    new_carrier = (
        carrier * ((1.0 - CLOCK_DELTA / DENSITY_LIFETIME) - (CLOCK_DELTA * GAIN_SLOPE_RATE) * light)
        + TRANSVERSE_DIFFUS * lap
        + (0.5 * GAIN_SLOPE_RATE) * share
    )
    new_grating = grating * (1.0 - CLOCK_DELTA / GRATING_LIFE) + COUPLING * (
        fi * lr - fr * li + bi * rr - br * ri
    )
    return new_fr, new_fi, new_br, new_bi, new_carrier, new_grating


def curvature(left, mid, right, weight_left, weight_right):
    index = lax.broadcasted_iota(jnp.int32, mid.shape, 1)
    below = jnp.where(index == 0, pltpu.roll(left, 1, 1) * weight_left, pltpu.roll(mid, 1, 1))
    above = jnp.where(
        index == LANES - 1,
        pltpu.roll(right, LANES - 1, 1) * weight_right,
        pltpu.roll(mid, LANES - 1, 1),
    )
    return below + above - 2.0 * mid


def send_fields_kernel(info, forward, backward, out, fields, sems):
    rows, columns = fields.shape[2:]
    half = columns // LANES
    at = rows_of(info, rows, True)
    copies = fetch(
        [(ref.at[:, at, :], fields.at[f]) for f, ref in enumerate((forward, backward))], sems
    )
    sizes = []
    for f in range(2):
        copies[f].wait()
        largest = jnp.maximum(jnp.abs(fields[f, 0]), jnp.abs(fields[f, 1]))
        size = size_of(largest)
        sizes.append((SCALE_LANE + f, size))
        for part in range(2):
            put_tiles(out, (2 * f + part) * half, encoded(fields[f, part], size))
    out[4 * half * rows :, :] = side_tile(sizes, rows)


def put_tiles(out, first, value):
    rows, columns = value.shape
    for j in range(columns // LANES):
        at = (first + j) * rows
        out[at : at + rows, :] = value[:, j * LANES : (j + 1) * LANES]


def history_rows(forward, backward, population, hole, s, at):
    return [
        forward.at[s, 0, at, :], forward.at[s, 1, at, :], backward.at[s, 0, at, :],
        backward.at[s, 1, at, :], population.at[s, at, :], hole.at[s, at, :],
    ]


def into_rows(parts, target, first, rows):
    return [(part, target.at[pl.ds(first + i * rows, rows), :]) for i, part in enumerate(parts)]


def send_later_kernel(steps, info, forward, backward, population, hole, final, *refs):
    targets, sems = refs[:-1], refs[-1]
    rows = targets[0].shape[0] // 6
    history = (forward, backward, population, hole)
    pairs = []
    for i, s in enumerate(steps):
        for k, other in enumerate((True, False)):
            at = rows_of(info, rows, other)
            pairs += into_rows(history_rows(*history, s, at), targets[2 * i + k], 0, rows)
    pairs += into_rows(history_rows(*history, 0, pl.ds(0, 2 * rows)), final, 0, 2 * rows)
    for copy in fetch(pairs, sems):
        copy.wait()


def send_first_kernel(
    s, info, loss, carrier, grating, forward, backward, population, hole,
    own_loss, own, own_carrier, own_grating, out, own_edge, states, ends, sems,
):
    rows, columns = own_carrier.shape
    theirs, mine = rows_of(info, rows, True), rows_of(info, rows, False)
    history = (forward, backward, population, hole)
    copies = fetch(
        [(carrier.at[theirs, :], states.at[0]), (grating.at[theirs, :], states.at[1])]
        + into_rows([loss.at[theirs, :]], out, 0, rows)
        + into_rows(history_rows(*history, s, theirs), out, 3 * rows, rows)
        + [(loss.at[mine, :], own_loss), (carrier.at[mine, :], own_carrier)]
        + [(grating.at[mine, :], own_grating)]
        + into_rows(history_rows(*history, s, mine), own, 0, rows)
        + [
            (part, ends.at[k, i])
            for k in range(2)
            for i, part in enumerate(
                history_rows(*history, 1, pl.ds(k * (2 * rows - TILE), TILE))
            )
        ],
        sems,
    )
    for copy in copies[:2]:
        copy.wait()
    sizes = []
    for i in range(2):
        size = size_of(jnp.abs(states[i]))
        sizes.append(jnp.broadcast_to(size, (1, columns)))
        out[(1 + i) * rows : (2 + i) * rows, :] = encoded(states[i], size)
    for copy in copies[2:]:
        copy.wait()
    low = info[4] == 0
    top = [ends[0, i].astype(jnp.float32)[:1] for i in range(6)]
    foot = [ends[1, i].astype(jnp.float32)[TILE - 1 :] for i in range(6)]
    own_edge[...] = jnp.concatenate([jnp.where(low, a, b) for a, b in zip(top, foot)])
    sizes += [jnp.where(low, b, a) for a, b in zip(top, foot)]
    sizes.append(jnp.zeros((TILE - 8, columns), jnp.float32))
    out[9 * rows :, :] = jnp.concatenate(sizes).astype(jnp.bfloat16)


def enter_kernel(
    info, forward, backward, other, source, tp, tq, inner, outer, field, work, matrices, sem, sems
):
    rows, width = field.shape[1] // 2, field.shape[2]
    columns = width // 2
    half = columns // LANES
    at = rows_of(info, rows, False)
    copies = fetch(
        [
            (ref.at[:, at, :], field.at[:, f * rows : (f + 1) * rows, :columns])
            for f, ref in enumerate((forward, backward))
        ],
        sems,
    )
    matrix_copies = fetch_matrices(source, matrices, sem)
    sizes = sizes_in(other[4 * half * rows :, :], 2)
    for f in range(2):
        for part in range(2):

            @pl.loop(0, half, unroll=2)
            def _(j):
                code = other[slab((2 * f + part) * half + j, rows), :]
                field[part, f * rows : (f + 1) * rows, lane(half + j)] = decoded(code, sizes[f])

    for held in copies:
        held.wait()
    filtered(field, work, matrices, matrix_copies)
    write_filtered(info, work, tp, tq, inner, outer)


def rows_update(
    info, tp, tq, inner, outer, carrier, grating, own, other, own_loss, other_loss,
    field, new_carrier, new_grating, sums_in, sums, cells, last
):
    rows, width = carrier.shape
    half = width // LANES // 2
    columns = half * LANES
    mid = jnp.where(info[0] == 0, 1.0, 0.0)
    wrap = 1.0 - mid
    low = info[4] == 0
    is_first, is_last = info[1], info[2]
    row_index = lax.broadcasted_iota(jnp.int32, (TILE, LANES), 0)
    zero = jnp.zeros((8, LANES), jnp.float32)

    def step(jj, most):
        for side in range(2):
            j = jj + side * half
            here = lane(j)
            left_at = lane(jnp.where(j == 0, 2 * half - 1, j - 1))
            right_at = lane(jnp.where(j == 2 * half - 1, 0, j + 1))
            swapped = lane(jj + (1 - side) * half)
            weight_left = jnp.where(jj == 0, wrap if side == 0 else mid, 1.0)
            weight_right = jnp.where(jj == half - 1, mid if side == 0 else wrap, 1.0)
            total = zero
            for r in range(0, rows, TILE):
                at = slice(r, r + TILE)

                held, begin = (own, other)[side]

                def part_of(i):
                    tile = begin + i * rows + r
                    return held[tile : tile + TILE, lane(jj)].astype(jnp.float32)

                loss = (own_loss, other_loss)[side][at, lane(jj)].astype(jnp.float32)
                f = [tp[part, r + 1 : r + 1 + TILE, here] for part in range(2)]
                b = [tq[part, r + 7 : r + 7 + TILE, here] for part in range(2)]
                if r + TILE == rows:
                    for part in range(2):
                        facet = FRONT_FACET * tq[part, rows + 7 : rows + 8, here]
                        edge = jnp.where(
                            low, inner[part : part + 1, swapped], outer[part : part + 1, here]
                        )
                        edge = jnp.where(is_last, facet, edge)
                        f[part] = jnp.where(row_index == TILE - 1, edge, f[part])
                if r == 0:
                    for part in range(2):
                        facet = REAR_FACET * tp[part, 0:1, here]
                        edge = jnp.where(
                            low, outer[part : part + 1, here], inner[part : part + 1, swapped]
                        )
                        edge = jnp.where(is_first, facet, edge)
                        b[part] = jnp.where(row_index == 0, edge, b[part])
                c = carrier[at, here]
                lap = curvature(
                    carrier[at, left_at], c, carrier[at, right_at], weight_left, weight_right
                )
                out = updated(
                    *f, *b, [part_of(i) for i in range(4)], part_of(4), part_of(5), loss,
                    c, grating[at, here], lap,
                )
                field[0, r : r + TILE, here] = out[0]
                field[1, r : r + TILE, here] = out[1]
                field[0, rows + r : rows + r + TILE, here] = out[2]
                field[1, rows + r : rows + r + TILE, here] = out[3]
                new_carrier[at, here] = out[4]
                new_grating[at, here] = out[5]
                z = (info[3] + r + row_index).astype(jnp.float32)
                weighted = (1.0 + 2.0 * z / (cells - 1)) * ((c + out[4]) if last else c)
                for k in range(0, TILE, 8):
                    total = total + weighted[k : k + 8]
                if last and side == 1:
                    for k in range(0, TILE, 8):
                        most = (
                            jnp.maximum(most[0], jnp.abs(out[4][k : k + 8])),
                            jnp.maximum(most[1], jnp.abs(out[5][k : k + 8])),
                        )
            summed = jnp.sum(total, axis=0, keepdims=True)
            sums[:, here] = summed if sums_in is None else summed + sums_in[:, here]
        return most

    return lax.fori_loop(0, half, step, (zero, zero))


def first_step_kernel(
    cells, info, tp, tq, inner, outer, my_carrier, my_grating, loss, own, own_edge, other, source,
    new_tp, new_tq, new_inner, new_outer, new_carrier, new_grating, sums,
    carrier, grating, field, work, matrices, sem,
):
    matrix_copies = fetch_matrices(source, matrices, sem)
    rows, columns = my_carrier.shape
    half = columns // LANES
    extra = other[9 * rows :, :].astype(jnp.float32)
    sizes = [extra[0:1, 0:1], extra[1:2, 0:1]]
    new_outer[2:8, :columns] = own_edge[...]
    new_outer[2:8, columns:] = extra[2:8]
    for i, (whole, mine) in enumerate(((carrier, my_carrier), (grating, my_grating))):
        whole[:, :columns] = mine[...]

        @pl.loop(0, half, unroll=2)
        def _(j):
            whole[:, lane(half + j)] = decoded(
                other[(1 + i) * rows : (2 + i) * rows, lane(j)], sizes[i]
            )

    rows_update(
        info, tp, tq, inner, outer, carrier, grating, (own, 0), (other, 3 * rows), loss, other,
        field, new_carrier, new_grating, None, sums, cells, False,
    )
    filtered(field, work, matrices, matrix_copies)
    write_filtered(info, work, new_tp, new_tq, new_inner, new_outer)


def middle_step_kernel(
    cells, info, tp, tq, inner, outer, carrier, grating, loss, own, other, other_loss, sums_in,
    source, new_tp, new_tq, new_inner, new_outer, new_carrier, new_grating, sums,
    field, work, matrices, sem,
):
    matrix_copies = fetch_matrices(source, matrices, sem)
    rows_update(
        info, tp, tq, inner, outer, carrier, grating, (own, 0), (other, 0), loss, other_loss,
        field, new_carrier, new_grating, sums_in, sums, cells, False,
    )
    filtered(field, work, matrices, matrix_copies)
    write_filtered(info, work, new_tp, new_tq, new_inner, new_outer)
    rows = carrier.shape[0]
    low = info[4] == 0
    for part in range(2):
        new_outer[2 + part : 3 + part, :] = jnp.where(
            low, new_tp[part, 1:2, :], new_tq[part, rows + 6 : rows + 7, :]
        )
    for i, ref in enumerate((new_carrier, new_grating)):
        new_outer[4 + i : 5 + i, :] = jnp.where(low, ref[0:1, :], ref[rows - 1 : rows, :])
    columns = loss.shape[1]
    for part, ref in enumerate((loss, other_loss)):
        top = ref[:TILE, :].astype(jnp.float32)[:1]
        foot = ref[rows - TILE :, :].astype(jnp.float32)[TILE - 1 :]
        new_outer[6:7, part * columns : (part + 1) * columns] = jnp.where(low, top, foot)


def row_beyond(info, tp, tq, outer, beyond):
    rows = tp.shape[1] - 8
    low = info[4] == 0
    xr, xi, carrier, grating = (outer[i : i + 1, :] for i in range(2, 6))
    yr, yi = (
        jnp.where(low, tp[part, 0:1, :], tq[part, rows + 7 : rows + 8, :]) for part in range(2)
    )
    rr, ri, lr, li, population, hole = (beyond[i : i + 1, :] for i in range(2, 8))
    loss = outer[6:7, :]
    surplus = population - 1.0
    gain_re = 1.0 + 0.5 * (GAIN_SLOPE_RATE * surplus - loss)
    gain_im = (0.5 * GAIN_SLOPE_RATE * ALPHA_LINEWIDTH) * surplus
    joined = COUPLING * hole
    drive = (2.0 * CLOCK_DELTA * GAIN_SLOPE_RATE) * surplus * carrier
    mix = (2.0 * CLOCK_DELTA) * grating
    near_re, near_im = jnp.where(low, lr, rr), jnp.where(low, li, ri)
    far_re, far_im = jnp.where(low, rr, lr), jnp.where(low, ri, li)
    new_re = gain_re * xr - gain_im * xi + joined * yi - drive * near_re + mix * far_re
    new_im = gain_re * xi + gain_im * xr - joined * yr - drive * near_im + mix * far_im
    return new_re, new_im


def leave_kernel(
    cells, info, tp, tq, inner, outer, beyond, carrier, grating, loss, own, other, other_loss,
    sums_in, source, kept, kept_carrier, kept_grating, sides, sent, edge, shares,
    sums, new_carrier, new_grating, field, work, matrices, sem,
):
    matrix_copies = fetch_matrices(source, matrices, sem)
    rows, width = carrier.shape
    columns = width // 2
    half = columns // LANES
    most = rows_update(
        info, tp, tq, inner, outer, carrier, grating, (own, 0), (other, 0), loss, other_loss,
        field, new_carrier, new_grating, sums_in, sums, cells, True,
    )
    mid = jnp.where(info[0] == 0, 1.0, 0.0)
    wrap = 1.0 - mid
    kept_carrier[...] = new_carrier[:, :columns]
    kept_grating[...] = new_grating[:, :columns]
    first, before = new_carrier[:, 0:1] * wrap, new_carrier[:, columns - 1 : columns] * mid
    after, final = new_carrier[:, columns : columns + 1] * mid, new_carrier[:, width - 1 :] * wrap
    sides[0] = jnp.broadcast_to(final, (rows, LANES))
    sides[1] = jnp.broadcast_to(after, (rows, LANES))
    pairs = []
    for at, value in ((0, before), (2, first)):
        coarse = value.astype(jnp.bfloat16).astype(jnp.float32)
        pairs += [(at, coarse), (at + 1, value - coarse)]
    for i, field_of in enumerate((new_carrier, new_grating)):
        size = size_of(most[i])
        pairs.append((SCALE_LANE + 2 + i, size))

        @pl.loop(0, half, unroll=2)
        def _(j):
            sent[slab((4 + i) * half + j, rows), :] = encoded(field_of[:, lane(half + j)], size)

    for part, value in enumerate(row_beyond(info, tp, tq, outer, beyond)):
        field[part, 2 * rows :, :] = jnp.broadcast_to(value, (8, width))
    filtered(field, work, matrices, matrix_copies)
    zero = jnp.zeros((8, LANES), jnp.float32)
    for f in range(2):

        def unmix(g, most):
            at = pl.ds(pl.multiple_of(g * 8 + f * rows, 8), 8)
            for j, pair in enumerate(gathered(work, at)):
                for part in range(2):
                    if j < half:
                        kept[part, at, j * LANES : (j + 1) * LANES] = pair[part]
                    else:
                        work[j, at, part * LANES : (part + 1) * LANES] = pair[part]
                        most = jnp.maximum(most, jnp.abs(pair[part]))
            return most

        size = size_of(lax.fori_loop(0, rows // 8, unmix, zero))
        pairs.append((SCALE_LANE + f, size))

        @pl.loop(0, half, unroll=2)
        def _(j):
            for part in range(2):
                value = work[half + j, f * rows : (f + 1) * rows, part * LANES : (part + 1) * LANES]
                sent[slab((2 * f + part) * half + j, rows), :] = encoded(value, size)

    ends = gathered(work, slice(2 * rows, 2 * rows + 8))
    for part in range(2):
        for j in range(half):
            edge[part : part + 1, j * LANES : (j + 1) * LANES] = ends[j][part][:1]
    far = jnp.concatenate([ends[j][part][:1] for part in range(2) for j in range(half, 2 * half)])
    size = size_of(jnp.abs(far))
    pairs.append((SCALE_LANE + 4, size))
    sent[6 * half * rows : (6 * half + 1) * rows, :] = side_tile(pairs, rows)
    spare = jnp.zeros((rows - 2 * half, LANES), jnp.float32)
    sent[(6 * half + 1) * rows :, :] = encoded(jnp.concatenate([far, spare]), size)
    tile = jnp.concatenate([sums[:, j * LANES : (j + 1) * LANES] for j in range(2 * half)])
    near, far = tile[:half], tile[half:]
    first = info[0] == 0
    to_first, to_second = jnp.where(first, near, far), jnp.where(first, far, near)
    shares[0] = to_first
    shares[1] = to_second


def spread_kernel(info, shares, out):
    for i in range(out.shape[0]):
        out[i] = shares[i % 2]


def total_kernel(cells, info, partial, out):
    total = partial[0]
    for i in range(1, partial.shape[0]):
        total = total + partial[i]
    out[...] = total * (CLOCK_DELTA / math.sqrt(cells))


def final_kernel(
    info, kept, kept_carrier, kept_grating, sides, came, edge, loss, history,
    out_forward, out_backward, out_carrier, out_grating,
    tp, tq, carrier, grating,
):
    rows, columns = kept_carrier.shape
    half = columns // LANES
    mine = info[4] * rows
    theirs = (1 - info[4]) * rows
    low = info[4] == 0
    extra = came[6 * half * rows : (6 * half + 1) * rows, :]
    size_forward, size_backward, size_carrier, size_grating, size_edge = sizes_in(extra, 5)
    ends = decoded(came[(6 * half + 1) * rows :, :], size_edge)
    extra = extra.astype(jnp.float32)

    def at(start, offset, count):
        return pl.ds(pl.multiple_of(start + offset, 8), count)

    for part in range(2):
        tp[part, at(mine, 0, rows), :] = kept[part, :rows, :]
        tq[part, at(mine, 8, rows), :] = kept[part, rows:, :]
    carrier[at(mine, 0, rows), LANES : LANES + columns] = kept_carrier[...]
    carrier[at(mine, 0, rows), :LANES] = sides[0]
    carrier[at(mine, 0, rows), LANES + columns :] = sides[1]
    carrier[at(theirs, 0, rows), :LANES] = jnp.broadcast_to(
        extra[:, 0:1] + extra[:, 1:2], (rows, LANES)
    )
    carrier[at(theirs, 0, rows), LANES + columns :] = jnp.broadcast_to(
        extra[:, 2:3] + extra[:, 3:4], (rows, LANES)
    )
    grating[at(mine, 0, rows), :] = kept_grating[...]

    @pl.loop(0, half, unroll=2)
    def _(j):
        carrier[at(theirs, 0, rows), lane(1 + j)] = decoded(
            came[slab(4 * half + j, rows), :], size_carrier
        )
        grating[at(theirs, 0, rows), lane(j)] = decoded(
            came[slab(5 * half + j, rows), :], size_grating
        )
        for part in range(2):
            tp[part, at(theirs, 0, rows), lane(j)] = decoded(
                came[slab(part * half + j, rows), :], size_forward
            )
            tq[part, at(theirs, 8, rows), lane(j)] = decoded(
                came[slab((2 + part) * half + j, rows), :], size_backward
            )

    all_rows = 2 * rows
    for part in range(2):
        near = edge[part : part + 1, :]
        far = jnp.concatenate([ends[part * half + j : part * half + j + 1] for j in range(half)], axis=1)
        next_edge = jnp.where(low, far, near)
        before_edge = jnp.where(low, near, far)
        front = FRONT_FACET * tq[part, all_rows + 7 : all_rows + 8, :]
        rear = REAR_FACET * tp[part, 0:1, :]
        tp[part, all_rows : all_rows + 1, :] = jnp.where(info[2], front, next_edge)
        tq[part, 7:8, :] = jnp.where(info[1], rear, before_edge)

    @pl.loop(0, half)
    def _(j):
        here = lane(j)
        for r in range(0, all_rows, TILE):
            row = slice(r, r + TILE)
            c = carrier[row, lane(j + 1)]
            lap = curvature(carrier[row, lane(j)], c, carrier[row, lane(j + 2)], 1.0, 1.0)
            parts = [
                history[i * all_rows + r : i * all_rows + r + TILE, here].astype(jnp.float32)
                for i in range(6)
            ]
            out = updated(
                tp[0, r + 1 : r + 1 + TILE, here], tp[1, r + 1 : r + 1 + TILE, here],
                tq[0, r + 7 : r + 7 + TILE, here], tq[1, r + 7 : r + 7 + TILE, here],
                parts[:4], parts[4], parts[5],
                loss[row, here].astype(jnp.float32), c, grating[row, here], lap,
            )
            out_forward[0, row, here] = out[0]
            out_forward[1, row, here] = out[1]
            out_backward[0, row, here] = out[2]
            out_backward[1, row, here] = out[3]
            out_carrier[row, here] = out[4]
            out_grating[row, here] = out[5]


def position(rows, whole):
    x, block, count = lax.axis_index("gx"), lax.axis_index("gz"), lax.axis_size("gz")
    high = lax.rem(x + block, 2)
    if whole:
        return x, block == 0, block == count - 1, block * rows, high
    place = 2 * block + high
    return x, place == 0, place == 2 * count - 1, place * rows, high


def whole_spec(shape):
    return pl.BlockSpec(shape, lambda i, n=len(shape): (0,) * n)


def call(name, kernel, rows, inputs, outputs, scratch, flops=0, grant=24, whole=False):
    arrays = [x[0] if isinstance(x, tuple) else x for x in inputs]
    specs = [x[1] if isinstance(x, tuple) else whole_spec(x.shape) for x in inputs]
    shapes = [jax.ShapeDtypeStruct(*out) for out in outputs]
    moved = sum(math.prod(s.shape) * s.dtype.itemsize for s in shapes)

    def body(*refs):
        kernel(position(rows, whole), *refs)

    return pl.pallas_call(
        body,
        grid=(1,),
        in_specs=specs,
        out_specs=[whole_spec(s.shape) for s in shapes],
        scratch_shapes=scratch,
        out_shape=shapes,
        compiler_params=pltpu.CompilerParams(vmem_limit_bytes=grant * 1024 * 1024),
        cost_estimate=pl.CostEstimate(
            flops=flops, bytes_accessed=moved + 4 * 1024 * 1024, transcendentals=0
        ),
        name=name,
    )(*arrays)


def per_pair(
    ending_rightward_adjoint,
    ending_leftward_adjoint,
    ending_population_adjoint,
    ending_holeburn_adjoint,
    history_rightward,
    history_leftward,
    history_population,
    history_holeburn,
    segment_passive_attenuation,
):
    cell_rows, columns = ending_population_adjoint.shape
    passes = history_population.shape[0]
    rows = cell_rows // 2
    half = columns // LANES
    blocks = 2 * half
    width = 2 * columns
    count = lax.axis_size("gz")
    cells = cell_rows * count
    x = lax.axis_index("gx")
    f32, bf16 = jnp.float32, jnp.bfloat16
    swap = [(0, 1), (1, 0)]
    in_place = pl.BlockSpec(memory_space=pltpu.HBM)

    def held(*arrays):
        return [(a, in_place) for a in arrays]

    def tiles(n):
        return ((n * rows, LANES), bf16)

    ends = held(ending_rightward_adjoint, ending_leftward_adjoint)
    planes = held(ending_population_adjoint, ending_holeburn_adjoint)
    history = held(history_rightward, history_leftward, history_population, history_holeburn)
    losses = held(segment_passive_attenuation)
    matrices = pltpu.with_memory_space_constraint(
        jnp.asarray(lateral_matrices(width, blocks)), pltpu.HBM
    )
    matrix_input = held(matrices)
    work = [
        pltpu.VMEM((blocks, 2 * rows, 2 * LANES), f32),
        pltpu.VMEM(matrices.shape, bf16),
        pltpu.SemaphoreType.DMA((2,)),
    ]
    field_scratch = pltpu.VMEM((2, 2 * rows, width), f32)
    def state_out(outer_rows):
        state = ((2, rows + 8, width), f32)
        return [state, state, ((2, width), f32), ((outer_rows, width), f32)]

    plane = ((rows, width), f32)
    plane_scratch = pltpu.VMEM((rows, width), f32)
    half_plane = ((rows, columns), f32)
    work_flops = 2 * 3 * 2 * rows * blocks * (2 * LANES) ** 2

    (coded,) = call(
        "send_fields", send_fields_kernel, rows, ends, [tiles(4 * half + 1)],
        [pltpu.VMEM((2, 2, rows, columns), f32), pltpu.SemaphoreType.DMA((2,))], grant=62,
    )
    other_fields = lax.ppermute(coded, "gx", swap)
    loss, own_first, my_carrier, my_grating, sent_first, own_edge = call(
        "send_first", functools.partial(send_first_kernel, passes - 1), rows,
        [*losses, *planes, *history],
        [((rows, columns), bf16), ((6 * rows, columns), bf16), half_plane, half_plane,
         ((9 * rows + TILE, columns), bf16), ((6, columns), f32)],
        [pltpu.VMEM((2, rows, columns), f32), pltpu.VMEM((2, 6, TILE, columns), bf16),
         pltpu.SemaphoreType.DMA((30,))], grant=62,
    )
    steps = range(passes - 2, 0, -1)
    history_last, *later = call(
        "send_later", functools.partial(send_later_kernel, steps), rows, history,
        [((6 * cell_rows, columns), bf16)] + [((6 * rows, columns), bf16)] * (2 * len(steps)),
        [pltpu.SemaphoreType.DMA((12 * len(steps) + 6,))], grant=62,
    )
    sent_first, history_last, later, other_fields = lax.optimization_barrier(
        (sent_first, history_last, later, other_fields)
    )
    other_first = lax.ppermute(sent_first, "gx", swap)

    line = ("gz", "gx")
    neighbours = []
    for b in range(count - 1):
        top = (1 + b) % 2
        neighbours += [(2 * b + top, 2 * b + 2 + top), (2 * b + 2 + top, 2 * b + top)]

    def edges(inner, outer):
        outer = lax.ppermute(outer, line, neighbours)
        return lax.ppermute(inner, "gx", swap), outer

    tp, tq, inner, outer = call(
        "enter", enter_kernel, rows, [*ends, other_fields, *matrix_input],
        state_out(2), [field_scratch, *work, pltpu.SemaphoreType.DMA((2,))], work_flops,
    )
    inner, outer = edges(inner, outer)

    other_loss = (other_first, pl.BlockSpec((rows, columns), lambda i: (0, 0)))
    carrier = grating = sums = other = own = None
    for index, s in enumerate(range(passes - 1, 0, -1)):
        if index < len(steps):
            sent, own_next = later[2 * index : 2 * index + 2]
            if index == 0:
                sent, outer = lax.optimization_barrier((sent, outer))
            else:
                sent, inner, outer = lax.optimization_barrier((sent, inner, outer))
            coming = lax.ppermute(sent, "gx", swap)
        shared = [tp, tq, inner, outer]
        if index == 0:
            tp, tq, inner, outer, carrier, grating, sums = call(
                "first_step", functools.partial(first_step_kernel, cells), rows,
                [*shared, my_carrier, my_grating, loss, own_first, own_edge, other_first,
                 *matrix_input],
                [*state_out(8), plane, plane, ((1, width), f32)],
                [plane_scratch, plane_scratch, field_scratch, *work], work_flops,
            )
        elif s > 1:
            tp, tq, inner, outer, carrier, grating, sums = call(
                "middle_step", functools.partial(middle_step_kernel, cells), rows,
                [*shared, carrier, grating, loss, own, other, other_loss, sums, *matrix_input],
                [*state_out(7), plane, plane, ((1, width), f32)],
                [field_scratch, *work], work_flops,
            )
        else:
            kept, kept_carrier, kept_grating, sides, sent, edge, shares = call(
                "leave", functools.partial(leave_kernel, cells), rows,
                [*shared, beyond, carrier, grating, loss, own, other, other_loss, sums, *matrix_input],
                [((2, 2 * rows, columns), f32), half_plane, half_plane, ((2, rows, LANES), f32),
                 tiles(6 * half + 2), ((2, columns), f32), ((2, half, LANES), f32)],
                [pltpu.VMEM((1, width), f32), plane_scratch, plane_scratch,
                 pltpu.VMEM((2, 2 * rows + 8, width), f32),
                 pltpu.VMEM((blocks, 2 * rows + TILE, 2 * LANES), f32), *work[1:]],
                work_flops,
            )
        if s > 1:
            inner, outer = edges(inner, outer)
            own, other = own_next, coming
            if index == 0:
                beyond = outer

    came = lax.ppermute(sent, "gx", swap)
    (shares,) = call(
        "spread", spread_kernel, rows, [shares], [((2 * count, half, LANES), f32)], [],
    )
    shares = lax.all_to_all(shares, line, 0, 0, tiled=True)

    outs = call(
        "final", final_kernel, cell_rows,
        [kept, kept_carrier, kept_grating, sides, came, edge,
         segment_passive_attenuation, history_last],
        [((2, cell_rows, columns), f32), ((2, cell_rows, columns), f32),
         ((cell_rows, columns), f32), ((cell_rows, columns), f32)],
        [pltpu.VMEM((2, cell_rows + 8, columns), f32), pltpu.VMEM((2, cell_rows + 8, columns), f32),
         pltpu.VMEM((cell_rows, columns + 2 * LANES), f32), pltpu.VMEM((cell_rows, columns), f32)],
        whole=True,
    )
    shares, *outs = lax.optimization_barrier((shares, *outs))
    (total,) = call(
        "total", functools.partial(total_kernel, cells), rows, [shares], [((half, LANES), f32)], [],
    )
    return (*outs, total.reshape(columns))


def shared_by_pairs(mesh, arguments):
    population = arguments[6]
    passes, cells, width = population.shape
    rows, columns = cells // mesh.shape["gz"], width // mesh.shape["gx"]
    return (
        mesh.shape["gx"] == 2
        and passes >= 4
        and 4 * columns <= rows * LANES
        and rows % (2 * TILE) == 0
        and columns % LANES == 0
        and (columns // LANES) & (columns // LANES - 1) == 0
        and width <= 4096
    )


def solution(mesh):
    def run(*arguments):
        body = per_pair if shared_by_pairs(mesh, arguments) else per_device
        return jax.shard_map(
            body,
            mesh=mesh,
            in_specs=(
                P(None, "gz", "gx"),
                P(None, "gz", "gx"),
                P("gz", "gx"),
                P("gz", "gx"),
                P(None, None, "gz", "gx"),
                P(None, None, "gz", "gx"),
                P(None, "gz", "gx"),
                P(None, "gz", "gx"),
                P("gz", "gx"),
            ),
            out_specs=(
                P(None, "gz", "gx"), P(None, "gz", "gx"), P("gz", "gx"), P("gz", "gx"), P("gx"),
            ),
            check_vma=False,
        )(*arguments)

    return run
```

```python
import functools
import math

import jax
import jax.numpy as jnp
import ml_dtypes
import numpy as np
from jax import lax
from jax.experimental import pallas as pl
from jax.experimental.pallas import tpu as pltpu
from jax.sharding import PartitionSpec as P

DIFF = 512


FRONT_FACET = 0.3
REAR_FACET = 0.9
GAIN_SLOPE_RATE = 0.3
ALPHA_LINEWIDTH = 2.0
COUPLING = 0.5
CLOCK_DELTA = 0.3
DENSITY_LIFETIME = 2.0
GRATING_LIFE = 0.75
TRANSVERSE_DIFFUS = 0.2


def passed_along(value, axis, steps):
    count = lax.axis_size(axis)
    initial, last = (max(0, -steps), min(count, count - steps))
    return lax.ppermute(value, axis, [(source, source + steps) for source in range(initial, last)])


def with_halo(block, sides, width):
    for axis, dim in sides:
        count = lax.axis_size(axis)
        forward = [(i, i + 1) for i in range(count - 1)]
        backward = [(target, source) for source, target in forward]
        low = lax.ppermute(
            lax.slice_in_dim(block, block.shape[dim] - width, None, axis=dim), axis, forward
        )
        high = lax.ppermute(lax.slice_in_dim(block, 0, width, axis=dim), axis, backward)
        block = jnp.concatenate([low, block, high], axis=dim)
    return block


def rotate(source_re, source_im, cosine, sine, form, sign):
    exact = lax.Precision.HIGHEST
    out_re = jnp.einsum(form, source_re, cosine, precision=exact) + sign * jnp.einsum(
        form, source_im, sine, precision=exact
    )
    out_im = jnp.einsum(form, source_im, cosine, precision=exact) - sign * jnp.einsum(
        form, source_re, sine, precision=exact
    )
    return (out_re, out_im)


def transform(stacked):
    count = stacked.shape[1]
    width = stacked.shape[2]
    second = min(128, width // 2)
    first = width // second
    two_pi = 2.0 * math.pi
    index_a = jnp.arange(first, dtype=jnp.int32)
    index_b = jnp.arange(second, dtype=jnp.int32)
    angle_a = two_pi * (index_a[:, None] * index_a[None, :] % first).astype(jnp.float32) / first
    angle_b = two_pi * (index_b[:, None] * index_b[None, :] % second).astype(jnp.float32) / second
    angle_t = two_pi * (index_a[:, None] * index_b[None, :] % width).astype(jnp.float32) / width
    cos_a, sin_a = (jnp.cos(angle_a), jnp.sin(angle_a))
    cos_b, sin_b = (jnp.cos(angle_b), jnp.sin(angle_b))
    cos_t, sin_t = (jnp.cos(angle_t), jnp.sin(angle_t))
    wavenum = index_a[:, None] + first * index_b[None, :]
    signed = jnp.where(wavenum < width // 2, wavenum, wavenum - width)
    phase = (signed * signed).astype(jnp.float32) * (DIFF / (width / 2) ** 2)
    cos_p, sin_p = (jnp.cos(phase), jnp.sin(phase))
    real_in = stacked[0].reshape(count, first, second)
    imag_in = stacked[1].reshape(count, first, second)
    step_re, step_im = rotate(real_in, imag_in, cos_a, sin_a, "nab,ak->nkb", 1.0)
    twist_re = step_re * cos_t + step_im * sin_t
    twist_im = step_im * cos_t - step_re * sin_t
    spec_re, spec_im = rotate(twist_re, twist_im, cos_b, sin_b, "nkb,bj->nkj", 1.0)
    moved_re = spec_re * cos_p - spec_im * sin_p
    moved_im = spec_re * sin_p + spec_im * cos_p
    back_re, back_im = rotate(moved_re, moved_im, cos_b, sin_b, "nkj,jb->nkb", -1.0)
    untw_re = back_re * cos_t - back_im * sin_t
    untw_im = back_im * cos_t + back_re * sin_t
    final_re, final_im = rotate(untw_re, untw_im, cos_a, sin_a, "nkb,ka->nab", -1.0)
    return jnp.stack([final_re.reshape(count, width), final_im.reshape(count, width)]) / width


def added_up(value, axis):
    count = lax.axis_size(axis)
    if count & (count - 1):
        return lax.psum(value, axis)
    reach = 1
    while reach < count:
        value = value + lax.ppermute(value, axis, [(i, i ^ reach) for i in range(count)])
        reach *= 2
    return value


def lateral_work(parts):
    return (transform(parts[0]), transform(parts[1]))


def multiplier_revision(
    population_multiplier,
    holeburn_multiplier,
    measured_rightward,
    measured_leftward,
    rightward_wave,
    leftward_wave,
    population_level,
    holeburn_magnitude,
    attenuation_factor,
    transverse_curvature,
):
    rightward_inphase, rightward_quadrature = (rightward_wave[0], rightward_wave[1])
    leftward_inphase, leftward_quadrature = (leftward_wave[0], leftward_wave[1])
    measured_rightward_inphase, measured_rightward_quadrature = (
        measured_rightward[0],
        measured_rightward[1],
    )
    measured_leftward_inphase, measured_leftward_quadrature = (
        measured_leftward[0],
        measured_leftward[1],
    )
    surplus_population = population_level - 1.0
    amplification_inphase = 1.0 + 0.5 * (GAIN_SLOPE_RATE * surplus_population - attenuation_factor)
    amplification_quadrature = 0.5 * GAIN_SLOPE_RATE * ALPHA_LINEWIDTH * surplus_population
    joined_waves = COUPLING * holeburn_magnitude
    population_derivative = (
        2.0 * CLOCK_DELTA * GAIN_SLOPE_RATE * surplus_population * population_multiplier
    )
    holeburn_derivative = 2.0 * CLOCK_DELTA * holeburn_multiplier
    revised_rightward_inphase = (
        amplification_inphase * measured_rightward_inphase
        - amplification_quadrature * measured_rightward_quadrature
        + joined_waves * measured_leftward_quadrature
        - population_derivative * rightward_inphase
        + holeburn_derivative * leftward_inphase
    )
    revised_rightward_quadrature = (
        amplification_inphase * measured_rightward_quadrature
        + amplification_quadrature * measured_rightward_inphase
        - joined_waves * measured_leftward_inphase
        - population_derivative * rightward_quadrature
        + holeburn_derivative * leftward_quadrature
    )
    revised_leftward_inphase = (
        amplification_inphase * measured_leftward_inphase
        - amplification_quadrature * measured_leftward_quadrature
        + joined_waves * measured_rightward_quadrature
        - population_derivative * leftward_inphase
        + holeburn_derivative * rightward_inphase
    )
    revised_leftward_quadrature = (
        amplification_inphase * measured_leftward_quadrature
        + amplification_quadrature * measured_leftward_inphase
        - joined_waves * measured_rightward_inphase
        - population_derivative * leftward_quadrature
        + holeburn_derivative * rightward_quadrature
    )
    light_intensity = (
        rightward_inphase * rightward_inphase
        + rightward_quadrature * rightward_quadrature
        + leftward_inphase * leftward_inphase
        + leftward_quadrature * leftward_quadrature
    )
    amplification_share = (
        measured_rightward_inphase * (rightward_inphase + ALPHA_LINEWIDTH * rightward_quadrature)
        + measured_rightward_quadrature
        * (rightward_quadrature - ALPHA_LINEWIDTH * rightward_inphase)
        + measured_leftward_inphase * (leftward_inphase + ALPHA_LINEWIDTH * leftward_quadrature)
        + measured_leftward_quadrature * (leftward_quadrature - ALPHA_LINEWIDTH * leftward_inphase)
    )
    revised_population = (
        population_multiplier
        * (1.0 - CLOCK_DELTA / DENSITY_LIFETIME - CLOCK_DELTA * GAIN_SLOPE_RATE * light_intensity)
        + TRANSVERSE_DIFFUS * transverse_curvature
        + 0.5 * GAIN_SLOPE_RATE * amplification_share
    )
    fresh_holeburn = holeburn_multiplier * (1.0 - CLOCK_DELTA / GRATING_LIFE) + COUPLING * (
        measured_rightward_quadrature * leftward_inphase
        - measured_rightward_inphase * leftward_quadrature
        + measured_leftward_quadrature * rightward_inphase
        - measured_leftward_inphase * rightward_quadrature
    )
    return (
        jnp.stack([revised_rightward_inphase, revised_rightward_quadrature]),
        jnp.stack([revised_leftward_inphase, revised_leftward_quadrature]),
        revised_population,
        fresh_holeburn,
    )


def per_device(
    ending_rightward_adjoint,
    ending_leftward_adjoint,
    ending_population_adjoint,
    ending_holeburn_adjoint,
    history_rightward,
    history_leftward,
    history_population,
    history_holeburn,
    segment_passive_attenuation,
):
    columns = ending_rightward_adjoint.shape[2]
    rows = ending_rightward_adjoint.shape[1]
    blocks = lax.axis_size("gz")
    position = lax.axis_index("gz")
    cells = rows * blocks
    zpos = (position * rows + jnp.arange(rows, dtype=jnp.int32)).astype(jnp.float32)
    scaling_factor = 1.0 + 2.0 * zpos / (cells - 1)
    rightward_multiplier, leftward_multiplier = (ending_rightward_adjoint, ending_leftward_adjoint)
    population_multiplier, holeburn_multiplier = (
        ending_population_adjoint,
        ending_holeburn_adjoint,
    )
    attenuation_factor = segment_passive_attenuation.astype(jnp.float32)
    shape_curve = jnp.zeros((columns,), jnp.float32)
    for moment_position in range(history_rightward.shape[0] - 1, -1, -1):
        shape_curve = shape_curve + jnp.sum(scaling_factor[:, None] * population_multiplier, axis=0)
        above = passed_along(rightward_multiplier[:, :1, :], "gz", -1)
        below = passed_along(leftward_multiplier[:, -1:, :], "gz", 1)
        top_row = jnp.where(
            position == blocks - 1, FRONT_FACET * leftward_multiplier[:, -1:, :], above
        )
        bottom_row = jnp.where(position == 0, REAR_FACET * rightward_multiplier[:, :1, :], below)
        lam_fwd = jnp.concatenate([rightward_multiplier[:, 1:, :], top_row], axis=1)
        lam_bwd = jnp.concatenate([bottom_row, leftward_multiplier[:, :-1, :]], axis=1)
        whole_fwd, whole_bwd = (
            lax.all_gather(lam_fwd, "gx", axis=2, tiled=True),
            lax.all_gather(lam_bwd, "gx", axis=2, tiled=True),
        )
        start = lax.axis_index("gx") * columns
        done_fwd, done_bwd = lateral_work((whole_fwd, whole_bwd))
        measured_rightward = lax.dynamic_slice_in_dim(done_fwd, start, columns, 2)
        measured_leftward = lax.dynamic_slice_in_dim(done_bwd, start, columns, 2)
        bordered_array = with_halo(population_multiplier, (("gx", 1),), 1)
        transverse_curvature = (
            bordered_array[:, 2:] + bordered_array[:, :-2] - 2.0 * population_multiplier
        )
        rightward_multiplier, leftward_multiplier, population_multiplier, holeburn_multiplier = (
            multiplier_revision(
                population_multiplier,
                holeburn_multiplier,
                measured_rightward,
                measured_leftward,
                history_rightward[moment_position].astype(jnp.float32),
                history_leftward[moment_position].astype(jnp.float32),
                history_population[moment_position].astype(jnp.float32),
                history_holeburn[moment_position].astype(jnp.float32),
                attenuation_factor,
                transverse_curvature,
            )
        )
    total = added_up(shape_curve, "gz")
    derivative_vector = CLOCK_DELTA * total / math.sqrt(cells)
    return (
        rightward_multiplier,
        leftward_multiplier,
        population_multiplier,
        holeburn_multiplier,
        derivative_vector,
    )

LANES = 128
TILE = 16
POWER = 12
STRETCH = 1211.0
SCALE_LANE = 8


def lateral_matrices(width, blocks):
    lanes = width // blocks
    k = np.arange(width)
    signed = np.where(k < width // 2, k, k - width).astype(np.float64)
    response = np.fft.ifft(np.exp(1j * signed * signed * (DIFF / (width / 2) ** 2)))
    step = np.arange(lanes)
    shift = lanes * np.arange(blocks)[:, None, None] + step[None, None, :] - step[None, :, None]
    kernels = np.fft.fft(response[shift % width], axis=0) / blocks
    top = np.concatenate([kernels.real, kernels.imag], axis=2)
    low = np.concatenate([-kernels.imag, kernels.real], axis=2)
    whole = np.concatenate([top, low], axis=1)
    first = whole.astype(ml_dtypes.bfloat16)
    rest = (whole - first.astype(np.float64)).astype(ml_dtypes.bfloat16)
    return np.stack([first, rest], axis=1)


def block_dft(values, sign):
    count = len(values)
    if count == 1:
        return values
    even = block_dft(values[0::2], sign)
    odd = block_dft(values[1::2], sign)
    out = [None] * count
    for k in range(count // 2):
        (er, ei), (wr, wi) = even[k], odd[k]
        if 4 * k == count:
            plus, minus = (er - wi, ei + wr), (er + wi, ei - wr)
            out[k], out[k + count // 2] = (plus, minus) if sign > 0 else (minus, plus)
            continue
        if k:
            c, s = math.cos(2 * math.pi * k / count), sign * math.sin(2 * math.pi * k / count)
            if 8 * k == count:
                wr, wi = (c * (wr - wi), c * (wr + wi)) if sign > 0 else (c * (wr + wi), c * (wi - wr))
            elif 8 * k == 3 * count:
                wr, wi = (c * (wr + wi), c * (wi - wr)) if sign > 0 else (c * (wr - wi), c * (wr + wi))
            else:
                wr, wi = c * wr - s * wi, c * wi + s * wr
        out[k] = (er + wr, ei + wi)
        out[k + count // 2] = (er - wr, ei - wi)
    return out


def lane(j):
    return pl.ds(pl.multiple_of(j * LANES, LANES), LANES)


def slab(j, rows):
    return pl.ds(pl.multiple_of(j * rows, rows), rows)


def fetch(pairs, sems, first=0):
    copies = [pltpu.make_async_copy(a, b, sems.at[first + i]) for i, (a, b) in enumerate(pairs)]
    for copy in copies:
        copy.start()
    return copies


def rows_of(info, rows, other):
    part = 1 - info[4] if other else info[4]
    return pl.ds(pl.multiple_of(part * rows, rows), rows)


def spread(field, work):
    rows = field.shape[1]
    blocks = work.shape[0]

    @pl.loop(0, rows // 8, unroll=2 if rows % 16 == 0 else 3)
    def _(g):
        at = slab(g, 8)
        values = [
            (field[0, at, j * LANES : (j + 1) * LANES], field[1, at, j * LANES : (j + 1) * LANES])
            for j in range(blocks)
        ]
        for q, (re, im) in enumerate(block_dft(values, -1)):
            work[q, at, :LANES] = re
            work[q, at, LANES:] = im


def fetch_matrices(source, matrices, sem):
    count = matrices.shape[0] // 2
    parts = [pl.ds(i * count, count) for i in range(2)]
    return fetch([(source.at[part], matrices.at[part]) for part in parts], sem)


def multiply(work, matrices, copies):
    rows = work.shape[1]
    count = work.shape[0] // len(copies)
    for i, copy in enumerate(copies):
        copy.wait()

        @pl.loop(i * count, (i + 1) * count, unroll=True)
        def _(q):
            value = work[q]
            first = value.astype(jnp.bfloat16)
            rest = (value - first.astype(jnp.float32)).astype(jnp.bfloat16)
            both = jnp.dot(
                jnp.concatenate([first, rest]), matrices[q, 0], preferred_element_type=jnp.float32
            )
            fine = jnp.dot(first, matrices[q, 1], preferred_element_type=jnp.float32)
            work[q] = both[:rows] + (both[rows:] + fine)


def gathered(work, at):
    values = [(work[q, at, :LANES], work[q, at, LANES:]) for q in range(work.shape[0])]
    return block_dft(values, 1)


def filtered(field, work, matrices, copies):
    spread(field, work)
    multiply(work, matrices, copies)


def write_filtered(info, work, forward, backward, inner, outer):
    rows = work.shape[1] // 2
    for target, base, offset in ((forward, 0, 0), (backward, rows, 8)):

        @pl.loop(0, rows // 8, unroll=2)
        def _(g):
            here = pl.ds(pl.multiple_of(g * 8 + offset, 8), 8)
            for j, pair in enumerate(gathered(work, pl.ds(pl.multiple_of(g * 8 + base, 8), 8))):
                for part in range(2):
                    target[part, here, j * LANES : (j + 1) * LANES] = pair[part]

    low = info[4] == 0
    for part in range(2):
        first, last = forward[part, 0:1, :], backward[part, rows + 7 : rows + 8, :]
        inner[part : part + 1, :] = jnp.where(low, last, first)
        outer[part : part + 1, :] = jnp.where(low, first, last)


def size_of(largest):
    top = jnp.max(jnp.max(largest, axis=1, keepdims=True), axis=0, keepdims=True)
    return jnp.maximum(top, 1e-30).astype(jnp.bfloat16).astype(jnp.float32)


def encoded(value, size):
    unit = value * (STRETCH / size)
    square = unit * unit
    fourth = square * square
    return (fourth * fourth * square * (unit * jnp.abs(unit))).astype(jnp.bfloat16)


def decoded(code, size):
    value = code.astype(jnp.float32)
    root = jnp.exp2(jnp.log(jnp.abs(value)) * (1.0 / (POWER * math.log(2.0)))) * (size / STRETCH)
    return jnp.where(value < 0.0, -root, root)


def side_tile(columns, rows):
    index = lax.broadcasted_iota(jnp.int32, (rows, LANES), 1)
    tile = jnp.zeros((rows, LANES), jnp.float32)
    for at, column in columns:
        tile = jnp.where(index == at, column, tile)
    return tile.astype(jnp.bfloat16)


def sizes_in(tile, count):
    value = tile.astype(jnp.float32)
    return [value[0:1, SCALE_LANE + i : SCALE_LANE + i + 1] for i in range(count)]


def updated(fr, fi, br, bi, wave, population, hole, loss, carrier, grating, lap):
    rr, ri, lr, li = wave
    surplus = population - 1.0
    gain_re = 1.0 + 0.5 * (GAIN_SLOPE_RATE * surplus - loss)
    gain_im = (0.5 * GAIN_SLOPE_RATE * ALPHA_LINEWIDTH) * surplus
    joined = COUPLING * hole
    drive = (2.0 * CLOCK_DELTA * GAIN_SLOPE_RATE) * surplus * carrier
    mix = (2.0 * CLOCK_DELTA) * grating
    new_fr = gain_re * fr - gain_im * fi + joined * bi - drive * rr + mix * lr
    new_fi = gain_re * fi + gain_im * fr - joined * br - drive * ri + mix * li
    new_br = gain_re * br - gain_im * bi + joined * fi - drive * lr + mix * rr
    new_bi = gain_re * bi + gain_im * br - joined * fr - drive * li + mix * ri
    light = rr * rr + ri * ri + lr * lr + li * li
    share = (
        fr * (rr + ALPHA_LINEWIDTH * ri)
        + fi * (ri - ALPHA_LINEWIDTH * rr)
        + br * (lr + ALPHA_LINEWIDTH * li)
        + bi * (li - ALPHA_LINEWIDTH * lr)
    )
    new_carrier = (
        carrier * ((1.0 - CLOCK_DELTA / DENSITY_LIFETIME) - (CLOCK_DELTA * GAIN_SLOPE_RATE) * light)
        + TRANSVERSE_DIFFUS * lap
        + (0.5 * GAIN_SLOPE_RATE) * share
    )
    new_grating = grating * (1.0 - CLOCK_DELTA / GRATING_LIFE) + COUPLING * (
        fi * lr - fr * li + bi * rr - br * ri
    )
    return new_fr, new_fi, new_br, new_bi, new_carrier, new_grating


def curvature(left, mid, right, weight_left, weight_right):
    index = lax.broadcasted_iota(jnp.int32, mid.shape, 1)
    below = jnp.where(index == 0, pltpu.roll(left, 1, 1) * weight_left, pltpu.roll(mid, 1, 1))
    above = jnp.where(
        index == LANES - 1,
        pltpu.roll(right, LANES - 1, 1) * weight_right,
        pltpu.roll(mid, LANES - 1, 1),
    )
    return below + above - 2.0 * mid


def send_fields_kernel(info, forward, backward, out, fields, sems):
    rows, columns = fields.shape[2:]
    half = columns // LANES
    at = rows_of(info, rows, True)
    copies = fetch(
        [(ref.at[:, at, :], fields.at[f]) for f, ref in enumerate((forward, backward))], sems
    )
    sizes = []
    for f in range(2):
        copies[f].wait()
        largest = jnp.maximum(jnp.abs(fields[f, 0]), jnp.abs(fields[f, 1]))
        size = size_of(largest)
        sizes.append((SCALE_LANE + f, size))
        for part in range(2):
            put_tiles(out, (2 * f + part) * half, encoded(fields[f, part], size))
    out[4 * half * rows :, :] = side_tile(sizes, rows)


def put_tiles(out, first, value):
    rows, columns = value.shape
    for j in range(columns // LANES):
        at = (first + j) * rows
        out[at : at + rows, :] = value[:, j * LANES : (j + 1) * LANES]


def history_rows(forward, backward, population, hole, s, at):
    return [
        forward.at[s, 0, at, :], forward.at[s, 1, at, :], backward.at[s, 0, at, :],
        backward.at[s, 1, at, :], population.at[s, at, :], hole.at[s, at, :],
    ]


def into_rows(parts, target, first, rows):
    return [(part, target.at[pl.ds(first + i * rows, rows), :]) for i, part in enumerate(parts)]


def send_later_kernel(steps, info, forward, backward, population, hole, final, *refs):
    targets, sems = refs[:-1], refs[-1]
    rows = targets[0].shape[0] // 6
    history = (forward, backward, population, hole)
    pairs = []
    for i, s in enumerate(steps):
        for k, other in enumerate((True, False)):
            at = rows_of(info, rows, other)
            pairs += into_rows(history_rows(*history, s, at), targets[2 * i + k], 0, rows)
    pairs += into_rows(history_rows(*history, 0, pl.ds(0, 2 * rows)), final, 0, 2 * rows)
    for copy in fetch(pairs, sems):
        copy.wait()


def send_first_kernel(
    s, info, loss, carrier, grating, forward, backward, population, hole,
    own_loss, own, own_carrier, own_grating, out, own_edge, states, ends, sems,
):
    rows, columns = own_carrier.shape
    theirs, mine = rows_of(info, rows, True), rows_of(info, rows, False)
    history = (forward, backward, population, hole)
    copies = fetch(
        [(carrier.at[theirs, :], states.at[0]), (grating.at[theirs, :], states.at[1])]
        + into_rows([loss.at[theirs, :]], out, 0, rows)
        + into_rows(history_rows(*history, s, theirs), out, 3 * rows, rows)
        + [(loss.at[mine, :], own_loss), (carrier.at[mine, :], own_carrier)]
        + [(grating.at[mine, :], own_grating)]
        + into_rows(history_rows(*history, s, mine), own, 0, rows)
        + [
            (part, ends.at[k, i])
            for k in range(2)
            for i, part in enumerate(
                history_rows(*history, 1, pl.ds(k * (2 * rows - TILE), TILE))
            )
        ],
        sems,
    )
    for copy in copies[:2]:
        copy.wait()
    sizes = []
    for i in range(2):
        size = size_of(jnp.abs(states[i]))
        sizes.append(jnp.broadcast_to(size, (1, columns)))
        out[(1 + i) * rows : (2 + i) * rows, :] = encoded(states[i], size)
    for copy in copies[2:]:
        copy.wait()
    low = info[4] == 0
    top = [ends[0, i].astype(jnp.float32)[:1] for i in range(6)]
    foot = [ends[1, i].astype(jnp.float32)[TILE - 1 :] for i in range(6)]
    own_edge[...] = jnp.concatenate([jnp.where(low, a, b) for a, b in zip(top, foot)])
    sizes += [jnp.where(low, b, a) for a, b in zip(top, foot)]
    sizes.append(jnp.zeros((TILE - 8, columns), jnp.float32))
    out[9 * rows :, :] = jnp.concatenate(sizes).astype(jnp.bfloat16)


def enter_kernel(
    info, forward, backward, other, source, tp, tq, inner, outer, field, work, matrices, sem, sems
):
    rows, width = field.shape[1] // 2, field.shape[2]
    columns = width // 2
    half = columns // LANES
    at = rows_of(info, rows, False)
    copies = fetch(
        [
            (ref.at[:, at, :], field.at[:, f * rows : (f + 1) * rows, :columns])
            for f, ref in enumerate((forward, backward))
        ],
        sems,
    )
    matrix_copies = fetch_matrices(source, matrices, sem)
    sizes = sizes_in(other[4 * half * rows :, :], 2)
    for f in range(2):
        for part in range(2):

            @pl.loop(0, half, unroll=2)
            def _(j):
                code = other[slab((2 * f + part) * half + j, rows), :]
                field[part, f * rows : (f + 1) * rows, lane(half + j)] = decoded(code, sizes[f])

    for held in copies:
        held.wait()
    filtered(field, work, matrices, matrix_copies)
    write_filtered(info, work, tp, tq, inner, outer)


def rows_update(
    info, tp, tq, inner, outer, carrier, grating, own, other, own_loss, other_loss,
    field, new_carrier, new_grating, sums_in, sums, cells, last
):
    rows, width = carrier.shape
    half = width // LANES // 2
    columns = half * LANES
    mid = jnp.where(info[0] == 0, 1.0, 0.0)
    wrap = 1.0 - mid
    low = info[4] == 0
    is_first, is_last = info[1], info[2]
    row_index = lax.broadcasted_iota(jnp.int32, (TILE, LANES), 0)
    zero = jnp.zeros((8, LANES), jnp.float32)

    def step(jj, most):
        for side in range(2):
            j = jj + side * half
            here = lane(j)
            left_at = lane(jnp.where(j == 0, 2 * half - 1, j - 1))
            right_at = lane(jnp.where(j == 2 * half - 1, 0, j + 1))
            swapped = lane(jj + (1 - side) * half)
            weight_left = jnp.where(jj == 0, wrap if side == 0 else mid, 1.0)
            weight_right = jnp.where(jj == half - 1, mid if side == 0 else wrap, 1.0)
            total = zero
            for r in range(0, rows, TILE):
                at = slice(r, r + TILE)

                held, begin = (own, other)[side]

                def part_of(i):
                    tile = begin + i * rows + r
                    return held[tile : tile + TILE, lane(jj)].astype(jnp.float32)

                loss = (own_loss, other_loss)[side][at, lane(jj)].astype(jnp.float32)
                f = [tp[part, r + 1 : r + 1 + TILE, here] for part in range(2)]
                b = [tq[part, r + 7 : r + 7 + TILE, here] for part in range(2)]
                if r + TILE == rows:
                    for part in range(2):
                        facet = FRONT_FACET * tq[part, rows + 7 : rows + 8, here]
                        edge = jnp.where(
                            low, inner[part : part + 1, swapped], outer[part : part + 1, here]
                        )
                        edge = jnp.where(is_last, facet, edge)
                        f[part] = jnp.where(row_index == TILE - 1, edge, f[part])
                if r == 0:
                    for part in range(2):
                        facet = REAR_FACET * tp[part, 0:1, here]
                        edge = jnp.where(
                            low, outer[part : part + 1, here], inner[part : part + 1, swapped]
                        )
                        edge = jnp.where(is_first, facet, edge)
                        b[part] = jnp.where(row_index == 0, edge, b[part])
                c = carrier[at, here]
                lap = curvature(
                    carrier[at, left_at], c, carrier[at, right_at], weight_left, weight_right
                )
                out = updated(
                    *f, *b, [part_of(i) for i in range(4)], part_of(4), part_of(5), loss,
                    c, grating[at, here], lap,
                )
                field[0, r : r + TILE, here] = out[0]
                field[1, r : r + TILE, here] = out[1]
                field[0, rows + r : rows + r + TILE, here] = out[2]
                field[1, rows + r : rows + r + TILE, here] = out[3]
                new_carrier[at, here] = out[4]
                new_grating[at, here] = out[5]
                z = (info[3] + r + row_index).astype(jnp.float32)
                weighted = (1.0 + 2.0 * z / (cells - 1)) * ((c + out[4]) if last else c)
                for k in range(0, TILE, 8):
                    total = total + weighted[k : k + 8]
                if last and side == 1:
                    for k in range(0, TILE, 8):
                        most = (
                            jnp.maximum(most[0], jnp.abs(out[4][k : k + 8])),
                            jnp.maximum(most[1], jnp.abs(out[5][k : k + 8])),
                        )
            summed = jnp.sum(total, axis=0, keepdims=True)
            sums[:, here] = summed if sums_in is None else summed + sums_in[:, here]
        return most

    return lax.fori_loop(0, half, step, (zero, zero), unroll=2)


def first_step_kernel(
    cells, info, tp, tq, inner, outer, my_carrier, my_grating, loss, own, own_edge, other, source,
    new_tp, new_tq, new_inner, new_outer, new_carrier, new_grating, sums,
    carrier, grating, field, work, matrices, sem,
):
    matrix_copies = fetch_matrices(source, matrices, sem)
    rows, columns = my_carrier.shape
    half = columns // LANES
    extra = other[9 * rows :, :].astype(jnp.float32)
    sizes = [extra[0:1, 0:1], extra[1:2, 0:1]]
    new_outer[2:8, :columns] = own_edge[...]
    new_outer[2:8, columns:] = extra[2:8]
    for i, (whole, mine) in enumerate(((carrier, my_carrier), (grating, my_grating))):
        whole[:, :columns] = mine[...]

        @pl.loop(0, half, unroll=2)
        def _(j):
            whole[:, lane(half + j)] = decoded(
                other[(1 + i) * rows : (2 + i) * rows, lane(j)], sizes[i]
            )

    rows_update(
        info, tp, tq, inner, outer, carrier, grating, (own, 0), (other, 3 * rows), loss, other,
        field, new_carrier, new_grating, None, sums, cells, False,
    )
    filtered(field, work, matrices, matrix_copies)
    write_filtered(info, work, new_tp, new_tq, new_inner, new_outer)


def middle_step_kernel(
    cells, info, tp, tq, inner, outer, carrier, grating, loss, own, other, other_loss, sums_in,
    source, new_tp, new_tq, new_inner, new_outer, new_carrier, new_grating, sums,
    field, work, matrices, sem,
):
    matrix_copies = fetch_matrices(source, matrices, sem)
    rows_update(
        info, tp, tq, inner, outer, carrier, grating, (own, 0), (other, 0), loss, other_loss,
        field, new_carrier, new_grating, sums_in, sums, cells, False,
    )
    filtered(field, work, matrices, matrix_copies)
    write_filtered(info, work, new_tp, new_tq, new_inner, new_outer)
    rows = carrier.shape[0]
    low = info[4] == 0
    for part in range(2):
        new_outer[2 + part : 3 + part, :] = jnp.where(
            low, new_tp[part, 1:2, :], new_tq[part, rows + 6 : rows + 7, :]
        )
    for i, ref in enumerate((new_carrier, new_grating)):
        new_outer[4 + i : 5 + i, :] = jnp.where(low, ref[0:1, :], ref[rows - 1 : rows, :])
    columns = loss.shape[1]
    for part, ref in enumerate((loss, other_loss)):
        top = ref[:TILE, :].astype(jnp.float32)[:1]
        foot = ref[rows - TILE :, :].astype(jnp.float32)[TILE - 1 :]
        new_outer[6:7, part * columns : (part + 1) * columns] = jnp.where(low, top, foot)


def row_beyond(info, tp, tq, outer, beyond):
    rows = tp.shape[1] - 8
    low = info[4] == 0
    xr, xi, carrier, grating = (outer[i : i + 1, :] for i in range(2, 6))
    yr, yi = (
        jnp.where(low, tp[part, 0:1, :], tq[part, rows + 7 : rows + 8, :]) for part in range(2)
    )
    rr, ri, lr, li, population, hole = (beyond[i : i + 1, :] for i in range(2, 8))
    loss = outer[6:7, :]
    surplus = population - 1.0
    gain_re = 1.0 + 0.5 * (GAIN_SLOPE_RATE * surplus - loss)
    gain_im = (0.5 * GAIN_SLOPE_RATE * ALPHA_LINEWIDTH) * surplus
    joined = COUPLING * hole
    drive = (2.0 * CLOCK_DELTA * GAIN_SLOPE_RATE) * surplus * carrier
    mix = (2.0 * CLOCK_DELTA) * grating
    near_re, near_im = jnp.where(low, lr, rr), jnp.where(low, li, ri)
    far_re, far_im = jnp.where(low, rr, lr), jnp.where(low, ri, li)
    new_re = gain_re * xr - gain_im * xi + joined * yi - drive * near_re + mix * far_re
    new_im = gain_re * xi + gain_im * xr - joined * yr - drive * near_im + mix * far_im
    return new_re, new_im


def leave_kernel(
    cells, info, tp, tq, inner, outer, beyond, carrier, grating, loss, own, other, other_loss,
    sums_in, source, kept, kept_carrier, kept_grating, sides, sent, edge, shares,
    sums, new_carrier, new_grating, field, work, matrices, sem,
):
    matrix_copies = fetch_matrices(source, matrices, sem)
    rows, width = carrier.shape
    columns = width // 2
    half = columns // LANES
    most = rows_update(
        info, tp, tq, inner, outer, carrier, grating, (own, 0), (other, 0), loss, other_loss,
        field, new_carrier, new_grating, sums_in, sums, cells, True,
    )
    mid = jnp.where(info[0] == 0, 1.0, 0.0)
    wrap = 1.0 - mid
    kept_carrier[...] = new_carrier[:, :columns]
    kept_grating[...] = new_grating[:, :columns]
    first, before = new_carrier[:, 0:1] * wrap, new_carrier[:, columns - 1 : columns] * mid
    after, final = new_carrier[:, columns : columns + 1] * mid, new_carrier[:, width - 1 :] * wrap
    sides[0] = jnp.broadcast_to(final, (rows, LANES))
    sides[1] = jnp.broadcast_to(after, (rows, LANES))
    pairs = []
    for at, value in ((0, before), (2, first)):
        coarse = value.astype(jnp.bfloat16).astype(jnp.float32)
        pairs += [(at, coarse), (at + 1, value - coarse)]
    for i, field_of in enumerate((new_carrier, new_grating)):
        size = size_of(most[i])
        pairs.append((SCALE_LANE + 2 + i, size))

        @pl.loop(0, half, unroll=2)
        def _(j):
            sent[slab((4 + i) * half + j, rows), :] = encoded(field_of[:, lane(half + j)], size)

    for part, value in enumerate(row_beyond(info, tp, tq, outer, beyond)):
        field[part, 2 * rows :, :] = jnp.broadcast_to(value, (8, width))
    filtered(field, work, matrices, matrix_copies)
    zero = jnp.zeros((8, LANES), jnp.float32)
    for f in range(2):

        def unmix(g, most):
            at = pl.ds(pl.multiple_of(g * 8 + f * rows, 8), 8)
            for j, pair in enumerate(gathered(work, at)):
                for part in range(2):
                    if j < half:
                        kept[part, at, j * LANES : (j + 1) * LANES] = pair[part]
                    else:
                        work[j, at, part * LANES : (part + 1) * LANES] = pair[part]
                        most = jnp.maximum(most, jnp.abs(pair[part]))
            return most

        size = size_of(lax.fori_loop(0, rows // 8, unmix, zero, unroll=2))
        pairs.append((SCALE_LANE + f, size))

        @pl.loop(0, half, unroll=2)
        def _(j):
            for part in range(2):
                value = work[half + j, f * rows : (f + 1) * rows, part * LANES : (part + 1) * LANES]
                sent[slab((2 * f + part) * half + j, rows), :] = encoded(value, size)

    ends = gathered(work, slice(2 * rows, 2 * rows + 8))
    for part in range(2):
        for j in range(half):
            edge[part : part + 1, j * LANES : (j + 1) * LANES] = ends[j][part][:1]
    far = jnp.concatenate([ends[j][part][:1] for part in range(2) for j in range(half, 2 * half)])
    size = size_of(jnp.abs(far))
    pairs.append((SCALE_LANE + 4, size))
    sent[6 * half * rows : (6 * half + 1) * rows, :] = side_tile(pairs, rows)
    spare = jnp.zeros((rows - 2 * half, LANES), jnp.float32)
    sent[(6 * half + 1) * rows :, :] = encoded(jnp.concatenate([far, spare]), size)
    tile = jnp.concatenate([sums[:, j * LANES : (j + 1) * LANES] for j in range(2 * half)])
    near, far = tile[:half], tile[half:]
    first = info[0] == 0
    to_first, to_second = jnp.where(first, near, far), jnp.where(first, far, near)
    shares[0] = to_first
    shares[1] = to_second


def spread_kernel(info, shares, out):
    for i in range(out.shape[0]):
        out[i] = shares[i % 2]


def total_kernel(cells, info, partial, out):
    total = partial[0]
    for i in range(1, partial.shape[0]):
        total = total + partial[i]
    out[...] = total * (CLOCK_DELTA / math.sqrt(cells))


def final_kernel(
    info, kept, kept_carrier, kept_grating, sides, came, edge, loss, history,
    out_forward, out_backward, out_carrier, out_grating,
    tp, tq, carrier, grating,
):
    rows, columns = kept_carrier.shape
    half = columns // LANES
    mine = info[4] * rows
    theirs = (1 - info[4]) * rows
    low = info[4] == 0
    extra = came[6 * half * rows : (6 * half + 1) * rows, :]
    size_forward, size_backward, size_carrier, size_grating, size_edge = sizes_in(extra, 5)
    ends = decoded(came[(6 * half + 1) * rows :, :], size_edge)
    extra = extra.astype(jnp.float32)

    def at(start, offset, count):
        return pl.ds(pl.multiple_of(start + offset, 8), count)

    for part in range(2):
        tp[part, at(mine, 0, rows), :] = kept[part, :rows, :]
        tq[part, at(mine, 8, rows), :] = kept[part, rows:, :]
    carrier[at(mine, 0, rows), LANES : LANES + columns] = kept_carrier[...]
    carrier[at(mine, 0, rows), :LANES] = sides[0]
    carrier[at(mine, 0, rows), LANES + columns :] = sides[1]
    carrier[at(theirs, 0, rows), :LANES] = jnp.broadcast_to(
        extra[:, 0:1] + extra[:, 1:2], (rows, LANES)
    )
    carrier[at(theirs, 0, rows), LANES + columns :] = jnp.broadcast_to(
        extra[:, 2:3] + extra[:, 3:4], (rows, LANES)
    )
    grating[at(mine, 0, rows), :] = kept_grating[...]

    @pl.loop(0, half, unroll=2)
    def _(j):
        carrier[at(theirs, 0, rows), lane(1 + j)] = decoded(
            came[slab(4 * half + j, rows), :], size_carrier
        )
        grating[at(theirs, 0, rows), lane(j)] = decoded(
            came[slab(5 * half + j, rows), :], size_grating
        )
        for part in range(2):
            tp[part, at(theirs, 0, rows), lane(j)] = decoded(
                came[slab(part * half + j, rows), :], size_forward
            )
            tq[part, at(theirs, 8, rows), lane(j)] = decoded(
                came[slab((2 + part) * half + j, rows), :], size_backward
            )

    all_rows = 2 * rows
    for part in range(2):
        near = edge[part : part + 1, :]
        far = jnp.concatenate([ends[part * half + j : part * half + j + 1] for j in range(half)], axis=1)
        next_edge = jnp.where(low, far, near)
        before_edge = jnp.where(low, near, far)
        front = FRONT_FACET * tq[part, all_rows + 7 : all_rows + 8, :]
        rear = REAR_FACET * tp[part, 0:1, :]
        tp[part, all_rows : all_rows + 1, :] = jnp.where(info[2], front, next_edge)
        tq[part, 7:8, :] = jnp.where(info[1], rear, before_edge)

    @pl.loop(0, half, unroll=2)
    def _(j):
        here = lane(j)
        for r in range(0, all_rows, TILE):
            row = slice(r, r + TILE)
            c = carrier[row, lane(j + 1)]
            lap = curvature(carrier[row, lane(j)], c, carrier[row, lane(j + 2)], 1.0, 1.0)
            parts = [
                history[i * all_rows + r : i * all_rows + r + TILE, here].astype(jnp.float32)
                for i in range(6)
            ]
            out = updated(
                tp[0, r + 1 : r + 1 + TILE, here], tp[1, r + 1 : r + 1 + TILE, here],
                tq[0, r + 7 : r + 7 + TILE, here], tq[1, r + 7 : r + 7 + TILE, here],
                parts[:4], parts[4], parts[5],
                loss[row, here].astype(jnp.float32), c, grating[row, here], lap,
            )
            out_forward[0, row, here] = out[0]
            out_forward[1, row, here] = out[1]
            out_backward[0, row, here] = out[2]
            out_backward[1, row, here] = out[3]
            out_carrier[row, here] = out[4]
            out_grating[row, here] = out[5]


def position(rows, whole):
    x, block, count = lax.axis_index("gx"), lax.axis_index("gz"), lax.axis_size("gz")
    high = lax.rem(x + block, 2)
    if whole:
        return x, block == 0, block == count - 1, block * rows, high
    place = 2 * block + high
    return x, place == 0, place == 2 * count - 1, place * rows, high


def whole_spec(shape):
    return pl.BlockSpec(shape, lambda i, n=len(shape): (0,) * n)


def call(name, kernel, rows, inputs, outputs, scratch, flops=0, grant=24, whole=False):
    arrays = [x[0] if isinstance(x, tuple) else x for x in inputs]
    specs = [x[1] if isinstance(x, tuple) else whole_spec(x.shape) for x in inputs]
    shapes = [jax.ShapeDtypeStruct(*out) for out in outputs]
    moved = sum(math.prod(s.shape) * s.dtype.itemsize for s in shapes)

    def body(*refs):
        kernel(position(rows, whole), *refs)

    return pl.pallas_call(
        body,
        grid=(1,),
        in_specs=specs,
        out_specs=[whole_spec(s.shape) for s in shapes],
        scratch_shapes=scratch,
        out_shape=shapes,
        compiler_params=pltpu.CompilerParams(vmem_limit_bytes=grant * 1024 * 1024),
        cost_estimate=pl.CostEstimate(
            flops=flops, bytes_accessed=moved + 4 * 1024 * 1024, transcendentals=0
        ),
        name=name,
    )(*arrays)


def per_pair(
    ending_rightward_adjoint,
    ending_leftward_adjoint,
    ending_population_adjoint,
    ending_holeburn_adjoint,
    history_rightward,
    history_leftward,
    history_population,
    history_holeburn,
    segment_passive_attenuation,
):
    cell_rows, columns = ending_population_adjoint.shape
    passes = history_population.shape[0]
    rows = cell_rows // 2
    half = columns // LANES
    blocks = 2 * half
    width = 2 * columns
    count = lax.axis_size("gz")
    cells = cell_rows * count
    x = lax.axis_index("gx")
    f32, bf16 = jnp.float32, jnp.bfloat16
    swap = [(0, 1), (1, 0)]
    in_place = pl.BlockSpec(memory_space=pltpu.HBM)

    def held(*arrays):
        return [(a, in_place) for a in arrays]

    def tiles(n):
        return ((n * rows, LANES), bf16)

    ends = held(ending_rightward_adjoint, ending_leftward_adjoint)
    planes = held(ending_population_adjoint, ending_holeburn_adjoint)
    history = held(history_rightward, history_leftward, history_population, history_holeburn)
    losses = held(segment_passive_attenuation)
    matrices = pltpu.with_memory_space_constraint(
        jnp.asarray(lateral_matrices(width, blocks)), pltpu.HBM
    )
    matrix_input = held(matrices)
    work = [
        pltpu.VMEM((blocks, 2 * rows, 2 * LANES), f32),
        pltpu.VMEM(matrices.shape, bf16),
        pltpu.SemaphoreType.DMA((2,)),
    ]
    field_scratch = pltpu.VMEM((2, 2 * rows, width), f32)
    def state_out(outer_rows):
        state = ((2, rows + 8, width), f32)
        return [state, state, ((2, width), f32), ((outer_rows, width), f32)]

    plane = ((rows, width), f32)
    plane_scratch = pltpu.VMEM((rows, width), f32)
    half_plane = ((rows, columns), f32)
    work_flops = 2 * 3 * 2 * rows * blocks * (2 * LANES) ** 2

    (coded,) = call(
        "send_fields", send_fields_kernel, rows, ends, [tiles(4 * half + 1)],
        [pltpu.VMEM((2, 2, rows, columns), f32), pltpu.SemaphoreType.DMA((2,))], grant=62,
    )
    other_fields = lax.ppermute(coded, "gx", swap)
    loss, own_first, my_carrier, my_grating, sent_first, own_edge = call(
        "send_first", functools.partial(send_first_kernel, passes - 1), rows,
        [*losses, *planes, *history],
        [((rows, columns), bf16), ((6 * rows, columns), bf16), half_plane, half_plane,
         ((9 * rows + TILE, columns), bf16), ((6, columns), f32)],
        [pltpu.VMEM((2, rows, columns), f32), pltpu.VMEM((2, 6, TILE, columns), bf16),
         pltpu.SemaphoreType.DMA((30,))], grant=62,
    )
    steps = range(passes - 2, 0, -1)
    history_last, *later = call(
        "send_later", functools.partial(send_later_kernel, steps), rows, history,
        [((6 * cell_rows, columns), bf16)] + [((6 * rows, columns), bf16)] * (2 * len(steps)),
        [pltpu.SemaphoreType.DMA((12 * len(steps) + 6,))], grant=62,
    )
    sent_first, history_last, later, other_fields = lax.optimization_barrier(
        (sent_first, history_last, later, other_fields)
    )
    other_first = lax.ppermute(sent_first, "gx", swap)

    line = ("gz", "gx")
    neighbours = []
    for b in range(count - 1):
        top = (1 + b) % 2
        neighbours += [(2 * b + top, 2 * b + 2 + top), (2 * b + 2 + top, 2 * b + top)]

    def edges(inner, outer):
        outer = lax.ppermute(outer, line, neighbours)
        return lax.ppermute(inner, "gx", swap), outer

    tp, tq, inner, outer = call(
        "enter", enter_kernel, rows, [*ends, other_fields, *matrix_input],
        state_out(2), [field_scratch, *work, pltpu.SemaphoreType.DMA((2,))], work_flops,
    )
    inner, outer = edges(inner, outer)

    other_loss = (other_first, pl.BlockSpec((rows, columns), lambda i: (0, 0)))
    carrier = grating = sums = other = own = None
    for index, s in enumerate(range(passes - 1, 0, -1)):
        if index < len(steps):
            sent, own_next = later[2 * index : 2 * index + 2]
            sent, inner, outer = lax.optimization_barrier((sent, inner, outer))
            coming = lax.ppermute(sent, "gx", swap)
        shared = [tp, tq, inner, outer]
        if index == 0:
            tp, tq, inner, outer, carrier, grating, sums = call(
                "first_step", functools.partial(first_step_kernel, cells), rows,
                [*shared, my_carrier, my_grating, loss, own_first, own_edge, other_first,
                 *matrix_input],
                [*state_out(8), plane, plane, ((1, width), f32)],
                [plane_scratch, plane_scratch, field_scratch, *work], work_flops,
            )
        elif s > 1:
            tp, tq, inner, outer, carrier, grating, sums = call(
                "middle_step", functools.partial(middle_step_kernel, cells), rows,
                [*shared, carrier, grating, loss, own, other, other_loss, sums, *matrix_input],
                [*state_out(7), plane, plane, ((1, width), f32)],
                [field_scratch, *work], work_flops,
            )
        else:
            kept, kept_carrier, kept_grating, sides, sent, edge, shares = call(
                "leave", functools.partial(leave_kernel, cells), rows,
                [*shared, beyond, carrier, grating, loss, own, other, other_loss, sums, *matrix_input],
                [((2, 2 * rows, columns), f32), half_plane, half_plane, ((2, rows, LANES), f32),
                 tiles(6 * half + 2), ((2, columns), f32), ((2, half, LANES), f32)],
                [pltpu.VMEM((1, width), f32), plane_scratch, plane_scratch,
                 pltpu.VMEM((2, 2 * rows + 8, width), f32),
                 pltpu.VMEM((blocks, 2 * rows + TILE, 2 * LANES), f32), *work[1:]],
                work_flops,
            )
        if s > 1:
            inner, outer = edges(inner, outer)
            own, other = own_next, coming
            if index == 0:
                beyond = outer

    came = lax.ppermute(sent, "gx", swap)
    (shares,) = call(
        "spread", spread_kernel, rows, [shares], [((2 * count, half, LANES), f32)], [],
    )
    shares = lax.all_to_all(shares, line, 0, 0, tiled=True)

    outs = call(
        "final", final_kernel, cell_rows,
        [kept, kept_carrier, kept_grating, sides, came, edge,
         segment_passive_attenuation, history_last],
        [((2, cell_rows, columns), f32), ((2, cell_rows, columns), f32),
         ((cell_rows, columns), f32), ((cell_rows, columns), f32)],
        [pltpu.VMEM((2, cell_rows + 8, columns), f32), pltpu.VMEM((2, cell_rows + 8, columns), f32),
         pltpu.VMEM((cell_rows, columns + 2 * LANES), f32), pltpu.VMEM((cell_rows, columns), f32)],
        whole=True,
    )
    shares, *outs = lax.optimization_barrier((shares, *outs))
    (total,) = call(
        "total", functools.partial(total_kernel, cells), rows, [shares], [((half, LANES), f32)], [],
    )
    return (*outs, total.reshape(columns))


def shared_by_pairs(mesh, arguments):
    population = arguments[6]
    passes, cells, width = population.shape
    rows, columns = cells // mesh.shape["gz"], width // mesh.shape["gx"]
    return (
        mesh.shape["gx"] == 2
        and passes >= 4
        and 4 * columns <= rows * LANES
        and rows % (2 * TILE) == 0
        and columns % LANES == 0
        and (columns // LANES) & (columns // LANES - 1) == 0
        and width <= 4096
    )


def solution(mesh):
    def run(*arguments):
        body = per_pair if shared_by_pairs(mesh, arguments) else per_device
        return jax.shard_map(
            body,
            mesh=mesh,
            in_specs=(
                P(None, "gz", "gx"),
                P(None, "gz", "gx"),
                P("gz", "gx"),
                P("gz", "gx"),
                P(None, None, "gz", "gx"),
                P(None, None, "gz", "gx"),
                P(None, "gz", "gx"),
                P(None, "gz", "gx"),
                P("gz", "gx"),
            ),
            out_specs=(
                P(None, "gz", "gx"), P(None, "gz", "gx"), P("gz", "gx"), P("gz", "gx"), P("gx"),
            ),
            check_vma=False,
        )(*arguments)

    return run
```

```python
import functools
import math

import jax
import jax.numpy as jnp
import ml_dtypes
import numpy as np
from jax import lax
from jax.experimental import pallas as pl
from jax.experimental.pallas import tpu as pltpu
from jax.sharding import PartitionSpec as P

DIFF = 512


FRONT_FACET = 0.3
REAR_FACET = 0.9
GAIN_SLOPE_RATE = 0.3
ALPHA_LINEWIDTH = 2.0
COUPLING = 0.5
CLOCK_DELTA = 0.3
DENSITY_LIFETIME = 2.0
GRATING_LIFE = 0.75
TRANSVERSE_DIFFUS = 0.2


def passed_along(value, axis, steps):
    count = lax.axis_size(axis)
    initial, last = (max(0, -steps), min(count, count - steps))
    return lax.ppermute(value, axis, [(source, source + steps) for source in range(initial, last)])


def with_halo(block, sides, width):
    for axis, dim in sides:
        count = lax.axis_size(axis)
        forward = [(i, i + 1) for i in range(count - 1)]
        backward = [(target, source) for source, target in forward]
        low = lax.ppermute(
            lax.slice_in_dim(block, block.shape[dim] - width, None, axis=dim), axis, forward
        )
        high = lax.ppermute(lax.slice_in_dim(block, 0, width, axis=dim), axis, backward)
        block = jnp.concatenate([low, block, high], axis=dim)
    return block


def rotate(source_re, source_im, cosine, sine, form, sign):
    exact = lax.Precision.HIGHEST
    out_re = jnp.einsum(form, source_re, cosine, precision=exact) + sign * jnp.einsum(
        form, source_im, sine, precision=exact
    )
    out_im = jnp.einsum(form, source_im, cosine, precision=exact) - sign * jnp.einsum(
        form, source_re, sine, precision=exact
    )
    return (out_re, out_im)


def transform(stacked):
    count = stacked.shape[1]
    width = stacked.shape[2]
    second = min(128, width // 2)
    first = width // second
    two_pi = 2.0 * math.pi
    index_a = jnp.arange(first, dtype=jnp.int32)
    index_b = jnp.arange(second, dtype=jnp.int32)
    angle_a = two_pi * (index_a[:, None] * index_a[None, :] % first).astype(jnp.float32) / first
    angle_b = two_pi * (index_b[:, None] * index_b[None, :] % second).astype(jnp.float32) / second
    angle_t = two_pi * (index_a[:, None] * index_b[None, :] % width).astype(jnp.float32) / width
    cos_a, sin_a = (jnp.cos(angle_a), jnp.sin(angle_a))
    cos_b, sin_b = (jnp.cos(angle_b), jnp.sin(angle_b))
    cos_t, sin_t = (jnp.cos(angle_t), jnp.sin(angle_t))
    wavenum = index_a[:, None] + first * index_b[None, :]
    signed = jnp.where(wavenum < width // 2, wavenum, wavenum - width)
    phase = (signed * signed).astype(jnp.float32) * (DIFF / (width / 2) ** 2)
    cos_p, sin_p = (jnp.cos(phase), jnp.sin(phase))
    real_in = stacked[0].reshape(count, first, second)
    imag_in = stacked[1].reshape(count, first, second)
    step_re, step_im = rotate(real_in, imag_in, cos_a, sin_a, "nab,ak->nkb", 1.0)
    twist_re = step_re * cos_t + step_im * sin_t
    twist_im = step_im * cos_t - step_re * sin_t
    spec_re, spec_im = rotate(twist_re, twist_im, cos_b, sin_b, "nkb,bj->nkj", 1.0)
    moved_re = spec_re * cos_p - spec_im * sin_p
    moved_im = spec_re * sin_p + spec_im * cos_p
    back_re, back_im = rotate(moved_re, moved_im, cos_b, sin_b, "nkj,jb->nkb", -1.0)
    untw_re = back_re * cos_t - back_im * sin_t
    untw_im = back_im * cos_t + back_re * sin_t
    final_re, final_im = rotate(untw_re, untw_im, cos_a, sin_a, "nkb,ka->nab", -1.0)
    return jnp.stack([final_re.reshape(count, width), final_im.reshape(count, width)]) / width


def added_up(value, axis):
    count = lax.axis_size(axis)
    if count & (count - 1):
        return lax.psum(value, axis)
    reach = 1
    while reach < count:
        value = value + lax.ppermute(value, axis, [(i, i ^ reach) for i in range(count)])
        reach *= 2
    return value


def lateral_work(parts):
    return (transform(parts[0]), transform(parts[1]))


def multiplier_revision(
    population_multiplier,
    holeburn_multiplier,
    measured_rightward,
    measured_leftward,
    rightward_wave,
    leftward_wave,
    population_level,
    holeburn_magnitude,
    attenuation_factor,
    transverse_curvature,
):
    rightward_inphase, rightward_quadrature = (rightward_wave[0], rightward_wave[1])
    leftward_inphase, leftward_quadrature = (leftward_wave[0], leftward_wave[1])
    measured_rightward_inphase, measured_rightward_quadrature = (
        measured_rightward[0],
        measured_rightward[1],
    )
    measured_leftward_inphase, measured_leftward_quadrature = (
        measured_leftward[0],
        measured_leftward[1],
    )
    surplus_population = population_level - 1.0
    amplification_inphase = 1.0 + 0.5 * (GAIN_SLOPE_RATE * surplus_population - attenuation_factor)
    amplification_quadrature = 0.5 * GAIN_SLOPE_RATE * ALPHA_LINEWIDTH * surplus_population
    joined_waves = COUPLING * holeburn_magnitude
    population_derivative = (
        2.0 * CLOCK_DELTA * GAIN_SLOPE_RATE * surplus_population * population_multiplier
    )
    holeburn_derivative = 2.0 * CLOCK_DELTA * holeburn_multiplier
    revised_rightward_inphase = (
        amplification_inphase * measured_rightward_inphase
        - amplification_quadrature * measured_rightward_quadrature
        + joined_waves * measured_leftward_quadrature
        - population_derivative * rightward_inphase
        + holeburn_derivative * leftward_inphase
    )
    revised_rightward_quadrature = (
        amplification_inphase * measured_rightward_quadrature
        + amplification_quadrature * measured_rightward_inphase
        - joined_waves * measured_leftward_inphase
        - population_derivative * rightward_quadrature
        + holeburn_derivative * leftward_quadrature
    )
    revised_leftward_inphase = (
        amplification_inphase * measured_leftward_inphase
        - amplification_quadrature * measured_leftward_quadrature
        + joined_waves * measured_rightward_quadrature
        - population_derivative * leftward_inphase
        + holeburn_derivative * rightward_inphase
    )
    revised_leftward_quadrature = (
        amplification_inphase * measured_leftward_quadrature
        + amplification_quadrature * measured_leftward_inphase
        - joined_waves * measured_rightward_inphase
        - population_derivative * leftward_quadrature
        + holeburn_derivative * rightward_quadrature
    )
    light_intensity = (
        rightward_inphase * rightward_inphase
        + rightward_quadrature * rightward_quadrature
        + leftward_inphase * leftward_inphase
        + leftward_quadrature * leftward_quadrature
    )
    amplification_share = (
        measured_rightward_inphase * (rightward_inphase + ALPHA_LINEWIDTH * rightward_quadrature)
        + measured_rightward_quadrature
        * (rightward_quadrature - ALPHA_LINEWIDTH * rightward_inphase)
        + measured_leftward_inphase * (leftward_inphase + ALPHA_LINEWIDTH * leftward_quadrature)
        + measured_leftward_quadrature * (leftward_quadrature - ALPHA_LINEWIDTH * leftward_inphase)
    )
    revised_population = (
        population_multiplier
        * (1.0 - CLOCK_DELTA / DENSITY_LIFETIME - CLOCK_DELTA * GAIN_SLOPE_RATE * light_intensity)
        + TRANSVERSE_DIFFUS * transverse_curvature
        + 0.5 * GAIN_SLOPE_RATE * amplification_share
    )
    fresh_holeburn = holeburn_multiplier * (1.0 - CLOCK_DELTA / GRATING_LIFE) + COUPLING * (
        measured_rightward_quadrature * leftward_inphase
        - measured_rightward_inphase * leftward_quadrature
        + measured_leftward_quadrature * rightward_inphase
        - measured_leftward_inphase * rightward_quadrature
    )
    return (
        jnp.stack([revised_rightward_inphase, revised_rightward_quadrature]),
        jnp.stack([revised_leftward_inphase, revised_leftward_quadrature]),
        revised_population,
        fresh_holeburn,
    )


def per_device(
    ending_rightward_adjoint,
    ending_leftward_adjoint,
    ending_population_adjoint,
    ending_holeburn_adjoint,
    history_rightward,
    history_leftward,
    history_population,
    history_holeburn,
    segment_passive_attenuation,
):
    columns = ending_rightward_adjoint.shape[2]
    rows = ending_rightward_adjoint.shape[1]
    blocks = lax.axis_size("gz")
    position = lax.axis_index("gz")
    cells = rows * blocks
    zpos = (position * rows + jnp.arange(rows, dtype=jnp.int32)).astype(jnp.float32)
    scaling_factor = 1.0 + 2.0 * zpos / (cells - 1)
    rightward_multiplier, leftward_multiplier = (ending_rightward_adjoint, ending_leftward_adjoint)
    population_multiplier, holeburn_multiplier = (
        ending_population_adjoint,
        ending_holeburn_adjoint,
    )
    attenuation_factor = segment_passive_attenuation.astype(jnp.float32)
    shape_curve = jnp.zeros((columns,), jnp.float32)
    for moment_position in range(history_rightward.shape[0] - 1, -1, -1):
        shape_curve = shape_curve + jnp.sum(scaling_factor[:, None] * population_multiplier, axis=0)
        above = passed_along(rightward_multiplier[:, :1, :], "gz", -1)
        below = passed_along(leftward_multiplier[:, -1:, :], "gz", 1)
        top_row = jnp.where(
            position == blocks - 1, FRONT_FACET * leftward_multiplier[:, -1:, :], above
        )
        bottom_row = jnp.where(position == 0, REAR_FACET * rightward_multiplier[:, :1, :], below)
        lam_fwd = jnp.concatenate([rightward_multiplier[:, 1:, :], top_row], axis=1)
        lam_bwd = jnp.concatenate([bottom_row, leftward_multiplier[:, :-1, :]], axis=1)
        whole_fwd, whole_bwd = (
            lax.all_gather(lam_fwd, "gx", axis=2, tiled=True),
            lax.all_gather(lam_bwd, "gx", axis=2, tiled=True),
        )
        start = lax.axis_index("gx") * columns
        done_fwd, done_bwd = lateral_work((whole_fwd, whole_bwd))
        measured_rightward = lax.dynamic_slice_in_dim(done_fwd, start, columns, 2)
        measured_leftward = lax.dynamic_slice_in_dim(done_bwd, start, columns, 2)
        bordered_array = with_halo(population_multiplier, (("gx", 1),), 1)
        transverse_curvature = (
            bordered_array[:, 2:] + bordered_array[:, :-2] - 2.0 * population_multiplier
        )
        rightward_multiplier, leftward_multiplier, population_multiplier, holeburn_multiplier = (
            multiplier_revision(
                population_multiplier,
                holeburn_multiplier,
                measured_rightward,
                measured_leftward,
                history_rightward[moment_position].astype(jnp.float32),
                history_leftward[moment_position].astype(jnp.float32),
                history_population[moment_position].astype(jnp.float32),
                history_holeburn[moment_position].astype(jnp.float32),
                attenuation_factor,
                transverse_curvature,
            )
        )
    total = added_up(shape_curve, "gz")
    derivative_vector = CLOCK_DELTA * total / math.sqrt(cells)
    return (
        rightward_multiplier,
        leftward_multiplier,
        population_multiplier,
        holeburn_multiplier,
        derivative_vector,
    )

LANES = 128
TILE = 16
POWER = 12
STRETCH = 1211.0
SCALE_LANE = 8


def lateral_matrices(width, blocks):
    lanes = width // blocks
    k = np.arange(width)
    signed = np.where(k < width // 2, k, k - width).astype(np.float64)
    response = np.fft.ifft(np.exp(1j * signed * signed * (DIFF / (width / 2) ** 2)))
    step = np.arange(lanes)
    shift = lanes * np.arange(blocks)[:, None, None] + step[None, None, :] - step[None, :, None]
    kernels = np.fft.fft(response[shift % width], axis=0) / blocks
    top = np.concatenate([kernels.real, kernels.imag], axis=2)
    low = np.concatenate([-kernels.imag, kernels.real], axis=2)
    whole = np.concatenate([top, low], axis=1)
    first = whole.astype(ml_dtypes.bfloat16)
    rest = (whole - first.astype(np.float64)).astype(ml_dtypes.bfloat16)
    return np.stack([first, rest], axis=1)


def block_dft(values, sign):
    count = len(values)
    if count == 1:
        return values
    even = block_dft(values[0::2], sign)
    odd = block_dft(values[1::2], sign)
    out = [None] * count
    for k in range(count // 2):
        (er, ei), (wr, wi) = even[k], odd[k]
        if 4 * k == count:
            plus, minus = (er - wi, ei + wr), (er + wi, ei - wr)
            out[k], out[k + count // 2] = (plus, minus) if sign > 0 else (minus, plus)
            continue
        if k:
            c, s = math.cos(2 * math.pi * k / count), sign * math.sin(2 * math.pi * k / count)
            if 8 * k == count:
                wr, wi = (c * (wr - wi), c * (wr + wi)) if sign > 0 else (c * (wr + wi), c * (wi - wr))
            elif 8 * k == 3 * count:
                wr, wi = (c * (wr + wi), c * (wi - wr)) if sign > 0 else (c * (wr - wi), c * (wr + wi))
            else:
                wr, wi = c * wr - s * wi, c * wi + s * wr
        out[k] = (er + wr, ei + wi)
        out[k + count // 2] = (er - wr, ei - wi)
    return out


def lane(j):
    return pl.ds(pl.multiple_of(j * LANES, LANES), LANES)


def slab(j, rows):
    return pl.ds(pl.multiple_of(j * rows, rows), rows)


def fetch(pairs, sems, first=0):
    copies = [pltpu.make_async_copy(a, b, sems.at[first + i]) for i, (a, b) in enumerate(pairs)]
    for copy in copies:
        copy.start()
    return copies


def rows_of(info, rows, other):
    part = 1 - info[4] if other else info[4]
    return pl.ds(pl.multiple_of(part * rows, rows), rows)


def spread(field, work):
    rows = field.shape[1]
    blocks = work.shape[0]

    @pl.loop(0, rows // 8, unroll=2 if rows % 16 == 0 else 3)
    def _(g):
        at = slab(g, 8)
        values = [
            (field[0, at, j * LANES : (j + 1) * LANES], field[1, at, j * LANES : (j + 1) * LANES])
            for j in range(blocks)
        ]
        for q, (re, im) in enumerate(block_dft(values, -1)):
            work[q, at, :LANES] = re
            work[q, at, LANES:] = im


def fetch_matrices(source, matrices, sem):
    count = matrices.shape[0] // 2
    parts = [pl.ds(i * count, count) for i in range(2)]
    return fetch([(source.at[part], matrices.at[part]) for part in parts], sem)


def multiply(work, matrices, copies):
    rows = work.shape[1]
    count = work.shape[0] // len(copies)
    for i, copy in enumerate(copies):
        copy.wait()

        @pl.loop(i * count, (i + 1) * count, unroll=True)
        def _(q):
            value = work[q]
            first = value.astype(jnp.bfloat16)
            rest = (value - first.astype(jnp.float32)).astype(jnp.bfloat16)
            both = jnp.dot(
                jnp.concatenate([first, rest]), matrices[q, 0], preferred_element_type=jnp.float32
            )
            fine = jnp.dot(first, matrices[q, 1], preferred_element_type=jnp.float32)
            work[q] = both[:rows] + (both[rows:] + fine)


def gathered(work, at):
    values = [(work[q, at, :LANES], work[q, at, LANES:]) for q in range(work.shape[0])]
    return block_dft(values, 1)


def filtered(field, work, matrices, copies):
    spread(field, work)
    multiply(work, matrices, copies)


def write_filtered(info, work, forward, backward, inner, outer):
    rows = work.shape[1] // 2
    for target, base, offset in ((forward, 0, 0), (backward, rows, 8)):

        @pl.loop(0, rows // 8, unroll=2)
        def _(g):
            here = pl.ds(pl.multiple_of(g * 8 + offset, 8), 8)
            for j, pair in enumerate(gathered(work, pl.ds(pl.multiple_of(g * 8 + base, 8), 8))):
                for part in range(2):
                    target[part, here, j * LANES : (j + 1) * LANES] = pair[part]

    low = info[4] == 0
    for part in range(2):
        first, last = forward[part, 0:1, :], backward[part, rows + 7 : rows + 8, :]
        inner[part : part + 1, :] = jnp.where(low, last, first)
        outer[part : part + 1, :] = jnp.where(low, first, last)


def size_of(largest):
    top = jnp.max(jnp.max(largest, axis=1, keepdims=True), axis=0, keepdims=True)
    return jnp.maximum(top, 1e-30).astype(jnp.bfloat16).astype(jnp.float32)


def encoded(value, size):
    unit = value * (STRETCH / size)
    square = unit * unit
    fourth = square * square
    return (fourth * fourth * square * (unit * jnp.abs(unit))).astype(jnp.bfloat16)


def decoded(code, size):
    value = code.astype(jnp.float32)
    root = jnp.exp2(jnp.log(jnp.abs(value)) * (1.0 / (POWER * math.log(2.0)))) * (size / STRETCH)
    return jnp.where(value < 0.0, -root, root)


def side_tile(columns, rows):
    index = lax.broadcasted_iota(jnp.int32, (rows, LANES), 1)
    tile = jnp.zeros((rows, LANES), jnp.float32)
    for at, column in columns:
        tile = jnp.where(index == at, column, tile)
    return tile.astype(jnp.bfloat16)


def sizes_in(tile, count):
    value = tile.astype(jnp.float32)
    return [value[0:1, SCALE_LANE + i : SCALE_LANE + i + 1] for i in range(count)]


def updated(fr, fi, br, bi, wave, population, hole, loss, carrier, grating, lap):
    rr, ri, lr, li = wave
    surplus = population - 1.0
    gain_re = 1.0 + 0.5 * (GAIN_SLOPE_RATE * surplus - loss)
    gain_im = (0.5 * GAIN_SLOPE_RATE * ALPHA_LINEWIDTH) * surplus
    joined = COUPLING * hole
    drive = (2.0 * CLOCK_DELTA * GAIN_SLOPE_RATE) * surplus * carrier
    mix = (2.0 * CLOCK_DELTA) * grating
    new_fr = gain_re * fr - gain_im * fi + joined * bi - drive * rr + mix * lr
    new_fi = gain_re * fi + gain_im * fr - joined * br - drive * ri + mix * li
    new_br = gain_re * br - gain_im * bi + joined * fi - drive * lr + mix * rr
    new_bi = gain_re * bi + gain_im * br - joined * fr - drive * li + mix * ri
    light = rr * rr + ri * ri + lr * lr + li * li
    share = (
        fr * (rr + ALPHA_LINEWIDTH * ri)
        + fi * (ri - ALPHA_LINEWIDTH * rr)
        + br * (lr + ALPHA_LINEWIDTH * li)
        + bi * (li - ALPHA_LINEWIDTH * lr)
    )
    new_carrier = (
        carrier * ((1.0 - CLOCK_DELTA / DENSITY_LIFETIME) - (CLOCK_DELTA * GAIN_SLOPE_RATE) * light)
        + TRANSVERSE_DIFFUS * lap
        + (0.5 * GAIN_SLOPE_RATE) * share
    )
    new_grating = grating * (1.0 - CLOCK_DELTA / GRATING_LIFE) + COUPLING * (
        fi * lr - fr * li + bi * rr - br * ri
    )
    return new_fr, new_fi, new_br, new_bi, new_carrier, new_grating


def curvature(left, mid, right, weight_left, weight_right):
    index = lax.broadcasted_iota(jnp.int32, mid.shape, 1)
    below = jnp.where(index == 0, pltpu.roll(left, 1, 1) * weight_left, pltpu.roll(mid, 1, 1))
    above = jnp.where(
        index == LANES - 1,
        pltpu.roll(right, LANES - 1, 1) * weight_right,
        pltpu.roll(mid, LANES - 1, 1),
    )
    return below + above - 2.0 * mid


def send_fields_kernel(info, forward, backward, out, fields, sems):
    rows, columns = fields.shape[2:]
    half = columns // LANES
    at = rows_of(info, rows, True)
    copies = fetch(
        [(ref.at[:, at, :], fields.at[f]) for f, ref in enumerate((forward, backward))], sems
    )
    sizes = []
    for f in range(2):
        copies[f].wait()
        largest = jnp.maximum(jnp.abs(fields[f, 0]), jnp.abs(fields[f, 1]))
        size = size_of(largest)
        sizes.append((SCALE_LANE + f, size))
        for part in range(2):
            put_tiles(out, (2 * f + part) * half, encoded(fields[f, part], size))
    out[4 * half * rows :, :] = side_tile(sizes, rows)


def put_tiles(out, first, value):
    rows, columns = value.shape
    for j in range(columns // LANES):
        at = (first + j) * rows
        out[at : at + rows, :] = value[:, j * LANES : (j + 1) * LANES]


def history_rows(forward, backward, population, hole, s, at):
    return [
        forward.at[s, 0, at, :], forward.at[s, 1, at, :], backward.at[s, 0, at, :],
        backward.at[s, 1, at, :], population.at[s, at, :], hole.at[s, at, :],
    ]


def into_rows(parts, target, first, rows):
    return [(part, target.at[pl.ds(first + i * rows, rows), :]) for i, part in enumerate(parts)]


def send_later_kernel(steps, info, forward, backward, population, hole, final, *refs):
    targets, sems = refs[:-1], refs[-1]
    rows = targets[0].shape[0] // 6
    history = (forward, backward, population, hole)
    pairs = []
    for i, s in enumerate(steps):
        for k, other in enumerate((True, False)):
            at = rows_of(info, rows, other)
            pairs += into_rows(history_rows(*history, s, at), targets[2 * i + k], 0, rows)
    pairs += into_rows(history_rows(*history, 0, pl.ds(0, 2 * rows)), final, 0, 2 * rows)
    for copy in fetch(pairs, sems):
        copy.wait()


def send_first_kernel(
    s, info, loss, carrier, grating, forward, backward, population, hole,
    own_loss, own, own_carrier, own_grating, out, own_edge, states, ends, sems,
):
    rows, columns = own_carrier.shape
    theirs, mine = rows_of(info, rows, True), rows_of(info, rows, False)
    history = (forward, backward, population, hole)
    copies = fetch(
        [(carrier.at[theirs, :], states.at[0]), (grating.at[theirs, :], states.at[1])]
        + into_rows([loss.at[theirs, :]], out, 0, rows)
        + into_rows(history_rows(*history, s, theirs), out, 3 * rows, rows)
        + [(loss.at[mine, :], own_loss), (carrier.at[mine, :], own_carrier)]
        + [(grating.at[mine, :], own_grating)]
        + into_rows(history_rows(*history, s, mine), own, 0, rows)
        + [
            (part, ends.at[k, i])
            for k in range(2)
            for i, part in enumerate(
                history_rows(*history, 1, pl.ds(k * (2 * rows - TILE), TILE))
            )
        ],
        sems,
    )
    for copy in copies[:2]:
        copy.wait()
    sizes = []
    for i in range(2):
        size = size_of(jnp.abs(states[i]))
        sizes.append(jnp.broadcast_to(size, (1, columns)))
        out[(1 + i) * rows : (2 + i) * rows, :] = encoded(states[i], size)
    for copy in copies[2:]:
        copy.wait()
    low = info[4] == 0
    top = [ends[0, i].astype(jnp.float32)[:1] for i in range(6)]
    foot = [ends[1, i].astype(jnp.float32)[TILE - 1 :] for i in range(6)]
    own_edge[...] = jnp.concatenate([jnp.where(low, a, b) for a, b in zip(top, foot)])
    sizes += [jnp.where(low, b, a) for a, b in zip(top, foot)]
    sizes.append(jnp.zeros((TILE - 8, columns), jnp.float32))
    out[9 * rows :, :] = jnp.concatenate(sizes).astype(jnp.bfloat16)


def enter_kernel(
    info, forward, backward, other, source, tp, tq, inner, outer, field, work, matrices, sem, sems
):
    rows, width = field.shape[1] // 2, field.shape[2]
    columns = width // 2
    half = columns // LANES
    at = rows_of(info, rows, False)
    copies = fetch(
        [
            (ref.at[:, at, :], field.at[:, f * rows : (f + 1) * rows, :columns])
            for f, ref in enumerate((forward, backward))
        ],
        sems,
    )
    matrix_copies = fetch_matrices(source, matrices, sem)
    sizes = sizes_in(other[4 * half * rows :, :], 2)
    for f in range(2):
        for part in range(2):

            @pl.loop(0, half, unroll=4)
            def _(j):
                code = other[slab((2 * f + part) * half + j, rows), :]
                field[part, f * rows : (f + 1) * rows, lane(half + j)] = decoded(code, sizes[f])

    for held in copies:
        held.wait()
    filtered(field, work, matrices, matrix_copies)
    write_filtered(info, work, tp, tq, inner, outer)


def rows_update(
    info, tp, tq, inner, outer, carrier, grating, own, other, own_loss, other_loss,
    field, new_carrier, new_grating, sums_in, sums, cells, last
):
    rows, width = carrier.shape
    half = width // LANES // 2
    columns = half * LANES
    mid = jnp.where(info[0] == 0, 1.0, 0.0)
    wrap = 1.0 - mid
    low = info[4] == 0
    is_first, is_last = info[1], info[2]
    row_index = lax.broadcasted_iota(jnp.int32, (TILE, LANES), 0)
    zero = jnp.zeros((8, LANES), jnp.float32)

    def step(jj, most):
        for side in range(2):
            j = jj + side * half
            here = lane(j)
            left_at = lane(jnp.where(j == 0, 2 * half - 1, j - 1))
            right_at = lane(jnp.where(j == 2 * half - 1, 0, j + 1))
            swapped = lane(jj + (1 - side) * half)
            weight_left = jnp.where(jj == 0, wrap if side == 0 else mid, 1.0)
            weight_right = jnp.where(jj == half - 1, mid if side == 0 else wrap, 1.0)
            total = zero
            for r in range(0, rows, TILE):
                at = slice(r, r + TILE)

                held, begin = (own, other)[side]

                def part_of(i):
                    tile = begin + i * rows + r
                    return held[tile : tile + TILE, lane(jj)].astype(jnp.float32)

                loss = (own_loss, other_loss)[side][at, lane(jj)].astype(jnp.float32)
                f = [tp[part, r + 1 : r + 1 + TILE, here] for part in range(2)]
                b = [tq[part, r + 7 : r + 7 + TILE, here] for part in range(2)]
                if r + TILE == rows:
                    for part in range(2):
                        facet = FRONT_FACET * tq[part, rows + 7 : rows + 8, here]
                        edge = jnp.where(
                            low, inner[part : part + 1, swapped], outer[part : part + 1, here]
                        )
                        edge = jnp.where(is_last, facet, edge)
                        f[part] = jnp.where(row_index == TILE - 1, edge, f[part])
                if r == 0:
                    for part in range(2):
                        facet = REAR_FACET * tp[part, 0:1, here]
                        edge = jnp.where(
                            low, outer[part : part + 1, here], inner[part : part + 1, swapped]
                        )
                        edge = jnp.where(is_first, facet, edge)
                        b[part] = jnp.where(row_index == 0, edge, b[part])
                c = carrier[at, here]
                lap = curvature(
                    carrier[at, left_at], c, carrier[at, right_at], weight_left, weight_right
                )
                out = updated(
                    *f, *b, [part_of(i) for i in range(4)], part_of(4), part_of(5), loss,
                    c, grating[at, here], lap,
                )
                field[0, r : r + TILE, here] = out[0]
                field[1, r : r + TILE, here] = out[1]
                field[0, rows + r : rows + r + TILE, here] = out[2]
                field[1, rows + r : rows + r + TILE, here] = out[3]
                new_carrier[at, here] = out[4]
                new_grating[at, here] = out[5]
                z = (info[3] + r + row_index).astype(jnp.float32)
                weighted = (1.0 + 2.0 * z / (cells - 1)) * ((c + out[4]) if last else c)
                for k in range(0, TILE, 8):
                    total = total + weighted[k : k + 8]
                if last and side == 1:
                    for k in range(0, TILE, 8):
                        most = (
                            jnp.maximum(most[0], jnp.abs(out[4][k : k + 8])),
                            jnp.maximum(most[1], jnp.abs(out[5][k : k + 8])),
                        )
            summed = jnp.sum(total, axis=0, keepdims=True)
            sums[:, here] = summed if sums_in is None else summed + sums_in[:, here]
        return most

    return lax.fori_loop(0, half, step, (zero, zero), unroll=4)


def first_step_kernel(
    cells, info, tp, tq, inner, outer, my_carrier, my_grating, loss, own, own_edge, other, source,
    new_tp, new_tq, new_inner, new_outer, new_carrier, new_grating, sums,
    carrier, grating, field, work, matrices, sem,
):
    matrix_copies = fetch_matrices(source, matrices, sem)
    rows, columns = my_carrier.shape
    half = columns // LANES
    extra = other[9 * rows :, :].astype(jnp.float32)
    sizes = [extra[0:1, 0:1], extra[1:2, 0:1]]
    new_outer[2:8, :columns] = own_edge[...]
    new_outer[2:8, columns:] = extra[2:8]
    for i, (whole, mine) in enumerate(((carrier, my_carrier), (grating, my_grating))):
        whole[:, :columns] = mine[...]

        @pl.loop(0, half, unroll=2)
        def _(j):
            whole[:, lane(half + j)] = decoded(
                other[(1 + i) * rows : (2 + i) * rows, lane(j)], sizes[i]
            )

    rows_update(
        info, tp, tq, inner, outer, carrier, grating, (own, 0), (other, 3 * rows), loss, other,
        field, new_carrier, new_grating, None, sums, cells, False,
    )
    filtered(field, work, matrices, matrix_copies)
    write_filtered(info, work, new_tp, new_tq, new_inner, new_outer)


def middle_step_kernel(
    cells, info, tp, tq, inner, outer, carrier, grating, loss, own, other, other_loss, sums_in,
    source, new_tp, new_tq, new_inner, new_outer, new_carrier, new_grating, sums,
    field, work, matrices, sem,
):
    matrix_copies = fetch_matrices(source, matrices, sem)
    rows_update(
        info, tp, tq, inner, outer, carrier, grating, (own, 0), (other, 0), loss, other_loss,
        field, new_carrier, new_grating, sums_in, sums, cells, False,
    )
    filtered(field, work, matrices, matrix_copies)
    write_filtered(info, work, new_tp, new_tq, new_inner, new_outer)
    rows = carrier.shape[0]
    low = info[4] == 0
    for part in range(2):
        new_outer[2 + part : 3 + part, :] = jnp.where(
            low, new_tp[part, 1:2, :], new_tq[part, rows + 6 : rows + 7, :]
        )
    for i, ref in enumerate((new_carrier, new_grating)):
        new_outer[4 + i : 5 + i, :] = jnp.where(low, ref[0:1, :], ref[rows - 1 : rows, :])
    columns = loss.shape[1]
    for part, ref in enumerate((loss, other_loss)):
        top = ref[:TILE, :].astype(jnp.float32)[:1]
        foot = ref[rows - TILE :, :].astype(jnp.float32)[TILE - 1 :]
        new_outer[6:7, part * columns : (part + 1) * columns] = jnp.where(low, top, foot)


def row_beyond(info, tp, tq, outer, beyond):
    rows = tp.shape[1] - 8
    low = info[4] == 0
    xr, xi, carrier, grating = (outer[i : i + 1, :] for i in range(2, 6))
    yr, yi = (
        jnp.where(low, tp[part, 0:1, :], tq[part, rows + 7 : rows + 8, :]) for part in range(2)
    )
    rr, ri, lr, li, population, hole = (beyond[i : i + 1, :] for i in range(2, 8))
    loss = outer[6:7, :]
    surplus = population - 1.0
    gain_re = 1.0 + 0.5 * (GAIN_SLOPE_RATE * surplus - loss)
    gain_im = (0.5 * GAIN_SLOPE_RATE * ALPHA_LINEWIDTH) * surplus
    joined = COUPLING * hole
    drive = (2.0 * CLOCK_DELTA * GAIN_SLOPE_RATE) * surplus * carrier
    mix = (2.0 * CLOCK_DELTA) * grating
    near_re, near_im = jnp.where(low, lr, rr), jnp.where(low, li, ri)
    far_re, far_im = jnp.where(low, rr, lr), jnp.where(low, ri, li)
    new_re = gain_re * xr - gain_im * xi + joined * yi - drive * near_re + mix * far_re
    new_im = gain_re * xi + gain_im * xr - joined * yr - drive * near_im + mix * far_im
    return new_re, new_im


def leave_kernel(
    cells, info, tp, tq, inner, outer, beyond, carrier, grating, loss, own, other, other_loss,
    sums_in, source, kept, kept_carrier, kept_grating, sides, sent, edge, shares,
    sums, new_carrier, new_grating, field, work, matrices, sem,
):
    matrix_copies = fetch_matrices(source, matrices, sem)
    rows, width = carrier.shape
    columns = width // 2
    half = columns // LANES
    most = rows_update(
        info, tp, tq, inner, outer, carrier, grating, (own, 0), (other, 0), loss, other_loss,
        field, new_carrier, new_grating, sums_in, sums, cells, True,
    )
    mid = jnp.where(info[0] == 0, 1.0, 0.0)
    wrap = 1.0 - mid
    kept_carrier[...] = new_carrier[:, :columns]
    kept_grating[...] = new_grating[:, :columns]
    first, before = new_carrier[:, 0:1] * wrap, new_carrier[:, columns - 1 : columns] * mid
    after, final = new_carrier[:, columns : columns + 1] * mid, new_carrier[:, width - 1 :] * wrap
    sides[0] = jnp.broadcast_to(final, (rows, LANES))
    sides[1] = jnp.broadcast_to(after, (rows, LANES))
    pairs = []
    for at, value in ((0, before), (2, first)):
        coarse = value.astype(jnp.bfloat16).astype(jnp.float32)
        pairs += [(at, coarse), (at + 1, value - coarse)]
    for i, field_of in enumerate((new_carrier, new_grating)):
        size = size_of(most[i])
        pairs.append((SCALE_LANE + 2 + i, size))

        @pl.loop(0, half, unroll=2)
        def _(j):
            sent[slab((4 + i) * half + j, rows), :] = encoded(field_of[:, lane(half + j)], size)

    for part, value in enumerate(row_beyond(info, tp, tq, outer, beyond)):
        field[part, 2 * rows :, :] = jnp.broadcast_to(value, (8, width))
    filtered(field, work, matrices, matrix_copies)
    zero = jnp.zeros((8, LANES), jnp.float32)
    for f in range(2):

        def unmix(g, most):
            at = pl.ds(pl.multiple_of(g * 8 + f * rows, 8), 8)
            for j, pair in enumerate(gathered(work, at)):
                for part in range(2):
                    if j < half:
                        kept[part, at, j * LANES : (j + 1) * LANES] = pair[part]
                    else:
                        work[j, at, part * LANES : (part + 1) * LANES] = pair[part]
                        most = jnp.maximum(most, jnp.abs(pair[part]))
            return most

        size = size_of(lax.fori_loop(0, rows // 8, unmix, zero, unroll=2))
        pairs.append((SCALE_LANE + f, size))

        @pl.loop(0, half, unroll=2)
        def _(j):
            for part in range(2):
                value = work[half + j, f * rows : (f + 1) * rows, part * LANES : (part + 1) * LANES]
                sent[slab((2 * f + part) * half + j, rows), :] = encoded(value, size)

    ends = gathered(work, slice(2 * rows, 2 * rows + 8))
    for part in range(2):
        for j in range(half):
            edge[part : part + 1, j * LANES : (j + 1) * LANES] = ends[j][part][:1]
    far = jnp.concatenate([ends[j][part][:1] for part in range(2) for j in range(half, 2 * half)])
    size = size_of(jnp.abs(far))
    pairs.append((SCALE_LANE + 4, size))
    sent[6 * half * rows : (6 * half + 1) * rows, :] = side_tile(pairs, rows)
    spare = jnp.zeros((rows - 2 * half, LANES), jnp.float32)
    sent[(6 * half + 1) * rows :, :] = encoded(jnp.concatenate([far, spare]), size)
    tile = jnp.concatenate([sums[:, j * LANES : (j + 1) * LANES] for j in range(2 * half)])
    near, far = tile[:half], tile[half:]
    first = info[0] == 0
    to_first, to_second = jnp.where(first, near, far), jnp.where(first, far, near)
    shares[0] = to_first
    shares[1] = to_second


def spread_kernel(info, shares, out):
    for i in range(out.shape[0]):
        out[i] = shares[i % 2]


def total_kernel(cells, info, partial, out):
    total = partial[0]
    for i in range(1, partial.shape[0]):
        total = total + partial[i]
    out[...] = total * (CLOCK_DELTA / math.sqrt(cells))


def final_kernel(
    info, kept, kept_carrier, kept_grating, sides, came, edge, loss, history,
    out_forward, out_backward, out_carrier, out_grating,
    tp, tq, carrier, grating,
):
    rows, columns = kept_carrier.shape
    half = columns // LANES
    mine = info[4] * rows
    theirs = (1 - info[4]) * rows
    low = info[4] == 0
    extra = came[6 * half * rows : (6 * half + 1) * rows, :]
    size_forward, size_backward, size_carrier, size_grating, size_edge = sizes_in(extra, 5)
    ends = decoded(came[(6 * half + 1) * rows :, :], size_edge)
    extra = extra.astype(jnp.float32)

    def at(start, offset, count):
        return pl.ds(pl.multiple_of(start + offset, 8), count)

    for part in range(2):
        tp[part, at(mine, 0, rows), :] = kept[part, :rows, :]
        tq[part, at(mine, 8, rows), :] = kept[part, rows:, :]
    carrier[at(mine, 0, rows), LANES : LANES + columns] = kept_carrier[...]
    carrier[at(mine, 0, rows), :LANES] = sides[0]
    carrier[at(mine, 0, rows), LANES + columns :] = sides[1]
    carrier[at(theirs, 0, rows), :LANES] = jnp.broadcast_to(
        extra[:, 0:1] + extra[:, 1:2], (rows, LANES)
    )
    carrier[at(theirs, 0, rows), LANES + columns :] = jnp.broadcast_to(
        extra[:, 2:3] + extra[:, 3:4], (rows, LANES)
    )
    grating[at(mine, 0, rows), :] = kept_grating[...]

    @pl.loop(0, half, unroll=4)
    def _(j):
        carrier[at(theirs, 0, rows), lane(1 + j)] = decoded(
            came[slab(4 * half + j, rows), :], size_carrier
        )
        grating[at(theirs, 0, rows), lane(j)] = decoded(
            came[slab(5 * half + j, rows), :], size_grating
        )
        for part in range(2):
            tp[part, at(theirs, 0, rows), lane(j)] = decoded(
                came[slab(part * half + j, rows), :], size_forward
            )
            tq[part, at(theirs, 8, rows), lane(j)] = decoded(
                came[slab((2 + part) * half + j, rows), :], size_backward
            )

    all_rows = 2 * rows
    for part in range(2):
        near = edge[part : part + 1, :]
        far = jnp.concatenate([ends[part * half + j : part * half + j + 1] for j in range(half)], axis=1)
        next_edge = jnp.where(low, far, near)
        before_edge = jnp.where(low, near, far)
        front = FRONT_FACET * tq[part, all_rows + 7 : all_rows + 8, :]
        rear = REAR_FACET * tp[part, 0:1, :]
        tp[part, all_rows : all_rows + 1, :] = jnp.where(info[2], front, next_edge)
        tq[part, 7:8, :] = jnp.where(info[1], rear, before_edge)

    @pl.loop(0, half, unroll=4)
    def _(j):
        here = lane(j)
        for r in range(0, all_rows, TILE):
            row = slice(r, r + TILE)
            c = carrier[row, lane(j + 1)]
            lap = curvature(carrier[row, lane(j)], c, carrier[row, lane(j + 2)], 1.0, 1.0)
            parts = [
                history[i * all_rows + r : i * all_rows + r + TILE, here].astype(jnp.float32)
                for i in range(6)
            ]
            out = updated(
                tp[0, r + 1 : r + 1 + TILE, here], tp[1, r + 1 : r + 1 + TILE, here],
                tq[0, r + 7 : r + 7 + TILE, here], tq[1, r + 7 : r + 7 + TILE, here],
                parts[:4], parts[4], parts[5],
                loss[row, here].astype(jnp.float32), c, grating[row, here], lap,
            )
            out_forward[0, row, here] = out[0]
            out_forward[1, row, here] = out[1]
            out_backward[0, row, here] = out[2]
            out_backward[1, row, here] = out[3]
            out_carrier[row, here] = out[4]
            out_grating[row, here] = out[5]


def position(rows, whole):
    x, block, count = lax.axis_index("gx"), lax.axis_index("gz"), lax.axis_size("gz")
    high = lax.rem(x + block, 2)
    if whole:
        return x, block == 0, block == count - 1, block * rows, high
    place = 2 * block + high
    return x, place == 0, place == 2 * count - 1, place * rows, high


def whole_spec(shape):
    return pl.BlockSpec(shape, lambda i, n=len(shape): (0,) * n)


def call(name, kernel, rows, inputs, outputs, scratch, flops=0, grant=24, whole=False):
    arrays = [x[0] if isinstance(x, tuple) else x for x in inputs]
    specs = [x[1] if isinstance(x, tuple) else whole_spec(x.shape) for x in inputs]
    shapes = [jax.ShapeDtypeStruct(*out) for out in outputs]
    moved = sum(math.prod(s.shape) * s.dtype.itemsize for s in shapes)

    def body(*refs):
        kernel(position(rows, whole), *refs)

    return pl.pallas_call(
        body,
        grid=(1,),
        in_specs=specs,
        out_specs=[whole_spec(s.shape) for s in shapes],
        scratch_shapes=scratch,
        out_shape=shapes,
        compiler_params=pltpu.CompilerParams(vmem_limit_bytes=grant * 1024 * 1024),
        cost_estimate=pl.CostEstimate(
            flops=flops, bytes_accessed=moved + 4 * 1024 * 1024, transcendentals=0
        ),
        name=name,
    )(*arrays)


def per_pair(
    ending_rightward_adjoint,
    ending_leftward_adjoint,
    ending_population_adjoint,
    ending_holeburn_adjoint,
    history_rightward,
    history_leftward,
    history_population,
    history_holeburn,
    segment_passive_attenuation,
):
    cell_rows, columns = ending_population_adjoint.shape
    passes = history_population.shape[0]
    rows = cell_rows // 2
    half = columns // LANES
    blocks = 2 * half
    width = 2 * columns
    count = lax.axis_size("gz")
    cells = cell_rows * count
    x = lax.axis_index("gx")
    f32, bf16 = jnp.float32, jnp.bfloat16
    swap = [(0, 1), (1, 0)]
    in_place = pl.BlockSpec(memory_space=pltpu.HBM)

    def held(*arrays):
        return [(a, in_place) for a in arrays]

    def tiles(n):
        return ((n * rows, LANES), bf16)

    ends = held(ending_rightward_adjoint, ending_leftward_adjoint)
    planes = held(ending_population_adjoint, ending_holeburn_adjoint)
    history = held(history_rightward, history_leftward, history_population, history_holeburn)
    losses = held(segment_passive_attenuation)
    matrices = pltpu.with_memory_space_constraint(
        jnp.asarray(lateral_matrices(width, blocks)), pltpu.HBM
    )
    matrix_input = held(matrices)
    work = [
        pltpu.VMEM((blocks, 2 * rows, 2 * LANES), f32),
        pltpu.VMEM(matrices.shape, bf16),
        pltpu.SemaphoreType.DMA((2,)),
    ]
    field_scratch = pltpu.VMEM((2, 2 * rows, width), f32)
    def state_out(outer_rows):
        state = ((2, rows + 8, width), f32)
        return [state, state, ((2, width), f32), ((outer_rows, width), f32)]

    plane = ((rows, width), f32)
    plane_scratch = pltpu.VMEM((rows, width), f32)
    half_plane = ((rows, columns), f32)
    work_flops = 2 * 3 * 2 * rows * blocks * (2 * LANES) ** 2

    (coded,) = call(
        "send_fields", send_fields_kernel, rows, ends, [tiles(4 * half + 1)],
        [pltpu.VMEM((2, 2, rows, columns), f32), pltpu.SemaphoreType.DMA((2,))], grant=62,
    )
    other_fields = lax.ppermute(coded, "gx", swap)
    loss, own_first, my_carrier, my_grating, sent_first, own_edge = call(
        "send_first", functools.partial(send_first_kernel, passes - 1), rows,
        [*losses, *planes, *history],
        [((rows, columns), bf16), ((6 * rows, columns), bf16), half_plane, half_plane,
         ((9 * rows + TILE, columns), bf16), ((6, columns), f32)],
        [pltpu.VMEM((2, rows, columns), f32), pltpu.VMEM((2, 6, TILE, columns), bf16),
         pltpu.SemaphoreType.DMA((30,))], grant=62,
    )
    steps = range(passes - 2, 0, -1)
    history_last, *later = call(
        "send_later", functools.partial(send_later_kernel, steps), rows, history,
        [((6 * cell_rows, columns), bf16)] + [((6 * rows, columns), bf16)] * (2 * len(steps)),
        [pltpu.SemaphoreType.DMA((12 * len(steps) + 6,))], grant=62,
    )
    sent_first, history_last, later, other_fields = lax.optimization_barrier(
        (sent_first, history_last, later, other_fields)
    )
    other_first = lax.ppermute(sent_first, "gx", swap)

    line = ("gz", "gx")
    neighbours = []
    for b in range(count - 1):
        top = (1 + b) % 2
        neighbours += [(2 * b + top, 2 * b + 2 + top), (2 * b + 2 + top, 2 * b + top)]

    def edges(inner, outer):
        outer = lax.ppermute(outer, line, neighbours)
        return lax.ppermute(inner, "gx", swap), outer

    tp, tq, inner, outer = call(
        "enter", enter_kernel, rows, [*ends, other_fields, *matrix_input],
        state_out(2), [field_scratch, *work, pltpu.SemaphoreType.DMA((2,))], work_flops,
    )
    inner, outer = edges(inner, outer)

    other_loss = (other_first, pl.BlockSpec((rows, columns), lambda i: (0, 0)))
    carrier = grating = sums = other = own = None
    for index, s in enumerate(range(passes - 1, 0, -1)):
        if index < len(steps):
            sent, own_next = later[2 * index : 2 * index + 2]
            sent, inner, outer = lax.optimization_barrier((sent, inner, outer))
            coming = lax.ppermute(sent, "gx", swap)
        shared = [tp, tq, inner, outer]
        if index == 0:
            tp, tq, inner, outer, carrier, grating, sums = call(
                "first_step", functools.partial(first_step_kernel, cells), rows,
                [*shared, my_carrier, my_grating, loss, own_first, own_edge, other_first,
                 *matrix_input],
                [*state_out(8), plane, plane, ((1, width), f32)],
                [plane_scratch, plane_scratch, field_scratch, *work], work_flops,
            )
        elif s > 1:
            tp, tq, inner, outer, carrier, grating, sums = call(
                "middle_step", functools.partial(middle_step_kernel, cells), rows,
                [*shared, carrier, grating, loss, own, other, other_loss, sums, *matrix_input],
                [*state_out(7), plane, plane, ((1, width), f32)],
                [field_scratch, *work], work_flops,
            )
        else:
            kept, kept_carrier, kept_grating, sides, sent, edge, shares = call(
                "leave", functools.partial(leave_kernel, cells), rows,
                [*shared, beyond, carrier, grating, loss, own, other, other_loss, sums, *matrix_input],
                [((2, 2 * rows, columns), f32), half_plane, half_plane, ((2, rows, LANES), f32),
                 tiles(6 * half + 2), ((2, columns), f32), ((2, half, LANES), f32)],
                [pltpu.VMEM((1, width), f32), plane_scratch, plane_scratch,
                 pltpu.VMEM((2, 2 * rows + 8, width), f32),
                 pltpu.VMEM((blocks, 2 * rows + TILE, 2 * LANES), f32), *work[1:]],
                work_flops,
            )
        if s > 1:
            inner, outer = edges(inner, outer)
            own, other = own_next, coming
            if index == 0:
                beyond = outer

    came = lax.ppermute(sent, "gx", swap)
    (shares,) = call(
        "spread", spread_kernel, rows, [shares], [((2 * count, half, LANES), f32)], [],
    )
    shares = lax.all_to_all(shares, line, 0, 0, tiled=True)

    outs = call(
        "final", final_kernel, cell_rows,
        [kept, kept_carrier, kept_grating, sides, came, edge,
         segment_passive_attenuation, history_last],
        [((2, cell_rows, columns), f32), ((2, cell_rows, columns), f32),
         ((cell_rows, columns), f32), ((cell_rows, columns), f32)],
        [pltpu.VMEM((2, cell_rows + 8, columns), f32), pltpu.VMEM((2, cell_rows + 8, columns), f32),
         pltpu.VMEM((cell_rows, columns + 2 * LANES), f32), pltpu.VMEM((cell_rows, columns), f32)],
        whole=True,
    )
    shares, *outs = lax.optimization_barrier((shares, *outs))
    (total,) = call(
        "total", functools.partial(total_kernel, cells), rows, [shares], [((half, LANES), f32)], [],
    )
    return (*outs, total.reshape(columns))


def shared_by_pairs(mesh, arguments):
    population = arguments[6]
    passes, cells, width = population.shape
    rows, columns = cells // mesh.shape["gz"], width // mesh.shape["gx"]
    return (
        mesh.shape["gx"] == 2
        and passes >= 4
        and 4 * columns <= rows * LANES
        and rows % (2 * TILE) == 0
        and columns % LANES == 0
        and (columns // LANES) & (columns // LANES - 1) == 0
        and columns % (4 * LANES) == 0
        and width <= 4096
    )


def solution(mesh):
    def run(*arguments):
        body = per_pair if shared_by_pairs(mesh, arguments) else per_device
        return jax.shard_map(
            body,
            mesh=mesh,
            in_specs=(
                P(None, "gz", "gx"),
                P(None, "gz", "gx"),
                P("gz", "gx"),
                P("gz", "gx"),
                P(None, None, "gz", "gx"),
                P(None, None, "gz", "gx"),
                P(None, "gz", "gx"),
                P(None, "gz", "gx"),
                P("gz", "gx"),
            ),
            out_specs=(
                P(None, "gz", "gx"), P(None, "gz", "gx"), P("gz", "gx"), P("gz", "gx"), P("gx"),
            ),
            check_vma=False,
        )(*arguments)

    return run
```
